32 devices in a mesh: seq: 2 (over x), dp: 16 (over z, y, core).
Axes of the slice: x: 2, y: 2, z: 4, core: 2. Of those that a mesh axis runs over, the one named last changes fastest.
Arguments:
- tokens: bfloat16 [16, 1024, 768], P('dp', 'seq'), may hold values from -6 to 6
- cotangent: bfloat16 [16, 1024, 768], P('dp', 'seq'), may hold values from -6 to 6
- attn_weight: bfloat16 [768, 3072], P('dp'), may hold values from -0.21875 to 0.21875
- mlp_weight: bfloat16 [2, 768, 3072], P(None, 'dp'), may hold values from -0.21650635 to 0.21650635
- norms: bfloat16 [4, 768], P(None, 'dp'), may hold values from -1 to 1.5
- taps: bfloat16 [64, 768], P(None, 'dp'), may hold values from -0.375 to 0.375
- ssm_params: float32 [2, 768, 64], P(None, 'seq'), may hold values from -10 to 0.15309311, as said below
- attn_moments: float32 [2, 768, 3072], P(None, 'dp'), may hold values from -1.5 to 2, as said below
- mlp_moments: float32 [2, 2, 768, 3072], P(None, None, 'dp'), may hold values from -1.5 to 2, as said below
- norm_moments: float32 [2, 4, 768], P(None, None, 'dp'), may hold values from -1.5 to 2, as said below
- tap_moments: float32 [2, 64, 768], P(None, None, 'dp'), may hold values from -1.5 to 2, as said below
- ssm_moments: float32 [2, 2, 768, 64], P(None, None, 'seq'), may hold values from -1.5 to 2, as said below
Outputs:
- layer_out: bfloat16 [16, 1024, 768], P('dp', 'seq')
- input_grad: float32 [16, 1024, 768], P('dp', 'seq')
- attn_step: float32 [768, 3072], P('dp')
- attn_moments_new: float32 [2, 768, 3072], P(None, 'dp')
- mlp_step: float32 [2, 768, 3072], P(None, 'dp')
- mlp_moments_new: float32 [2, 2, 768, 3072], P(None, None, 'dp')
- norms_step: float32 [4, 768], P(None, 'dp')
- norm_moments_new: float32 [2, 4, 768], P(None, None, 'dp')
- taps_step: float32 [64, 768], P(None, 'dp')
- tap_moments_new: float32 [2, 64, 768], P(None, None, 'dp')
- ssm_step: float32 [2, 768, 64], P(None, 'seq')
- ssm_moments_new: float32 [2, 2, 768, 64], P(None, None, 'seq')
The draws below stay inside these ranges and needn't reach their ends.
Inputs may be any that keep to these rules, and one draw needn't show every extreme that they name: ssm_params[0] holds log rates from -10 to -3.5; ssm_params[1] holds coefficients. `attn_moments`: the second moments are positive. `mlp_moments`: the second moments are positive. `norm_moments`: the second moments are positive. `tap_moments`: the second moments are positive. `ssm_moments`: the second moments are positive.
All inputs are finite; a program needn't handle non-finite values.
Results may differ from the reference program's by a relative error of at most 0.01.
Values may be sent and summed in bfloat16 or wider, within the bound.
A program may use at most 320 MiB of HBM per device.

```python
import math
import jax
import jax.numpy as jnp
from jax import lax

D = 768
FF = 3072
NSTATE = 64
SHIFT = 64
LENGTH = 1024
SEQS = 16


def moment_pair(key, shape_dims):
    first_key, second_key = jax.random.split(key)
    averages = jnp.clip(0.3 * jax.random.normal(first_key, shape_dims, jnp.float32), -1.5, 1.5)
    squares = jnp.exp(jax.random.uniform(second_key, shape_dims, jnp.float32, math.log(0.05), math.log(2.0)))
    return jnp.stack([averages, squares]).astype(jnp.float32)


def draw_attn_moments(key, part):
    key = jax.random.fold_in(key, 21)
    return moment_pair(key, (D, 4 * D))


def draw_mlp_moments(key, part):
    key = jax.random.fold_in(key, 22)
    return moment_pair(key, (2, D, FF))


def draw_norm_moments(key, part):
    key = jax.random.fold_in(key, 23)
    return moment_pair(key, (4, D))


def draw_tap_moments(key, part):
    key = jax.random.fold_in(key, 24)
    return moment_pair(key, (SHIFT, D))


def draw_ssm_moments(key, part):
    key = jax.random.fold_in(key, 25)
    return moment_pair(key, (2, D, NSTATE))


def draw_mlp_weight(key, part):
    key = jax.random.fold_in(key, 31)
    raw_values = jnp.clip(jax.random.normal(key, (2, D, FF), jnp.float32), -6.0, 6.0)
    scales = jnp.array([D ** (-0.5), FF ** (-0.5)], jnp.float32)
    return (raw_values * scales[:, None, None]).astype(jnp.bfloat16)


def draw_norms(key, part):
    key = jax.random.fold_in(key, 41)
    first_key, second_key = jax.random.split(key)
    gains = jax.random.uniform(first_key, (2, D), jnp.float32, 0.5, 1.5)
    biases = jnp.clip(0.3 * jax.random.normal(second_key, (2, D), jnp.float32), -1.0, 1.0)
    return jnp.stack([gains[0], biases[0], gains[1], biases[1]]).astype(jnp.bfloat16)


def draw_taps(key, part):
    key = jax.random.fold_in(key, 51)
    raw_values = jnp.clip(jax.random.normal(key, (SHIFT, D), jnp.float32), -6.0, 6.0)
    return (raw_values * (1.0 / math.sqrt(SHIFT)) * 0.5).astype(jnp.bfloat16)


def draw_ssm_params(key, part):
    key = jax.random.fold_in(key, 61)
    first_key, second_key = jax.random.split(key)
    log_rates = jax.random.uniform(first_key, (D, NSTATE), jnp.float32, -10.0, -3.5)
    coefficient = jnp.clip(jax.random.normal(second_key, (D, NSTATE), jnp.float32), -5.0, 5.0)
    coefficient = coefficient * jnp.sqrt(2.0 * jnp.exp(log_rates) / NSTATE)
    return jnp.stack([log_rates, coefficient]).astype(jnp.float32)


def steps_of(own_key, dims, cuts, low, high):
    loudness = 1.0
    for position, shards_of in cuts:
        heights = jax.random.uniform(jax.random.fold_in(jax.random.fold_in(own_key, 6), position), (shards_of,), jnp.float32, low / len(cuts), high / len(cuts))
        loudness = loudness * jnp.repeat(jnp.exp(heights), dims[position] // shards_of).reshape((-1,) + (1,) * (len(dims) - 1 - position))
    return loudness


def gaussian(rng, extent, spread, reach, shards=(), dtype=jnp.bfloat16):
    factor_of = steps_of(rng, extent, shards, -0.22, 0.18) if shards else 1.0
    entries = jax.random.normal(rng, extent, jnp.float32) * spread * factor_of
    return jnp.minimum(jnp.maximum(entries, -reach), reach).astype(dtype)


def setup_inputs(seed: int = 0) -> dict:
    streams_of = jax.random.split(jax.random.key(seed), 13)
    tokens = gaussian(streams_of[0], (SEQS, LENGTH, D), 1.0, 6.0, ((0, 16), (1, 2)))
    cotangent = gaussian(streams_of[1], (SEQS, LENGTH, D), 1.0, 6.0, ((0, 16), (1, 2)))
    attn_weight = gaussian(streams_of[2], (D, 4 * D), D ** -0.5, 0.21875, ((0, 16),))
    mlp_weight = draw_mlp_weight(jax.random.fold_in(streams_of[12], 71), 0)
    norms = draw_norms(jax.random.fold_in(streams_of[12], 71), 0)
    taps = draw_taps(jax.random.fold_in(streams_of[12], 71), 0)
    ssm_params = draw_ssm_params(jax.random.fold_in(streams_of[12], 71), 0)
    attn_moments = draw_attn_moments(jax.random.fold_in(streams_of[12], 71), 0)
    mlp_moments = draw_mlp_moments(jax.random.fold_in(streams_of[12], 71), 0)
    norm_moments = draw_norm_moments(jax.random.fold_in(streams_of[12], 71), 0)
    tap_moments = draw_tap_moments(jax.random.fold_in(streams_of[12], 71), 0)
    ssm_moments = draw_ssm_moments(jax.random.fold_in(streams_of[12], 71), 0)
    return dict(tokens=tokens, cotangent=cotangent, attn_weight=attn_weight, mlp_weight=mlp_weight, norms=norms, taps=taps, ssm_params=ssm_params, attn_moments=attn_moments, mlp_moments=mlp_moments, norm_moments=norm_moments, tap_moments=tap_moments, ssm_moments=ssm_moments)


EPS_NORM = 1e-05
BETA_ONE = 0.9
BETA_TWO = 0.999
ADAM_EPS = 1e-08
LEARN_RATE = 0.001
SSM_LEARN_RATE = 0.00025
DECAY_RATE = 0.1
STEP_COUNT = 10.0

@jax.custom_vjp
def low(v):
    return lax.optimization_barrier(v.astype(jnp.bfloat16)).astype(jnp.float32)

@jax.custom_vjp
def low_back(v):
    return v

def low_keep(v):
    return (low(v), None)

def low_pass(kept, grad):
    return (grad,)

def back_keep(v):
    return (v, None)

def back_low(kept, grad):
    return (low(grad),)
low.defvjp(low_keep, low_pass)
low_back.defvjp(back_keep, back_low)

def matmul_high(left, right):
    return jnp.dot(left, right, precision=lax.Precision.HIGHEST, preferred_element_type=jnp.float32)

def layer_norm(values, gain_row, bias_row):
    average = lax.optimization_barrier(jnp.mean(values, axis=-1, keepdims=True))
    centred = values - average
    variance = lax.optimization_barrier(jnp.mean(centred * centred, axis=-1, keepdims=True))
    return centred * lax.rsqrt(variance + EPS_NORM) * gain_row + bias_row

def shift_mix(rim_rows, keys_part, taps_full):
    tap_count = taps_full.shape[0]
    row_count = keys_part.shape[0]
    extended = jnp.concatenate([rim_rows, keys_part], axis=0)
    summed = jnp.zeros_like(keys_part)
    for tap_index in range(tap_count):
        begin_row = tap_count - 1 - tap_index
        summed = summed + taps_full[tap_index] * extended[begin_row:begin_row + row_count]
    return summed

def kernel_rows(length_total, ssm_full):
    offsets = jnp.arange(length_total).astype(jnp.float32)

    def one_channel(channel_params):
        decay_rates = jnp.exp(channel_params[0])
        decays = jnp.exp(-decay_rates[:, None] * offsets[None, :])
        return lax.optimization_barrier(jnp.sum(channel_params[1][:, None] * decays, axis=0))
    return lax.map(jax.checkpoint(one_channel), jnp.swapaxes(ssm_full, 0, 1))

def sequence_forward(attn_full, mlp_full, norm_full, taps_full, spectrum, tokens_seq):
    model_width = tokens_seq.shape[1]
    length_total = tokens_seq.shape[0]
    normed = low(layer_norm(tokens_seq, norm_full[0], norm_full[1]))
    project = low_back(matmul_high(normed, attn_full[:, :3 * model_width]))
    queries = project[:, :model_width]
    keys_part = project[:, model_width:2 * model_width]
    values = project[:, 2 * model_width:]
    rim_rows = jnp.zeros((taps_full.shape[0] - 1, model_width), jnp.float32)
    shifted = shift_mix(rim_rows, keys_part, taps_full)
    mixed_rows = low_back(low(shifted * values))
    mixed_freq = jnp.fft.rfft(mixed_rows, n=2 * length_total, axis=0)
    conv_rows = jnp.fft.irfft(mixed_freq * spectrum, n=2 * length_total, axis=0)[:length_total]
    conv_rows = low_back(low(conv_rows))
    gated_rows = low(queries * conv_rows)
    branch = low_back(matmul_high(gated_rows, attn_full[:, 3 * model_width:]))
    residual_one = tokens_seq + branch
    normed_two = low(layer_norm(residual_one, norm_full[2], norm_full[3]))
    before = low_back(matmul_high(normed_two, mlp_full[0]))
    active = low(jax.nn.gelu(before))
    mlp_out = low_back(matmul_high(active, mlp_full[1].T))
    return residual_one + mlp_out

def forward(attn_full, mlp_full, norm_full, taps_full, ssm_full, tokens_all):
    length_total = tokens_all.shape[1]
    kernel = kernel_rows(length_total, ssm_full)
    spectrum = jnp.fft.rfft(kernel, n=2 * length_total, axis=1).T

    def scan_step(carried, tokens_seq):
        return (carried, jax.checkpoint(sequence_forward)(attn_full, mlp_full, norm_full, taps_full, spectrum, tokens_seq))
    carried, outputs = lax.scan(scan_step, jnp.zeros((), jnp.float32), tokens_all)
    return outputs

def adam_update(param_now, moments, gradient, learn_rate, decay_weight):
    first_new = BETA_ONE * moments[0] + (1.0 - BETA_ONE) * gradient
    second_new = BETA_TWO * moments[1] + (1.0 - BETA_TWO) * gradient * gradient
    first_hat = first_new / (1.0 - BETA_ONE ** STEP_COUNT)
    second_hat = second_new / (1.0 - BETA_TWO ** STEP_COUNT)
    step_size = learn_rate * (first_hat / (jnp.sqrt(second_hat) + ADAM_EPS) + decay_weight * param_now)
    return (step_size, jnp.stack([first_new, second_new]))

def reference(tokens, cotangent, attn_weight, mlp_weight, norms, taps, ssm_params, attn_moments, mlp_moments, norm_moments, tap_moments, ssm_moments):
    attn_full = attn_weight.astype(jnp.float32)
    mlp_full = mlp_weight.astype(jnp.float32)
    norm_full = norms.astype(jnp.float32)
    taps_full = taps.astype(jnp.float32)
    ssm_full = ssm_params.astype(jnp.float32)
    outputs, pullback = jax.vjp(forward, attn_full, mlp_full, norm_full, taps_full, ssm_full, tokens.astype(jnp.float32))
    grads = pullback(cotangent.astype(jnp.float32))
    grad_scale = 1.0 / math.sqrt(SEQS * LENGTH)
    attn_step, attn_moments_new = adam_update(attn_full, attn_moments, grads[0] * grad_scale, LEARN_RATE, DECAY_RATE)
    mlp_step, mlp_moments_new = adam_update(mlp_full, mlp_moments, grads[1] * grad_scale, LEARN_RATE, DECAY_RATE)
    norms_step, norm_moments_new = adam_update(norm_full, norm_moments, grads[2] * grad_scale, LEARN_RATE, 0.0)
    taps_step, tap_moments_new = adam_update(taps_full, tap_moments, grads[3] * grad_scale, LEARN_RATE, DECAY_RATE)
    ssm_step, ssm_moments_new = adam_update(ssm_full, ssm_moments, grads[4] * grad_scale, SSM_LEARN_RATE, 0.0)
    return (outputs.astype(jnp.bfloat16), grads[5], attn_step, attn_moments_new, mlp_step, mlp_moments_new, norms_step, norm_moments_new, taps_step, tap_moments_new, ssm_step, ssm_moments_new)
```

```python
from functools import partial
import math

import jax
import jax.numpy as jnp
import ml_dtypes
import numpy as np
from jax import lax
from jax.experimental import pallas as pl
from jax.experimental.pallas import tpu as pltpu
from jax.sharding import PartitionSpec as P

DFT_ROWS = 256


EPS_NORM = 1e-05
BETA_ONE = 0.9
BETA_TWO = 0.999
ADAM_EPS = 1e-08
LEARN_RATE = 0.001
SSM_LEARN_RATE = 0.00025
DECAY_RATE = 0.1
STEP_COUNT = 10.0
HIGHEST = lax.Precision.HIGHEST


def from_behind(block, axis, distance):
    devices = range(lax.axis_size(axis))
    route = [(i - distance, i) for i in devices if i - distance in devices]
    return lax.ppermute(block, axis, route)


def as_sent(value):

    def short(part):
        return part.astype(jnp.bfloat16) if part.dtype == jnp.float32 else part

    return jax.tree.map(short, value)


def layer_norm(values, gain_row, bias_row):
    average = jnp.mean(values, axis=-1, keepdims=True)
    centred = values - average
    variance = jnp.mean(centred * centred, axis=-1, keepdims=True)
    return centred * lax.rsqrt(variance + EPS_NORM) * gain_row + bias_row


def shift_mix(rim_rows, keys_part, taps_full):
    tap_count = taps_full.shape[0]
    row_count = keys_part.shape[0]
    extended = jnp.concatenate([rim_rows, keys_part], axis=0)
    summed = jnp.zeros_like(keys_part)
    for tap_index in range(tap_count):
        begin_row = tap_count - 1 - tap_index
        summed = summed + taps_full[tap_index] * extended[begin_row : begin_row + row_count]
    return summed


def kernel_rows(length_total, ssm_full):
    inner_count = math.gcd(length_total, 128)
    outer_count = length_total // inner_count
    decay_rates = jnp.exp(ssm_full[0])
    outer_offsets = (jnp.arange(outer_count) * inner_count).astype(jnp.float32)
    inner_offsets = jnp.arange(inner_count).astype(jnp.float32)
    outer_part = ssm_full[1][:, :, None] * jnp.exp(
        -decay_rates[:, :, None] * outer_offsets[None, None, :]
    )
    inner_part = jnp.exp(-decay_rates[:, :, None] * inner_offsets[None, None, :])
    kernel = jnp.einsum("cna,cnb->cab", outer_part, inner_part, precision=HIGHEST)
    return kernel.reshape(kernel.shape[0], length_total)


def dft_tables(length_total, first_count):
    full_length = 2 * length_total
    col_count = full_length // first_count
    half_rows = first_count // 2
    row_index = jnp.arange(half_rows, dtype=jnp.int32)
    freq_index = jnp.arange(first_count, dtype=jnp.int32)
    col_index = jnp.arange(col_count, dtype=jnp.int32)
    angle_first = (
        2.0
        * math.pi
        / first_count
        * (row_index[:, None] * freq_index[None, :] % first_count).astype(jnp.float32)
    )
    angle_twist = (
        2.0 * math.pi / full_length * (freq_index[:, None] * col_index[None, :]).astype(jnp.float32)
    )
    angle_last = (
        2.0
        * math.pi
        / col_count
        * (col_index[:, None] * col_index[None, :] % col_count).astype(jnp.float32)
    )
    return (
        jnp.cos(angle_first),
        jnp.sin(angle_first),
        jnp.cos(angle_twist),
        jnp.sin(angle_twist),
        jnp.cos(angle_last),
        jnp.sin(angle_last),
    )


def forward_dft(signal, tables):
    cos_first, sin_first, cos_twist, sin_twist, cos_last, sin_last = tables
    half_rows = cos_first.shape[0]
    col_count = cos_last.shape[0]
    folded = signal.reshape(signal.shape[0], half_rows, col_count)
    real_first = jnp.einsum("cmp,mk->ckp", folded, cos_first, precision=HIGHEST)
    imaginary_first = -jnp.einsum("cmp,mk->ckp", folded, sin_first, precision=HIGHEST)
    real_twist = real_first * cos_twist + imaginary_first * sin_twist
    imaginary_twist = imaginary_first * cos_twist - real_first * sin_twist
    real_last = jnp.einsum("ckp,pq->ckq", real_twist, cos_last, precision=HIGHEST) + jnp.einsum(
        "ckp,pq->ckq", imaginary_twist, sin_last, precision=HIGHEST
    )
    imaginary_last = jnp.einsum(
        "ckp,pq->ckq", imaginary_twist, cos_last, precision=HIGHEST
    ) - jnp.einsum("ckp,pq->ckq", real_twist, sin_last, precision=HIGHEST)
    return (real_last, imaginary_last)


def inverse_dft(spectrum, tables):
    cos_first, sin_first, cos_twist, sin_twist, cos_last, sin_last = tables
    real_part, imaginary_part = spectrum
    full_length = cos_first.shape[1] * cos_last.shape[0]
    real_inner = jnp.einsum("ckq,qp->ckp", real_part, cos_last, precision=HIGHEST) - jnp.einsum(
        "ckq,qp->ckp", imaginary_part, sin_last, precision=HIGHEST
    )
    imaginary_inner = jnp.einsum(
        "ckq,qp->ckp", imaginary_part, cos_last, precision=HIGHEST
    ) + jnp.einsum("ckq,qp->ckp", real_part, sin_last, precision=HIGHEST)
    real_twist = real_inner * cos_twist - imaginary_inner * sin_twist
    imaginary_twist = imaginary_inner * cos_twist + real_inner * sin_twist
    signal = jnp.einsum("ckp,mk->cmp", real_twist, cos_first, precision=HIGHEST) - jnp.einsum(
        "ckp,mk->cmp", imaginary_twist, sin_first, precision=HIGHEST
    )
    return signal.reshape(signal.shape[0], signal.shape[1] * signal.shape[2]) / full_length


def complex_product(left, right, conjugate_left):
    left_real, left_imaginary = left
    right_real, right_imaginary = right
    if conjugate_left:
        return (
            left_real * right_real + left_imaginary * right_imaginary,
            left_real * right_imaginary - left_imaginary * right_real,
        )
    return (
        left_real * right_real - left_imaginary * right_imaginary,
        left_real * right_imaginary + left_imaginary * right_real,
    )


def adam_update(param_now, moments, gradient, learn_rate, decay_weight):
    first_new = BETA_ONE * moments[0] + (1.0 - BETA_ONE) * gradient
    second_new = BETA_TWO * moments[1] + (1.0 - BETA_TWO) * gradient * gradient
    first_hat = first_new / (1.0 - BETA_ONE**STEP_COUNT)
    second_hat = second_new / (1.0 - BETA_TWO**STEP_COUNT)
    step_size = learn_rate * (
        first_hat / (jnp.sqrt(second_hat) + ADAM_EPS) + decay_weight * param_now
    )
    return (step_size, jnp.stack([first_new, second_new]))


def per_device(
    tokens,
    cotangent,
    attn_weight,
    mlp_weight,
    norms,
    taps,
    ssm_params,
    attn_moments,
    mlp_moments,
    norm_moments,
    tap_moments,
    ssm_moments,
):
    row_count = tokens.shape[1]
    model_width = tokens.shape[2]
    group_count = lax.axis_size("seq")
    owner_count = lax.axis_size("dp")
    length_total = row_count * group_count
    attn_full, mlp_full, norm_full, taps_full = (
        lax.all_gather(attn_weight, "dp", axis=0, tiled=True),
        lax.all_gather(mlp_weight, "dp", axis=1, tiled=True),
        lax.all_gather(norms, "dp", axis=1, tiled=True),
        lax.all_gather(taps, "dp", axis=1, tiled=True),
    )
    inputs = tokens[0].astype(jnp.float32)
    cot_rows = cotangent[0].astype(jnp.float32)
    norm_values = norm_full.astype(jnp.float32)
    taps_values = taps_full.astype(jnp.float32)
    tap_count = taps_values.shape[0]
    normed, norm_pull = jax.vjp(layer_norm, inputs, norm_values[0], norm_values[1])
    normed_low = normed.astype(jnp.bfloat16)
    project = jnp.dot(
        normed_low, attn_full[:, : 3 * model_width], preferred_element_type=jnp.float32
    )
    queries = project[:, :model_width]
    keys_part = project[:, model_width : 2 * model_width]
    values = project[:, 2 * model_width :]
    rim_rows = from_behind(
        keys_part[row_count - tap_count + 1 :].astype(jnp.bfloat16), "seq", 1
    ).astype(jnp.float32)
    shifted, shift_pull = jax.vjp(shift_mix, rim_rows, keys_part, taps_values)
    mixed_rows = (shifted * values).astype(jnp.bfloat16)
    moved_in = lax.all_to_all(mixed_rows.T, "seq", split_axis=0, concat_axis=1, tiled=True).astype(
        jnp.float32
    )
    tables = dft_tables(length_total, DFT_ROWS)
    kernel, kernel_pull = jax.vjp(partial(kernel_rows, length_total), ssm_params)
    kernel_freq = forward_dft(kernel, tables)
    input_freq = forward_dft(moved_in, tables)
    conv_channels = inverse_dft(complex_product(input_freq, kernel_freq, False), tables)
    conv_back = lax.all_to_all(
        conv_channels.astype(jnp.bfloat16), "seq", split_axis=1, concat_axis=0, tiled=True
    )
    conv_rows = conv_back.T.astype(jnp.float32)
    gated_rows = (queries * conv_rows).astype(jnp.bfloat16)
    branch = jnp.dot(
        gated_rows, attn_full[:, 3 * model_width :], preferred_element_type=jnp.float32
    )
    residual_one = inputs + branch
    normed_two, norm_two_pull = jax.vjp(layer_norm, residual_one, norm_values[2], norm_values[3])
    normed_two_low = normed_two.astype(jnp.bfloat16)
    before = jnp.dot(normed_two_low, mlp_full[0], preferred_element_type=jnp.float32)
    active, gelu_pull = jax.vjp(jax.nn.gelu, before)
    active_low = active.astype(jnp.bfloat16)
    mlp_out = jnp.einsum("tf,df->td", active_low, mlp_full[1], preferred_element_type=jnp.float32)
    layer_out = (residual_one + mlp_out).astype(jnp.bfloat16)
    attn_back, mlp_back = (
        lax.all_gather(attn_weight, "dp", axis=0, tiled=True),
        lax.all_gather(mlp_weight, "dp", axis=1, tiled=True),
    )
    grad_after = cotangent[0]
    grad_active = jnp.dot(grad_after, mlp_back[1], preferred_element_type=jnp.float32)
    grad_down = jnp.einsum("td,tf->df", grad_after, active_low, preferred_element_type=jnp.float32)
    grad_before = gelu_pull(grad_active)[0].astype(jnp.bfloat16)
    grad_up = jnp.einsum(
        "td,tf->df", normed_two_low, grad_before, preferred_element_type=jnp.float32
    )
    grad_normed_two = jnp.einsum(
        "tf,df->td", grad_before, mlp_back[0], preferred_element_type=jnp.float32
    )
    grad_residual_part, grad_gain_two, grad_bias_two = norm_two_pull(grad_normed_two)
    grad_residual = cot_rows + grad_residual_part
    grad_branch = grad_residual.astype(jnp.bfloat16)
    grad_out = jnp.einsum("td,te->de", gated_rows, grad_branch, preferred_element_type=jnp.float32)
    grad_gated = jnp.einsum(
        "te,de->td",
        grad_branch,
        attn_back[:, 3 * model_width :],
        preferred_element_type=jnp.float32,
    )
    grad_queries = grad_gated * conv_rows
    grad_conv = (grad_gated * queries).astype(jnp.bfloat16)
    grad_moved = lax.all_to_all(grad_conv.T, "seq", split_axis=0, concat_axis=1, tiled=True).astype(
        jnp.float32
    )
    grad_freq = forward_dft(grad_moved, tables)
    grad_input = inverse_dft(complex_product(kernel_freq, grad_freq, True), tables)
    grad_kernel = inverse_dft(complex_product(input_freq, grad_freq, True), tables)
    grad_ssm_local = kernel_pull(grad_kernel)[0]
    grad_ssm = lax.psum(grad_ssm_local, "dp")
    grad_mixed_back = lax.all_to_all(
        grad_input.astype(jnp.bfloat16), "seq", split_axis=1, concat_axis=0, tiled=True
    )
    grad_mixed = grad_mixed_back.T.astype(jnp.float32)
    grad_shifted = grad_mixed * values
    grad_values = grad_mixed * shifted
    grad_rim, grad_keys, grad_taps = shift_pull(grad_shifted)
    returned = from_behind(as_sent(grad_rim), "seq", -1).astype(grad_rim.dtype)
    grad_keys = grad_keys + jnp.pad(returned, ((row_count - tap_count + 1, 0), (0, 0)))
    grad_project = jnp.concatenate([grad_queries, grad_keys, grad_values], axis=1).astype(
        jnp.bfloat16
    )
    grad_qkv = jnp.einsum("td,te->de", normed_low, grad_project, preferred_element_type=jnp.float32)
    grad_normed = jnp.einsum(
        "te,de->td",
        grad_project,
        attn_back[:, : 3 * model_width],
        preferred_element_type=jnp.float32,
    )
    grad_input_part, grad_gain_one, grad_bias_one = norm_pull(grad_normed)
    input_grad = grad_residual + grad_input_part
    grad_attn = jnp.concatenate([grad_qkv, grad_out], axis=1)
    grad_mlp = jnp.stack([grad_up, grad_down])
    grad_norms = jnp.stack([grad_gain_one, grad_bias_one, grad_gain_two, grad_bias_two])
    owned_part = (
        lax.psum_scatter(
            grad_attn.astype(jnp.bfloat16), "dp", scatter_dimension=0, tiled=True
        ).astype(jnp.float32),
        lax.psum_scatter(
            grad_mlp.astype(jnp.bfloat16), "dp", scatter_dimension=1, tiled=True
        ).astype(jnp.float32),
        lax.psum_scatter(
            grad_norms.astype(jnp.bfloat16), "dp", scatter_dimension=1, tiled=True
        ).astype(jnp.float32),
        lax.psum_scatter(
            grad_taps.astype(jnp.bfloat16), "dp", scatter_dimension=1, tiled=True
        ).astype(jnp.float32),
    )
    summed = (
        lax.psum(owned_part[0].astype(jnp.bfloat16), "seq").astype(jnp.float32),
        lax.psum(owned_part[1].astype(jnp.bfloat16), "seq").astype(jnp.float32),
        lax.psum(owned_part[2].astype(jnp.bfloat16), "seq").astype(jnp.float32),
        lax.psum(owned_part[3].astype(jnp.bfloat16), "seq").astype(jnp.float32),
    )
    grad_scale = 1.0 / math.sqrt(owner_count * length_total)
    attn_step, attn_moments_new = adam_update(
        attn_weight.astype(jnp.float32),
        attn_moments,
        summed[0] * grad_scale,
        LEARN_RATE,
        DECAY_RATE,
    )
    mlp_step, mlp_moments_new = adam_update(
        mlp_weight.astype(jnp.float32), mlp_moments, summed[1] * grad_scale, LEARN_RATE, DECAY_RATE
    )
    norms_step, norm_moments_new = adam_update(
        norms.astype(jnp.float32), norm_moments, summed[2] * grad_scale, LEARN_RATE, 0.0
    )
    taps_step, tap_moments_new = adam_update(
        taps.astype(jnp.float32), tap_moments, summed[3] * grad_scale, LEARN_RATE, DECAY_RATE
    )
    ssm_step, ssm_moments_new = adam_update(
        ssm_params, ssm_moments, grad_ssm * grad_scale, SSM_LEARN_RATE, 0.0
    )
    return (
        layer_out[None],
        input_grad[None],
        attn_step,
        attn_moments_new,
        mlp_step,
        mlp_moments_new,
        norms_step,
        norm_moments_new,
        taps_step,
        tap_moments_new,
        ssm_step,
        ssm_moments_new,
    )


LANES = 128
RADIX = 8
HALF = 128


def transform_tables():
    rows = np.arange(HALF)
    length = RADIX * HALF
    waves = RADIX * rows[None, :, None] + np.arange(RADIX)[:, None, None] + 0.25
    angles = 2.0 * np.pi * np.mod(rows[None, None, :] * waves, length) / length
    cosines, sines = np.cos(angles), np.sin(angles)
    full = np.concatenate(
        [np.concatenate([cosines, sines], axis=2), np.concatenate([-sines, cosines], axis=2)], axis=1
    )

    def parts(matrix):
        matrix = matrix.astype(np.float32)
        high = matrix.astype(ml_dtypes.bfloat16)
        rest = (matrix - high.astype(np.float32)).astype(ml_dtypes.bfloat16)
        return np.stack([high, rest])

    return parts(full), parts(np.swapaxes(full, 1, 2))


def turned(value, angle):
    real, imaginary = value
    cosine, sine = math.cos(angle), math.sin(angle)
    if abs(sine) < 1e-12:
        return (real, imaginary) if cosine > 0 else (-real, -imaginary)
    if abs(cosine) < 1e-12:
        return (-imaginary, real) if sine > 0 else (imaginary, -real)
    return (real * cosine - imaginary * sine, real * sine + imaginary * cosine)


def small_transform(values, sign):
    count = len(values)
    if count == 1:
        return values
    even = small_transform(values[::2], sign)
    odd = small_transform(values[1::2], sign)
    low, high = [], []
    for index in range(count // 2):
        (er, ei), (tr, ti) = even[index], turned(odd[index], sign * 2.0 * math.pi * index / count)
        low.append((er + tr, ei + ti))
        high.append((er - tr, ei - ti))
    return low + high


def split(value):
    high = value.astype(jnp.bfloat16)
    return high, (value - high.astype(jnp.float32)).astype(jnp.bfloat16)


def dot(left, right):
    return jnp.dot(left, right, preferred_element_type=jnp.float32)


def each_tile(width, rows, step, body):
    for block in range(width // LANES):

        def one(index, carry, block=block):
            body(pl.multiple_of(index * step, step), pl.ds(block * LANES, LANES))
            return carry

        lax.fori_loop(0, rows // step, one, 0)


def to_waves(width, read, used, w_ref, high_ref, low_ref, store):
    def first(row, cols):
        inputs = []
        for part in range(used):
            x = read(part * HALF, row, cols)
            angle = -2.0 * math.pi * part / 32.0
            inputs.append((x * math.cos(angle), x * math.sin(angle)) if part else (x, jnp.zeros_like(x)))
        while len(inputs) < RADIX:
            inputs.append((jnp.zeros_like(x), jnp.zeros_like(x)))
        for wave, value in enumerate(small_transform(inputs, -1.0)):
            for place, part in enumerate(value):
                high, low = split(part)
                high_ref[wave, pl.ds(row + place * HALF, 16), cols] = high
                low_ref[wave, pl.ds(row + place * HALF, 16), cols] = low

    each_tile(width, HALF, 16, first)

    def second(wave, carry):
        high = high_ref[wave]
        store(wave, dot(w_ref[0, wave], high) + dot(w_ref[1, wave], high) + dot(w_ref[0, wave], low_ref[wave]))
        return carry

    lax.fori_loop(0, RADIX, second, 0)


def product(width, left_ref, right_ref, conjugate, high_ref, low_ref):
    sign = -1.0 if conjugate else 1.0

    def one(wave, carry):
        def tile(row, cols):
            lr, li = left_ref[wave, pl.ds(row, 16), cols], left_ref[wave, pl.ds(row + HALF, 16), cols] * sign
            rr, ri = right_ref[wave, pl.ds(row, 16), cols], right_ref[wave, pl.ds(row + HALF, 16), cols]
            for place, part in enumerate((lr * rr - li * ri, lr * ri + li * rr)):
                high, low = split(part)
                high_ref[wave, pl.ds(row + place * HALF, 16), cols] = high
                low_ref[wave, pl.ds(row + place * HALF, 16), cols] = low

        each_tile(width, HALF, 16, tile)
        return carry

    lax.fori_loop(0, RADIX, one, 0)


def from_waves(width, w_ref, high_ref, low_ref, back_ref, put):
    def second(wave, carry):
        high = high_ref[wave]
        back_ref[wave] = dot(w_ref[0, wave], high) + dot(w_ref[1, wave], high) + dot(w_ref[0, wave], low_ref[wave])
        return carry

    lax.fori_loop(0, RADIX, second, 0)
    scale = 1.0 / (RADIX * HALF)

    def first(row, cols):
        values = [
            (back_ref[wave, pl.ds(row, 16), cols], back_ref[wave, pl.ds(row + HALF, 16), cols])
            for wave in range(RADIX)
        ]
        for part, (real, imaginary) in enumerate(small_transform(values, 1.0)):
            angle = 2.0 * math.pi * part / 32.0
            put(part * HALF, row, cols, real * (math.cos(angle) * scale) - imaginary * (math.sin(angle) * scale))

    each_tile(width, HALF, 16, first)


def first_positions(width, count, w_ref, high_ref, low_ref):
    total = jnp.zeros((count, width), jnp.float32)
    for wave in range(RADIX):
        wh, wl = w_ref[0, wave, :count, :], w_ref[1, wave, :count, :]
        high = high_ref[wave]
        total = total + (dot(wh, high) + dot(wl, high) + dot(wh, low_ref[wave]))
    return total * (1.0 / (RADIX * HALF))


FINE = 32


def decay_sums(width, length, ssm_ref, coarse_ref, fine_ref, out_ref):
    modes = ssm_ref.shape[1]
    steps = length // FINE
    offsets = lax.broadcasted_iota(jnp.int32, (FINE, width), 0).astype(jnp.float32)
    starts = lax.broadcasted_iota(jnp.int32, (steps, width), 0).astype(jnp.float32) * FINE

    def powers(index, carry):
        base = pl.multiple_of(index * 8, 8)
        rates = jnp.exp(ssm_ref[0, pl.ds(base, 8), :])
        weights = ssm_ref[1, pl.ds(base, 8), :]
        for i in range(8):
            fine_ref[base + i] = jnp.exp(-rates[i : i + 1] * offsets)
            coarse_ref[base + i] = weights[i : i + 1] * jnp.exp(-rates[i : i + 1] * starts)
        return carry

    lax.fori_loop(0, modes // 8, powers, 0)
    for block in range(width // LANES):
        cols = pl.ds(block * LANES, LANES)

        def group(index, carry, cols=cols):
            def add(mode, sums):
                fine = fine_ref[mode, :, cols]
                rows = coarse_ref[mode, pl.ds(pl.multiple_of(index * 8, 8), 8), cols]
                return tuple(s + rows[i : i + 1] * fine for i, s in enumerate(sums))

            sums = lax.fori_loop(0, modes, add, tuple(jnp.zeros((FINE, LANES), jnp.float32) for _ in range(8)))
            for i, s in enumerate(sums):
                out_ref[pl.ds(pl.multiple_of(index * 8 * FINE, FINE) + i * FINE, FINE), cols] = s
            return carry

        lax.fori_loop(0, steps // 8, group, 0)


def decay_gradients(width, length, ssm_ref, grad_ref, out_ref):
    modes = ssm_ref.shape[1]
    steps = length // FINE
    for block in range(width // LANES):
        cols = pl.ds(block * LANES, LANES)
        offsets = lax.broadcasted_iota(jnp.int32, (FINE, LANES), 0).astype(jnp.float32)

        def group(index, carry, cols=cols, offsets=offsets):
            base = pl.multiple_of(index * 8, 8)
            rates = jnp.exp(ssm_ref[0, pl.ds(base, 8), cols])
            leaps = jnp.exp(-rates * FINE)
            plain_rows, slope_rows = [], []
            for modes_now in ((0, 1, 2, 3), (4, 5, 6, 7)):
                zero = offsets * 0.0
                leap_rows = [leaps[i : i + 1] for i in modes_now]

                def step(number, sums, leap_rows=leap_rows):
                    rows = grad_ref[pl.ds(pl.multiple_of((steps - 1 - number) * FINE, FINE), FINE), cols]
                    return tuple((v * leap + rows, w * leap + v) for (v, w), leap in zip(sums, leap_rows))

                sums = lax.fori_loop(0, steps, step, tuple((zero, zero) for _ in modes_now))
                for i, (v, w) in zip(modes_now, sums):
                    fine = jnp.exp(-rates[i : i + 1] * offsets)
                    plain = fine * v
                    slope = fine * w * (leaps[i : i + 1] * FINE) + plain * offsets
                    plain_rows.append(jnp.sum(plain, axis=0, keepdims=True))
                    slope_rows.append(jnp.sum(slope, axis=0, keepdims=True))
            out_ref[1, pl.ds(base, 8), cols] = jnp.concatenate(plain_rows, axis=0)
            out_ref[0, pl.ds(base, 8), cols] = (
                -ssm_ref[1, pl.ds(base, 8), cols] * rates * jnp.concatenate(slope_rows, axis=0)
            )
            return carry

        lax.fori_loop(0, modes // 8, group, 0)


def mixer_forward_body(
    proj_ref, taps_ref, ssm_ref, to_ref, from_ref,
    gated_ref, conv_ref, shifted_ref, kernel_w, taps_w, keys_w, mixed_w,
    line_ref, high_ref, low_ref, back_ref, coarse_ref, fine_ref,
):
    width = conv_ref.shape[1]
    length = conv_ref.shape[0]

    def keep(target):
        def store(wave, value):
            target[wave] = value

        return store

    def lines(base, row, cols):
        return line_ref[pl.ds(base + row, 16), cols]

    def column(place, cols):
        return pl.ds(place * width + cols.start, cols.size)

    decay_sums(width, length, ssm_ref, coarse_ref, fine_ref, line_ref)
    to_waves(width, lines, RADIX, to_ref, high_ref, low_ref, keep(kernel_w))
    to_waves(
        width, lambda base, row, cols: taps_ref[pl.ds(base + row, 16), cols],
        1, to_ref, high_ref, low_ref, keep(taps_w),
    )
    to_waves(
        width, lambda base, row, cols: proj_ref[pl.ds(base + row, 16), column(1, cols)],
        RADIX, to_ref, high_ref, low_ref, keep(keys_w),
    )
    product(width, taps_w, keys_w, False, high_ref, low_ref)

    def put_shifted(base, row, cols, value):
        rows = pl.ds(base + row, 16)
        shifted_ref[rows, cols] = value
        mixed = value * proj_ref[rows, column(2, cols)]
        line_ref[rows, cols] = mixed.astype(jnp.bfloat16).astype(jnp.float32)

    from_waves(width, from_ref, high_ref, low_ref, back_ref, put_shifted)
    to_waves(width, lines, RADIX, to_ref, high_ref, low_ref, keep(mixed_w))
    product(width, kernel_w, mixed_w, False, high_ref, low_ref)

    def put_conv(base, row, cols, value):
        rows = pl.ds(base + row, 16)
        rounded = value.astype(jnp.bfloat16)
        conv_ref[rows, cols] = rounded
        gated_ref[rows, cols] = (proj_ref[rows, cols] * rounded.astype(jnp.float32)).astype(jnp.bfloat16)

    from_waves(width, from_ref, high_ref, low_ref, back_ref, put_conv)


def mixer_backward_body(
    grad_ref, proj_ref, conv_ref, shifted_ref, kernel_w, taps_w, keys_w, mixed_w, ssm_ref, to_ref, from_ref,
    out_ref, taps_out_ref, ssm_out_ref,
    line_ref, decay_ref, wave_ref, high_ref, low_ref, back_ref,
):
    width = conv_ref.shape[1]
    length = conv_ref.shape[0]

    def keep(wave, value):
        wave_ref[wave] = value

    def lines(base, row, cols):
        return line_ref[pl.ds(base + row, 16), cols]

    def column(place, cols):
        return pl.ds(place * width + cols.start, cols.size)

    def read_conv_grad(base, row, cols):
        rows = pl.ds(base + row, 16)
        gradient = grad_ref[rows, cols].astype(jnp.float32)
        out_ref[rows, cols] = (gradient * conv_ref[rows, cols].astype(jnp.float32)).astype(jnp.bfloat16)
        return (gradient * proj_ref[rows, cols]).astype(jnp.bfloat16).astype(jnp.float32)

    to_waves(width, read_conv_grad, RADIX, to_ref, high_ref, low_ref, keep)
    product(width, kernel_w, wave_ref, True, high_ref, low_ref)

    def put_mixed(base, row, cols, value):
        rows = pl.ds(base + row, 16)
        gradient = value.astype(jnp.bfloat16).astype(jnp.float32)
        out_ref[rows, column(2, cols)] = (gradient * shifted_ref[rows, cols]).astype(jnp.bfloat16)
        line_ref[rows, cols] = gradient * proj_ref[rows, column(2, cols)]

    from_waves(width, from_ref, high_ref, low_ref, back_ref, put_mixed)
    product(width, mixed_w, wave_ref, True, high_ref, low_ref)

    def put_kernel(base, row, cols, value):
        decay_ref[pl.ds(base + row, 16), cols] = value

    from_waves(width, from_ref, high_ref, low_ref, back_ref, put_kernel)
    to_waves(width, lines, RADIX, to_ref, high_ref, low_ref, keep)
    product(width, taps_w, wave_ref, True, high_ref, low_ref)

    def put_keys(base, row, cols, value):
        out_ref[pl.ds(base + row, 16), column(1, cols)] = value.astype(jnp.bfloat16)

    from_waves(width, from_ref, high_ref, low_ref, back_ref, put_keys)
    product(width, keys_w, wave_ref, True, high_ref, low_ref)
    taps_out_ref[...] = first_positions(width, taps_out_ref.shape[0], from_ref, high_ref, low_ref)
    decay_gradients(width, length, ssm_ref, decay_ref, ssm_out_ref)


VMEM_LIMIT = 58 * 1024 * 1024


def mixer_forward(proj, taps, ssm, to_table, from_table):
    length, width = proj.shape[0], proj.shape[1] // 3
    modes = ssm.shape[1]
    f32, low = jnp.float32, jnp.bfloat16
    waves = (RADIX, 2 * HALF, width)
    vmem = pl.BlockSpec(memory_space=pltpu.VMEM)
    return pl.pallas_call(
        mixer_forward_body,
        out_shape=(
            jax.ShapeDtypeStruct((length, width), low),
            jax.ShapeDtypeStruct((length, width), low),
            jax.ShapeDtypeStruct((length, width), f32),
        )
        + (jax.ShapeDtypeStruct(waves, f32),) * 4,
        in_specs=[vmem] * 5,
        out_specs=(vmem,) * 7,
        scratch_shapes=[
            pltpu.VMEM((length, width), f32),
            pltpu.VMEM(waves, low),
            pltpu.VMEM(waves, low),
            pltpu.VMEM(waves, f32),
            pltpu.VMEM((modes, length // FINE, width), f32),
            pltpu.VMEM((modes, FINE, width), f32),
        ],
        compiler_params=pltpu.CompilerParams(vmem_limit_bytes=VMEM_LIMIT),
        name="mixer_forward",
    )(proj, taps, ssm, to_table, from_table)


def mixer_backward(grad, proj, conv, shifted, kernel_w, taps_w, keys_w, mixed_w, ssm, to_table, from_table, tap_count):
    length, width = conv.shape
    f32, low = jnp.float32, jnp.bfloat16
    waves = (RADIX, 2 * HALF, width)
    vmem = pl.BlockSpec(memory_space=pltpu.VMEM)
    return pl.pallas_call(
        mixer_backward_body,
        out_shape=(
            jax.ShapeDtypeStruct((length, 3 * width), low),
            jax.ShapeDtypeStruct((tap_count, width), f32),
            jax.ShapeDtypeStruct(ssm.shape, f32),
        ),
        in_specs=[vmem] * 11,
        out_specs=(vmem,) * 3,
        scratch_shapes=[
            pltpu.VMEM((length, width), f32),
            pltpu.VMEM((length, width), f32),
            pltpu.VMEM(waves, f32),
            pltpu.VMEM(waves, low),
            pltpu.VMEM(waves, low),
            pltpu.VMEM(waves, f32),
        ],
        compiler_params=pltpu.CompilerParams(vmem_limit_bytes=VMEM_LIMIT),
        name="mixer_backward",
    )(grad, proj, conv, shifted, kernel_w, taps_w, keys_w, mixed_w, ssm, to_table, from_table)


MESH = pl.DeviceIdType.MESH
TWO, FOUR = 2, 4


class Place:
    def __init__(self):
        self.s, self.d = lax.axis_index("seq"), lax.axis_index("dp")
        self.z, self.y, self.c = self.d // 4, (self.d // 2) % 2, self.d % 2

    def over_x(self):
        return (1 - self.s, self.d)

    def over_y(self):
        return (self.s, self.d + 2 - 4 * self.y)

    def over_core(self):
        return (self.s, self.d + 1 - 2 * self.c)

    def along_z(self, step):
        return (self.s, (self.d + 4 * step) % 16)

    def owner(self, index):
        return (self.s, index)


def send(source, target, send_sem, recv_sem, device):
    return pltpu.make_async_remote_copy(
        src_ref=source, dst_ref=target, send_sem=send_sem, recv_sem=recv_sem, device_id=device, device_id_type=MESH
    )


def greet_all(place):
    barrier = pltpu.get_barrier_semaphore()
    pl.semaphore_signal(barrier, inc=1, device_id=place.over_x(), device_id_type=MESH)

    def greet(step, carry):
        pl.semaphore_signal(
            barrier, inc=1, device_id=place.owner((place.d + step) % 16), device_id_type=MESH
        )
        return carry

    lax.fori_loop(1, 16, greet, 0)
    pl.semaphore_wait(barrier, 16)


def add_blocks(target, sources, count):
    def one(index, carry):
        total = sources[0](index).astype(jnp.float32)
        for source in sources[1:]:
            total = total + source(index).astype(jnp.float32)
        target(index, total)
        return carry

    lax.fori_loop(0, count, one, 0)


PIECES = (
    (0, 0, 1536, "whole"),
    (1, 0, 1536, "halved"),
    (0, 1536, 1536, "whole"),
    (1, 1536, 1536, "halved"),
    (3, 0, 1152, "apart"),
    (2, 0, 768, "halved"),
)


def reduce_body(*refs):
    count = len(PIECES)
    grads, refs = refs[:4], refs[4:]
    (small_ref, ssm_ref), refs = refs[:2], refs[2:]
    outs, refs = refs[:count], refs[count:]
    (small_out, ssm_out), refs = refs[:2], refs[2:]
    near, mine, from_x, from_y, from_z, final, last = (refs[i * count : (i + 1) * count] for i in range(7))
    refs = refs[7 * count :]
    small_all, small_sum, small_last, ssm_all, ssm_sum = refs[:5]
    (own_sem, core_s, core_r, x_s, x_r, y_s, y_r, z_s, z_r, f_s, f_r, sm_s, sm_r, ss_s, ss_r, sg_s, sg_r, last_sem) = refs[5:]
    place = Place()
    greet_all(place)

    def core_copy(k, h):
        source, start, width, way = PIECES[k]
        part = width // TWO if way == "halved" else width
        columns = grads[source].at[:, :, 1 - place.c, :, pl.ds(start + h * part, part)]
        return send(columns, near[k].at[h], core_s.at[k, h], core_r.at[k, h], place.over_core())

    def own_copy(k, h):
        source, start, width, way = PIECES[k]
        part = width // TWO if way == "halved" else width
        columns = grads[source].at[:, :, place.c, :, pl.ds(start + h * part, part)]
        return pltpu.make_async_copy(columns, mine[k].at[h], own_sem.at[k, h])

    def halves(k):
        return range(TWO if PIECES[k][3] == "halved" else 1)

    for k in range(count):
        for h in halves(k):
            core_copy(k, h).start()
            own_copy(k, h).start()

    def to_peer(source, target, send_sem, recv_sem, step):
        other = (place.d + step) % 16
        return send(source.at[other], target.at[place.d], send_sem.at[other], recv_sem.at[place.d], place.owner(other))

    def from_peer(target, send_sem, recv_sem, step):
        other = (place.d + step) % 16
        return send(target.at[other], target.at[other], send_sem.at[other], recv_sem.at[other], place.owner(other))

    def share(step):
        other = (place.d + step) % 16
        return send(
            ssm_sum.at[place.d], ssm_sum.at[place.d], sg_s.at[other], sg_r.at[place.d], place.owner(other)
        )

    def over_peers(action):
        def one(step, carry):
            action(step)
            return carry

        lax.fori_loop(1, 16, one, 0)

    over_peers(lambda step: to_peer(small_ref, small_all, sm_s, sm_r, step).start())
    over_peers(lambda step: to_peer(ssm_ref, ssm_all, ss_s, ss_r, step).start())

    def x_copy(k):
        return send(mine[k].at[1 - place.s], from_x[k], x_s.at[k], x_r.at[k], place.over_x())

    def kept(k):
        return mine[k].at[place.s] if PIECES[k][3] == "halved" else mine[k].at[0]

    def y_copy(k):
        return send(kept(k).at[:, 1 - place.y], from_y[k], y_s.at[k], y_r.at[k], place.over_y())

    def z_copy(k, step):
        other = (place.z + step) % 4
        return send(
            kept(k).at[other, place.y], from_z[k].at[step - 1], z_s.at[k, step - 1], z_r.at[k, step - 1],
            place.along_z(step),
        )

    def last_copy(k):
        return send(final[k], last[k], f_s.at[k], f_r.at[k], place.over_x())

    def add_core(k):
        for h in halves(k):
            core_copy(k, h).wait_recv()
            own_copy(k, h).wait()

            def put(index, total, h=h):
                mine[k][h, index // 2, index % 2] = total.astype(jnp.bfloat16)

            add_blocks(
                put,
                [lambda i, h=h: mine[k][h, i // 2, i % 2], lambda i, h=h: near[k][h, i // 2, i % 2]],
                8,
            )
        if PIECES[k][3] == "halved":
            x_copy(k).start()
        else:
            y_copy(k).start()

    def add_x(k):
        x_copy(k).wait_recv()

        def put(index, total):
            kept(k)[index // 2, index % 2] = total.astype(jnp.bfloat16)

        add_blocks(
            put, [lambda i: kept(k)[i // 2, i % 2], lambda i: from_x[k][i // 2, i % 2]], 8
        )
        y_copy(k).start()

    def add_y(k):
        y_copy(k).wait_recv()

        def put(index, total):
            kept(k)[index, place.y] = total.astype(jnp.bfloat16)

        add_blocks(put, [lambda i: kept(k)[i, place.y], lambda i: from_y[k][i]], 4)
        for step in range(1, 4):
            z_copy(k, step).start()

    def add_z(k):
        for step in range(1, 4):
            z_copy(k, step).wait_recv()
        total = kept(k)[place.z, place.y].astype(jnp.float32)
        for step in range(3):
            total = total + from_z[k][step].astype(jnp.float32)
        final[k][...] = total.astype(jnp.bfloat16)
        last_copy(k).start()

    def finish(k):
        last_copy(k).wait_recv()
        if PIECES[k][3] == "whole":
            outs[k][...] = (final[k][...].astype(jnp.float32) + last[k][...].astype(jnp.float32)).astype(
                outs[k].dtype
            )
        else:
            outs[k][place.s] = final[k][...]
            outs[k][1 - place.s] = last[k][...]

    for k in range(count):
        add_core(k)

    over_peers(lambda step: from_peer(ssm_all, ss_s, ss_r, step).wait_recv())
    ssm_all[place.d] = ssm_ref[place.d]
    total = ssm_all[0]
    for index in range(1, 16):
        total = total + ssm_all[index]
    ssm_sum[place.d] = total
    over_peers(lambda step: share(step).start())

    over_peers(lambda step: from_peer(small_all, sm_s, sm_r, step).wait_recv())
    total = small_ref[place.d].astype(jnp.float32)

    def add_small(step, total):
        return total + small_all[(place.d + step) % 16].astype(jnp.float32)

    small_sum[...] = lax.fori_loop(1, 16, add_small, total).astype(jnp.bfloat16)
    small_final = send(small_sum, small_last, last_sem.at[0], last_sem.at[1], place.over_x())
    small_final.start()

    order = [k for k in range(count) if PIECES[k][3] != "halved"]
    crossed = [k for k in range(count) if PIECES[k][3] == "halved"]
    for i in range(max(len(order), len(crossed))):
        if i < len(order):
            add_y(order[i])
        if i < len(crossed):
            add_x(crossed[i])
    for i in range(max(len(order), len(crossed))):
        if i < len(crossed):
            add_y(crossed[i])
        if i < len(order):
            add_z(order[i])
    for k in crossed:
        add_z(k)
    over_peers(lambda step: from_peer(ssm_sum, sg_s, sg_r, step).wait_recv())
    ssm_out[...] = ssm_sum[...]
    small_final.wait_recv()
    small_out[...] = small_sum[...].astype(jnp.float32) + small_last[...].astype(jnp.float32)
    for k in order + crossed:
        finish(k)

    for k in range(count):
        for h in halves(k):
            core_copy(k, h).wait_send()
        if PIECES[k][3] == "halved":
            x_copy(k).wait_send()
        y_copy(k).wait_send()
        for step in range(1, 4):
            z_copy(k, step).wait_send()
        last_copy(k).wait_send()
    small_final.wait_send()
    over_peers(lambda step: to_peer(small_ref, small_all, sm_s, sm_r, step).wait_send())
    over_peers(lambda step: to_peer(ssm_ref, ssm_all, ss_s, ss_r, step).wait_send())
    over_peers(lambda step: share(step).wait_send())


def reduce_gradients(down, up, out, qkv, small, ssm):
    f32, low = jnp.float32, jnp.bfloat16
    count = len(PIECES)
    owned = down.shape[3]
    vmem, anywhere = pl.BlockSpec(memory_space=pltpu.VMEM), pl.BlockSpec(memory_space=pl.ANY)
    results, near, mine, from_x, from_y, from_z, final, last = [], [], [], [], [], [], [], []
    for _, _, width, way in PIECES:
        halves = TWO if way == "halved" else 1
        part = width // halves
        results.append(jax.ShapeDtypeStruct((owned, part) if way == "whole" else (TWO, owned, part), f32 if way == "whole" else low))
        near.append(pltpu.VMEM((halves, FOUR, TWO, owned, part), low))
        mine.append(pltpu.VMEM((halves, FOUR, TWO, owned, part), low))
        from_x.append(pltpu.VMEM((FOUR, TWO, owned, part) if way == "halved" else (1, 1, 16, LANES), low))
        from_y.append(pltpu.VMEM((FOUR, owned, part), low))
        from_z.append(pltpu.VMEM((3, owned, part), low))
        final.append(pltpu.VMEM((owned, part), low))
        last.append(pltpu.VMEM((owned, part), low))
    dma = pltpu.SemaphoreType.DMA
    results += [jax.ShapeDtypeStruct(small.shape[1:], f32), jax.ShapeDtypeStruct(ssm.shape, f32)]
    return pl.pallas_call(
        reduce_body,
        out_shape=tuple(results),
        in_specs=[anywhere] * 4 + [vmem] * 2,
        out_specs=(vmem,) * (count + 2),
        scratch_shapes=near
        + mine
        + from_x
        + from_y
        + from_z
        + final
        + last
        + [
            pltpu.VMEM(small.shape, low),
            pltpu.VMEM(small.shape[1:], low),
            pltpu.VMEM(small.shape[1:], low),
            pltpu.VMEM(ssm.shape, f32),
            pltpu.VMEM(ssm.shape, f32),
            dma((count, TWO)),
            dma((count, TWO)),
            dma((count, TWO)),
            dma((count,)),
            dma((count,)),
            dma((count,)),
            dma((count,)),
            dma((count, 3)),
            dma((count, 3)),
            dma((count,)),
            dma((count,)),
            dma((16,)),
            dma((16,)),
            dma((16,)),
            dma((16,)),
            dma((16,)),
            dma((16,)),
            dma((2,)),
        ],
        compiler_params=pltpu.CompilerParams(
            collective_id=1, has_side_effects=True, vmem_limit_bytes=VMEM_LIMIT
        ),
        name="reduce_gradients",
    )(down, up, out, qkv, small, ssm)


def layer_norm_parts(values):
    average = jnp.mean(values, axis=-1, keepdims=True)
    centred = values - average
    variance = jnp.mean(centred * centred, axis=-1, keepdims=True)
    inverse = lax.rsqrt(variance + EPS_NORM)
    return centred * inverse, inverse


def layer_norm_back(upstream, normal, inverse, gain_row):
    weighted = upstream * gain_row
    average = jnp.mean(weighted, axis=-1, keepdims=True)
    overlap = jnp.mean(weighted * normal, axis=-1, keepdims=True)
    into = (weighted - average - normal * overlap) * inverse
    return into, jnp.sum(upstream * normal, axis=0), jnp.sum(upstream, axis=0)


def per_device_split(
    tokens,
    cotangent,
    attn_weight,
    mlp_weight,
    norms,
    taps,
    ssm_params,
    attn_moments,
    mlp_moments,
    norm_moments,
    tap_moments,
    ssm_moments,
):
    f32, low = jnp.float32, jnp.bfloat16
    rows, width = tokens.shape[1:]
    shares = lax.axis_size("seq")
    owners = lax.axis_size("dp")
    length = rows * shares
    part = width // shares
    half = lax.axis_index("seq")
    tap_count = taps.shape[0]
    to_table, from_table = map(jnp.asarray, transform_tables())

    owned = attn_weight.shape[0]
    columns = lax.dynamic_index_in_dim(attn_weight.reshape(owned, 4, shares, part), half, 2, False)
    qkv_shard = columns[:, :3].reshape(owned, 3 * part)
    small = lax.all_gather(jnp.concatenate([norms, taps]), "dp", axis=1, tiled=True).astype(f32)
    token_all = lax.all_gather(tokens[0], "seq", axis=0, tiled=True)
    qkv_full = lax.all_gather(qkv_shard, "dp", axis=0, tiled=True)
    out_full = lax.all_gather(attn_weight[:, 3 * width :], "dp", axis=0, tiled=True)
    mlp_full = lax.all_gather(mlp_weight, "dp", axis=1, tiled=True)
    norm_rows, tap_rows = small[:4], small[4:]
    tap_part = lax.dynamic_slice_in_dim(tap_rows, half * part, part, 1)
    ssm_turned = jnp.swapaxes(ssm_params, 1, 2)

    normal_all, inverse_all = layer_norm_parts(token_all.astype(f32))
    normed_low = (normal_all * norm_rows[0] + norm_rows[1]).astype(low)
    proj = dot(normed_low, qkv_full)
    gated, conv, shifted, kernel_w, taps_w, keys_w, mixed_w = mixer_forward(
        proj, jnp.pad(tap_part, ((0, HALF - tap_count), (0, 0))), ssm_turned, to_table, from_table
    )
    gated_rows = lax.all_to_all(gated, "seq", split_axis=0, concat_axis=1, tiled=True)
    inputs = tokens[0].astype(f32)
    residual = inputs + dot(gated_rows, out_full)
    normal_two, inverse_two = layer_norm_parts(residual)
    normed_two = (normal_two * norm_rows[2] + norm_rows[3]).astype(low)
    before = dot(normed_two, mlp_full[0])
    active, gelu_pull = jax.vjp(jax.nn.gelu, before)
    active_low = active.astype(low)
    grad_after = cotangent[0]
    layer_out = (
        residual + jnp.einsum("tf,df->td", active_low, mlp_full[1], preferred_element_type=f32)
    ).astype(low)
    grad_active = dot(grad_after, mlp_full[1])
    grad_down = jnp.einsum("td,tf->df", grad_after, active_low, preferred_element_type=f32)
    grad_before = gelu_pull(grad_active)[0].astype(low)
    grad_up = jnp.einsum("td,tf->df", normed_two, grad_before, preferred_element_type=f32)
    grad_normed_two = jnp.einsum("tf,df->td", grad_before, mlp_full[0], preferred_element_type=f32)
    into_two, gain_two, bias_two = layer_norm_back(grad_normed_two, normal_two, inverse_two, norm_rows[2])
    grad_residual = grad_after.astype(f32) + into_two
    grad_branch = grad_residual.astype(low)
    grad_out = jnp.einsum("td,te->de", gated_rows, grad_branch, preferred_element_type=f32)
    grad_gated = jnp.einsum("te,de->td", grad_branch, out_full, preferred_element_type=f32).astype(low)
    grad_gated_part = lax.all_to_all(grad_gated, "seq", split_axis=1, concat_axis=0, tiled=True)
    grad_proj, grad_taps, grad_ssm = mixer_backward(
        grad_gated_part, proj, conv, shifted, kernel_w, taps_w, keys_w, mixed_w,
        ssm_turned, to_table, from_table, tap_count,
    )
    grad_qkv = jnp.einsum("td,te->de", normed_low, grad_proj, preferred_element_type=f32)
    grad_normed = jnp.einsum("te,de->td", grad_proj, qkv_full, preferred_element_type=f32)
    grad_normed_rows = lax.psum_scatter(
        grad_normed.astype(low), "seq", scatter_dimension=0, tiled=True
    ).astype(f32)
    normal_one, inverse_one = layer_norm_parts(inputs)
    into_one, gain_one, bias_one = layer_norm_back(grad_normed_rows, normal_one, inverse_one, norm_rows[0])
    input_grad = grad_residual + into_one

    def by_owner(gradient):
        return gradient.astype(low).reshape(FOUR, TWO, TWO, owned, gradient.shape[1])

    scale = 1.0 / math.sqrt(owners * length)
    norm_part = jnp.stack([gain_one, bias_one, gain_two, bias_two])
    tap_spread = lax.dynamic_update_slice(jnp.zeros((tap_count, width), f32), grad_taps, (0, half * part))
    small_part = jnp.concatenate([norm_part, tap_spread, jnp.zeros((LANES - 4 - tap_count, width), f32)])
    sums = reduce_gradients(
        by_owner(grad_down),
        by_owner(grad_up),
        by_owner(grad_out),
        by_owner(grad_qkv),
        small_part.astype(low).T.reshape(owners, owned, LANES),
        grad_ssm.reshape(owners, -1, part),
    )
    down_sum = jnp.concatenate([sums[0], sums[2]], axis=1)
    up_sum = jnp.concatenate([sums[1][0], sums[1][1], sums[3][0], sums[3][1]], axis=1).astype(f32)
    qkv_sum = jnp.swapaxes(sums[4].reshape(shares, owned, 3, part), 0, 1).swapaxes(1, 2)
    attn_sum = jnp.concatenate(
        [qkv_sum.reshape(owned, 3 * width), sums[5][0], sums[5][1]], axis=1
    )
    mlp_sum = jnp.stack([up_sum, down_sum])
    small_sum = sums[6].T[: 4 + tap_count]
    ssm_sum = jnp.swapaxes(sums[7].reshape(ssm_turned.shape), 1, 2)

    attn_step, attn_new = adam_update(
        attn_weight.astype(f32), attn_moments, attn_sum.astype(f32) * scale, LEARN_RATE, DECAY_RATE
    )
    mlp_step, mlp_new = adam_update(
        mlp_weight.astype(f32), mlp_moments, mlp_sum.astype(f32) * scale, LEARN_RATE, DECAY_RATE
    )
    norms_step, norm_new = adam_update(norms.astype(f32), norm_moments, small_sum[:4] * scale, LEARN_RATE, 0.0)
    taps_step, tap_new = adam_update(taps.astype(f32), tap_moments, small_sum[4:] * scale, LEARN_RATE, DECAY_RATE)
    ssm_step, ssm_new = adam_update(ssm_params, ssm_moments, ssm_sum * scale, SSM_LEARN_RATE, 0.0)
    return (
        layer_out[None],
        input_grad[None],
        attn_step,
        attn_new,
        mlp_step,
        mlp_new,
        norms_step,
        norm_new,
        taps_step,
        tap_new,
        ssm_step,
        ssm_new,
    )


def solution(mesh):
    fits = (mesh.shape["seq"], mesh.shape["dp"]) == (2, 16)

    def chosen(tokens, *others):
        plan = per_device_split if fits and tokens.shape[1] * 2 == RADIX * HALF else per_device
        return plan(tokens, *others)

    return jax.shard_map(
        chosen,
        mesh=mesh,
        in_specs=(
            P("dp", "seq", None),
            P("dp", "seq", None),
            P("dp", None),
            P(None, "dp", None),
            P(None, "dp"),
            P(None, "dp"),
            P(None, "seq", None),
            P(None, "dp", None),
            P(None, None, "dp", None),
            P(None, None, "dp"),
            P(None, None, "dp"),
            P(None, None, "seq", None),
        ),
        out_specs=(
            P("dp", "seq", None),
            P("dp", "seq", None),
            P("dp", None),
            P(None, "dp", None),
            P(None, "dp", None),
            P(None, None, "dp", None),
            P(None, "dp"),
            P(None, None, "dp"),
            P(None, "dp"),
            P(None, None, "dp"),
            P(None, "seq", None),
            P(None, None, "seq", None),
        ),
        check_vma=False,
    )
```

```python
from functools import partial
import math

import jax
import jax.numpy as jnp
import ml_dtypes
import numpy as np
from jax import lax
from jax.experimental import pallas as pl
from jax.experimental.pallas import tpu as pltpu
from jax.sharding import PartitionSpec as P

DFT_ROWS = 256


EPS_NORM = 1e-05
BETA_ONE = 0.9
BETA_TWO = 0.999
ADAM_EPS = 1e-08
LEARN_RATE = 0.001
SSM_LEARN_RATE = 0.00025
DECAY_RATE = 0.1
STEP_COUNT = 10.0
HIGHEST = lax.Precision.HIGHEST


def from_behind(block, axis, distance):
    devices = range(lax.axis_size(axis))
    route = [(i - distance, i) for i in devices if i - distance in devices]
    return lax.ppermute(block, axis, route)


def as_sent(value):

    def short(part):
        return part.astype(jnp.bfloat16) if part.dtype == jnp.float32 else part

    return jax.tree.map(short, value)


def layer_norm(values, gain_row, bias_row):
    average = jnp.mean(values, axis=-1, keepdims=True)
    centred = values - average
    variance = jnp.mean(centred * centred, axis=-1, keepdims=True)
    return centred * lax.rsqrt(variance + EPS_NORM) * gain_row + bias_row


def shift_mix(rim_rows, keys_part, taps_full):
    tap_count = taps_full.shape[0]
    row_count = keys_part.shape[0]
    extended = jnp.concatenate([rim_rows, keys_part], axis=0)
    summed = jnp.zeros_like(keys_part)
    for tap_index in range(tap_count):
        begin_row = tap_count - 1 - tap_index
        summed = summed + taps_full[tap_index] * extended[begin_row : begin_row + row_count]
    return summed


def kernel_rows(length_total, ssm_full):
    inner_count = math.gcd(length_total, 128)
    outer_count = length_total // inner_count
    decay_rates = jnp.exp(ssm_full[0])
    outer_offsets = (jnp.arange(outer_count) * inner_count).astype(jnp.float32)
    inner_offsets = jnp.arange(inner_count).astype(jnp.float32)
    outer_part = ssm_full[1][:, :, None] * jnp.exp(
        -decay_rates[:, :, None] * outer_offsets[None, None, :]
    )
    inner_part = jnp.exp(-decay_rates[:, :, None] * inner_offsets[None, None, :])
    kernel = jnp.einsum("cna,cnb->cab", outer_part, inner_part, precision=HIGHEST)
    return kernel.reshape(kernel.shape[0], length_total)


def dft_tables(length_total, first_count):
    full_length = 2 * length_total
    col_count = full_length // first_count
    half_rows = first_count // 2
    row_index = jnp.arange(half_rows, dtype=jnp.int32)
    freq_index = jnp.arange(first_count, dtype=jnp.int32)
    col_index = jnp.arange(col_count, dtype=jnp.int32)
    angle_first = (
        2.0
        * math.pi
        / first_count
        * (row_index[:, None] * freq_index[None, :] % first_count).astype(jnp.float32)
    )
    angle_twist = (
        2.0 * math.pi / full_length * (freq_index[:, None] * col_index[None, :]).astype(jnp.float32)
    )
    angle_last = (
        2.0
        * math.pi
        / col_count
        * (col_index[:, None] * col_index[None, :] % col_count).astype(jnp.float32)
    )
    return (
        jnp.cos(angle_first),
        jnp.sin(angle_first),
        jnp.cos(angle_twist),
        jnp.sin(angle_twist),
        jnp.cos(angle_last),
        jnp.sin(angle_last),
    )


def forward_dft(signal, tables):
    cos_first, sin_first, cos_twist, sin_twist, cos_last, sin_last = tables
    half_rows = cos_first.shape[0]
    col_count = cos_last.shape[0]
    folded = signal.reshape(signal.shape[0], half_rows, col_count)
    real_first = jnp.einsum("cmp,mk->ckp", folded, cos_first, precision=HIGHEST)
    imaginary_first = -jnp.einsum("cmp,mk->ckp", folded, sin_first, precision=HIGHEST)
    real_twist = real_first * cos_twist + imaginary_first * sin_twist
    imaginary_twist = imaginary_first * cos_twist - real_first * sin_twist
    real_last = jnp.einsum("ckp,pq->ckq", real_twist, cos_last, precision=HIGHEST) + jnp.einsum(
        "ckp,pq->ckq", imaginary_twist, sin_last, precision=HIGHEST
    )
    imaginary_last = jnp.einsum(
        "ckp,pq->ckq", imaginary_twist, cos_last, precision=HIGHEST
    ) - jnp.einsum("ckp,pq->ckq", real_twist, sin_last, precision=HIGHEST)
    return (real_last, imaginary_last)


def inverse_dft(spectrum, tables):
    cos_first, sin_first, cos_twist, sin_twist, cos_last, sin_last = tables
    real_part, imaginary_part = spectrum
    full_length = cos_first.shape[1] * cos_last.shape[0]
    real_inner = jnp.einsum("ckq,qp->ckp", real_part, cos_last, precision=HIGHEST) - jnp.einsum(
        "ckq,qp->ckp", imaginary_part, sin_last, precision=HIGHEST
    )
    imaginary_inner = jnp.einsum(
        "ckq,qp->ckp", imaginary_part, cos_last, precision=HIGHEST
    ) + jnp.einsum("ckq,qp->ckp", real_part, sin_last, precision=HIGHEST)
    real_twist = real_inner * cos_twist - imaginary_inner * sin_twist
    imaginary_twist = imaginary_inner * cos_twist + real_inner * sin_twist
    signal = jnp.einsum("ckp,mk->cmp", real_twist, cos_first, precision=HIGHEST) - jnp.einsum(
        "ckp,mk->cmp", imaginary_twist, sin_first, precision=HIGHEST
    )
    return signal.reshape(signal.shape[0], signal.shape[1] * signal.shape[2]) / full_length


def complex_product(left, right, conjugate_left):
    left_real, left_imaginary = left
    right_real, right_imaginary = right
    if conjugate_left:
        return (
            left_real * right_real + left_imaginary * right_imaginary,
            left_real * right_imaginary - left_imaginary * right_real,
        )
    return (
        left_real * right_real - left_imaginary * right_imaginary,
        left_real * right_imaginary + left_imaginary * right_real,
    )


def adam_update(param_now, moments, gradient, learn_rate, decay_weight):
    first_new = BETA_ONE * moments[0] + (1.0 - BETA_ONE) * gradient
    second_new = BETA_TWO * moments[1] + (1.0 - BETA_TWO) * gradient * gradient
    first_hat = first_new / (1.0 - BETA_ONE**STEP_COUNT)
    second_hat = second_new / (1.0 - BETA_TWO**STEP_COUNT)
    step_size = learn_rate * (
        first_hat / (jnp.sqrt(second_hat) + ADAM_EPS) + decay_weight * param_now
    )
    return (step_size, jnp.stack([first_new, second_new]))


def per_device(
    tokens,
    cotangent,
    attn_weight,
    mlp_weight,
    norms,
    taps,
    ssm_params,
    attn_moments,
    mlp_moments,
    norm_moments,
    tap_moments,
    ssm_moments,
):
    row_count = tokens.shape[1]
    model_width = tokens.shape[2]
    group_count = lax.axis_size("seq")
    owner_count = lax.axis_size("dp")
    length_total = row_count * group_count
    attn_full, mlp_full, norm_full, taps_full = (
        lax.all_gather(attn_weight, "dp", axis=0, tiled=True),
        lax.all_gather(mlp_weight, "dp", axis=1, tiled=True),
        lax.all_gather(norms, "dp", axis=1, tiled=True),
        lax.all_gather(taps, "dp", axis=1, tiled=True),
    )
    inputs = tokens[0].astype(jnp.float32)
    cot_rows = cotangent[0].astype(jnp.float32)
    norm_values = norm_full.astype(jnp.float32)
    taps_values = taps_full.astype(jnp.float32)
    tap_count = taps_values.shape[0]
    normed, norm_pull = jax.vjp(layer_norm, inputs, norm_values[0], norm_values[1])
    normed_low = normed.astype(jnp.bfloat16)
    project = jnp.dot(
        normed_low, attn_full[:, : 3 * model_width], preferred_element_type=jnp.float32
    )
    queries = project[:, :model_width]
    keys_part = project[:, model_width : 2 * model_width]
    values = project[:, 2 * model_width :]
    rim_rows = from_behind(
        keys_part[row_count - tap_count + 1 :].astype(jnp.bfloat16), "seq", 1
    ).astype(jnp.float32)
    shifted, shift_pull = jax.vjp(shift_mix, rim_rows, keys_part, taps_values)
    mixed_rows = (shifted * values).astype(jnp.bfloat16)
    moved_in = lax.all_to_all(mixed_rows.T, "seq", split_axis=0, concat_axis=1, tiled=True).astype(
        jnp.float32
    )
    tables = dft_tables(length_total, DFT_ROWS)
    kernel, kernel_pull = jax.vjp(partial(kernel_rows, length_total), ssm_params)
    kernel_freq = forward_dft(kernel, tables)
    input_freq = forward_dft(moved_in, tables)
    conv_channels = inverse_dft(complex_product(input_freq, kernel_freq, False), tables)
    conv_back = lax.all_to_all(
        conv_channels.astype(jnp.bfloat16), "seq", split_axis=1, concat_axis=0, tiled=True
    )
    conv_rows = conv_back.T.astype(jnp.float32)
    gated_rows = (queries * conv_rows).astype(jnp.bfloat16)
    branch = jnp.dot(
        gated_rows, attn_full[:, 3 * model_width :], preferred_element_type=jnp.float32
    )
    residual_one = inputs + branch
    normed_two, norm_two_pull = jax.vjp(layer_norm, residual_one, norm_values[2], norm_values[3])
    normed_two_low = normed_two.astype(jnp.bfloat16)
    before = jnp.dot(normed_two_low, mlp_full[0], preferred_element_type=jnp.float32)
    active, gelu_pull = jax.vjp(jax.nn.gelu, before)
    active_low = active.astype(jnp.bfloat16)
    mlp_out = jnp.einsum("tf,df->td", active_low, mlp_full[1], preferred_element_type=jnp.float32)
    layer_out = (residual_one + mlp_out).astype(jnp.bfloat16)
    attn_back, mlp_back = (
        lax.all_gather(attn_weight, "dp", axis=0, tiled=True),
        lax.all_gather(mlp_weight, "dp", axis=1, tiled=True),
    )
    grad_after = cotangent[0]
    grad_active = jnp.dot(grad_after, mlp_back[1], preferred_element_type=jnp.float32)
    grad_down = jnp.einsum("td,tf->df", grad_after, active_low, preferred_element_type=jnp.float32)
    grad_before = gelu_pull(grad_active)[0].astype(jnp.bfloat16)
    grad_up = jnp.einsum(
        "td,tf->df", normed_two_low, grad_before, preferred_element_type=jnp.float32
    )
    grad_normed_two = jnp.einsum(
        "tf,df->td", grad_before, mlp_back[0], preferred_element_type=jnp.float32
    )
    grad_residual_part, grad_gain_two, grad_bias_two = norm_two_pull(grad_normed_two)
    grad_residual = cot_rows + grad_residual_part
    grad_branch = grad_residual.astype(jnp.bfloat16)
    grad_out = jnp.einsum("td,te->de", gated_rows, grad_branch, preferred_element_type=jnp.float32)
    grad_gated = jnp.einsum(
        "te,de->td",
        grad_branch,
        attn_back[:, 3 * model_width :],
        preferred_element_type=jnp.float32,
    )
    grad_queries = grad_gated * conv_rows
    grad_conv = (grad_gated * queries).astype(jnp.bfloat16)
    grad_moved = lax.all_to_all(grad_conv.T, "seq", split_axis=0, concat_axis=1, tiled=True).astype(
        jnp.float32
    )
    grad_freq = forward_dft(grad_moved, tables)
    grad_input = inverse_dft(complex_product(kernel_freq, grad_freq, True), tables)
    grad_kernel = inverse_dft(complex_product(input_freq, grad_freq, True), tables)
    grad_ssm_local = kernel_pull(grad_kernel)[0]
    grad_ssm = lax.psum(grad_ssm_local, "dp")
    grad_mixed_back = lax.all_to_all(
        grad_input.astype(jnp.bfloat16), "seq", split_axis=1, concat_axis=0, tiled=True
    )
    grad_mixed = grad_mixed_back.T.astype(jnp.float32)
    grad_shifted = grad_mixed * values
    grad_values = grad_mixed * shifted
    grad_rim, grad_keys, grad_taps = shift_pull(grad_shifted)
    returned = from_behind(as_sent(grad_rim), "seq", -1).astype(grad_rim.dtype)
    grad_keys = grad_keys + jnp.pad(returned, ((row_count - tap_count + 1, 0), (0, 0)))
    grad_project = jnp.concatenate([grad_queries, grad_keys, grad_values], axis=1).astype(
        jnp.bfloat16
    )
    grad_qkv = jnp.einsum("td,te->de", normed_low, grad_project, preferred_element_type=jnp.float32)
    grad_normed = jnp.einsum(
        "te,de->td",
        grad_project,
        attn_back[:, : 3 * model_width],
        preferred_element_type=jnp.float32,
    )
    grad_input_part, grad_gain_one, grad_bias_one = norm_pull(grad_normed)
    input_grad = grad_residual + grad_input_part
    grad_attn = jnp.concatenate([grad_qkv, grad_out], axis=1)
    grad_mlp = jnp.stack([grad_up, grad_down])
    grad_norms = jnp.stack([grad_gain_one, grad_bias_one, grad_gain_two, grad_bias_two])
    owned_part = (
        lax.psum_scatter(
            grad_attn.astype(jnp.bfloat16), "dp", scatter_dimension=0, tiled=True
        ).astype(jnp.float32),
        lax.psum_scatter(
            grad_mlp.astype(jnp.bfloat16), "dp", scatter_dimension=1, tiled=True
        ).astype(jnp.float32),
        lax.psum_scatter(
            grad_norms.astype(jnp.bfloat16), "dp", scatter_dimension=1, tiled=True
        ).astype(jnp.float32),
        lax.psum_scatter(
            grad_taps.astype(jnp.bfloat16), "dp", scatter_dimension=1, tiled=True
        ).astype(jnp.float32),
    )
    summed = (
        lax.psum(owned_part[0].astype(jnp.bfloat16), "seq").astype(jnp.float32),
        lax.psum(owned_part[1].astype(jnp.bfloat16), "seq").astype(jnp.float32),
        lax.psum(owned_part[2].astype(jnp.bfloat16), "seq").astype(jnp.float32),
        lax.psum(owned_part[3].astype(jnp.bfloat16), "seq").astype(jnp.float32),
    )
    grad_scale = 1.0 / math.sqrt(owner_count * length_total)
    attn_step, attn_moments_new = adam_update(
        attn_weight.astype(jnp.float32),
        attn_moments,
        summed[0] * grad_scale,
        LEARN_RATE,
        DECAY_RATE,
    )
    mlp_step, mlp_moments_new = adam_update(
        mlp_weight.astype(jnp.float32), mlp_moments, summed[1] * grad_scale, LEARN_RATE, DECAY_RATE
    )
    norms_step, norm_moments_new = adam_update(
        norms.astype(jnp.float32), norm_moments, summed[2] * grad_scale, LEARN_RATE, 0.0
    )
    taps_step, tap_moments_new = adam_update(
        taps.astype(jnp.float32), tap_moments, summed[3] * grad_scale, LEARN_RATE, DECAY_RATE
    )
    ssm_step, ssm_moments_new = adam_update(
        ssm_params, ssm_moments, grad_ssm * grad_scale, SSM_LEARN_RATE, 0.0
    )
    return (
        layer_out[None],
        input_grad[None],
        attn_step,
        attn_moments_new,
        mlp_step,
        mlp_moments_new,
        norms_step,
        norm_moments_new,
        taps_step,
        tap_moments_new,
        ssm_step,
        ssm_moments_new,
    )


LANES = 128
RADIX = 8
HALF = 128


def transform_tables():
    rows = np.arange(HALF)
    length = RADIX * HALF
    waves = RADIX * rows[None, :, None] + np.arange(RADIX)[:, None, None] + 0.25
    angles = 2.0 * np.pi * np.mod(rows[None, None, :] * waves, length) / length
    cosines, sines = np.cos(angles), np.sin(angles)
    full = np.concatenate(
        [np.concatenate([cosines, sines], axis=2), np.concatenate([-sines, cosines], axis=2)], axis=1
    )

    def parts(matrix):
        matrix = matrix.astype(np.float32)
        high = matrix.astype(ml_dtypes.bfloat16)
        rest = (matrix - high.astype(np.float32)).astype(ml_dtypes.bfloat16)
        return np.stack([high, rest])

    return parts(full), parts(np.swapaxes(full, 1, 2))


def turned(value, angle):
    real, imaginary = value
    cosine, sine = math.cos(angle), math.sin(angle)
    if abs(sine) < 1e-12:
        return (real, imaginary) if cosine > 0 else (-real, -imaginary)
    if abs(cosine) < 1e-12:
        return (-imaginary, real) if sine > 0 else (imaginary, -real)
    return (real * cosine - imaginary * sine, real * sine + imaginary * cosine)


def small_transform(values, sign):
    count = len(values)
    if count == 1:
        return values
    even = small_transform(values[::2], sign)
    odd = small_transform(values[1::2], sign)
    low, high = [], []
    for index in range(count // 2):
        (er, ei), (tr, ti) = even[index], turned(odd[index], sign * 2.0 * math.pi * index / count)
        low.append((er + tr, ei + ti))
        high.append((er - tr, ei - ti))
    return low + high


def split(value):
    high = value.astype(jnp.bfloat16)
    return high, (value - high.astype(jnp.float32)).astype(jnp.bfloat16)


def dot(left, right):
    return jnp.dot(left, right, preferred_element_type=jnp.float32)


def each_tile(width, rows, step, body):
    for block in range(width // LANES):

        def one(index, carry, block=block):
            body(pl.multiple_of(index * step, step), pl.ds(block * LANES, LANES))
            return carry

        lax.fori_loop(0, rows // step, one, 0)


def to_waves(width, read, used, w_ref, high_ref, low_ref, store):
    def first(row, cols):
        inputs = []
        for part in range(used):
            x = read(part * HALF, row, cols)
            angle = -2.0 * math.pi * part / 32.0
            inputs.append((x * math.cos(angle), x * math.sin(angle)) if part else (x, jnp.zeros_like(x)))
        while len(inputs) < RADIX:
            inputs.append((jnp.zeros_like(x), jnp.zeros_like(x)))
        for wave, value in enumerate(small_transform(inputs, -1.0)):
            for place, part in enumerate(value):
                high, low = split(part)
                high_ref[wave, pl.ds(row + place * HALF, 16), cols] = high
                low_ref[wave, pl.ds(row + place * HALF, 16), cols] = low

    each_tile(width, HALF, 16, first)

    def second(wave, carry):
        high = high_ref[wave]
        store(wave, dot(w_ref[0, wave], high) + dot(w_ref[1, wave], high) + dot(w_ref[0, wave], low_ref[wave]))
        return carry

    lax.fori_loop(0, RADIX, second, 0)


def product(width, left_ref, right_ref, conjugate, high_ref, low_ref):
    sign = -1.0 if conjugate else 1.0

    def one(wave, carry):
        def tile(row, cols):
            lr, li = left_ref[wave, pl.ds(row, 16), cols], left_ref[wave, pl.ds(row + HALF, 16), cols] * sign
            rr, ri = right_ref[wave, pl.ds(row, 16), cols], right_ref[wave, pl.ds(row + HALF, 16), cols]
            for place, part in enumerate((lr * rr - li * ri, lr * ri + li * rr)):
                high, low = split(part)
                high_ref[wave, pl.ds(row + place * HALF, 16), cols] = high
                low_ref[wave, pl.ds(row + place * HALF, 16), cols] = low

        each_tile(width, HALF, 16, tile)
        return carry

    lax.fori_loop(0, RADIX, one, 0)


def from_waves(width, w_ref, high_ref, low_ref, back_ref, put):
    def second(wave, carry):
        high = high_ref[wave]
        back_ref[wave] = dot(w_ref[0, wave], high) + dot(w_ref[1, wave], high) + dot(w_ref[0, wave], low_ref[wave])
        return carry

    lax.fori_loop(0, RADIX, second, 0)
    scale = 1.0 / (RADIX * HALF)

    def first(row, cols):
        values = [
            (back_ref[wave, pl.ds(row, 16), cols], back_ref[wave, pl.ds(row + HALF, 16), cols])
            for wave in range(RADIX)
        ]
        for part, (real, imaginary) in enumerate(small_transform(values, 1.0)):
            angle = 2.0 * math.pi * part / 32.0
            put(part * HALF, row, cols, real * (math.cos(angle) * scale) - imaginary * (math.sin(angle) * scale))

    each_tile(width, HALF, 16, first)


def first_positions(width, count, w_ref, high_ref, low_ref):
    total = jnp.zeros((count, width), jnp.float32)
    for wave in range(RADIX):
        wh, wl = w_ref[0, wave, :count, :], w_ref[1, wave, :count, :]
        high = high_ref[wave]
        total = total + (dot(wh, high) + dot(wl, high) + dot(wh, low_ref[wave]))
    return total * (1.0 / (RADIX * HALF))


FINE = 32


def decay_sums(width, length, ssm_ref, out_ref):
    modes = ssm_ref.shape[1]
    steps = length // FINE
    out_ref[...] = jnp.zeros(out_ref.shape, jnp.float32)
    for block in range(width // LANES):
        cols = pl.ds(block * LANES, LANES)
        offsets = lax.broadcasted_iota(jnp.int32, (FINE, LANES), 0).astype(jnp.float32)

        def group(index, carry, cols=cols, offsets=offsets):
            base = pl.multiple_of(index * 8, 8)
            rates = jnp.exp(ssm_ref[0, pl.ds(base, 8), cols])
            leaps = jnp.exp(-rates * FINE)
            weights = ssm_ref[1, pl.ds(base, 8), cols]
            terms = tuple(weights[i : i + 1] * jnp.exp(-rates[i : i + 1] * offsets) for i in range(8))
            leap_rows = [leaps[i : i + 1] for i in range(8)]

            def step(number, terms, leap_rows=leap_rows):
                rows = pl.ds(pl.multiple_of(number * FINE, FINE), FINE)
                total = out_ref[rows, cols]
                for term in terms:
                    total = total + term
                out_ref[rows, cols] = total
                return tuple(term * leap for term, leap in zip(terms, leap_rows))

            lax.fori_loop(0, steps, step, terms)
            return carry

        lax.fori_loop(0, modes // 8, group, 0)


def decay_gradients(width, length, ssm_ref, grad_ref, out_ref):
    modes = ssm_ref.shape[1]
    steps = length // FINE
    for block in range(width // LANES):
        cols = pl.ds(block * LANES, LANES)
        offsets = lax.broadcasted_iota(jnp.int32, (FINE, LANES), 0).astype(jnp.float32)

        def group(index, carry, cols=cols, offsets=offsets):
            base = pl.multiple_of(index * 8, 8)
            rates = jnp.exp(ssm_ref[0, pl.ds(base, 8), cols])
            leaps = jnp.exp(-rates * FINE)
            plain_rows, slope_rows = [], []
            for modes_now in ((0, 1, 2, 3), (4, 5, 6, 7)):
                zero = offsets * 0.0
                leap_rows = [leaps[i : i + 1] for i in modes_now]

                def step(number, sums, leap_rows=leap_rows):
                    rows = grad_ref[pl.ds(pl.multiple_of((steps - 1 - number) * FINE, FINE), FINE), cols]
                    return tuple((v * leap + rows, w * leap + v) for (v, w), leap in zip(sums, leap_rows))

                sums = lax.fori_loop(0, steps, step, tuple((zero, zero) for _ in modes_now))
                for i, (v, w) in zip(modes_now, sums):
                    fine = jnp.exp(-rates[i : i + 1] * offsets)
                    plain = fine * v
                    slope = fine * w * (leaps[i : i + 1] * FINE) + plain * offsets
                    plain_rows.append(jnp.sum(plain, axis=0, keepdims=True))
                    slope_rows.append(jnp.sum(slope, axis=0, keepdims=True))
            out_ref[1, pl.ds(base, 8), cols] = jnp.concatenate(plain_rows, axis=0)
            out_ref[0, pl.ds(base, 8), cols] = (
                -ssm_ref[1, pl.ds(base, 8), cols] * rates * jnp.concatenate(slope_rows, axis=0)
            )
            return carry

        lax.fori_loop(0, modes // 8, group, 0)


def layer_norm_parts(values):
    average = jnp.mean(values, axis=-1, keepdims=True)
    centred = values - average
    variance = jnp.mean(centred * centred, axis=-1, keepdims=True)
    inverse = lax.rsqrt(variance + EPS_NORM)
    return centred * inverse, inverse


MESH = pl.DeviceIdType.MESH
TWO, FOUR = 2, 4
TAP_ROWS = 64
VMEM_LIMIT = 58 * 1024 * 1024


class Place:
    def __init__(self):
        self.s, self.d = lax.axis_index("seq"), lax.axis_index("dp")
        self.z, self.y, self.c = self.d // 4, (self.d // 2) % 2, self.d % 2

    def over_x(self):
        return (1 - self.s, self.d)

    def over_y(self):
        return (self.s, self.d + 2 - 4 * self.y)

    def over_core(self):
        return (self.s, self.d + 1 - 2 * self.c)

    def along_z(self, step):
        return (self.s, (self.d + 4 * step) % 16)

    def owner(self, index):
        return (self.s, index)


def send(source, target, send_sem, recv_sem, device):
    return pltpu.make_async_remote_copy(
        src_ref=source, dst_ref=target, send_sem=send_sem, recv_sem=recv_sem, device_id=device, device_id_type=MESH
    )


def greet_all(place):
    barrier = pltpu.get_barrier_semaphore()
    pl.semaphore_signal(barrier, inc=1, device_id=place.over_x(), device_id_type=MESH)

    def greet(step, carry):
        pl.semaphore_signal(
            barrier, inc=1, device_id=place.owner((place.d + step) % 16), device_id_type=MESH
        )
        return carry

    lax.fori_loop(1, 16, greet, 0)
    pl.semaphore_wait(barrier, 16)


WEIGHTS = (
    ("up", 0, 1536, "halved"),
    ("up", 1536, 1536, "halved"),
    ("out", 0, 768, "whole"),
    ("down", 0, 1536, "whole"),
    ("down", 1536, 1536, "whole"),
)


def forward_body(
    token_ref, qkv_ref, out_shard, mlp_shard, small_ref, ssm_ref, to_ref, from_ref,
    qkv_full, out_full, up_full, down_full, small_t, normed_ref, proj_ref, rows_ref,
    conv_ref, shifted_ref, kernel_w, taps_w, keys_w, mixed_w,
    token_all, small_all, gated_ref, line_ref, high_ref, low_ref, back_ref,
    own_sem, z_s, z_r, y_s, y_r, x_s, x_r, core_s, core_r, small_s, small_r, side_s, side_r,
):
    length, width = conv_ref.shape
    own_rows = token_ref.shape[0]
    place = Place()
    qkv = len(WEIGHTS)
    shards = {"up": mlp_shard.at[0], "down": mlp_shard.at[1], "out": out_shard}
    fulls = {"up": up_full, "down": down_full, "out": out_full}

    def columns(k):
        source, start, count, way = WEIGHTS[k]
        if way == "whole":
            return source, pl.ds(start, count)
        return source, pl.ds(pl.multiple_of(start + place.s * (count // 2), LANES), count // 2)

    def z_copy(k, step):
        if k == qkv:
            source, target = qkv_ref, qkv_full.at[place.z, place.y, place.c]
        else:
            name, cols = columns(k)
            source, target = shards[name].at[:, cols], fulls[name].at[place.z, place.y, place.c, :, cols]
        return send(source, target, z_s.at[k, step - 1], z_r.at[k, step - 1], place.along_z(step))

    def y_copy(k):
        if k == qkv:
            blocks = qkv_full.at[:, place.y, place.c]
        else:
            name, cols = columns(k)
            blocks = fulls[name].at[:, place.y, place.c, :, cols]
        return send(blocks, blocks, y_s.at[k], y_r.at[k], place.over_y())

    def x_copy(k):
        name, cols = columns(k)
        blocks = fulls[name].at[:, :, place.c, :, cols]
        return send(blocks, blocks, x_s.at[k], x_r.at[k], place.over_x())

    def core_copy(k):
        if k == qkv:
            blocks = qkv_full.at[:, :, place.c]
        else:
            name, start, count, _ = WEIGHTS[k]
            blocks = fulls[name].at[:, :, place.c, :, pl.ds(start, count)]
        return send(blocks, blocks, core_s.at[k], core_r.at[k], place.over_core())

    def own_copies():
        copies = []
        for k in range(qkv):
            name, cols = columns(k)
            target = fulls[name].at[place.z, place.y, place.c, :, cols]
            copies.append(pltpu.make_async_copy(shards[name].at[:, cols], target, own_sem.at[k]))
        return copies

    def start_z(k):
        for step in range(1, 4):
            z_copy(k, step).start()

    def z_to_y(k):
        for step in range(1, 4):
            z_copy(k, step).wait_recv()
        y_copy(k).start()

    def y_on(k):
        y_copy(k).wait_recv()
        if k != qkv and WEIGHTS[k][3] == "halved":
            x_copy(k).start()
        else:
            core_copy(k).start()

    def x_on(k):
        x_copy(k).wait_recv()
        core_copy(k).start()

    def small_copy(step):
        other = (place.d + step) % 16
        return send(small_ref, small_all.at[place.d], small_s.at[other], small_r.at[place.d], place.owner(other))

    def small_arrival(step):
        other = (place.d + step) % 16
        return send(small_ref, small_all.at[other], small_s.at[other], small_r.at[other], place.owner(other))

    def over_peers(action):
        def one(step, carry):
            action(step)
            return carry

        lax.fori_loop(1, 16, one, 0)

    token_copy = send(token_ref, token_all.at[place.s], side_s.at[0], side_r.at[0], place.over_x())
    gated_copy = send(
        gated_ref.at[1 - place.s], rows_ref.at[place.s], side_s.at[1], side_r.at[1], place.over_x()
    )

    greet_all(place)
    over_peers(lambda step: small_copy(step).start())
    start_z(qkv)
    token_copy.start()
    for copy in own_copies():
        copy.start()
    qkv_full[place.z, place.y, place.c] = qkv_ref[...]
    small_all[place.d] = small_ref[...]

    def keep(target):
        def store(wave, value):
            target[wave] = value

        return store

    def lines(base, row, cols):
        return line_ref[pl.ds(base + row, 16), cols]

    def column(index, cols):
        return pl.ds(index * width + cols.start, cols.size)

    decay_sums(width, length, ssm_ref, line_ref)
    z_to_y(qkv)
    for k in range(qkv):
        if k < 2:
            start_z(k)
    to_waves(width, lines, RADIX, to_ref, high_ref, low_ref, keep(kernel_w))
    over_peers(lambda step: small_arrival(step).wait_recv())
    small_t[...] = small_all[...].reshape(16 * small_all.shape[1], LANES).astype(jnp.float32).T
    taps_cols = pl.multiple_of(place.s * width, LANES)

    def read_taps(base, row, cols):
        taps = small_t[pl.ds(base + row, 16), pl.ds(pl.multiple_of(taps_cols + cols.start, LANES), LANES)]
        inside = lax.broadcasted_iota(jnp.int32, taps.shape, 0) + (base + row) < TAP_ROWS
        return jnp.where(inside, taps, 0.0)

    y_on(qkv)
    to_waves(width, read_taps, 1, to_ref, high_ref, low_ref, keep(taps_w))

    def normalize(source, begin):
        def one(index, carry):
            row = pl.multiple_of(index * 32, 32)
            normal, _ = layer_norm_parts(source[pl.ds(row, 32), :].astype(jnp.float32))
            scaled = normal * small_t[TAP_ROWS : TAP_ROWS + 1, :] + small_t[TAP_ROWS + 1 : TAP_ROWS + 2, :]
            normed_ref[pl.ds(pl.multiple_of(begin + row, 32), 32), :] = scaled.astype(jnp.bfloat16)
            return carry

        lax.fori_loop(0, own_rows // 32, one, 0)

    def project(begin):
        weight = qkv_full[...].reshape(normed_ref.shape[1], 3 * width)

        def one(index, carry):
            row = pl.ds(pl.multiple_of(begin + index * 256, 256), 256)
            proj_ref[row, :] = dot(normed_ref[row, :], weight)
            return carry

        lax.fori_loop(0, own_rows // 256, one, 0)

    own_begin, other_begin = place.s * own_rows, (1 - place.s) * own_rows
    normalize(token_ref, own_begin)
    for copy in own_copies():
        copy.wait()
    z_to_y(0)
    start_z(2)
    token_copy.wait_recv()
    normalize(token_all.at[1 - place.s], other_begin)
    core_copy(qkv).wait_recv()
    project(own_begin)
    z_to_y(1)
    y_on(0)
    start_z(3)
    project(other_begin)
    z_to_y(2)
    start_z(4)
    y_on(1)
    to_waves(
        width, lambda base, row, cols: proj_ref[pl.ds(base + row, 16), column(1, cols)],
        RADIX, to_ref, high_ref, low_ref, keep(keys_w),
    )
    product(width, taps_w, keys_w, False, high_ref, low_ref)
    y_on(2)
    x_on(0)

    def put_shifted(base, row, cols, value):
        rows = pl.ds(base + row, 16)
        shifted_ref[rows, cols] = value
        mixed = value * proj_ref[rows, column(2, cols)]
        line_ref[rows, cols] = mixed.astype(jnp.bfloat16).astype(jnp.float32)

    from_waves(width, from_ref, high_ref, low_ref, back_ref, put_shifted)
    z_to_y(3)
    to_waves(width, lines, RADIX, to_ref, high_ref, low_ref, keep(mixed_w))
    x_on(1)
    product(width, kernel_w, mixed_w, False, high_ref, low_ref)

    def put_conv(base, row, cols, value):
        rows = pl.ds(base + row, 16)
        rounded = value.astype(jnp.bfloat16)
        conv_ref[rows, cols] = rounded
        gated = (proj_ref[rows, cols] * rounded.astype(jnp.float32)).astype(jnp.bfloat16)
        gated_ref[base // own_rows, pl.ds(base % own_rows + row, 16), cols] = gated

    from_waves(width, from_ref, high_ref, low_ref, back_ref, put_conv)
    gated_copy.start()
    z_to_y(4)
    y_on(3)
    rows_ref[place.s] = gated_ref[place.s]
    y_on(4)
    gated_copy.wait_recv()
    for k in range(qkv):
        core_copy(k).wait_recv()

    over_peers(lambda step: small_copy(step).wait_send())
    token_copy.wait_send()
    gated_copy.wait_send()
    for k in range(qkv + 1):
        for step in range(1, 4):
            z_copy(k, step).wait_send()
        y_copy(k).wait_send()
        core_copy(k).wait_send()
        if k != qkv and WEIGHTS[k][3] == "halved":
            x_copy(k).wait_send()


def mixer_backward_body(
    grad_ref, proj_ref, conv_ref, shifted_ref, kernel_w, taps_w, keys_w, mixed_w, ssm_ref, to_ref, from_ref,
    out_ref, taps_out_ref, ssm_out_ref,
    line_ref, decay_ref, wave_ref, high_ref, low_ref, back_ref,
):
    width = conv_ref.shape[1]
    length = conv_ref.shape[0]

    def keep(wave, value):
        wave_ref[wave] = value

    def lines(base, row, cols):
        return line_ref[pl.ds(base + row, 16), cols]

    def column(place, cols):
        return pl.ds(place * width + cols.start, cols.size)

    def read_conv_grad(base, row, cols):
        rows = pl.ds(base + row, 16)
        gradient = grad_ref[rows, cols].astype(jnp.float32)
        out_ref[rows, cols] = (gradient * conv_ref[rows, cols].astype(jnp.float32)).astype(jnp.bfloat16)
        return (gradient * proj_ref[rows, cols]).astype(jnp.bfloat16).astype(jnp.float32)

    to_waves(width, read_conv_grad, RADIX, to_ref, high_ref, low_ref, keep)
    product(width, kernel_w, wave_ref, True, high_ref, low_ref)

    def put_mixed(base, row, cols, value):
        rows = pl.ds(base + row, 16)
        gradient = value.astype(jnp.bfloat16).astype(jnp.float32)
        out_ref[rows, column(2, cols)] = (gradient * shifted_ref[rows, cols]).astype(jnp.bfloat16)
        line_ref[rows, cols] = gradient * proj_ref[rows, column(2, cols)]

    from_waves(width, from_ref, high_ref, low_ref, back_ref, put_mixed)
    product(width, mixed_w, wave_ref, True, high_ref, low_ref)

    def put_kernel(base, row, cols, value):
        decay_ref[pl.ds(base + row, 16), cols] = value

    from_waves(width, from_ref, high_ref, low_ref, back_ref, put_kernel)
    to_waves(width, lines, RADIX, to_ref, high_ref, low_ref, keep)
    product(width, taps_w, wave_ref, True, high_ref, low_ref)

    def put_keys(base, row, cols, value):
        out_ref[pl.ds(base + row, 16), column(1, cols)] = value.astype(jnp.bfloat16)

    from_waves(width, from_ref, high_ref, low_ref, back_ref, put_keys)
    product(width, keys_w, wave_ref, True, high_ref, low_ref)
    taps_out_ref[...] = first_positions(width, taps_out_ref.shape[0], from_ref, high_ref, low_ref)
    decay_gradients(width, length, ssm_ref, decay_ref, ssm_out_ref)


def forward_mixer(tokens, qkv_shard, out_shard, mlp_shard, small, ssm, to_table, from_table):
    own_rows, model = tokens.shape
    owned = qkv_shard.shape[0]
    width = qkv_shard.shape[1] // 3
    length = 2 * own_rows
    hidden = mlp_shard.shape[2]
    f32, low = jnp.float32, jnp.bfloat16
    waves = (RADIX, 2 * HALF, width)
    vmem, anywhere = pl.BlockSpec(memory_space=pltpu.VMEM), pl.BlockSpec(memory_space=pl.ANY)
    shape = jax.ShapeDtypeStruct
    owners = (FOUR, TWO, TWO, owned)
    count = len(WEIGHTS)
    dma = pltpu.SemaphoreType.DMA
    return pl.pallas_call(
        forward_body,
        out_shape=(
            shape(owners + (3 * width,), low),
            shape(owners + (model,), low),
            shape(owners + (hidden,), low),
            shape(owners + (hidden,), low),
            shape((LANES, model), f32),
            shape((length, model), low),
            shape((length, 3 * width), f32),
            shape((2, own_rows, width), low),
            shape((length, width), low),
            shape((length, width), f32),
        )
        + (shape(waves, f32),) * 4,
        in_specs=[vmem, vmem, anywhere, anywhere, vmem, vmem, vmem, vmem],
        out_specs=(vmem, anywhere, anywhere, anywhere) + (vmem,) * 10,
        scratch_shapes=[
            pltpu.VMEM((2, own_rows, model), low),
            pltpu.VMEM((16,) + small.shape, low),
            pltpu.VMEM((2, own_rows, width), low),
            pltpu.VMEM((length, width), f32),
            pltpu.VMEM(waves, low),
            pltpu.VMEM(waves, low),
            pltpu.VMEM(waves, f32),
            dma((count,)),
            dma((count + 1, 3)),
            dma((count + 1, 3)),
            dma((count + 1,)),
            dma((count + 1,)),
            dma((count + 1,)),
            dma((count + 1,)),
            dma((count + 1,)),
            dma((count + 1,)),
            dma((16,)),
            dma((16,)),
            dma((2,)),
            dma((2,)),
        ],
        compiler_params=pltpu.CompilerParams(collective_id=2, has_side_effects=True, vmem_limit_bytes=VMEM_LIMIT),
        name="forward_mixer",
    )(tokens, qkv_shard, out_shard, mlp_shard, small, ssm, to_table, from_table)


def mixer_backward(grad, proj, conv, shifted, kernel_w, taps_w, keys_w, mixed_w, ssm, to_table, from_table, tap_count):
    length, width = conv.shape
    f32, low = jnp.float32, jnp.bfloat16
    waves = (RADIX, 2 * HALF, width)
    vmem = pl.BlockSpec(memory_space=pltpu.VMEM)
    return pl.pallas_call(
        mixer_backward_body,
        out_shape=(
            jax.ShapeDtypeStruct((length, 3 * width), low),
            jax.ShapeDtypeStruct((tap_count, width), f32),
            jax.ShapeDtypeStruct(ssm.shape, f32),
        ),
        in_specs=[vmem] * 11,
        out_specs=(vmem,) * 3,
        scratch_shapes=[
            pltpu.VMEM((length, width), f32),
            pltpu.VMEM((length, width), f32),
            pltpu.VMEM(waves, f32),
            pltpu.VMEM(waves, low),
            pltpu.VMEM(waves, low),
            pltpu.VMEM(waves, f32),
        ],
        compiler_params=pltpu.CompilerParams(vmem_limit_bytes=VMEM_LIMIT),
        name="mixer_backward",
    )(grad, proj, conv, shifted, kernel_w, taps_w, keys_w, mixed_w, ssm, to_table, from_table)


def add_blocks(target, sources, count):
    def one(index, carry):
        total = sources[0](index).astype(jnp.float32)
        for source in sources[1:]:
            total = total + source(index).astype(jnp.float32)
        target(index, total)
        return carry

    lax.fori_loop(0, count, one, 0)


PIECES = (
    (0, 0, 1536, "whole"),
    (1, 0, 1536, "halved"),
    (0, 1536, 1536, "whole"),
    (1, 1536, 1536, "halved"),
    (3, 0, 1152, "apart"),
    (2, 0, 768, "halved"),
)


def reduce_body(*refs):
    count = len(PIECES)
    grads, refs = refs[:4], refs[4:]
    (small_ref, ssm_ref), refs = refs[:2], refs[2:]
    outs, refs = refs[:count], refs[count:]
    (small_out, ssm_out), refs = refs[:2], refs[2:]
    near, mine, from_x, from_y, from_z, final, last = (refs[i * count : (i + 1) * count] for i in range(7))
    refs = refs[7 * count :]
    small_all, small_sum, small_last, ssm_all, ssm_sum = refs[:5]
    (own_sem, core_s, core_r, x_s, x_r, y_s, y_r, z_s, z_r, f_s, f_r, sm_s, sm_r, ss_s, ss_r, sg_s, sg_r, last_sem) = refs[5:]
    place = Place()
    greet_all(place)

    def core_copy(k, h):
        source, start, width, way = PIECES[k]
        part = width // TWO if way == "halved" else width
        columns = grads[source].at[:, :, 1 - place.c, :, pl.ds(start + h * part, part)]
        return send(columns, near[k].at[h], core_s.at[k, h], core_r.at[k, h], place.over_core())

    def own_copy(k, h):
        source, start, width, way = PIECES[k]
        part = width // TWO if way == "halved" else width
        columns = grads[source].at[:, :, place.c, :, pl.ds(start + h * part, part)]
        return pltpu.make_async_copy(columns, mine[k].at[h], own_sem.at[k, h])

    def halves(k):
        return range(TWO if PIECES[k][3] == "halved" else 1)

    for k in range(count):
        for h in halves(k):
            core_copy(k, h).start()
            own_copy(k, h).start()

    def to_peer(source, target, send_sem, recv_sem, step):
        other = (place.d + step) % 16
        return send(source.at[other], target.at[place.d], send_sem.at[other], recv_sem.at[place.d], place.owner(other))

    def from_peer(target, send_sem, recv_sem, step):
        other = (place.d + step) % 16
        return send(target.at[other], target.at[other], send_sem.at[other], recv_sem.at[other], place.owner(other))

    def share(step):
        other = (place.d + step) % 16
        return send(
            ssm_sum.at[place.d], ssm_sum.at[place.d], sg_s.at[other], sg_r.at[place.d], place.owner(other)
        )

    def over_peers(action):
        def one(step, carry):
            action(step)
            return carry

        lax.fori_loop(1, 16, one, 0)

    over_peers(lambda step: to_peer(small_ref, small_all, sm_s, sm_r, step).start())
    over_peers(lambda step: to_peer(ssm_ref, ssm_all, ss_s, ss_r, step).start())

    def x_copy(k):
        return send(mine[k].at[1 - place.s], from_x[k], x_s.at[k], x_r.at[k], place.over_x())

    def kept(k):
        return mine[k].at[place.s] if PIECES[k][3] == "halved" else mine[k].at[0]

    def y_copy(k):
        return send(kept(k).at[:, 1 - place.y], from_y[k], y_s.at[k], y_r.at[k], place.over_y())

    def z_copy(k, step):
        other = (place.z + step) % 4
        return send(
            kept(k).at[other, place.y], from_z[k].at[step - 1], z_s.at[k, step - 1], z_r.at[k, step - 1],
            place.along_z(step),
        )

    def last_copy(k):
        return send(final[k], last[k], f_s.at[k], f_r.at[k], place.over_x())

    def add_core(k):
        for h in halves(k):
            core_copy(k, h).wait_recv()
            own_copy(k, h).wait()

            def put(index, total, h=h):
                mine[k][h, index // 2, index % 2] = total.astype(jnp.bfloat16)

            add_blocks(
                put,
                [lambda i, h=h: mine[k][h, i // 2, i % 2], lambda i, h=h: near[k][h, i // 2, i % 2]],
                8,
            )
        if PIECES[k][3] == "halved":
            x_copy(k).start()
        else:
            y_copy(k).start()

    def add_x(k):
        x_copy(k).wait_recv()

        def put(index, total):
            kept(k)[index // 2, index % 2] = total.astype(jnp.bfloat16)

        add_blocks(
            put, [lambda i: kept(k)[i // 2, i % 2], lambda i: from_x[k][i // 2, i % 2]], 8
        )
        y_copy(k).start()

    def add_y(k):
        y_copy(k).wait_recv()

        def put(index, total):
            kept(k)[index, place.y] = total.astype(jnp.bfloat16)

        add_blocks(put, [lambda i: kept(k)[i, place.y], lambda i: from_y[k][i]], 4)
        for step in range(1, 4):
            z_copy(k, step).start()

    def add_z(k):
        for step in range(1, 4):
            z_copy(k, step).wait_recv()
        total = kept(k)[place.z, place.y].astype(jnp.float32)
        for step in range(3):
            total = total + from_z[k][step].astype(jnp.float32)
        final[k][...] = total.astype(jnp.bfloat16)
        last_copy(k).start()

    def finish(k):
        last_copy(k).wait_recv()
        if PIECES[k][3] == "whole":
            outs[k][...] = (final[k][...].astype(jnp.float32) + last[k][...].astype(jnp.float32)).astype(
                outs[k].dtype
            )
        else:
            outs[k][place.s] = final[k][...]
            outs[k][1 - place.s] = last[k][...]

    for k in range(count):
        add_core(k)

    over_peers(lambda step: from_peer(ssm_all, ss_s, ss_r, step).wait_recv())
    ssm_all[place.d] = ssm_ref[place.d]
    total = ssm_all[0]
    for index in range(1, 16):
        total = total + ssm_all[index]
    ssm_sum[place.d] = total
    over_peers(lambda step: share(step).start())

    over_peers(lambda step: from_peer(small_all, sm_s, sm_r, step).wait_recv())
    total = small_ref[place.d].astype(jnp.float32)

    def add_small(step, total):
        return total + small_all[(place.d + step) % 16].astype(jnp.float32)

    small_sum[...] = lax.fori_loop(1, 16, add_small, total).astype(jnp.bfloat16)
    small_final = send(small_sum, small_last, last_sem.at[0], last_sem.at[1], place.over_x())
    small_final.start()

    order = [k for k in range(count) if PIECES[k][3] != "halved"]
    crossed = [k for k in range(count) if PIECES[k][3] == "halved"]
    for i in range(max(len(order), len(crossed))):
        if i < len(order):
            add_y(order[i])
        if i < len(crossed):
            add_x(crossed[i])
    for i in range(max(len(order), len(crossed))):
        if i < len(crossed):
            add_y(crossed[i])
        if i < len(order):
            add_z(order[i])
    for k in crossed:
        add_z(k)
    over_peers(lambda step: from_peer(ssm_sum, sg_s, sg_r, step).wait_recv())
    ssm_out[...] = ssm_sum[...]
    small_final.wait_recv()
    small_out[...] = small_sum[...].astype(jnp.float32) + small_last[...].astype(jnp.float32)
    for k in order + crossed:
        finish(k)

    for k in range(count):
        for h in halves(k):
            core_copy(k, h).wait_send()
        if PIECES[k][3] == "halved":
            x_copy(k).wait_send()
        y_copy(k).wait_send()
        for step in range(1, 4):
            z_copy(k, step).wait_send()
        last_copy(k).wait_send()
    small_final.wait_send()
    over_peers(lambda step: to_peer(small_ref, small_all, sm_s, sm_r, step).wait_send())
    over_peers(lambda step: to_peer(ssm_ref, ssm_all, ss_s, ss_r, step).wait_send())
    over_peers(lambda step: share(step).wait_send())


def reduce_gradients(down, up, out, qkv, small, ssm):
    f32, low = jnp.float32, jnp.bfloat16
    count = len(PIECES)
    owned = down.shape[3]
    vmem, anywhere = pl.BlockSpec(memory_space=pltpu.VMEM), pl.BlockSpec(memory_space=pl.ANY)
    results, near, mine, from_x, from_y, from_z, final, last = [], [], [], [], [], [], [], []
    for _, _, width, way in PIECES:
        halves = TWO if way == "halved" else 1
        part = width // halves
        results.append(jax.ShapeDtypeStruct((owned, part) if way == "whole" else (TWO, owned, part), f32 if way == "whole" else low))
        near.append(pltpu.VMEM((halves, FOUR, TWO, owned, part), low))
        mine.append(pltpu.VMEM((halves, FOUR, TWO, owned, part), low))
        from_x.append(pltpu.VMEM((FOUR, TWO, owned, part) if way == "halved" else (1, 1, 16, LANES), low))
        from_y.append(pltpu.VMEM((FOUR, owned, part), low))
        from_z.append(pltpu.VMEM((3, owned, part), low))
        final.append(pltpu.VMEM((owned, part), low))
        last.append(pltpu.VMEM((owned, part), low))
    dma = pltpu.SemaphoreType.DMA
    results += [jax.ShapeDtypeStruct(small.shape[1:], f32), jax.ShapeDtypeStruct(ssm.shape, f32)]
    return pl.pallas_call(
        reduce_body,
        out_shape=tuple(results),
        in_specs=[anywhere] * 4 + [vmem] * 2,
        out_specs=(vmem,) * (count + 2),
        scratch_shapes=near
        + mine
        + from_x
        + from_y
        + from_z
        + final
        + last
        + [
            pltpu.VMEM(small.shape, low),
            pltpu.VMEM(small.shape[1:], low),
            pltpu.VMEM(small.shape[1:], low),
            pltpu.VMEM(ssm.shape, f32),
            pltpu.VMEM(ssm.shape, f32),
            dma((count, TWO)),
            dma((count, TWO)),
            dma((count, TWO)),
            dma((count,)),
            dma((count,)),
            dma((count,)),
            dma((count,)),
            dma((count, 3)),
            dma((count, 3)),
            dma((count,)),
            dma((count,)),
            dma((16,)),
            dma((16,)),
            dma((16,)),
            dma((16,)),
            dma((16,)),
            dma((16,)),
            dma((2,)),
        ],
        compiler_params=pltpu.CompilerParams(
            collective_id=1, has_side_effects=True, vmem_limit_bytes=VMEM_LIMIT
        ),
        name="reduce_gradients",
    )(down, up, out, qkv, small, ssm)


def layer_norm_back(upstream, normal, inverse, gain_row):
    weighted = upstream * gain_row
    average = jnp.mean(weighted, axis=-1, keepdims=True)
    overlap = jnp.mean(weighted * normal, axis=-1, keepdims=True)
    into = (weighted - average - normal * overlap) * inverse
    return into, jnp.sum(upstream * normal, axis=0), jnp.sum(upstream, axis=0)


def per_device_split(
    tokens,
    cotangent,
    attn_weight,
    mlp_weight,
    norms,
    taps,
    ssm_params,
    attn_moments,
    mlp_moments,
    norm_moments,
    tap_moments,
    ssm_moments,
):
    f32, low = jnp.float32, jnp.bfloat16
    rows, width = tokens.shape[1:]
    shares = lax.axis_size("seq")
    owners = lax.axis_size("dp")
    length = rows * shares
    part = width // shares
    half = lax.axis_index("seq")
    tap_count = taps.shape[0]
    to_table, from_table = map(jnp.asarray, transform_tables())

    owned = attn_weight.shape[0]
    columns = lax.dynamic_index_in_dim(attn_weight.reshape(owned, 4, shares, part), half, 2, False)
    qkv_shard = columns[:, :3].reshape(owned, 3 * part)
    small = jnp.concatenate([taps, norms, jnp.zeros((LANES - 4 - tap_count, owned), low)]).T
    ssm_turned = jnp.swapaxes(ssm_params, 1, 2)
    (
        qkv_full, out_full, up_full, down_full, small_full, normed_low, proj, gated_parts,
        conv, shifted, kernel_w, taps_w, keys_w, mixed_w,
    ) = forward_mixer(
        tokens[0], qkv_shard, attn_weight[:, 3 * width :], mlp_weight, small, ssm_turned, to_table, from_table
    )
    qkv_full = qkv_full.reshape(width, 3 * part)
    out_full = out_full.reshape(width, width)
    mlp_full = (up_full.reshape(width, -1), down_full.reshape(width, -1))
    norm_rows = small_full[tap_count : tap_count + 4]
    gated_rows = jnp.concatenate([gated_parts[0], gated_parts[1]], axis=1)
    inputs = tokens[0].astype(f32)
    residual = inputs + dot(gated_rows, out_full)
    normal_two, inverse_two = layer_norm_parts(residual)
    normed_two = (normal_two * norm_rows[2] + norm_rows[3]).astype(low)
    before = dot(normed_two, mlp_full[0])
    active, gelu_pull = jax.vjp(jax.nn.gelu, before)
    active_low = active.astype(low)
    grad_after = cotangent[0]
    layer_out = (
        residual + jnp.einsum("tf,df->td", active_low, mlp_full[1], preferred_element_type=f32)
    ).astype(low)
    grad_active = dot(grad_after, mlp_full[1])
    grad_down = jnp.einsum("td,tf->df", grad_after, active_low, preferred_element_type=f32)
    grad_before = gelu_pull(grad_active)[0].astype(low)
    grad_up = jnp.einsum("td,tf->df", normed_two, grad_before, preferred_element_type=f32)
    grad_normed_two = jnp.einsum("tf,df->td", grad_before, mlp_full[0], preferred_element_type=f32)
    into_two, gain_two, bias_two = layer_norm_back(grad_normed_two, normal_two, inverse_two, norm_rows[2])
    grad_residual = grad_after.astype(f32) + into_two
    grad_branch = grad_residual.astype(low)
    grad_out = jnp.einsum("td,te->de", gated_rows, grad_branch, preferred_element_type=f32)
    grad_gated = jnp.einsum("te,de->td", grad_branch, out_full, preferred_element_type=f32).astype(low)
    grad_gated_part = lax.all_to_all(grad_gated, "seq", split_axis=1, concat_axis=0, tiled=True)
    grad_proj, grad_taps, grad_ssm = mixer_backward(
        grad_gated_part, proj, conv, shifted, kernel_w, taps_w, keys_w, mixed_w,
        ssm_turned, to_table, from_table, tap_count,
    )
    grad_qkv = jnp.einsum("td,te->de", normed_low, grad_proj, preferred_element_type=f32)
    grad_normed = jnp.einsum("te,de->td", grad_proj, qkv_full, preferred_element_type=f32)
    grad_normed_rows = lax.psum_scatter(
        grad_normed.astype(low), "seq", scatter_dimension=0, tiled=True
    ).astype(f32)
    normal_one, inverse_one = layer_norm_parts(inputs)
    into_one, gain_one, bias_one = layer_norm_back(grad_normed_rows, normal_one, inverse_one, norm_rows[0])
    input_grad = grad_residual + into_one

    def by_owner(gradient):
        return gradient.astype(low).reshape(FOUR, TWO, TWO, owned, gradient.shape[1])

    scale = 1.0 / math.sqrt(owners * length)
    norm_part = jnp.stack([gain_one, bias_one, gain_two, bias_two])
    tap_spread = lax.dynamic_update_slice(jnp.zeros((tap_count, width), f32), grad_taps, (0, half * part))
    small_part = jnp.concatenate([norm_part, tap_spread, jnp.zeros((LANES - 4 - tap_count, width), f32)])
    sums = reduce_gradients(
        by_owner(grad_down),
        by_owner(grad_up),
        by_owner(grad_out),
        by_owner(grad_qkv),
        small_part.astype(low).T.reshape(owners, owned, LANES),
        grad_ssm.reshape(owners, -1, part),
    )
    down_sum = jnp.concatenate([sums[0], sums[2]], axis=1)
    up_sum = jnp.concatenate([sums[1][0], sums[1][1], sums[3][0], sums[3][1]], axis=1).astype(f32)
    qkv_sum = jnp.swapaxes(sums[4].reshape(shares, owned, 3, part), 0, 1).swapaxes(1, 2)
    attn_sum = jnp.concatenate(
        [qkv_sum.reshape(owned, 3 * width), sums[5][0], sums[5][1]], axis=1
    )
    mlp_sum = jnp.stack([up_sum, down_sum])
    small_sum = sums[6].T[: 4 + tap_count]
    ssm_sum = jnp.swapaxes(sums[7].reshape(ssm_turned.shape), 1, 2)

    attn_step, attn_new = adam_update(
        attn_weight.astype(f32), attn_moments, attn_sum.astype(f32) * scale, LEARN_RATE, DECAY_RATE
    )
    mlp_step, mlp_new = adam_update(
        mlp_weight.astype(f32), mlp_moments, mlp_sum.astype(f32) * scale, LEARN_RATE, DECAY_RATE
    )
    norms_step, norm_new = adam_update(norms.astype(f32), norm_moments, small_sum[:4] * scale, LEARN_RATE, 0.0)
    taps_step, tap_new = adam_update(taps.astype(f32), tap_moments, small_sum[4:] * scale, LEARN_RATE, DECAY_RATE)
    ssm_step, ssm_new = adam_update(ssm_params, ssm_moments, ssm_sum * scale, SSM_LEARN_RATE, 0.0)
    return (
        layer_out[None],
        input_grad[None],
        attn_step,
        attn_new,
        mlp_step,
        mlp_new,
        norms_step,
        norm_new,
        taps_step,
        tap_new,
        ssm_step,
        ssm_new,
    )


def solution(mesh):
    fits = (mesh.shape["seq"], mesh.shape["dp"]) == (2, 16)

    def chosen(tokens, cotangent, attn_weight, mlp_weight, norms, taps, *others):
        fast = fits and tokens.shape[1:] == (RADIX * HALF // 2, 6 * LANES) and taps.shape[0] == TAP_ROWS
        plan = per_device_split if fast else per_device
        return plan(tokens, cotangent, attn_weight, mlp_weight, norms, taps, *others)

    return jax.shard_map(
        chosen,
        mesh=mesh,
        in_specs=(
            P("dp", "seq", None),
            P("dp", "seq", None),
            P("dp", None),
            P(None, "dp", None),
            P(None, "dp"),
            P(None, "dp"),
            P(None, "seq", None),
            P(None, "dp", None),
            P(None, None, "dp", None),
            P(None, None, "dp"),
            P(None, None, "dp"),
            P(None, None, "seq", None),
        ),
        out_specs=(
            P("dp", "seq", None),
            P("dp", "seq", None),
            P("dp", None),
            P(None, "dp", None),
            P(None, "dp", None),
            P(None, None, "dp", None),
            P(None, "dp"),
            P(None, None, "dp"),
            P(None, "dp"),
            P(None, None, "dp"),
            P(None, "seq", None),
            P(None, None, "seq", None),
        ),
        check_vma=False,
    )
```

```python
from functools import partial
import math

import jax
import jax.numpy as jnp
import ml_dtypes
import numpy as np
from jax import lax
from jax.experimental import pallas as pl
from jax.experimental.pallas import tpu as pltpu
from jax.sharding import PartitionSpec as P

DFT_ROWS = 256


EPS_NORM = 1e-05
BETA_ONE = 0.9
BETA_TWO = 0.999
ADAM_EPS = 1e-08
LEARN_RATE = 0.001
SSM_LEARN_RATE = 0.00025
DECAY_RATE = 0.1
STEP_COUNT = 10.0
HIGHEST = lax.Precision.HIGHEST


def from_behind(block, axis, distance):
    devices = range(lax.axis_size(axis))
    route = [(i - distance, i) for i in devices if i - distance in devices]
    return lax.ppermute(block, axis, route)


def as_sent(value):

    def short(part):
        return part.astype(jnp.bfloat16) if part.dtype == jnp.float32 else part

    return jax.tree.map(short, value)


def layer_norm(values, gain_row, bias_row):
    average = jnp.mean(values, axis=-1, keepdims=True)
    centred = values - average
    variance = jnp.mean(centred * centred, axis=-1, keepdims=True)
    return centred * lax.rsqrt(variance + EPS_NORM) * gain_row + bias_row


def shift_mix(rim_rows, keys_part, taps_full):
    tap_count = taps_full.shape[0]
    row_count = keys_part.shape[0]
    extended = jnp.concatenate([rim_rows, keys_part], axis=0)
    summed = jnp.zeros_like(keys_part)
    for tap_index in range(tap_count):
        begin_row = tap_count - 1 - tap_index
        summed = summed + taps_full[tap_index] * extended[begin_row : begin_row + row_count]
    return summed


def kernel_rows(length_total, ssm_full):
    inner_count = math.gcd(length_total, 128)
    outer_count = length_total // inner_count
    decay_rates = jnp.exp(ssm_full[0])
    outer_offsets = (jnp.arange(outer_count) * inner_count).astype(jnp.float32)
    inner_offsets = jnp.arange(inner_count).astype(jnp.float32)
    outer_part = ssm_full[1][:, :, None] * jnp.exp(
        -decay_rates[:, :, None] * outer_offsets[None, None, :]
    )
    inner_part = jnp.exp(-decay_rates[:, :, None] * inner_offsets[None, None, :])
    kernel = jnp.einsum("cna,cnb->cab", outer_part, inner_part, precision=HIGHEST)
    return kernel.reshape(kernel.shape[0], length_total)


def dft_tables(length_total, first_count):
    full_length = 2 * length_total
    col_count = full_length // first_count
    half_rows = first_count // 2
    row_index = jnp.arange(half_rows, dtype=jnp.int32)
    freq_index = jnp.arange(first_count, dtype=jnp.int32)
    col_index = jnp.arange(col_count, dtype=jnp.int32)
    angle_first = (
        2.0
        * math.pi
        / first_count
        * (row_index[:, None] * freq_index[None, :] % first_count).astype(jnp.float32)
    )
    angle_twist = (
        2.0 * math.pi / full_length * (freq_index[:, None] * col_index[None, :]).astype(jnp.float32)
    )
    angle_last = (
        2.0
        * math.pi
        / col_count
        * (col_index[:, None] * col_index[None, :] % col_count).astype(jnp.float32)
    )
    return (
        jnp.cos(angle_first),
        jnp.sin(angle_first),
        jnp.cos(angle_twist),
        jnp.sin(angle_twist),
        jnp.cos(angle_last),
        jnp.sin(angle_last),
    )


def forward_dft(signal, tables):
    cos_first, sin_first, cos_twist, sin_twist, cos_last, sin_last = tables
    half_rows = cos_first.shape[0]
    col_count = cos_last.shape[0]
    folded = signal.reshape(signal.shape[0], half_rows, col_count)
    real_first = jnp.einsum("cmp,mk->ckp", folded, cos_first, precision=HIGHEST)
    imaginary_first = -jnp.einsum("cmp,mk->ckp", folded, sin_first, precision=HIGHEST)
    real_twist = real_first * cos_twist + imaginary_first * sin_twist
    imaginary_twist = imaginary_first * cos_twist - real_first * sin_twist
    real_last = jnp.einsum("ckp,pq->ckq", real_twist, cos_last, precision=HIGHEST) + jnp.einsum(
        "ckp,pq->ckq", imaginary_twist, sin_last, precision=HIGHEST
    )
    imaginary_last = jnp.einsum(
        "ckp,pq->ckq", imaginary_twist, cos_last, precision=HIGHEST
    ) - jnp.einsum("ckp,pq->ckq", real_twist, sin_last, precision=HIGHEST)
    return (real_last, imaginary_last)


def inverse_dft(spectrum, tables):
    cos_first, sin_first, cos_twist, sin_twist, cos_last, sin_last = tables
    real_part, imaginary_part = spectrum
    full_length = cos_first.shape[1] * cos_last.shape[0]
    real_inner = jnp.einsum("ckq,qp->ckp", real_part, cos_last, precision=HIGHEST) - jnp.einsum(
        "ckq,qp->ckp", imaginary_part, sin_last, precision=HIGHEST
    )
    imaginary_inner = jnp.einsum(
        "ckq,qp->ckp", imaginary_part, cos_last, precision=HIGHEST
    ) + jnp.einsum("ckq,qp->ckp", real_part, sin_last, precision=HIGHEST)
    real_twist = real_inner * cos_twist - imaginary_inner * sin_twist
    imaginary_twist = imaginary_inner * cos_twist + real_inner * sin_twist
    signal = jnp.einsum("ckp,mk->cmp", real_twist, cos_first, precision=HIGHEST) - jnp.einsum(
        "ckp,mk->cmp", imaginary_twist, sin_first, precision=HIGHEST
    )
    return signal.reshape(signal.shape[0], signal.shape[1] * signal.shape[2]) / full_length


def complex_product(left, right, conjugate_left):
    left_real, left_imaginary = left
    right_real, right_imaginary = right
    if conjugate_left:
        return (
            left_real * right_real + left_imaginary * right_imaginary,
            left_real * right_imaginary - left_imaginary * right_real,
        )
    return (
        left_real * right_real - left_imaginary * right_imaginary,
        left_real * right_imaginary + left_imaginary * right_real,
    )


def adam_update(param_now, moments, gradient, learn_rate, decay_weight):
    first_new = BETA_ONE * moments[0] + (1.0 - BETA_ONE) * gradient
    second_new = BETA_TWO * moments[1] + (1.0 - BETA_TWO) * gradient * gradient
    first_hat = first_new / (1.0 - BETA_ONE**STEP_COUNT)
    second_hat = second_new / (1.0 - BETA_TWO**STEP_COUNT)
    step_size = learn_rate * (
        first_hat / (jnp.sqrt(second_hat) + ADAM_EPS) + decay_weight * param_now
    )
    return (step_size, jnp.stack([first_new, second_new]))


def per_device(
    tokens,
    cotangent,
    attn_weight,
    mlp_weight,
    norms,
    taps,
    ssm_params,
    attn_moments,
    mlp_moments,
    norm_moments,
    tap_moments,
    ssm_moments,
):
    row_count = tokens.shape[1]
    model_width = tokens.shape[2]
    group_count = lax.axis_size("seq")
    owner_count = lax.axis_size("dp")
    length_total = row_count * group_count
    attn_full, mlp_full, norm_full, taps_full = (
        lax.all_gather(attn_weight, "dp", axis=0, tiled=True),
        lax.all_gather(mlp_weight, "dp", axis=1, tiled=True),
        lax.all_gather(norms, "dp", axis=1, tiled=True),
        lax.all_gather(taps, "dp", axis=1, tiled=True),
    )
    inputs = tokens[0].astype(jnp.float32)
    cot_rows = cotangent[0].astype(jnp.float32)
    norm_values = norm_full.astype(jnp.float32)
    taps_values = taps_full.astype(jnp.float32)
    tap_count = taps_values.shape[0]
    normed, norm_pull = jax.vjp(layer_norm, inputs, norm_values[0], norm_values[1])
    normed_low = normed.astype(jnp.bfloat16)
    project = jnp.dot(
        normed_low, attn_full[:, : 3 * model_width], preferred_element_type=jnp.float32
    )
    queries = project[:, :model_width]
    keys_part = project[:, model_width : 2 * model_width]
    values = project[:, 2 * model_width :]
    rim_rows = from_behind(
        keys_part[row_count - tap_count + 1 :].astype(jnp.bfloat16), "seq", 1
    ).astype(jnp.float32)
    shifted, shift_pull = jax.vjp(shift_mix, rim_rows, keys_part, taps_values)
    mixed_rows = (shifted * values).astype(jnp.bfloat16)
    moved_in = lax.all_to_all(mixed_rows.T, "seq", split_axis=0, concat_axis=1, tiled=True).astype(
        jnp.float32
    )
    tables = dft_tables(length_total, DFT_ROWS)
    kernel, kernel_pull = jax.vjp(partial(kernel_rows, length_total), ssm_params)
    kernel_freq = forward_dft(kernel, tables)
    input_freq = forward_dft(moved_in, tables)
    conv_channels = inverse_dft(complex_product(input_freq, kernel_freq, False), tables)
    conv_back = lax.all_to_all(
        conv_channels.astype(jnp.bfloat16), "seq", split_axis=1, concat_axis=0, tiled=True
    )
    conv_rows = conv_back.T.astype(jnp.float32)
    gated_rows = (queries * conv_rows).astype(jnp.bfloat16)
    branch = jnp.dot(
        gated_rows, attn_full[:, 3 * model_width :], preferred_element_type=jnp.float32
    )
    residual_one = inputs + branch
    normed_two, norm_two_pull = jax.vjp(layer_norm, residual_one, norm_values[2], norm_values[3])
    normed_two_low = normed_two.astype(jnp.bfloat16)
    before = jnp.dot(normed_two_low, mlp_full[0], preferred_element_type=jnp.float32)
    active, gelu_pull = jax.vjp(jax.nn.gelu, before)
    active_low = active.astype(jnp.bfloat16)
    mlp_out = jnp.einsum("tf,df->td", active_low, mlp_full[1], preferred_element_type=jnp.float32)
    layer_out = (residual_one + mlp_out).astype(jnp.bfloat16)
    attn_back, mlp_back = (
        lax.all_gather(attn_weight, "dp", axis=0, tiled=True),
        lax.all_gather(mlp_weight, "dp", axis=1, tiled=True),
    )
    grad_after = cotangent[0]
    grad_active = jnp.dot(grad_after, mlp_back[1], preferred_element_type=jnp.float32)
    grad_down = jnp.einsum("td,tf->df", grad_after, active_low, preferred_element_type=jnp.float32)
    grad_before = gelu_pull(grad_active)[0].astype(jnp.bfloat16)
    grad_up = jnp.einsum(
        "td,tf->df", normed_two_low, grad_before, preferred_element_type=jnp.float32
    )
    grad_normed_two = jnp.einsum(
        "tf,df->td", grad_before, mlp_back[0], preferred_element_type=jnp.float32
    )
    grad_residual_part, grad_gain_two, grad_bias_two = norm_two_pull(grad_normed_two)
    grad_residual = cot_rows + grad_residual_part
    grad_branch = grad_residual.astype(jnp.bfloat16)
    grad_out = jnp.einsum("td,te->de", gated_rows, grad_branch, preferred_element_type=jnp.float32)
    grad_gated = jnp.einsum(
        "te,de->td",
        grad_branch,
        attn_back[:, 3 * model_width :],
        preferred_element_type=jnp.float32,
    )
    grad_queries = grad_gated * conv_rows
    grad_conv = (grad_gated * queries).astype(jnp.bfloat16)
    grad_moved = lax.all_to_all(grad_conv.T, "seq", split_axis=0, concat_axis=1, tiled=True).astype(
        jnp.float32
    )
    grad_freq = forward_dft(grad_moved, tables)
    grad_input = inverse_dft(complex_product(kernel_freq, grad_freq, True), tables)
    grad_kernel = inverse_dft(complex_product(input_freq, grad_freq, True), tables)
    grad_ssm_local = kernel_pull(grad_kernel)[0]
    grad_ssm = lax.psum(grad_ssm_local, "dp")
    grad_mixed_back = lax.all_to_all(
        grad_input.astype(jnp.bfloat16), "seq", split_axis=1, concat_axis=0, tiled=True
    )
    grad_mixed = grad_mixed_back.T.astype(jnp.float32)
    grad_shifted = grad_mixed * values
    grad_values = grad_mixed * shifted
    grad_rim, grad_keys, grad_taps = shift_pull(grad_shifted)
    returned = from_behind(as_sent(grad_rim), "seq", -1).astype(grad_rim.dtype)
    grad_keys = grad_keys + jnp.pad(returned, ((row_count - tap_count + 1, 0), (0, 0)))
    grad_project = jnp.concatenate([grad_queries, grad_keys, grad_values], axis=1).astype(
        jnp.bfloat16
    )
    grad_qkv = jnp.einsum("td,te->de", normed_low, grad_project, preferred_element_type=jnp.float32)
    grad_normed = jnp.einsum(
        "te,de->td",
        grad_project,
        attn_back[:, : 3 * model_width],
        preferred_element_type=jnp.float32,
    )
    grad_input_part, grad_gain_one, grad_bias_one = norm_pull(grad_normed)
    input_grad = grad_residual + grad_input_part
    grad_attn = jnp.concatenate([grad_qkv, grad_out], axis=1)
    grad_mlp = jnp.stack([grad_up, grad_down])
    grad_norms = jnp.stack([grad_gain_one, grad_bias_one, grad_gain_two, grad_bias_two])
    owned_part = (
        lax.psum_scatter(
            grad_attn.astype(jnp.bfloat16), "dp", scatter_dimension=0, tiled=True
        ).astype(jnp.float32),
        lax.psum_scatter(
            grad_mlp.astype(jnp.bfloat16), "dp", scatter_dimension=1, tiled=True
        ).astype(jnp.float32),
        lax.psum_scatter(
            grad_norms.astype(jnp.bfloat16), "dp", scatter_dimension=1, tiled=True
        ).astype(jnp.float32),
        lax.psum_scatter(
            grad_taps.astype(jnp.bfloat16), "dp", scatter_dimension=1, tiled=True
        ).astype(jnp.float32),
    )
    summed = (
        lax.psum(owned_part[0].astype(jnp.bfloat16), "seq").astype(jnp.float32),
        lax.psum(owned_part[1].astype(jnp.bfloat16), "seq").astype(jnp.float32),
        lax.psum(owned_part[2].astype(jnp.bfloat16), "seq").astype(jnp.float32),
        lax.psum(owned_part[3].astype(jnp.bfloat16), "seq").astype(jnp.float32),
    )
    grad_scale = 1.0 / math.sqrt(owner_count * length_total)
    attn_step, attn_moments_new = adam_update(
        attn_weight.astype(jnp.float32),
        attn_moments,
        summed[0] * grad_scale,
        LEARN_RATE,
        DECAY_RATE,
    )
    mlp_step, mlp_moments_new = adam_update(
        mlp_weight.astype(jnp.float32), mlp_moments, summed[1] * grad_scale, LEARN_RATE, DECAY_RATE
    )
    norms_step, norm_moments_new = adam_update(
        norms.astype(jnp.float32), norm_moments, summed[2] * grad_scale, LEARN_RATE, 0.0
    )
    taps_step, tap_moments_new = adam_update(
        taps.astype(jnp.float32), tap_moments, summed[3] * grad_scale, LEARN_RATE, DECAY_RATE
    )
    ssm_step, ssm_moments_new = adam_update(
        ssm_params, ssm_moments, grad_ssm * grad_scale, SSM_LEARN_RATE, 0.0
    )
    return (
        layer_out[None],
        input_grad[None],
        attn_step,
        attn_moments_new,
        mlp_step,
        mlp_moments_new,
        norms_step,
        norm_moments_new,
        taps_step,
        tap_moments_new,
        ssm_step,
        ssm_moments_new,
    )


LANES = 128
RADIX = 8
HALF = 128


def transform_tables():
    rows = np.arange(HALF)
    length = RADIX * HALF
    waves = RADIX * rows[None, :, None] + np.arange(RADIX)[:, None, None] + 0.25
    angles = 2.0 * np.pi * np.mod(rows[None, None, :] * waves, length) / length
    cosines, sines = np.cos(angles), np.sin(angles)
    full = np.concatenate(
        [np.concatenate([cosines, sines], axis=2), np.concatenate([-sines, cosines], axis=2)], axis=1
    )


    def parts(matrix):
        matrix = matrix.astype(np.float32)
        high = matrix.astype(ml_dtypes.bfloat16)
        rest = (matrix - high.astype(np.float32)).astype(ml_dtypes.bfloat16)
        return np.stack([high, rest])

    return parts(full), parts(np.swapaxes(full, 1, 2))


def turned(value, angle):
    real, imaginary = value
    cosine, sine = math.cos(angle), math.sin(angle)
    if abs(sine) < 1e-12:
        return (real, imaginary) if cosine > 0 else (-real, -imaginary)
    if abs(cosine) < 1e-12:
        return (-imaginary, real) if sine > 0 else (imaginary, -real)
    return (real * cosine - imaginary * sine, real * sine + imaginary * cosine)


def small_transform(values, sign):
    count = len(values)
    if count == 1:
        return values
    even = small_transform(values[::2], sign)
    odd = small_transform(values[1::2], sign)
    low, high = [], []
    for index in range(count // 2):
        (er, ei), (tr, ti) = even[index], turned(odd[index], sign * 2.0 * math.pi * index / count)
        low.append((er + tr, ei + ti))
        high.append((er - tr, ei - ti))
    return low + high


def dot(left, right):
    return jnp.dot(left, right, preferred_element_type=jnp.float32)


def keep_parts(high_ref, low_ref, wave, row, cols, value):
    high = value.astype(jnp.bfloat16)
    high_ref[wave, pl.ds(row, 16), cols] = high
    if low_ref is not None:
        low_ref[wave, pl.ds(row, 16), cols] = (value - high.astype(jnp.float32)).astype(jnp.bfloat16)


def table_dot(table_high, table_low, high_ref, low_ref, wave):
    high = high_ref[wave]
    total = dot(table_high, high) + dot(table_low, high)
    return total if low_ref is None else total + dot(table_high, low_ref[wave])


def each_tile(width, rows, step, body):
    for block in range(width // LANES):

        def one(index, carry, block=block):
            body(pl.multiple_of(index * step, step), pl.ds(block * LANES, LANES))
            return carry

        lax.fori_loop(0, rows // step, one, 0)


def to_waves(width, read, used, w_ref, high_ref, low_ref, store):
    def first(row, cols):
        inputs = []
        for part in range(used):
            x = read(part * HALF, row, cols)
            angle = -2.0 * math.pi * part / 32.0
            inputs.append((x * math.cos(angle), x * math.sin(angle)) if part else (x, jnp.zeros_like(x)))
        while len(inputs) < RADIX:
            inputs.append((jnp.zeros_like(x), jnp.zeros_like(x)))
        for wave, value in enumerate(small_transform(inputs, -1.0)):
            for place, part in enumerate(value):
                keep_parts(high_ref, low_ref, wave, row + place * HALF, cols, part)

    each_tile(width, HALF, 16, first)

    def second(wave, carry):
        store(wave, table_dot(w_ref[0, wave], w_ref[1, wave], high_ref, low_ref, wave))
        return carry

    lax.fori_loop(0, RADIX, second, 0)


def product(width, left_ref, right_ref, conjugate, high_ref, low_ref):
    sign = -1.0 if conjugate else 1.0

    def one(wave, carry):
        def tile(row, cols):
            lr, li = left_ref[wave, pl.ds(row, 16), cols], left_ref[wave, pl.ds(row + HALF, 16), cols] * sign
            rr, ri = right_ref[wave, pl.ds(row, 16), cols], right_ref[wave, pl.ds(row + HALF, 16), cols]
            for place, part in enumerate((lr * rr - li * ri, lr * ri + li * rr)):
                keep_parts(high_ref, low_ref, wave, row + place * HALF, cols, part)

        each_tile(width, HALF, 16, tile)
        return carry

    lax.fori_loop(0, RADIX, one, 0)


def from_waves(width, w_ref, high_ref, low_ref, back_ref, put):
    def second(wave, carry):
        back_ref[wave] = table_dot(w_ref[0, wave], w_ref[1, wave], high_ref, low_ref, wave)
        return carry

    lax.fori_loop(0, RADIX, second, 0)
    scale = 1.0 / (RADIX * HALF)

    def first(row, cols):
        values = [
            (back_ref[wave, pl.ds(row, 16), cols], back_ref[wave, pl.ds(row + HALF, 16), cols])
            for wave in range(RADIX)
        ]
        for part, (real, imaginary) in enumerate(small_transform(values, 1.0)):
            angle = 2.0 * math.pi * part / 32.0
            put(part * HALF, row, cols, real * (math.cos(angle) * scale) - imaginary * (math.sin(angle) * scale))

    each_tile(width, HALF, 16, first)


def first_positions(width, count, w_ref, high_ref, low_ref):
    total = jnp.zeros((count, width), jnp.float32)
    for wave in range(RADIX):
        total = total + table_dot(w_ref[0, wave, :count, :], w_ref[1, wave, :count, :], high_ref, low_ref, wave)
    return total * (1.0 / (RADIX * HALF))


FINE = 32


def decay_sums(width, length, ssm_ref, out_ref):
    modes = ssm_ref.shape[1]
    steps = length // FINE
    out_ref[...] = jnp.zeros(out_ref.shape, jnp.float32)
    for block in range(width // LANES):
        cols = pl.ds(block * LANES, LANES)
        offsets = lax.broadcasted_iota(jnp.int32, (FINE, LANES), 0).astype(jnp.float32)

        def group(index, carry, cols=cols, offsets=offsets):
            base = pl.multiple_of(index * 8, 8)
            rates = jnp.exp(ssm_ref[0, pl.ds(base, 8), cols])
            leaps = jnp.exp(-rates * FINE)
            weights = ssm_ref[1, pl.ds(base, 8), cols]
            terms = tuple(weights[i : i + 1] * jnp.exp(-rates[i : i + 1] * offsets) for i in range(8))
            leap_rows = [jnp.broadcast_to(leaps[i : i + 1], (FINE, LANES)) for i in range(8)]

            def step(number, terms, leap_rows=leap_rows):
                rows = pl.ds(pl.multiple_of(number * FINE, FINE), FINE)
                total = out_ref[rows, cols]
                for term in terms:
                    total = total + term
                out_ref[rows, cols] = total
                return tuple(term * leap for term, leap in zip(terms, leap_rows))

            lax.fori_loop(0, steps, step, terms, unroll=4)
            return carry

        lax.fori_loop(0, modes // 8, group, 0)


def decay_gradients(block, length, ssm_ref, grad_ref, out_ref):
    modes = ssm_ref.shape[1]
    steps = length // FINE
    cols = pl.ds(block * LANES, LANES)
    offsets = lax.broadcasted_iota(jnp.int32, (FINE, LANES), 0).astype(jnp.float32)

    def group(index, carry):
        base = pl.multiple_of(index * 8, 8)
        rates = jnp.exp(ssm_ref[0, pl.ds(base, 8), cols])
        leaps = jnp.exp(-rates * FINE)
        plain_rows, slope_rows = [], []
        for modes_now in ((0, 1, 2, 3), (4, 5, 6, 7)):
            zero = offsets * 0.0
            leap_rows = [jnp.broadcast_to(leaps[i : i + 1], (FINE, LANES)) for i in modes_now]

            def step(number, sums, leap_rows=leap_rows):
                rows = grad_ref[pl.ds(pl.multiple_of((steps - 1 - number) * FINE, FINE), FINE), cols]
                return tuple((v * leap + rows, w * leap + v) for (v, w), leap in zip(sums, leap_rows))

            sums = lax.fori_loop(0, steps, step, tuple((zero, zero) for _ in modes_now), unroll=8)
            for i, (v, w) in zip(modes_now, sums):
                fine = jnp.exp(-rates[i : i + 1] * offsets)
                plain = fine * v
                slope = fine * w * (leaps[i : i + 1] * FINE) + plain * offsets
                plain_rows.append(jnp.sum(plain, axis=0, keepdims=True))
                slope_rows.append(jnp.sum(slope, axis=0, keepdims=True))
        out_ref[modes // 8 + index, :, cols] = jnp.concatenate(plain_rows, axis=0)
        out_ref[index, :, cols] = (
            -ssm_ref[1, pl.ds(base, 8), cols] * rates * jnp.concatenate(slope_rows, axis=0)
        )
        return carry

    lax.fori_loop(0, modes // 8, group, 0)


def layer_norm_parts(values):
    average = jnp.mean(values, axis=-1, keepdims=True)
    centred = values - average
    variance = jnp.mean(centred * centred, axis=-1, keepdims=True)
    inverse = lax.rsqrt(variance + EPS_NORM)
    return centred * inverse, inverse


def layer_norm_back(upstream, normal, inverse, gain_row):
    weighted = upstream * gain_row
    average = jnp.mean(weighted, axis=-1, keepdims=True)
    overlap = jnp.mean(weighted * normal, axis=-1, keepdims=True)
    into = (weighted - average - normal * overlap) * inverse
    return into, jnp.sum(upstream * normal, axis=0, keepdims=True), jnp.sum(upstream, axis=0, keepdims=True)


MESH = pl.DeviceIdType.MESH
TWO, FOUR = 2, 4
TAP_ROWS = 64
VMEM_LIMIT = 62 * 1024 * 1024


class Place:
    def __init__(self):
        self.s, self.d = lax.axis_index("seq"), lax.axis_index("dp")
        self.z, self.y, self.c = self.d // 4, (self.d // 2) % 2, self.d % 2

    def over_x(self):
        return (1 - self.s, self.d)

    def over_y(self):
        return (self.s, self.d + 2 - 4 * self.y)

    def over_core(self):
        return (self.s, self.d + 1 - 2 * self.c)

    def along_z(self, step):
        return (self.s, (self.d + 4 * step) % 16)

    def owner(self, index):
        return (self.s, index)


def send(source, target, send_sem, recv_sem, device):
    return pltpu.make_async_remote_copy(
        src_ref=source, dst_ref=target, send_sem=send_sem, recv_sem=recv_sem, device_id=device, device_id_type=MESH
    )


def greet_all(place):
    barrier = pltpu.get_barrier_semaphore()
    pl.semaphore_signal(barrier, inc=1, device_id=place.over_x(), device_id_type=MESH)

    def greet(step, carry):
        pl.semaphore_signal(
            barrier, inc=1, device_id=place.owner((place.d + step) % 16), device_id_type=MESH
        )
        return carry

    lax.fori_loop(1, 16, greet, 0)
    pl.semaphore_wait(barrier, 16)


WEIGHTS = (
    ("up", 0, 1536, "halved"),
    ("up", 1536, 1536, "halved"),
    ("out", 0, 768, "whole"),
    ("down", 0, 1536, "whole"),
    ("down", 1536, 1536, "whole"),
)


def forward_body(
    token_ref, qkv_ref, out_shard, mlp_shard, small_ref, ssm_ref, to_ref, from_ref,
    qkv_full, out_full, up_full, down_full, small_t, normed_ref, proj_ref, rows_ref,
    conv_ref, shifted_ref, kernel_w, taps_w, keys_w, mixed_w,
    token_all, small_all, gated_ref, line_ref, high_ref, low_ref, back_ref,
    own_sem, z_s, z_r, y_s, y_r, x_s, x_r, core_s, core_r, small_s, small_r, side_s, side_r,
):
    length, width = conv_ref.shape
    own_rows = token_ref.shape[0]
    place = Place()
    qkv = len(WEIGHTS)
    shards = {"up": mlp_shard.at[0], "down": mlp_shard.at[1], "out": out_shard}
    fulls = {"up": up_full, "down": down_full, "out": out_full}

    def columns(k):
        source, start, count, way = WEIGHTS[k]
        if way == "whole":
            return source, pl.ds(start, count)
        return source, pl.ds(pl.multiple_of(start + place.s * (count // 2), LANES), count // 2)

    def z_copy(k, step):
        if k == qkv:
            source, target = qkv_ref, qkv_full.at[place.z, place.y, place.c]
        else:
            name, cols = columns(k)
            source, target = shards[name].at[:, cols], fulls[name].at[place.z, place.y, place.c, :, cols]
        return send(source, target, z_s.at[k, step - 1], z_r.at[k, step - 1], place.along_z(step))

    def y_copy(k):
        if k == qkv:
            blocks = qkv_full.at[:, place.y, place.c]
        else:
            name, cols = columns(k)
            blocks = fulls[name].at[:, place.y, place.c, :, cols]
        return send(blocks, blocks, y_s.at[k], y_r.at[k], place.over_y())

    def x_copy(k):
        name, cols = columns(k)
        blocks = fulls[name].at[:, :, place.c, :, cols]
        return send(blocks, blocks, x_s.at[k], x_r.at[k], place.over_x())

    def core_copy(k):
        if k == qkv:
            blocks = qkv_full.at[:, :, place.c]
        else:
            name, start, count, _ = WEIGHTS[k]
            blocks = fulls[name].at[:, :, place.c, :, pl.ds(start, count)]
        return send(blocks, blocks, core_s.at[k], core_r.at[k], place.over_core())

    def own_copies():
        copies = []
        for k in range(qkv):
            name, cols = columns(k)
            target = fulls[name].at[place.z, place.y, place.c, :, cols]
            copies.append(pltpu.make_async_copy(shards[name].at[:, cols], target, own_sem.at[k]))
        return copies

    def start_z(k):
        for step in range(1, 4):
            z_copy(k, step).start()

    def z_to_y(k):
        for step in range(1, 4):
            z_copy(k, step).wait_recv()
        y_copy(k).start()

    def y_on(k):
        y_copy(k).wait_recv()
        if k != qkv and WEIGHTS[k][3] == "halved":
            x_copy(k).start()
        else:
            core_copy(k).start()

    def x_on(k):
        x_copy(k).wait_recv()
        core_copy(k).start()

    def small_copy(step):
        other = (place.d + step) % 16
        return send(small_ref, small_all.at[place.d], small_s.at[other], small_r.at[place.d], place.owner(other))

    def small_arrival(step):
        other = (place.d + step) % 16
        return send(small_ref, small_all.at[other], small_s.at[other], small_r.at[other], place.owner(other))

    def over_peers(action):
        def one(step, carry):
            action(step)
            return carry

        lax.fori_loop(1, 16, one, 0)

    token_copy = send(token_ref, token_all.at[place.s], side_s.at[0], side_r.at[0], place.over_x())
    gated_copy = send(
        gated_ref.at[1 - place.s], rows_ref.at[place.s], side_s.at[1], side_r.at[1], place.over_x()
    )

    greet_all(place)
    over_peers(lambda step: small_copy(step).start())
    start_z(qkv)
    token_copy.start()
    for copy in own_copies():
        copy.start()
    qkv_full[place.z, place.y, place.c] = qkv_ref[...]
    small_all[place.d] = small_ref[...]

    def keep(target):
        def store(wave, value):
            target[wave] = value

        return store

    def lines(base, row, cols):
        return line_ref[pl.ds(base + row, 16), cols]

    def column(index, cols):
        return pl.ds(index * width + cols.start, cols.size)

    decay_sums(width, length, ssm_ref, line_ref)
    z_to_y(qkv)
    for k in range(qkv):
        if k < 2:
            start_z(k)
    to_waves(width, lines, RADIX, to_ref, high_ref, low_ref, keep(kernel_w))
    over_peers(lambda step: small_arrival(step).wait_recv())
    small_t[...] = small_all[...].reshape(16 * small_all.shape[1], LANES).astype(jnp.float32).T
    taps_cols = pl.multiple_of(place.s * width, LANES)

    def read_taps(base, row, cols):
        taps = small_t[pl.ds(base + row, 16), pl.ds(pl.multiple_of(taps_cols + cols.start, LANES), LANES)]
        inside = lax.broadcasted_iota(jnp.int32, taps.shape, 0) + (base + row) < TAP_ROWS
        return jnp.where(inside, taps, 0.0)

    y_on(qkv)
    to_waves(width, read_taps, 1, to_ref, high_ref, low_ref, keep(taps_w))

    def normalize(source, begin):
        def one(index, carry):
            row = pl.multiple_of(index * 32, 32)
            normal, _ = layer_norm_parts(source[pl.ds(row, 32), :].astype(jnp.float32))
            scaled = normal * small_t[TAP_ROWS : TAP_ROWS + 1, :] + small_t[TAP_ROWS + 1 : TAP_ROWS + 2, :]
            normed_ref[pl.ds(pl.multiple_of(begin + row, 32), 32), :] = scaled.astype(jnp.bfloat16)
            return carry

        lax.fori_loop(0, own_rows // 32, one, 0)

    def project(begin):
        weight = qkv_full[...].reshape(normed_ref.shape[1], 3 * width)

        def one(index, carry):
            row = pl.ds(pl.multiple_of(begin + index * 256, 256), 256)
            proj_ref[row, :] = dot(normed_ref[row, :], weight)
            return carry

        lax.fori_loop(0, own_rows // 256, one, 0)

    own_begin, other_begin = place.s * own_rows, (1 - place.s) * own_rows
    normalize(token_ref, own_begin)
    for copy in own_copies():
        copy.wait()
    z_to_y(0)
    start_z(2)
    token_copy.wait_recv()
    normalize(token_all.at[1 - place.s], other_begin)
    core_copy(qkv).wait_recv()
    project(own_begin)
    z_to_y(1)
    y_on(0)
    start_z(3)
    project(other_begin)
    z_to_y(2)
    start_z(4)
    y_on(1)
    to_waves(
        width, lambda base, row, cols: proj_ref[pl.ds(base + row, 16), column(1, cols)],
        RADIX, to_ref, high_ref, low_ref, keep(keys_w),
    )
    product(width, taps_w, keys_w, False, high_ref, low_ref)
    y_on(2)
    x_on(0)

    def put_shifted(base, row, cols, value):
        rows = pl.ds(base + row, 16)
        shifted_ref[rows, cols] = value
        mixed = value * proj_ref[rows, column(2, cols)]
        line_ref[rows, cols] = mixed.astype(jnp.bfloat16).astype(jnp.float32)

    from_waves(width, from_ref, high_ref, low_ref, back_ref, put_shifted)
    z_to_y(3)
    to_waves(width, lines, RADIX, to_ref, high_ref, low_ref, keep(mixed_w))
    x_on(1)
    product(width, kernel_w, mixed_w, False, high_ref, low_ref)

    def put_conv(base, row, cols, value):
        rows = pl.ds(base + row, 16)
        rounded = value.astype(jnp.bfloat16)
        conv_ref[rows, cols] = rounded
        gated = (proj_ref[rows, cols] * rounded.astype(jnp.float32)).astype(jnp.bfloat16)
        gated_ref[base // own_rows, pl.ds(base % own_rows + row, 16), cols] = gated

    from_waves(width, from_ref, high_ref, low_ref, back_ref, put_conv)
    gated_copy.start()
    z_to_y(4)
    y_on(3)
    rows_ref[place.s] = gated_ref[place.s]
    y_on(4)
    gated_copy.wait_recv()
    for k in range(qkv):
        core_copy(k).wait_recv()

    over_peers(lambda step: small_copy(step).wait_send())
    token_copy.wait_send()
    gated_copy.wait_send()
    for k in range(qkv + 1):
        for step in range(1, 4):
            z_copy(k, step).wait_send()
        y_copy(k).wait_send()
        core_copy(k).wait_send()
        if k != qkv and WEIGHTS[k][3] == "halved":
            x_copy(k).wait_send()


def forward_mixer(tokens, qkv_shard, out_shard, mlp_shard, small, ssm, to_table, from_table):
    own_rows, model = tokens.shape
    owned = qkv_shard.shape[0]
    width = qkv_shard.shape[1] // 3
    length = 2 * own_rows
    hidden = mlp_shard.shape[2]
    f32, low = jnp.float32, jnp.bfloat16
    waves = (RADIX, 2 * HALF, width)
    vmem, anywhere = pl.BlockSpec(memory_space=pltpu.VMEM), pl.BlockSpec(memory_space=pl.ANY)
    shape = jax.ShapeDtypeStruct
    owners = (FOUR, TWO, TWO, owned)
    count = len(WEIGHTS)
    dma = pltpu.SemaphoreType.DMA
    return pl.pallas_call(
        forward_body,
        out_shape=(
            shape(owners + (3 * width,), low),
            shape(owners + (model,), low),
            shape(owners + (hidden,), low),
            shape(owners + (hidden,), low),
            shape((LANES, model), f32),
            shape((length, model), low),
            shape((length, 3 * width), f32),
            shape((2, own_rows, width), low),
            shape((length, width), low),
            shape((length, width), f32),
        )
        + (shape(waves, f32),) * 4,
        in_specs=[vmem, vmem, anywhere, anywhere, vmem, vmem, vmem, vmem],
        out_specs=(vmem, anywhere, anywhere, anywhere) + (vmem,) * 10,
        scratch_shapes=[
            pltpu.VMEM((2, own_rows, model), low),
            pltpu.VMEM((16,) + small.shape, low),
            pltpu.VMEM((2, own_rows, width), low),
            pltpu.VMEM((length, width), f32),
            pltpu.VMEM(waves, low),
            pltpu.VMEM(waves, low),
            pltpu.VMEM(waves, f32),
            dma((count,)),
            dma((count + 1, 3)),
            dma((count + 1, 3)),
            dma((count + 1,)),
            dma((count + 1,)),
            dma((count + 1,)),
            dma((count + 1,)),
            dma((count + 1,)),
            dma((count + 1,)),
            dma((16,)),
            dma((16,)),
            dma((2,)),
            dma((2,)),
        ],
        compiler_params=pltpu.CompilerParams(collective_id=2, has_side_effects=True, vmem_limit_bytes=VMEM_LIMIT),
        name="forward_mixer",
    )(tokens, qkv_shard, out_shard, mlp_shard, small, ssm, to_table, from_table)


PIECES = (
    ("down", 0, 1536, "whole"),
    ("up", 1536, 1536, "halved"),
    ("down", 1536, 1536, "whole"),
    ("out", 0, 768, "halved"),
    ("up", 0, 1536, "whole"),
    ("qkv", 0, 1152, "apart"),
)
QKV = len(PIECES) - 1


def add_blocks(put, sources, count):
    def one(index, carry):
        total = sources[0](index).astype(jnp.float32)
        for source in sources[1:]:
            total = total + source(index).astype(jnp.float32)
        put(index, total)
        return carry

    lax.fori_loop(0, count, one, 0)


def piece_halves(k):
    return TWO if PIECES[k][3] == "halved" else 1


def backward_body(*refs):
    count = len(PIECES)
    (
        gated_grad_ref, proj_ref, conv_ref, shifted_ref, kernel_w, taps_w, keys_w, mixed_w, ssm_ref, to_ref, from_ref,
        normed_ref, qkv_ref, token_ref, residual_ref, small_t, norm_two_ref, down_ref, up_ref, out_ref,
    ), refs = refs[:20], refs[20:]
    outs, refs = refs[:count], refs[count:]
    (small_out, ssm_out, input_out), refs = refs[:3], refs[3:]
    near, refs = refs[:count], refs[count:]
    from_x = dict(zip([k for k in range(count) if piece_halves(k) == TWO], refs))
    refs = refs[len(from_x):]
    from_y, from_z, final, last = (refs[i * count : (i + 1) * count] for i in range(4))
    refs = refs[4 * count :]
    (
        own_ref, grad_all, query_ref, value_ref, spectrum, line_ref, decay_ref, wave_ref, high_ref, back_ref,
        grad_proj, qkv_grad, gn_send, gn_own, gn_last, small_rows, small_ref, small_all, small_sum, small_last,
        ssm_ref_all, ssm_all, ssm_sum,
    ), refs = refs[:23], refs[23:]
    (
        load_sem, own_sem, core_s, core_r, x_s, x_r, y_s, y_r, z_s, z_r, f_s, f_r, sm_s, sm_r, ss_s, ss_r, sg_s, sg_r,
        side_s, side_r,
    ) = refs
    length, width = conv_ref.shape
    own_rows = token_ref.shape[0]
    place = Place()
    grads = {"down": down_ref, "up": up_ref, "out": out_ref, "qkv": qkv_grad}

    def core_copy(k, h):
        source, start, columns, _ = PIECES[k]
        part = columns // piece_halves(k)
        blocks = grads[source].at[:, :, 1 - place.c, :, pl.ds(start + h * part, part)]
        return send(blocks, near[k].at[h], core_s.at[k, h], core_r.at[k, h], place.over_core())

    def own_copy(k, h):
        source, start, columns, _ = PIECES[k]
        part = columns // piece_halves(k)
        blocks = grads[source].at[:, :, place.c, :, pl.ds(start + h * part, part)]
        return pltpu.make_async_copy(blocks, own_ref.at[k % 2, :, :, :, pl.ds(h * part, part)], own_sem.at[k % 2, h])

    def x_copy(k):
        return send(near[k].at[1 - place.s], from_x[k], x_s.at[k], x_r.at[k], place.over_x())

    def kept(k):
        return near[k].at[place.s] if piece_halves(k) == TWO else near[k].at[0]

    def y_copy(k):
        return send(kept(k).at[:, 1 - place.y], from_y[k], y_s.at[k], y_r.at[k], place.over_y())

    def z_copy(k, step):
        other = (place.z + step) % 4
        return send(
            kept(k).at[other, place.y], from_z[k].at[step - 1], z_s.at[k, step - 1], z_r.at[k, step - 1],
            place.along_z(step),
        )

    def last_copy(k):
        return send(final[k], last[k], f_s.at[k], f_r.at[k], place.over_x())

    def load_own(k):
        for h in range(piece_halves(k)):
            own_copy(k, h).start()

    def add_core(k):
        part = PIECES[k][2] // piece_halves(k)
        for h in range(piece_halves(k)):
            core_copy(k, h).wait_recv()
            if k != QKV:
                own_copy(k, h).wait()

            def own(i, h=h):
                if k == QKV:
                    return qkv_grad[i // 2, i % 2, place.c]
                return own_ref[k % 2, i // 2, i % 2, :, h * part : (h + 1) * part]

            def put(i, total, h=h):
                near[k][h, i // 2, i % 2] = total.astype(jnp.bfloat16)

            add_blocks(put, [own, lambda i, h=h: near[k][h, i // 2, i % 2]], 8)
        if piece_halves(k) == TWO:
            x_copy(k).start()
        else:
            y_copy(k).start()

    def add_x(k):
        x_copy(k).wait_recv()

        def put(i, total):
            kept(k)[i // 2, i % 2] = total.astype(jnp.bfloat16)

        add_blocks(put, [lambda i: kept(k)[i // 2, i % 2], lambda i: from_x[k][i // 2, i % 2]], 8)
        y_copy(k).start()

    def add_y(k):
        y_copy(k).wait_recv()

        def put(i, total):
            kept(k)[i, place.y] = total.astype(jnp.bfloat16)

        add_blocks(put, [lambda i: kept(k)[i, place.y], lambda i: from_y[k][i]], 4)
        for step in range(1, 4):
            z_copy(k, step).start()

    def add_z(k):
        for step in range(1, 4):
            z_copy(k, step).wait_recv()
        total = kept(k)[place.z, place.y].astype(jnp.float32)
        for step in range(3):
            total = total + from_z[k][step].astype(jnp.float32)
        final[k][...] = total.astype(jnp.bfloat16)
        last_copy(k).start()

    def finish(k):
        last_copy(k).wait_recv()
        if PIECES[k][3] == "whole":
            outs[k][...] = final[k][...].astype(jnp.float32) + last[k][...].astype(jnp.float32)
        else:
            outs[k][place.s] = final[k][...]
            outs[k][1 - place.s] = last[k][...]

    def over_peers(action):
        def one(step, carry):
            action(step)
            return carry

        lax.fori_loop(1, 16, one, 0)

    def to_peer(source, target, send_sem, recv_sem, step):
        other = (place.d + step) % 16
        return send(source.at[other], target.at[place.d], send_sem.at[other], recv_sem.at[place.d], place.owner(other))

    def from_peer(target, send_sem, recv_sem, step):
        other = (place.d + step) % 16
        return send(target.at[other], target.at[other], send_sem.at[other], recv_sem.at[other], place.owner(other))

    def share(step):
        other = (place.d + step) % 16
        return send(ssm_sum.at[place.d], ssm_sum.at[place.d], sg_s.at[other], sg_r.at[place.d], place.owner(other))

    grad_copy = send(
        gated_grad_ref.at[:, pl.ds(pl.multiple_of((1 - place.s) * width, LANES), width)], grad_all.at[place.s],
        side_s.at[0], side_r.at[0], place.over_x(),
    )
    gn_copy = send(gn_send, gn_last, side_s.at[1], side_r.at[1], place.over_x())
    small_copy = send(small_sum, small_last, side_s.at[2], side_r.at[2], place.over_x())
    spectra = (kernel_w, mixed_w, taps_w, keys_w)

    def load_spectrum(i):
        return pltpu.make_async_copy(spectra[i], spectrum.at[i % 2], load_sem.at[i % 2])

    query_copy = pltpu.make_async_copy(proj_ref.at[:, pl.ds(0, width)], query_ref, load_sem.at[2])
    value_copy = pltpu.make_async_copy(proj_ref.at[:, pl.ds(2 * width, width)], value_ref, load_sem.at[3])

    greet_all(place)
    grad_copy.start()
    for k in range(QKV):
        for h in range(piece_halves(k)):
            core_copy(k, h).start()
    load_own(0)
    load_own(1)
    query_copy.start()
    value_copy.start()
    load_spectrum(0).start()
    load_spectrum(1).start()
    grad_all[place.s] = gated_grad_ref[:, pl.ds(pl.multiple_of(place.s * width, LANES), width)]
    for k in range(QKV):
        add_core(k)
        if k + 2 < QKV:
            load_own(k + 2)

    def keep(wave, value):
        wave_ref[wave] = value

    def lines(base, row, cols):
        return line_ref[pl.ds(base + row, 16), cols]

    def column(index, cols):
        return pl.ds(index * width + cols.start, cols.size)

    def read_conv_grad(base, row, cols):
        rows = pl.ds(base + row, 16)
        gradient = grad_all[base // own_rows, pl.ds(base % own_rows + row, 16), cols].astype(jnp.float32)
        grad_proj[rows, cols] = (gradient * conv_ref[rows, cols].astype(jnp.float32)).astype(jnp.bfloat16)
        return (gradient * query_ref[rows, cols]).astype(jnp.bfloat16).astype(jnp.float32)

    query_copy.wait()
    value_copy.wait()
    grad_copy.wait_recv()
    to_waves(width, read_conv_grad, RADIX, to_ref, high_ref, None, keep)
    add_y(0)
    load_spectrum(0).wait()
    product(width, spectrum.at[0], wave_ref, True, high_ref, None)
    load_spectrum(2).start()

    def put_mixed(base, row, cols, value):
        rows = pl.ds(base + row, 16)
        gradient = value.astype(jnp.bfloat16).astype(jnp.float32)
        grad_proj[rows, column(2, cols)] = (gradient * shifted_ref[rows, cols]).astype(jnp.bfloat16)
        line_ref[rows, cols] = gradient * value_ref[rows, cols]

    from_waves(width, from_ref, high_ref, None, back_ref, put_mixed)
    add_x(1)
    load_spectrum(1).wait()
    product(width, spectrum.at[1], wave_ref, True, high_ref, None)
    load_spectrum(3).start()

    def put_kernel(base, row, cols, value):
        decay_ref[pl.ds(base + row, 16), cols] = value

    from_waves(width, from_ref, high_ref, None, back_ref, put_kernel)
    add_y(2)
    to_waves(width, lines, RADIX, to_ref, high_ref, None, keep)
    add_z(0)
    load_spectrum(2).wait()
    product(width, spectrum.at[0], wave_ref, True, high_ref, None)

    def put_keys(base, row, cols, value):
        grad_proj[pl.ds(base + row, 16), column(1, cols)] = value.astype(jnp.bfloat16)

    from_waves(width, from_ref, high_ref, None, back_ref, put_keys)
    add_x(3)

    def project_back(begin, put):
        def one(index, carry):
            row = pl.multiple_of(index * 256, 256)
            value = lax.dot_general(
                grad_proj[pl.ds(pl.multiple_of(begin + row, 256), 256), :], qkv_ref[...], (((1,), (1,)), ((), ())),
                preferred_element_type=jnp.float32,
            )
            put(pl.ds(row, 256), value)
            return carry

        lax.fori_loop(0, own_rows // 256, one, 0)

    def put_send(rows, value):
        gn_send[rows, :] = value.astype(jnp.bfloat16)

    def put_own(rows, value):
        gn_own[rows, :] = value

    project_back((1 - place.s) * own_rows, put_send)
    gn_copy.start()
    for pair in range(TWO):
        columns = 2 * 4 * qkv_grad.shape[3]
        value = lax.dot_general(
            normed_ref[:, pair * columns : (pair + 1) * columns], grad_proj[...], (((0,), (0,)), ((), ())),
            preferred_element_type=jnp.float32,
        )
        qkv_grad[2 * pair : 2 * pair + 2] = value.astype(jnp.bfloat16).reshape((2,) + qkv_grad.shape[1:])
    core_copy(QKV, 0).start()
    add_y(4)
    project_back(place.s * own_rows, put_own)
    add_core(QKV)
    add_y(1)
    load_spectrum(3).wait()
    product(width, spectrum.at[1], wave_ref, True, high_ref, None)
    small_rows[...] = jnp.zeros(small_rows.shape, jnp.float32)
    small_rows[:TAP_ROWS, pl.ds(pl.multiple_of(place.s * width, LANES), width)] = first_positions(
        width, TAP_ROWS, from_ref, high_ref, None
    )
    add_z(2)
    add_y(3)
    decay_gradients(0, length, ssm_ref, decay_ref, ssm_ref_all)
    add_y(QKV)
    add_z(4)
    decay_gradients(1, length, ssm_ref, decay_ref, ssm_ref_all)
    add_z(1)
    add_z(3)
    decay_gradients(2, length, ssm_ref, decay_ref, ssm_ref_all)
    over_peers(lambda step: to_peer(ssm_ref_all, ssm_all, ss_s, ss_r, step).start())
    gn_copy.wait_recv()

    def norm_back(index, sums):
        rows = pl.ds(pl.multiple_of(index * 32, 32), 32)
        normal, inverse = layer_norm_parts(token_ref[rows, :].astype(jnp.float32))
        upstream = gn_own[rows, :] + gn_last[rows, :].astype(jnp.float32)
        into, gain, bias = layer_norm_back(upstream, normal, inverse, small_t[TAP_ROWS : TAP_ROWS + 1, :])
        input_out[rows, :] = residual_ref[rows, :] + into
        return sums[0] + gain, sums[1] + bias

    zero = jnp.sum(norm_two_ref[...], axis=0, keepdims=True) * 0.0
    gain, bias = lax.fori_loop(0, own_rows // 32, norm_back, (zero, zero))
    small_rows[TAP_ROWS : TAP_ROWS + 1, :] = gain
    small_rows[TAP_ROWS + 1 : TAP_ROWS + 2, :] = bias
    small_rows[TAP_ROWS + 2 : TAP_ROWS + 4, :] = norm_two_ref[...]
    small_ref[...] = small_rows[...].T.astype(jnp.bfloat16).reshape(small_ref.shape)
    over_peers(lambda step: to_peer(small_ref, small_all, sm_s, sm_r, step).start())
    add_z(QKV)

    over_peers(lambda step: from_peer(ssm_all, ss_s, ss_r, step).wait_recv())
    ssm_all[place.d] = ssm_ref_all[place.d]
    total = ssm_all[0]
    for index in range(1, 16):
        total = total + ssm_all[index]
    ssm_sum[place.d] = total
    over_peers(lambda step: share(step).start())
    over_peers(lambda step: from_peer(small_all, sm_s, sm_r, step).wait_recv())

    def add_small(step, total):
        return total + small_all[(place.d + step) % 16].astype(jnp.float32)

    small_sum[...] = lax.fori_loop(1, 16, add_small, small_ref[place.d].astype(jnp.float32)).astype(jnp.bfloat16)
    small_copy.start()
    for k in range(count):
        finish(k)
    over_peers(lambda step: from_peer(ssm_sum, sg_s, sg_r, step).wait_recv())
    ssm_out[...] = ssm_sum[...]
    small_copy.wait_recv()
    small_out[...] = small_sum[...].astype(jnp.float32) + small_last[...].astype(jnp.float32)

    for k in range(count):
        for h in range(piece_halves(k)):
            core_copy(k, h).wait_send()
        if piece_halves(k) == TWO:
            x_copy(k).wait_send()
        y_copy(k).wait_send()
        for step in range(1, 4):
            z_copy(k, step).wait_send()
        last_copy(k).wait_send()
    for copy in (grad_copy, gn_copy, small_copy):
        copy.wait_send()
    over_peers(lambda step: to_peer(small_ref, small_all, sm_s, sm_r, step).wait_send())
    over_peers(lambda step: to_peer(ssm_ref_all, ssm_all, ss_s, ss_r, step).wait_send())
    over_peers(lambda step: share(step).wait_send())


def backward_mixer(
    gated_grad, proj, conv, shifted, kernel_w, taps_w, keys_w, mixed_w, ssm, to_table, from_table, normed, qkv, tokens,
    residual, small, norm_two, down, up, out,
):
    f32, low = jnp.float32, jnp.bfloat16
    count = len(PIECES)
    length, width = conv.shape
    own_rows, model = tokens.shape
    owned = down.shape[3]
    waves = (RADIX, 2 * HALF, width)
    vmem, anywhere = pl.BlockSpec(memory_space=pltpu.VMEM), pl.BlockSpec(memory_space=pl.ANY)
    results, near, from_x, from_y, from_z, final, last = [], [], [], [], [], [], []
    for k, (_, _, columns, way) in enumerate(PIECES):
        halves = piece_halves(k)
        part = columns // halves
        whole = way == "whole"
        results.append(jax.ShapeDtypeStruct((owned, part) if whole else (TWO, owned, part), f32 if whole else low))
        near.append(pltpu.VMEM((halves, FOUR, TWO, owned, part), low))
        if halves == TWO:
            from_x.append(pltpu.VMEM((FOUR, TWO, owned, part), low))
        from_y.append(pltpu.VMEM((FOUR, owned, part), low))
        from_z.append(pltpu.VMEM((3, owned, part), low))
        final.append(pltpu.VMEM((owned, part), low))
        last.append(pltpu.VMEM((owned, part), low))
    dma = pltpu.SemaphoreType.DMA
    slots = (16, 8, width)
    packed = (16, owned, LANES)
    results += [
        jax.ShapeDtypeStruct(packed[1:], f32),
        jax.ShapeDtypeStruct(slots, f32),
        jax.ShapeDtypeStruct((own_rows, model), f32),
    ]
    return pl.pallas_call(
        backward_body,
        out_shape=tuple(results),
        in_specs=[vmem, anywhere, vmem, vmem] + [anywhere] * 4 + [vmem] * 9 + [anywhere] * 3,
        out_specs=(vmem,) * len(results),
        scratch_shapes=near
        + from_x
        + from_y
        + from_z
        + final
        + last
        + [
            pltpu.VMEM((2, FOUR, TWO, owned, 1536), low),
            pltpu.VMEM((2, own_rows, width), low),
            pltpu.VMEM((length, width), f32),
            pltpu.VMEM((length, width), f32),
            pltpu.VMEM((2,) + waves, f32),
            pltpu.VMEM((length, width), f32),
            pltpu.VMEM((length, width), f32),
            pltpu.VMEM(waves, f32),
            pltpu.VMEM(waves, low),
            pltpu.VMEM(waves, f32),
            pltpu.VMEM((length, 3 * width), low),
            pltpu.VMEM((FOUR, TWO, TWO, owned, 3 * width), low),
            pltpu.VMEM((own_rows, model), low),
            pltpu.VMEM((own_rows, model), f32),
            pltpu.VMEM((own_rows, model), low),
            pltpu.VMEM((LANES, model), f32),
            pltpu.VMEM(packed, low),
            pltpu.VMEM(packed, low),
            pltpu.VMEM(packed[1:], low),
            pltpu.VMEM(packed[1:], low),
            pltpu.VMEM(slots, f32),
            pltpu.VMEM(slots, f32),
            pltpu.VMEM(slots, f32),
            dma((4,)),
            dma((2, TWO)),
            dma((count, TWO)),
            dma((count, TWO)),
        ]
        + [dma((count,))] * 4
        + [dma((count, 3))] * 2
        + [dma((count,))] * 2
        + [dma((16,))] * 6
        + [dma((3,))] * 2,
        compiler_params=pltpu.CompilerParams(collective_id=1, has_side_effects=True, vmem_limit_bytes=VMEM_LIMIT),
        name="backward_mixer",
    )(
        gated_grad, proj, conv, shifted, kernel_w, taps_w, keys_w, mixed_w, ssm, to_table, from_table, normed, qkv, tokens,
        residual, small, norm_two, down, up, out,
    )


def per_device_split(
    tokens,
    cotangent,
    attn_weight,
    mlp_weight,
    norms,
    taps,
    ssm_params,
    attn_moments,
    mlp_moments,
    norm_moments,
    tap_moments,
    ssm_moments,
):
    f32, low = jnp.float32, jnp.bfloat16
    rows, width = tokens.shape[1:]
    shares = lax.axis_size("seq")
    owners = lax.axis_size("dp")
    length = rows * shares
    part = width // shares
    half = lax.axis_index("seq")
    tap_count = taps.shape[0]
    to_table, from_table = map(jnp.asarray, transform_tables())

    owned = attn_weight.shape[0]
    columns = lax.dynamic_index_in_dim(attn_weight.reshape(owned, 4, shares, part), half, 2, False)
    qkv_shard = columns[:, :3].reshape(owned, 3 * part)
    small = jnp.concatenate([taps, norms, jnp.zeros((LANES - 4 - tap_count, owned), low)]).T
    ssm_turned = jnp.swapaxes(ssm_params, 1, 2)
    (
        qkv_full, out_full, up_full, down_full, small_full, normed_low, proj, gated_parts,
        conv, shifted, kernel_w, taps_w, keys_w, mixed_w,
    ) = forward_mixer(
        tokens[0], qkv_shard, attn_weight[:, 3 * width :], mlp_weight, small, ssm_turned, to_table, from_table
    )
    qkv_full = qkv_full.reshape(width, 3 * part)
    out_full = out_full.reshape(width, width)
    mlp_full = (up_full.reshape(width, -1), down_full.reshape(width, -1))
    norm_rows = small_full[tap_count : tap_count + 4]
    gated_rows = jnp.concatenate([gated_parts[0], gated_parts[1]], axis=1)
    inputs = tokens[0].astype(f32)
    residual = inputs + dot(gated_rows, out_full)
    normal_two, inverse_two = layer_norm_parts(residual)
    normed_two = (normal_two * norm_rows[2] + norm_rows[3]).astype(low)
    before = dot(normed_two, mlp_full[0])
    active, gelu_pull = jax.vjp(jax.nn.gelu, before)
    active_low = active.astype(low)
    grad_after = cotangent[0]
    layer_out = (
        residual + jnp.einsum("tf,df->td", active_low, mlp_full[1], preferred_element_type=f32)
    ).astype(low)
    grad_active = dot(grad_after, mlp_full[1])
    grad_down = jnp.einsum("td,tf->df", grad_after, active_low, preferred_element_type=f32)
    grad_before = gelu_pull(grad_active)[0].astype(low)
    grad_up = jnp.einsum("td,tf->df", normed_two, grad_before, preferred_element_type=f32)
    grad_normed_two = jnp.einsum("tf,df->td", grad_before, mlp_full[0], preferred_element_type=f32)
    into_two, gain_two, bias_two = layer_norm_back(grad_normed_two, normal_two, inverse_two, norm_rows[2])
    grad_residual = grad_after.astype(f32) + into_two
    grad_branch = grad_residual.astype(low)
    grad_out = jnp.einsum("td,te->de", gated_rows, grad_branch, preferred_element_type=f32)
    grad_gated = jnp.einsum("te,de->td", grad_branch, out_full, preferred_element_type=f32).astype(low)

    def by_owner(gradient):
        return gradient.astype(low).reshape(FOUR, TWO, TWO, owned, gradient.shape[1])

    scale = 1.0 / math.sqrt(owners * length)
    sums = backward_mixer(
        grad_gated, proj, conv, shifted, kernel_w, taps_w, keys_w, mixed_w, ssm_turned, to_table, from_table,
        normed_low, qkv_full, tokens[0], grad_residual, small_full, jnp.concatenate([gain_two, bias_two]),
        by_owner(grad_down), by_owner(grad_up), by_owner(grad_out),
    )
    down_sum = jnp.concatenate([sums[0], sums[2]], axis=1)
    up_sum = jnp.concatenate([sums[4], sums[1][0].astype(f32), sums[1][1].astype(f32)], axis=1)
    qkv_sum = jnp.swapaxes(sums[5].reshape(shares, owned, 3, part), 0, 1).swapaxes(1, 2)
    attn_sum = jnp.concatenate([qkv_sum.reshape(owned, 3 * width), sums[3][0], sums[3][1]], axis=1)
    mlp_sum = jnp.stack([up_sum, down_sum])
    small_sum = sums[6].T
    small_sum = jnp.concatenate([small_sum[tap_count : tap_count + 4], small_sum[:tap_count]])
    ssm_sum = jnp.swapaxes(sums[7].reshape(ssm_turned.shape), 1, 2)
    input_grad = sums[8]

    attn_step, attn_new = adam_update(
        attn_weight.astype(f32), attn_moments, attn_sum.astype(f32) * scale, LEARN_RATE, DECAY_RATE
    )
    mlp_step, mlp_new = adam_update(
        mlp_weight.astype(f32), mlp_moments, mlp_sum.astype(f32) * scale, LEARN_RATE, DECAY_RATE
    )
    norms_step, norm_new = adam_update(norms.astype(f32), norm_moments, small_sum[:4] * scale, LEARN_RATE, 0.0)
    taps_step, tap_new = adam_update(taps.astype(f32), tap_moments, small_sum[4:] * scale, LEARN_RATE, DECAY_RATE)
    ssm_step, ssm_new = adam_update(ssm_params, ssm_moments, ssm_sum * scale, SSM_LEARN_RATE, 0.0)
    return (
        layer_out[None],
        input_grad[None],
        attn_step,
        attn_new,
        mlp_step,
        mlp_new,
        norms_step,
        norm_new,
        taps_step,
        tap_new,
        ssm_step,
        ssm_new,
    )


def solution(mesh):
    fits = (mesh.shape["seq"], mesh.shape["dp"]) == (2, 16)

    def chosen(tokens, cotangent, attn_weight, mlp_weight, norms, taps, *others):
        fast = fits and tokens.shape[1:] == (RADIX * HALF // 2, 6 * LANES) and taps.shape[0] == TAP_ROWS
        plan = per_device_split if fast else per_device
        return plan(tokens, cotangent, attn_weight, mlp_weight, norms, taps, *others)

    return jax.shard_map(
        chosen,
        mesh=mesh,
        in_specs=(
            P("dp", "seq", None),
            P("dp", "seq", None),
            P("dp", None),
            P(None, "dp", None),
            P(None, "dp"),
            P(None, "dp"),
            P(None, "seq", None),
            P(None, "dp", None),
            P(None, None, "dp", None),
            P(None, None, "dp"),
            P(None, None, "dp"),
            P(None, None, "seq", None),
        ),
        out_specs=(
            P("dp", "seq", None),
            P("dp", "seq", None),
            P("dp", None),
            P(None, "dp", None),
            P(None, "dp", None),
            P(None, None, "dp", None),
            P(None, "dp"),
            P(None, None, "dp"),
            P(None, "dp"),
            P(None, None, "dp"),
            P(None, "seq", None),
            P(None, None, "seq", None),
        ),
        check_vma=False,
    )
```

```python
from functools import partial
import math

import jax
import jax.numpy as jnp
import ml_dtypes
import numpy as np
from jax import lax
from jax.experimental import pallas as pl
from jax.experimental.pallas import tpu as pltpu
from jax.sharding import PartitionSpec as P

DFT_ROWS = 256


EPS_NORM = 1e-05
BETA_ONE = 0.9
BETA_TWO = 0.999
ADAM_EPS = 1e-08
LEARN_RATE = 0.001
SSM_LEARN_RATE = 0.00025
DECAY_RATE = 0.1
STEP_COUNT = 10.0
HIGHEST = lax.Precision.HIGHEST


def from_behind(block, axis, distance):
    devices = range(lax.axis_size(axis))
    route = [(i - distance, i) for i in devices if i - distance in devices]
    return lax.ppermute(block, axis, route)


def as_sent(value):

    def short(part):
        return part.astype(jnp.bfloat16) if part.dtype == jnp.float32 else part

    return jax.tree.map(short, value)


def layer_norm(values, gain_row, bias_row):
    average = jnp.mean(values, axis=-1, keepdims=True)
    centred = values - average
    variance = jnp.mean(centred * centred, axis=-1, keepdims=True)
    return centred * lax.rsqrt(variance + EPS_NORM) * gain_row + bias_row


def shift_mix(rim_rows, keys_part, taps_full):
    tap_count = taps_full.shape[0]
    row_count = keys_part.shape[0]
    extended = jnp.concatenate([rim_rows, keys_part], axis=0)
    summed = jnp.zeros_like(keys_part)
    for tap_index in range(tap_count):
        begin_row = tap_count - 1 - tap_index
        summed = summed + taps_full[tap_index] * extended[begin_row : begin_row + row_count]
    return summed


def kernel_rows(length_total, ssm_full):
    inner_count = math.gcd(length_total, 128)
    outer_count = length_total // inner_count
    decay_rates = jnp.exp(ssm_full[0])
    outer_offsets = (jnp.arange(outer_count) * inner_count).astype(jnp.float32)
    inner_offsets = jnp.arange(inner_count).astype(jnp.float32)
    outer_part = ssm_full[1][:, :, None] * jnp.exp(
        -decay_rates[:, :, None] * outer_offsets[None, None, :]
    )
    inner_part = jnp.exp(-decay_rates[:, :, None] * inner_offsets[None, None, :])
    kernel = jnp.einsum("cna,cnb->cab", outer_part, inner_part, precision=HIGHEST)
    return kernel.reshape(kernel.shape[0], length_total)


def dft_tables(length_total, first_count):
    full_length = 2 * length_total
    col_count = full_length // first_count
    half_rows = first_count // 2
    row_index = jnp.arange(half_rows, dtype=jnp.int32)
    freq_index = jnp.arange(first_count, dtype=jnp.int32)
    col_index = jnp.arange(col_count, dtype=jnp.int32)
    angle_first = (
        2.0
        * math.pi
        / first_count
        * (row_index[:, None] * freq_index[None, :] % first_count).astype(jnp.float32)
    )
    angle_twist = (
        2.0 * math.pi / full_length * (freq_index[:, None] * col_index[None, :]).astype(jnp.float32)
    )
    angle_last = (
        2.0
        * math.pi
        / col_count
        * (col_index[:, None] * col_index[None, :] % col_count).astype(jnp.float32)
    )
    return (
        jnp.cos(angle_first),
        jnp.sin(angle_first),
        jnp.cos(angle_twist),
        jnp.sin(angle_twist),
        jnp.cos(angle_last),
        jnp.sin(angle_last),
    )


def forward_dft(signal, tables):
    cos_first, sin_first, cos_twist, sin_twist, cos_last, sin_last = tables
    half_rows = cos_first.shape[0]
    col_count = cos_last.shape[0]
    folded = signal.reshape(signal.shape[0], half_rows, col_count)
    real_first = jnp.einsum("cmp,mk->ckp", folded, cos_first, precision=HIGHEST)
    imaginary_first = -jnp.einsum("cmp,mk->ckp", folded, sin_first, precision=HIGHEST)
    real_twist = real_first * cos_twist + imaginary_first * sin_twist
    imaginary_twist = imaginary_first * cos_twist - real_first * sin_twist
    real_last = jnp.einsum("ckp,pq->ckq", real_twist, cos_last, precision=HIGHEST) + jnp.einsum(
        "ckp,pq->ckq", imaginary_twist, sin_last, precision=HIGHEST
    )
    imaginary_last = jnp.einsum(
        "ckp,pq->ckq", imaginary_twist, cos_last, precision=HIGHEST
    ) - jnp.einsum("ckp,pq->ckq", real_twist, sin_last, precision=HIGHEST)
    return (real_last, imaginary_last)


def inverse_dft(spectrum, tables):
    cos_first, sin_first, cos_twist, sin_twist, cos_last, sin_last = tables
    real_part, imaginary_part = spectrum
    full_length = cos_first.shape[1] * cos_last.shape[0]
    real_inner = jnp.einsum("ckq,qp->ckp", real_part, cos_last, precision=HIGHEST) - jnp.einsum(
        "ckq,qp->ckp", imaginary_part, sin_last, precision=HIGHEST
    )
    imaginary_inner = jnp.einsum(
        "ckq,qp->ckp", imaginary_part, cos_last, precision=HIGHEST
    ) + jnp.einsum("ckq,qp->ckp", real_part, sin_last, precision=HIGHEST)
    real_twist = real_inner * cos_twist - imaginary_inner * sin_twist
    imaginary_twist = imaginary_inner * cos_twist + real_inner * sin_twist
    signal = jnp.einsum("ckp,mk->cmp", real_twist, cos_first, precision=HIGHEST) - jnp.einsum(
        "ckp,mk->cmp", imaginary_twist, sin_first, precision=HIGHEST
    )
    return signal.reshape(signal.shape[0], signal.shape[1] * signal.shape[2]) / full_length


def complex_product(left, right, conjugate_left):
    left_real, left_imaginary = left
    right_real, right_imaginary = right
    if conjugate_left:
        return (
            left_real * right_real + left_imaginary * right_imaginary,
            left_real * right_imaginary - left_imaginary * right_real,
        )
    return (
        left_real * right_real - left_imaginary * right_imaginary,
        left_real * right_imaginary + left_imaginary * right_real,
    )


def adam_update(param_now, moments, gradient, learn_rate, decay_weight):
    first_new = BETA_ONE * moments[0] + (1.0 - BETA_ONE) * gradient
    second_new = BETA_TWO * moments[1] + (1.0 - BETA_TWO) * gradient * gradient
    first_hat = first_new / (1.0 - BETA_ONE**STEP_COUNT)
    second_hat = second_new / (1.0 - BETA_TWO**STEP_COUNT)
    step_size = learn_rate * (
        first_hat / (jnp.sqrt(second_hat) + ADAM_EPS) + decay_weight * param_now
    )
    return (step_size, jnp.stack([first_new, second_new]))


def per_device(
    tokens,
    cotangent,
    attn_weight,
    mlp_weight,
    norms,
    taps,
    ssm_params,
    attn_moments,
    mlp_moments,
    norm_moments,
    tap_moments,
    ssm_moments,
):
    row_count = tokens.shape[1]
    model_width = tokens.shape[2]
    group_count = lax.axis_size("seq")
    owner_count = lax.axis_size("dp")
    length_total = row_count * group_count
    attn_full, mlp_full, norm_full, taps_full = (
        lax.all_gather(attn_weight, "dp", axis=0, tiled=True),
        lax.all_gather(mlp_weight, "dp", axis=1, tiled=True),
        lax.all_gather(norms, "dp", axis=1, tiled=True),
        lax.all_gather(taps, "dp", axis=1, tiled=True),
    )
    inputs = tokens[0].astype(jnp.float32)
    cot_rows = cotangent[0].astype(jnp.float32)
    norm_values = norm_full.astype(jnp.float32)
    taps_values = taps_full.astype(jnp.float32)
    tap_count = taps_values.shape[0]
    normed, norm_pull = jax.vjp(layer_norm, inputs, norm_values[0], norm_values[1])
    normed_low = normed.astype(jnp.bfloat16)
    project = jnp.dot(
        normed_low, attn_full[:, : 3 * model_width], preferred_element_type=jnp.float32
    )
    queries = project[:, :model_width]
    keys_part = project[:, model_width : 2 * model_width]
    values = project[:, 2 * model_width :]
    rim_rows = from_behind(
        keys_part[row_count - tap_count + 1 :].astype(jnp.bfloat16), "seq", 1
    ).astype(jnp.float32)
    shifted, shift_pull = jax.vjp(shift_mix, rim_rows, keys_part, taps_values)
    mixed_rows = (shifted * values).astype(jnp.bfloat16)
    moved_in = lax.all_to_all(mixed_rows.T, "seq", split_axis=0, concat_axis=1, tiled=True).astype(
        jnp.float32
    )
    tables = dft_tables(length_total, DFT_ROWS)
    kernel, kernel_pull = jax.vjp(partial(kernel_rows, length_total), ssm_params)
    kernel_freq = forward_dft(kernel, tables)
    input_freq = forward_dft(moved_in, tables)
    conv_channels = inverse_dft(complex_product(input_freq, kernel_freq, False), tables)
    conv_back = lax.all_to_all(
        conv_channels.astype(jnp.bfloat16), "seq", split_axis=1, concat_axis=0, tiled=True
    )
    conv_rows = conv_back.T.astype(jnp.float32)
    gated_rows = (queries * conv_rows).astype(jnp.bfloat16)
    branch = jnp.dot(
        gated_rows, attn_full[:, 3 * model_width :], preferred_element_type=jnp.float32
    )
    residual_one = inputs + branch
    normed_two, norm_two_pull = jax.vjp(layer_norm, residual_one, norm_values[2], norm_values[3])
    normed_two_low = normed_two.astype(jnp.bfloat16)
    before = jnp.dot(normed_two_low, mlp_full[0], preferred_element_type=jnp.float32)
    active, gelu_pull = jax.vjp(jax.nn.gelu, before)
    active_low = active.astype(jnp.bfloat16)
    mlp_out = jnp.einsum("tf,df->td", active_low, mlp_full[1], preferred_element_type=jnp.float32)
    layer_out = (residual_one + mlp_out).astype(jnp.bfloat16)
    attn_back, mlp_back = (
        lax.all_gather(attn_weight, "dp", axis=0, tiled=True),
        lax.all_gather(mlp_weight, "dp", axis=1, tiled=True),
    )
    grad_after = cotangent[0]
    grad_active = jnp.dot(grad_after, mlp_back[1], preferred_element_type=jnp.float32)
    grad_down = jnp.einsum("td,tf->df", grad_after, active_low, preferred_element_type=jnp.float32)
    grad_before = gelu_pull(grad_active)[0].astype(jnp.bfloat16)
    grad_up = jnp.einsum(
        "td,tf->df", normed_two_low, grad_before, preferred_element_type=jnp.float32
    )
    grad_normed_two = jnp.einsum(
        "tf,df->td", grad_before, mlp_back[0], preferred_element_type=jnp.float32
    )
    grad_residual_part, grad_gain_two, grad_bias_two = norm_two_pull(grad_normed_two)
    grad_residual = cot_rows + grad_residual_part
    grad_branch = grad_residual.astype(jnp.bfloat16)
    grad_out = jnp.einsum("td,te->de", gated_rows, grad_branch, preferred_element_type=jnp.float32)
    grad_gated = jnp.einsum(
        "te,de->td",
        grad_branch,
        attn_back[:, 3 * model_width :],
        preferred_element_type=jnp.float32,
    )
    grad_queries = grad_gated * conv_rows
    grad_conv = (grad_gated * queries).astype(jnp.bfloat16)
    grad_moved = lax.all_to_all(grad_conv.T, "seq", split_axis=0, concat_axis=1, tiled=True).astype(
        jnp.float32
    )
    grad_freq = forward_dft(grad_moved, tables)
    grad_input = inverse_dft(complex_product(kernel_freq, grad_freq, True), tables)
    grad_kernel = inverse_dft(complex_product(input_freq, grad_freq, True), tables)
    grad_ssm_local = kernel_pull(grad_kernel)[0]
    grad_ssm = lax.psum(grad_ssm_local, "dp")
    grad_mixed_back = lax.all_to_all(
        grad_input.astype(jnp.bfloat16), "seq", split_axis=1, concat_axis=0, tiled=True
    )
    grad_mixed = grad_mixed_back.T.astype(jnp.float32)
    grad_shifted = grad_mixed * values
    grad_values = grad_mixed * shifted
    grad_rim, grad_keys, grad_taps = shift_pull(grad_shifted)
    returned = from_behind(as_sent(grad_rim), "seq", -1).astype(grad_rim.dtype)
    grad_keys = grad_keys + jnp.pad(returned, ((row_count - tap_count + 1, 0), (0, 0)))
    grad_project = jnp.concatenate([grad_queries, grad_keys, grad_values], axis=1).astype(
        jnp.bfloat16
    )
    grad_qkv = jnp.einsum("td,te->de", normed_low, grad_project, preferred_element_type=jnp.float32)
    grad_normed = jnp.einsum(
        "te,de->td",
        grad_project,
        attn_back[:, : 3 * model_width],
        preferred_element_type=jnp.float32,
    )
    grad_input_part, grad_gain_one, grad_bias_one = norm_pull(grad_normed)
    input_grad = grad_residual + grad_input_part
    grad_attn = jnp.concatenate([grad_qkv, grad_out], axis=1)
    grad_mlp = jnp.stack([grad_up, grad_down])
    grad_norms = jnp.stack([grad_gain_one, grad_bias_one, grad_gain_two, grad_bias_two])
    owned_part = (
        lax.psum_scatter(
            grad_attn.astype(jnp.bfloat16), "dp", scatter_dimension=0, tiled=True
        ).astype(jnp.float32),
        lax.psum_scatter(
            grad_mlp.astype(jnp.bfloat16), "dp", scatter_dimension=1, tiled=True
        ).astype(jnp.float32),
        lax.psum_scatter(
            grad_norms.astype(jnp.bfloat16), "dp", scatter_dimension=1, tiled=True
        ).astype(jnp.float32),
        lax.psum_scatter(
            grad_taps.astype(jnp.bfloat16), "dp", scatter_dimension=1, tiled=True
        ).astype(jnp.float32),
    )
    summed = (
        lax.psum(owned_part[0].astype(jnp.bfloat16), "seq").astype(jnp.float32),
        lax.psum(owned_part[1].astype(jnp.bfloat16), "seq").astype(jnp.float32),
        lax.psum(owned_part[2].astype(jnp.bfloat16), "seq").astype(jnp.float32),
        lax.psum(owned_part[3].astype(jnp.bfloat16), "seq").astype(jnp.float32),
    )
    grad_scale = 1.0 / math.sqrt(owner_count * length_total)
    attn_step, attn_moments_new = adam_update(
        attn_weight.astype(jnp.float32),
        attn_moments,
        summed[0] * grad_scale,
        LEARN_RATE,
        DECAY_RATE,
    )
    mlp_step, mlp_moments_new = adam_update(
        mlp_weight.astype(jnp.float32), mlp_moments, summed[1] * grad_scale, LEARN_RATE, DECAY_RATE
    )
    norms_step, norm_moments_new = adam_update(
        norms.astype(jnp.float32), norm_moments, summed[2] * grad_scale, LEARN_RATE, 0.0
    )
    taps_step, tap_moments_new = adam_update(
        taps.astype(jnp.float32), tap_moments, summed[3] * grad_scale, LEARN_RATE, DECAY_RATE
    )
    ssm_step, ssm_moments_new = adam_update(
        ssm_params, ssm_moments, grad_ssm * grad_scale, SSM_LEARN_RATE, 0.0
    )
    return (
        layer_out[None],
        input_grad[None],
        attn_step,
        attn_moments_new,
        mlp_step,
        mlp_moments_new,
        norms_step,
        norm_moments_new,
        taps_step,
        tap_moments_new,
        ssm_step,
        ssm_moments_new,
    )


LANES = 128
RADIX = 8
HALF = 128


def transform_tables():
    rows = np.arange(HALF)
    length = RADIX * HALF
    waves = RADIX * rows[None, :, None] + np.arange(RADIX)[:, None, None] + 0.25
    angles = 2.0 * np.pi * np.mod(rows[None, None, :] * waves, length) / length
    cosines, sines = np.cos(angles), np.sin(angles)
    full = np.concatenate(
        [np.concatenate([cosines, sines], axis=2), np.concatenate([-sines, cosines], axis=2)], axis=1
    )


    def parts(matrix):
        matrix = matrix.astype(np.float32)
        high = matrix.astype(ml_dtypes.bfloat16)
        rest = (matrix - high.astype(np.float32)).astype(ml_dtypes.bfloat16)
        return np.stack([high, rest])

    return parts(full), parts(np.swapaxes(full, 1, 2))


def turned(value, angle):
    real, imaginary = value
    cosine, sine = math.cos(angle), math.sin(angle)
    if abs(sine) < 1e-12:
        return (real, imaginary) if cosine > 0 else (-real, -imaginary)
    if abs(cosine) < 1e-12:
        return (-imaginary, real) if sine > 0 else (imaginary, -real)
    return (real * cosine - imaginary * sine, real * sine + imaginary * cosine)


def small_transform(values, sign):
    count = len(values)
    if count == 1:
        return values
    even = small_transform(values[::2], sign)
    odd = small_transform(values[1::2], sign)
    low, high = [], []
    for index in range(count // 2):
        (er, ei), (tr, ti) = even[index], turned(odd[index], sign * 2.0 * math.pi * index / count)
        low.append((er + tr, ei + ti))
        high.append((er - tr, ei - ti))
    return low + high


def dot(left, right):
    return jnp.dot(left, right, preferred_element_type=jnp.float32)


def keep_parts(high_ref, low_ref, wave, row, cols, value):
    high = value.astype(jnp.bfloat16)
    high_ref[wave, pl.ds(row, 16), cols] = high
    if low_ref is not None:
        low_ref[wave, pl.ds(row, 16), cols] = (value - high.astype(jnp.float32)).astype(jnp.bfloat16)


def table_dot(table_high, table_low, high_ref, low_ref, wave):
    high = high_ref[wave]
    total = dot(table_high, high) + dot(table_low, high)
    return total if low_ref is None else total + dot(table_high, low_ref[wave])


def each_tile(width, rows, step, body):
    for block in range(width // LANES):

        def one(index, carry, block=block):
            body(pl.multiple_of(index * step, step), pl.ds(block * LANES, LANES))
            return carry

        lax.fori_loop(0, rows // step, one, 0)


def to_waves(width, read, used, w_ref, high_ref, low_ref, store):
    def first(row, cols):
        inputs = []
        for part in range(used):
            x = read(part * HALF, row, cols)
            angle = -2.0 * math.pi * part / 32.0
            inputs.append((x * math.cos(angle), x * math.sin(angle)) if part else (x, jnp.zeros_like(x)))
        while len(inputs) < RADIX:
            inputs.append((jnp.zeros_like(x), jnp.zeros_like(x)))
        for wave, value in enumerate(small_transform(inputs, -1.0)):
            for place, part in enumerate(value):
                keep_parts(high_ref, low_ref, wave, row + place * HALF, cols, part)

    each_tile(width, HALF, 16, first)

    def second(wave, carry):
        store(wave, table_dot(w_ref[0, wave], w_ref[1, wave], high_ref, low_ref, wave))
        return carry

    lax.fori_loop(0, RADIX, second, 0)


def product(width, left_ref, right_ref, conjugate, high_ref, low_ref):
    sign = -1.0 if conjugate else 1.0

    def one(wave, carry):
        def tile(row, cols):
            lr, li = left_ref[wave, pl.ds(row, 16), cols], left_ref[wave, pl.ds(row + HALF, 16), cols] * sign
            rr, ri = right_ref[wave, pl.ds(row, 16), cols], right_ref[wave, pl.ds(row + HALF, 16), cols]
            for place, part in enumerate((lr * rr - li * ri, lr * ri + li * rr)):
                keep_parts(high_ref, low_ref, wave, row + place * HALF, cols, part)

        each_tile(width, HALF, 16, tile)
        return carry

    lax.fori_loop(0, RADIX, one, 0)


def from_waves(width, w_ref, high_ref, low_ref, back_ref, put):
    def second(wave, carry):
        back_ref[wave] = table_dot(w_ref[0, wave], w_ref[1, wave], high_ref, low_ref, wave)
        return carry

    lax.fori_loop(0, RADIX, second, 0)
    scale = 1.0 / (RADIX * HALF)

    def first(row, cols):
        values = [
            (back_ref[wave, pl.ds(row, 16), cols], back_ref[wave, pl.ds(row + HALF, 16), cols])
            for wave in range(RADIX)
        ]
        for part, (real, imaginary) in enumerate(small_transform(values, 1.0)):
            angle = 2.0 * math.pi * part / 32.0
            put(part * HALF, row, cols, real * (math.cos(angle) * scale) - imaginary * (math.sin(angle) * scale))

    each_tile(width, HALF, 16, first)


def first_positions(width, count, w_ref, high_ref, low_ref):
    total = jnp.zeros((count, width), jnp.float32)
    for wave in range(RADIX):
        total = total + table_dot(w_ref[0, wave, :count, :], w_ref[1, wave, :count, :], high_ref, low_ref, wave)
    return total * (1.0 / (RADIX * HALF))


FINE = 32


def decay_sums(width, length, ssm_ref, out_ref):
    modes = ssm_ref.shape[1]
    steps = length // FINE
    out_ref[...] = jnp.zeros(out_ref.shape, jnp.float32)
    for block in range(width // LANES):
        cols = pl.ds(block * LANES, LANES)
        offsets = lax.broadcasted_iota(jnp.int32, (FINE, LANES), 0).astype(jnp.float32)

        def group(index, carry, cols=cols, offsets=offsets):
            base = pl.multiple_of(index * 8, 8)
            rates = jnp.exp(ssm_ref[0, pl.ds(base, 8), cols])
            leaps = jnp.exp(-rates * FINE)
            weights = ssm_ref[1, pl.ds(base, 8), cols]
            terms = tuple(weights[i : i + 1] * jnp.exp(-rates[i : i + 1] * offsets) for i in range(8))
            leap_rows = [jnp.broadcast_to(leaps[i : i + 1], (FINE, LANES)) for i in range(8)]

            def step(number, terms, leap_rows=leap_rows):
                rows = pl.ds(pl.multiple_of(number * FINE, FINE), FINE)
                total = out_ref[rows, cols]
                for term in terms:
                    total = total + term
                out_ref[rows, cols] = total
                return tuple(term * leap for term, leap in zip(terms, leap_rows))

            lax.fori_loop(0, steps, step, terms, unroll=4)
            return carry

        lax.fori_loop(0, modes // 8, group, 0)


def decay_gradients(block, length, ssm_ref, grad_ref, out_ref):
    modes = ssm_ref.shape[1]
    steps = length // FINE
    cols = pl.ds(block * LANES, LANES)
    offsets = lax.broadcasted_iota(jnp.int32, (FINE, LANES), 0).astype(jnp.float32)

    def group(index, carry):
        base = pl.multiple_of(index * 8, 8)
        rates = jnp.exp(ssm_ref[0, pl.ds(base, 8), cols])
        leaps = jnp.exp(-rates * FINE)
        plain_rows, slope_rows = [], []
        for modes_now in ((0, 1, 2, 3), (4, 5, 6, 7)):
            zero = offsets * 0.0
            leap_rows = [jnp.broadcast_to(leaps[i : i + 1], (FINE, LANES)) for i in modes_now]

            def step(number, sums, leap_rows=leap_rows):
                rows = grad_ref[pl.ds(pl.multiple_of((steps - 1 - number) * FINE, FINE), FINE), cols]
                return tuple((v * leap + rows, w * leap + v) for (v, w), leap in zip(sums, leap_rows))

            sums = lax.fori_loop(0, steps, step, tuple((zero, zero) for _ in modes_now), unroll=8)
            for i, (v, w) in zip(modes_now, sums):
                fine = jnp.exp(-rates[i : i + 1] * offsets)
                plain = fine * v
                slope = fine * w * (leaps[i : i + 1] * FINE) + plain * offsets
                plain_rows.append(jnp.sum(plain, axis=0, keepdims=True))
                slope_rows.append(jnp.sum(slope, axis=0, keepdims=True))
        out_ref[modes // 8 + index, :, cols] = jnp.concatenate(plain_rows, axis=0)
        out_ref[index, :, cols] = (
            -ssm_ref[1, pl.ds(base, 8), cols] * rates * jnp.concatenate(slope_rows, axis=0)
        )
        return carry

    lax.fori_loop(0, modes // 8, group, 0)


def layer_norm_parts(values):
    average = jnp.mean(values, axis=-1, keepdims=True)
    centred = values - average
    variance = jnp.mean(centred * centred, axis=-1, keepdims=True)
    inverse = lax.rsqrt(variance + EPS_NORM)
    return centred * inverse, inverse


def layer_norm_back(upstream, normal, inverse, gain_row):
    weighted = upstream * gain_row
    average = jnp.mean(weighted, axis=-1, keepdims=True)
    overlap = jnp.mean(weighted * normal, axis=-1, keepdims=True)
    into = (weighted - average - normal * overlap) * inverse
    return into, jnp.sum(upstream * normal, axis=0, keepdims=True), jnp.sum(upstream, axis=0, keepdims=True)


MESH = pl.DeviceIdType.MESH
TWO, FOUR = 2, 4
TAP_ROWS = 64
VMEM_LIMIT = 62 * 1024 * 1024


class Place:
    def __init__(self):
        self.s, self.d = lax.axis_index("seq"), lax.axis_index("dp")
        self.z, self.y, self.c = self.d // 4, (self.d // 2) % 2, self.d % 2

    def over_x(self):
        return (1 - self.s, self.d)

    def over_y(self):
        return (self.s, self.d + 2 - 4 * self.y)

    def over_core(self):
        return (self.s, self.d + 1 - 2 * self.c)

    def along_z(self, step):
        return (self.s, (self.d + 4 * step) % 16)

    def owner(self, index):
        return (self.s, index)


def send(source, target, send_sem, recv_sem, device):
    return pltpu.make_async_remote_copy(
        src_ref=source, dst_ref=target, send_sem=send_sem, recv_sem=recv_sem, device_id=device, device_id_type=MESH
    )


def greet_all(place):
    barrier = pltpu.get_barrier_semaphore()
    pl.semaphore_signal(barrier, inc=1, device_id=place.over_x(), device_id_type=MESH)

    def greet(step, carry):
        pl.semaphore_signal(
            barrier, inc=1, device_id=place.owner((place.d + step) % 16), device_id_type=MESH
        )
        return carry

    lax.fori_loop(1, 16, greet, 0)
    pl.semaphore_wait(barrier, 16)


WEIGHTS = (
    ("out", 0, 768, "whole"),
    ("up", 0, 1536, "halved"),
    ("down", 0, 1536, "whole"),
    ("up", 1536, 1536, "halved"),
    ("down", 1536, 1536, "whole"),
)
OUT_W, UP_FIRST, DOWN_FIRST, UP_LAST, DOWN_LAST, QKV_W = range(len(WEIGHTS) + 1)
HIDDEN_BLOCK = 768


def dot_right(left, right):
    return lax.dot_general(left, right, (((1,), (1,)), ((), ())), preferred_element_type=jnp.float32)


def dot_left(left, right):
    return lax.dot_general(left, right, (((0,), (0,)), ((), ())), preferred_element_type=jnp.float32)


def gelu_parts(x):
    slope = math.sqrt(2.0 / math.pi)
    square = x * x
    bent = jnp.tanh(slope * x * (1.0 + 0.044715 * square))
    upper = 0.5 + 0.5 * bent
    return x * upper, upper + 0.5 * x * (1.0 - bent * bent) * (slope * (1.0 + 3.0 * 0.044715 * square))


def forward_body(
    token_ref, cotangent_ref, attn_shard, mlp_shard, small_ref, ssm_ref, to_ref, from_ref,
    qkv_full, up_full, down_full, small_t, normed_ref, query_out, value_out, conv_ref, shifted_ref,
    kernel_out, taps_out, keys_out, mixed_out, layer_out, residual_grad, norm_two_out, gated_grad, up_grad, down_grad, out_grad,
    qkv_ref, token_all, small_all, gated_ref, rows_ref, out_full, grad_send,
    own_sem, z_s, z_r, y_s, y_r, x_s, x_r, core_s, core_r, small_s, small_r, side_s, side_r, store_sem, load_sem,
):
    length, width = conv_ref.shape
    own_rows, model = token_ref.shape
    place = Place()
    f32, low = jnp.float32, jnp.bfloat16
    shards = {"up": mlp_shard.at[0], "down": mlp_shard.at[1], "out": attn_shard.at[:, pl.ds(3 * model, model)]}
    fulls = {"up": up_full, "down": down_full, "out": out_full}

    def columns(k):
        source, start, count, way = WEIGHTS[k]
        if way == "whole":
            return source, pl.ds(start, count)
        return source, pl.ds(pl.multiple_of(start + place.s * (count // 2), LANES), count // 2)

    def z_copy(k, step):
        if k == QKV_W:
            source, target = qkv_ref, qkv_full.at[place.z, place.y, place.c]
        else:
            name, cols = columns(k)
            source, target = shards[name].at[:, cols], fulls[name].at[place.z, place.y, place.c, :, cols]
        return send(source, target, z_s.at[k, step - 1], z_r.at[k, step - 1], place.along_z(step))

    def y_copy(k):
        if k == QKV_W:
            blocks = qkv_full.at[:, place.y, place.c]
        else:
            name, cols = columns(k)
            blocks = fulls[name].at[:, place.y, place.c, :, cols]
        return send(blocks, blocks, y_s.at[k], y_r.at[k], place.over_y())

    def x_copy(k):
        name, cols = columns(k)
        blocks = fulls[name].at[:, :, place.c, :, cols]
        return send(blocks, blocks, x_s.at[k], x_r.at[k], place.over_x())

    def core_copy(k):
        if k == QKV_W:
            blocks = qkv_full.at[:, :, place.c]
        else:
            name, start, count, _ = WEIGHTS[k]
            blocks = fulls[name].at[:, :, place.c, :, pl.ds(start, count)]
        return send(blocks, blocks, core_s.at[k], core_r.at[k], place.over_core())

    def own_copies():
        copies = []
        for k in range(QKV_W):
            name, cols = columns(k)
            target = fulls[name].at[place.z, place.y, place.c, :, cols]
            copies.append(pltpu.make_async_copy(shards[name].at[:, cols], target, own_sem.at[k]))
        return copies

    def start_z(k):
        for step in range(1, 4):
            z_copy(k, step).start()

    def wait_z(k):
        for step in range(1, 4):
            z_copy(k, step).wait_recv()

    def over_peers(action):
        def one(step, carry):
            action(step)
            return carry

        lax.fori_loop(1, 16, one, 0)

    def small_copy(step):
        other = (place.d + step) % 16
        return send(small_ref, small_all.at[place.d], small_s.at[other], small_r.at[place.d], place.owner(other))

    def small_arrival(step):
        other = (place.d + step) % 16
        return send(small_ref, small_all.at[other], small_s.at[other], small_r.at[other], place.owner(other))

    token_copy = send(token_ref, token_all.at[place.s], side_s.at[0], side_r.at[0], place.over_x())
    gated_copy = send(gated_ref.at[1 - place.s], rows_ref.at[place.s], side_s.at[1], side_r.at[1], place.over_x())
    grad_copy = send(grad_send, gated_grad.at[place.s], side_s.at[2], side_r.at[2], place.over_x())

    def step_one():
        wait_z(QKV_W)
        y_copy(QKV_W).start()
        start_z(OUT_W)
        for copy in own_copies():
            copy.wait()

    def step_two():
        wait_z(OUT_W)
        start_z(UP_FIRST)

    def step_three():
        y_copy(QKV_W).wait_recv()
        core_copy(QKV_W).start()
        y_copy(OUT_W).start()

    def step_four():
        wait_z(UP_FIRST)
        start_z(DOWN_FIRST)

    def step_five():
        y_copy(OUT_W).wait_recv()
        core_copy(OUT_W).start()
        y_copy(UP_FIRST).start()

    def step_six():
        y_copy(UP_FIRST).wait_recv()
        x_copy(UP_FIRST).start()

    def step_seven():
        wait_z(DOWN_FIRST)
        y_copy(DOWN_FIRST).start()
        start_z(UP_LAST)

    def step_eight():
        wait_z(UP_LAST)
        start_z(DOWN_LAST)

    def step_nine():
        x_copy(UP_FIRST).wait_recv()
        core_copy(UP_FIRST).start()

    def step_ten():
        y_copy(DOWN_FIRST).wait_recv()
        core_copy(DOWN_FIRST).start()
        y_copy(UP_LAST).start()

    def step_eleven():
        y_copy(UP_LAST).wait_recv()
        x_copy(UP_LAST).start()

    def step_twelve():
        wait_z(DOWN_LAST)
        y_copy(DOWN_LAST).start()

    def step_thirteen():
        x_copy(UP_LAST).wait_recv()
        core_copy(UP_LAST).start()

    def step_fourteen():
        y_copy(DOWN_LAST).wait_recv()
        core_copy(DOWN_LAST).start()

    for j in range(3):
        cols = pl.ds(pl.multiple_of((2 * j + place.s) * width, LANES), width)
        qkv_ref[:, j * width : (j + 1) * width] = attn_shard[:, cols]
    greet_all(place)
    start_z(QKV_W)
    over_peers(lambda step: small_copy(step).start())
    token_copy.start()
    for copy in own_copies():
        copy.start()
    qkv_full[place.z, place.y, place.c] = qkv_ref[...]
    small_all[place.d] = small_ref[...]

    def mixer(line_ref, high_ref, low_ref, back_ref, proj_ref, kernel_w, other_w, keys_w):
        def keep(target):
            def store(wave, value):
                target[wave] = value

            return store

        def lines(base, row, cols):
            return line_ref[pl.ds(base + row, 16), cols]

        def column(index, cols):
            return pl.ds(index * width + cols.start, cols.size)

        stores = [
            pltpu.make_async_copy(kernel_w, kernel_out, store_sem.at[0]),
            pltpu.make_async_copy(other_w, taps_out, store_sem.at[1]),
            pltpu.make_async_copy(keys_w, keys_out, store_sem.at[2]),
            pltpu.make_async_copy(other_w, mixed_out, store_sem.at[3]),
            pltpu.make_async_copy(proj_ref.at[:, pl.ds(0, width)], query_out, store_sem.at[4]),
            pltpu.make_async_copy(proj_ref.at[:, pl.ds(2 * width, width)], value_out, store_sem.at[5]),
        ]
        decay_sums(width, length, ssm_ref, line_ref)
        step_one()
        to_waves(width, lines, RADIX, to_ref, high_ref, low_ref, keep(kernel_w))
        stores[0].start()
        over_peers(lambda step: small_arrival(step).wait_recv())
        small_t[...] = small_all[...].reshape(16 * small_all.shape[1], LANES).astype(f32).T
        taps_cols = pl.multiple_of(place.s * width, LANES)

        def read_taps(base, row, cols):
            taps = small_t[pl.ds(base + row, 16), pl.ds(pl.multiple_of(taps_cols + cols.start, LANES), LANES)]
            inside = lax.broadcasted_iota(jnp.int32, taps.shape, 0) + (base + row) < TAP_ROWS
            return jnp.where(inside, taps, 0.0)

        def normalize(source, begin):
            def one(index, carry):
                row = pl.multiple_of(index * 32, 32)
                normal, _ = layer_norm_parts(source[pl.ds(row, 32), :].astype(f32))
                scaled = normal * small_t[TAP_ROWS : TAP_ROWS + 1, :] + small_t[TAP_ROWS + 1 : TAP_ROWS + 2, :]
                normed_ref[pl.ds(pl.multiple_of(begin + row, 32), 32), :] = scaled.astype(low)
                return carry

            lax.fori_loop(0, own_rows // 32, one, 0)

        def project(begin):
            weight = qkv_full[...].reshape(model, 3 * width)

            def one(index, carry):
                row = pl.ds(pl.multiple_of(begin + index * 256, 256), 256)
                proj_ref[row, :] = dot(normed_ref[row, :], weight)
                return carry

            lax.fori_loop(0, own_rows // 256, one, 0)

        own_begin, other_begin = place.s * own_rows, (1 - place.s) * own_rows
        normalize(token_ref, own_begin)
        step_two()
        token_copy.wait_recv()
        normalize(token_all.at[1 - place.s], other_begin)
        step_three()
        to_waves(width, read_taps, 1, to_ref, high_ref, low_ref, keep(other_w))
        stores[1].start()
        step_four()
        core_copy(QKV_W).wait_recv()
        project(own_begin)
        project(other_begin)
        stores[4].start()
        stores[5].start()
        step_five()
        to_waves(
            width, lambda base, row, cols: proj_ref[pl.ds(base + row, 16), column(1, cols)],
            RADIX, to_ref, high_ref, low_ref, keep(keys_w),
        )
        stores[2].start()
        product(width, other_w, keys_w, False, high_ref, low_ref)
        step_six()

        def put_shifted(base, row, cols, value):
            rows = pl.ds(base + row, 16)
            shifted_ref[rows, cols] = value
            mixed = value * proj_ref[rows, column(2, cols)]
            line_ref[rows, cols] = mixed.astype(low).astype(f32)

        from_waves(width, from_ref, high_ref, low_ref, back_ref, put_shifted)
        step_seven()
        stores[1].wait()
        to_waves(width, lines, RADIX, to_ref, high_ref, low_ref, keep(other_w))
        stores[3].start()
        product(width, kernel_w, other_w, False, high_ref, low_ref)
        step_eight()

        def put_conv(base, row, cols, value):
            rows = pl.ds(base + row, 16)
            rounded = value.astype(low)
            conv_ref[rows, cols] = rounded
            gated = (proj_ref[rows, cols] * rounded.astype(f32)).astype(low)
            gated_ref[base // own_rows, pl.ds(base % own_rows + row, 16), cols] = gated

        from_waves(width, from_ref, high_ref, low_ref, back_ref, put_conv)
        gated_copy.start()
        for i in (0, 2, 3, 4, 5):
            stores[i].wait()

    waves = (RADIX, 2 * HALF, width)
    pl.run_scoped(
        mixer,
        pltpu.VMEM((length, width), f32),
        pltpu.VMEM(waves, low),
        pltpu.VMEM(waves, low),
        pltpu.VMEM(waves, f32),
        pltpu.VMEM((length, 3 * width), f32),
        pltpu.VMEM(waves, f32),
        pltpu.VMEM(waves, f32),
        pltpu.VMEM(waves, f32),
    )
    rows_ref[place.s] = gated_ref[place.s]

    def feed_forward(
        up_w, down_w, up_g, down_g, residual_ref, normed_two, normed_turned, cot_turned, active_ref, before_ref,
        out_sum, normed_grad,
    ):
        block_shape = up_g.shape
        blocks = up_full.shape[4] // HIDDEN_BLOCK

        def load(j):
            cols = pl.ds(j * HIDDEN_BLOCK, HIDDEN_BLOCK)
            return [
                pltpu.make_async_copy(full.at[:, :, :, :, cols], held.at[j % 2], load_sem.at[i, j % 2])
                for i, (full, held) in enumerate(((up_full, up_w), (down_full, down_w)))
            ]

        def store(j):
            cols = pl.ds(j * HIDDEN_BLOCK, HIDDEN_BLOCK)
            return [
                pltpu.make_async_copy(held, full.at[:, :, :, :, cols], store_sem.at[i])
                for i, (full, held) in enumerate(((up_grad, up_g), (down_grad, down_g)))
            ]

        step_nine()
        cot_turned[...] = cotangent_ref[...].T
        step_ten()
        core_copy(OUT_W).wait_recv()
        gated_copy.wait_recv()
        out_w = out_full[...].reshape(model, model)

        def branch(index, carry):
            rows = pl.ds(pl.multiple_of(index * 256, 256), 256)
            value = dot(rows_ref[0, rows, :], out_w[:width]) + dot(rows_ref[1, rows, :], out_w[width:])
            residual_ref[rows, :] = token_ref[rows, :].astype(f32) + value
            return carry

        lax.fori_loop(0, own_rows // 256, branch, 0)

        def normalize(index, carry):
            rows = pl.ds(pl.multiple_of(index * 32, 32), 32)
            normal, _ = layer_norm_parts(residual_ref[rows, :])
            scaled = normal * small_t[TAP_ROWS + 2 : TAP_ROWS + 3, :] + small_t[TAP_ROWS + 3 : TAP_ROWS + 4, :]
            normed_two[rows, :] = scaled.astype(low)
            return carry

        lax.fori_loop(0, own_rows // 32, normalize, 0)
        core_copy(UP_FIRST).wait_recv()
        core_copy(DOWN_FIRST).wait_recv()
        for copy in load(0) + load(1):
            copy.start()
        normed_turned[...] = normed_two[...].T
        step_eleven()
        step_twelve()
        for j in range(blocks):
            if j == blocks // 2:
                step_thirteen()
                step_fourteen()
                core_copy(UP_LAST).wait_recv()
                core_copy(DOWN_LAST).wait_recv()
                for copy in load(j) + load(j + 1):
                    copy.start()
            for copy in load(j):
                copy.wait()
            up = up_w[j % 2].reshape(model, HIDDEN_BLOCK)
            down = down_w[j % 2].reshape(model, HIDDEN_BLOCK)

            def rows_of(index, carry, up=up, down=down, j=j):
                rows = pl.ds(pl.multiple_of(index * 256, 256), 256)
                active, slope = gelu_parts(dot(normed_two[rows, :], up))
                active = active.astype(low)
                active_ref[rows, :] = active
                grad_before = (dot(cotangent_ref[rows, :], down) * slope).astype(low)
                before_ref[rows, :] = grad_before
                out_part = dot_right(active, down)
                grad_part = dot_right(grad_before, up)
                if j:
                    out_part = out_part + out_sum[rows, :]
                    grad_part = grad_part + normed_grad[rows, :]
                out_sum[rows, :] = out_part
                normed_grad[rows, :] = grad_part
                return carry

            lax.fori_loop(0, own_rows // 256, rows_of, 0)
            if j:
                for copy in store(j - 1):
                    copy.wait()
            down_g[...] = dot(cot_turned[...], active_ref[...]).astype(low).reshape(block_shape)
            up_g[...] = dot(normed_turned[...], before_ref[...]).astype(low).reshape(block_shape)
            for copy in store(j):
                copy.start()

        def norm_back(index, sums):
            rows = pl.ds(pl.multiple_of(index * 32, 32), 32)
            normal, inverse = layer_norm_parts(residual_ref[rows, :])
            into, gain, bias = layer_norm_back(
                normed_grad[rows, :], normal, inverse, small_t[TAP_ROWS + 2 : TAP_ROWS + 3, :]
            )
            total = cotangent_ref[rows, :].astype(f32) + into
            residual_grad[rows, :] = total
            active_ref[rows, :] = total.astype(low)
            layer_out[rows, :] = (residual_ref[rows, :] + out_sum[rows, :]).astype(low)
            return sums[0] + gain, sums[1] + bias

        zero = small_t[TAP_ROWS : TAP_ROWS + 1, :] * 0.0
        gain, bias = lax.fori_loop(0, own_rows // 32, norm_back, (zero, zero))
        norm_two_out[0:1, :] = gain
        norm_two_out[1:2, :] = bias
        part_shape = (2,) + out_full.shape[1:]
        other_w = out_full[pl.ds(2 * (1 - place.s), 2)].reshape(width, model)
        grad_send[...] = dot_right(active_ref[...], other_w).astype(low)
        grad_copy.start()
        own_w = out_full[pl.ds(2 * place.s, 2)].reshape(width, model)
        gated_grad[place.s] = dot_right(active_ref[...], own_w).astype(low)
        for h in range(2):
            out_grad[2 * h : 2 * h + 2] = dot_left(rows_ref[h], active_ref[...]).astype(low).reshape(part_shape)
        for copy in store(blocks - 1):
            copy.wait()
        grad_copy.wait_recv()

    block = (FOUR, TWO, TWO, out_full.shape[3], HIDDEN_BLOCK)
    pl.run_scoped(
        feed_forward,
        pltpu.VMEM((2,) + block, low),
        pltpu.VMEM((2,) + block, low),
        pltpu.VMEM(block, low),
        pltpu.VMEM(block, low),
        pltpu.VMEM((own_rows, model), f32),
        pltpu.VMEM((own_rows, model), low),
        pltpu.VMEM((model, own_rows), low),
        pltpu.VMEM((model, own_rows), low),
        pltpu.VMEM((own_rows, HIDDEN_BLOCK), low),
        pltpu.VMEM((own_rows, HIDDEN_BLOCK), low),
        pltpu.VMEM((own_rows, model), f32),
        pltpu.VMEM((own_rows, model), f32),
    )

    over_peers(lambda step: small_copy(step).wait_send())
    for copy in (token_copy, gated_copy, grad_copy):
        copy.wait_send()
    for k in range(QKV_W + 1):
        for step in range(1, 4):
            z_copy(k, step).wait_send()
        y_copy(k).wait_send()
        core_copy(k).wait_send()
        if k != QKV_W and WEIGHTS[k][3] == "halved":
            x_copy(k).wait_send()


def forward_layer(tokens, cotangent, attn_shard, mlp_shard, small, ssm, to_table, from_table):
    own_rows, model = tokens.shape
    owned = attn_shard.shape[0]
    width = model // 2
    length = 2 * own_rows
    hidden = mlp_shard.shape[2]
    f32, low = jnp.float32, jnp.bfloat16
    waves = (RADIX, 2 * HALF, width)
    vmem, anywhere = pl.BlockSpec(memory_space=pltpu.VMEM), pl.BlockSpec(memory_space=pl.ANY)
    shape = jax.ShapeDtypeStruct
    owners = (FOUR, TWO, TWO, owned)
    count = len(WEIGHTS) + 1
    dma = pltpu.SemaphoreType.DMA
    outs = (
        (shape(owners + (3 * width,), low), vmem),
        (shape(owners + (hidden,), low), anywhere),
        (shape(owners + (hidden,), low), anywhere),
        (shape((LANES, model), f32), vmem),
        (shape((length, model), low), vmem),
        (shape((length, width), f32), anywhere),
        (shape((length, width), f32), anywhere),
        (shape((length, width), low), vmem),
        (shape((length, width), f32), vmem),
        (shape(waves, f32), anywhere),
        (shape(waves, f32), anywhere),
        (shape(waves, f32), anywhere),
        (shape(waves, f32), anywhere),
        (shape((own_rows, model), low), vmem),
        (shape((own_rows, model), f32), vmem),
        (shape((2, model), f32), vmem),
        (shape((2, own_rows, width), low), vmem),
        (shape(owners + (hidden,), low), anywhere),
        (shape(owners + (hidden,), low), anywhere),
        (shape(owners + (model,), low), vmem),
    )
    return pl.pallas_call(
        forward_body,
        out_shape=tuple(out for out, _ in outs),
        in_specs=[vmem, vmem, vmem, anywhere, vmem, vmem, vmem, vmem],
        out_specs=tuple(spec for _, spec in outs),
        scratch_shapes=[
            pltpu.VMEM((owned, 3 * width), low),
            pltpu.VMEM((2, own_rows, model), low),
            pltpu.VMEM((16,) + small.shape, low),
            pltpu.VMEM((2, own_rows, width), low),
            pltpu.VMEM((2, own_rows, width), low),
            pltpu.VMEM(owners + (model,), low),
            pltpu.VMEM((own_rows, width), low),
            dma((count,)),
            dma((count, 3)),
            dma((count, 3)),
            dma((count,)),
            dma((count,)),
            dma((count,)),
            dma((count,)),
            dma((count,)),
            dma((count,)),
            dma((16,)),
            dma((16,)),
            dma((3,)),
            dma((3,)),
            dma((6,)),
            dma((2, 2)),
        ],
        compiler_params=pltpu.CompilerParams(collective_id=2, has_side_effects=True, vmem_limit_bytes=VMEM_LIMIT),
        name="forward_layer",
    )(tokens, cotangent, attn_shard, mlp_shard, small, ssm, to_table, from_table)


PIECES = (
    ("down", 0, 1536, "whole"),
    ("up", 1536, 1536, "halved"),
    ("down", 1536, 1536, "whole"),
    ("out", 0, 768, "halved"),
    ("up", 0, 1536, "whole"),
    ("qkv", 0, 1152, "apart"),
)
D0, U1, D1, OUT, U0, QKV = range(len(PIECES))


def add_blocks(put, sources, count):
    def one(index, carry):
        total = sources[0](index).astype(jnp.float32)
        for source in sources[1:]:
            total = total + source(index).astype(jnp.float32)
        put(index, total)
        return carry

    lax.fori_loop(0, count, one, 0)


def piece_halves(k):
    return TWO if PIECES[k][3] == "halved" else 1


def backward_body(*refs):
    count = len(PIECES)
    (
        grad_all, query_hbm, value_hbm, conv_ref, shifted_ref, kernel_w, taps_w, keys_w, mixed_w, ssm_ref, to_ref, from_ref,
        normed_ref, qkv_ref, token_ref, residual_ref, small_t, norm_two_ref, down_ref, up_ref, out_ref,
    ), refs = refs[:21], refs[21:]
    outs, refs = refs[:count], refs[count:]
    (small_out, ssm_out, input_out), refs = refs[:3], refs[3:]
    near, refs = refs[:count], refs[count:]
    from_x = dict(zip([k for k in range(count) if piece_halves(k) == TWO], refs))
    refs = refs[len(from_x):]
    from_y, from_z, final, last = (refs[i * count : (i + 1) * count] for i in range(4))
    refs = refs[4 * count :]
    (
        own_ref, query_ref, value_ref, spectrum, line_ref, decay_ref, wave_ref, high_ref, back_ref,
        grad_proj, qkv_grad, gn_send, gn_own, gn_last, small_rows, small_ref, small_all, small_sum, small_last,
        ssm_ref_all, ssm_all, ssm_sum,
    ), refs = refs[:22], refs[22:]
    (
        load_sem, own_sem, core_s, core_r, x_s, x_r, y_s, y_r, z_s, z_r, f_s, f_r, sm_s, sm_r, ss_s, ss_r, sg_s, sg_r,
        side_s, side_r,
    ) = refs
    length, width = conv_ref.shape
    own_rows = token_ref.shape[0]
    place = Place()
    grads = {"down": down_ref, "up": up_ref, "out": out_ref, "qkv": qkv_grad}

    def core_copy(k, h):
        source, start, columns, _ = PIECES[k]
        part = columns // piece_halves(k)
        blocks = grads[source].at[:, :, 1 - place.c, :, pl.ds(start + h * part, part)]
        return send(blocks, near[k].at[h], core_s.at[k, h], core_r.at[k, h], place.over_core())

    def own_copy(k, h):
        source, start, columns, _ = PIECES[k]
        part = columns // piece_halves(k)
        blocks = grads[source].at[:, :, place.c, :, pl.ds(start + h * part, part)]
        return pltpu.make_async_copy(blocks, own_ref.at[k % 2, :, :, :, pl.ds(h * part, part)], own_sem.at[k % 2, h])

    def x_copy(k):
        return send(near[k].at[1 - place.s], from_x[k], x_s.at[k], x_r.at[k], place.over_x())

    def kept(k):
        return near[k].at[place.s] if piece_halves(k) == TWO else near[k].at[0]

    def y_copy(k):
        return send(kept(k).at[:, 1 - place.y], from_y[k], y_s.at[k], y_r.at[k], place.over_y())

    def z_copy(k, step):
        other = (place.z + step) % 4
        return send(
            kept(k).at[other, place.y], from_z[k].at[step - 1], z_s.at[k, step - 1], z_r.at[k, step - 1],
            place.along_z(step),
        )

    def last_copy(k):
        return send(final[k], last[k], f_s.at[k], f_r.at[k], place.over_x())

    def load_own(k):
        for h in range(piece_halves(k)):
            own_copy(k, h).start()

    def add_core(k):
        part = PIECES[k][2] // piece_halves(k)
        for h in range(piece_halves(k)):
            core_copy(k, h).wait_recv()
            if k != QKV:
                own_copy(k, h).wait()

            def own(i, h=h):
                if k == QKV:
                    return qkv_grad[i // 2, i % 2, place.c]
                return own_ref[k % 2, i // 2, i % 2, :, h * part : (h + 1) * part]

            def put(i, total, h=h):
                near[k][h, i // 2, i % 2] = total.astype(jnp.bfloat16)

            add_blocks(put, [own, lambda i, h=h: near[k][h, i // 2, i % 2]], 8)

    def add_x(k):
        x_copy(k).wait_recv()

        def put(i, total):
            kept(k)[i // 2, i % 2] = total.astype(jnp.bfloat16)

        add_blocks(put, [lambda i: kept(k)[i // 2, i % 2], lambda i: from_x[k][i // 2, i % 2]], 8)

    def add_y(k):
        y_copy(k).wait_recv()

        def put(i, total):
            kept(k)[i, place.y] = total.astype(jnp.bfloat16)

        add_blocks(put, [lambda i: kept(k)[i, place.y], lambda i: from_y[k][i]], 4)

    def start_z(k):
        for step in range(1, 4):
            z_copy(k, step).start()

    def add_z(k):
        for step in range(1, 4):
            z_copy(k, step).wait_recv()
        total = kept(k)[place.z, place.y].astype(jnp.float32)
        for step in range(3):
            total = total + from_z[k][step].astype(jnp.float32)
        final[k][...] = total.astype(jnp.bfloat16)

    def finish(k):
        last_copy(k).wait_recv()
        if PIECES[k][3] == "whole":
            outs[k][...] = final[k][...].astype(jnp.float32) + last[k][...].astype(jnp.float32)
        else:
            outs[k][place.s] = final[k][...]
            outs[k][1 - place.s] = last[k][...]

    def over_peers(action):
        def one(step, carry):
            action(step)
            return carry

        lax.fori_loop(1, 16, one, 0)

    def to_peer(source, target, send_sem, recv_sem, step):
        other = (place.d + step) % 16
        return send(source.at[other], target.at[place.d], send_sem.at[other], recv_sem.at[place.d], place.owner(other))

    def from_peer(target, send_sem, recv_sem, step):
        other = (place.d + step) % 16
        return send(target.at[other], target.at[other], send_sem.at[other], recv_sem.at[other], place.owner(other))

    def share(step):
        other = (place.d + step) % 16
        return send(ssm_sum.at[place.d], ssm_sum.at[place.d], sg_s.at[other], sg_r.at[place.d], place.owner(other))

    gn_copy = send(gn_send, gn_last, side_s.at[1], side_r.at[1], place.over_x())
    small_copy = send(small_sum, small_last, side_s.at[2], side_r.at[2], place.over_x())
    spectra = (kernel_w, mixed_w, taps_w, keys_w)

    def load_spectrum(i):
        return pltpu.make_async_copy(spectra[i], spectrum.at[i % 2], load_sem.at[i % 2])

    query_copy = pltpu.make_async_copy(query_hbm, query_ref, load_sem.at[2])
    value_copy = pltpu.make_async_copy(value_hbm, value_ref, load_sem.at[3])

    greet_all(place)
    for k in (0, 1):
        for h in range(piece_halves(k)):
            core_copy(k, h).start()
        load_own(k)
    query_copy.start()
    value_copy.start()
    load_spectrum(0).start()
    load_spectrum(1).start()
    add_core(D0)
    y_copy(D0).start()
    for k in range(2, QKV):
        for h in range(piece_halves(k)):
            core_copy(k, h).start()
    load_own(2)
    add_core(U1)
    x_copy(U1).start()
    load_own(3)
    add_core(D1)
    load_own(4)
    add_core(OUT)
    add_core(U0)

    def keep(wave, value):
        wave_ref[wave] = value

    def lines(base, row, cols):
        return line_ref[pl.ds(base + row, 16), cols]

    def column(index, cols):
        return pl.ds(index * width + cols.start, cols.size)

    def read_conv_grad(base, row, cols):
        rows = pl.ds(base + row, 16)
        gradient = grad_all[base // own_rows, pl.ds(base % own_rows + row, 16), cols].astype(jnp.float32)
        grad_proj[rows, cols] = (gradient * conv_ref[rows, cols].astype(jnp.float32)).astype(jnp.bfloat16)
        return (gradient * query_ref[rows, cols]).astype(jnp.bfloat16).astype(jnp.float32)

    query_copy.wait()
    value_copy.wait()
    to_waves(width, read_conv_grad, RADIX, to_ref, high_ref, None, keep)
    add_y(D0)
    start_z(D0)
    y_copy(D1).start()
    load_spectrum(0).wait()
    product(width, spectrum.at[0], wave_ref, True, high_ref, None)
    load_spectrum(2).start()

    def put_mixed(base, row, cols, value):
        rows = pl.ds(base + row, 16)
        gradient = value.astype(jnp.bfloat16).astype(jnp.float32)
        grad_proj[rows, column(2, cols)] = (gradient * shifted_ref[rows, cols]).astype(jnp.bfloat16)
        line_ref[rows, cols] = gradient * value_ref[rows, cols]

    from_waves(width, from_ref, high_ref, None, back_ref, put_mixed)
    load_spectrum(1).wait()
    product(width, spectrum.at[1], wave_ref, True, high_ref, None)
    load_spectrum(3).start()

    def put_kernel(base, row, cols, value):
        decay_ref[pl.ds(base + row, 16), cols] = value

    from_waves(width, from_ref, high_ref, None, back_ref, put_kernel)
    add_x(U1)
    x_copy(OUT).start()
    to_waves(width, lines, RADIX, to_ref, high_ref, None, keep)
    add_y(D1)
    y_copy(U0).start()
    add_z(D0)
    start_z(D1)
    load_spectrum(2).wait()
    product(width, spectrum.at[0], wave_ref, True, high_ref, None)

    def put_keys(base, row, cols, value):
        grad_proj[pl.ds(base + row, 16), column(1, cols)] = value.astype(jnp.bfloat16)

    from_waves(width, from_ref, high_ref, None, back_ref, put_keys)
    add_x(OUT)

    def project_back(begin, put):
        def one(index, carry):
            row = pl.multiple_of(index * 256, 256)
            value = lax.dot_general(
                grad_proj[pl.ds(pl.multiple_of(begin + row, 256), 256), :], qkv_ref[...], (((1,), (1,)), ((), ())),
                preferred_element_type=jnp.float32,
            )
            put(pl.ds(row, 256), value)
            return carry

        lax.fori_loop(0, own_rows // 256, one, 0)

    def put_send(rows, value):
        gn_send[rows, :] = value.astype(jnp.bfloat16)

    def put_own(rows, value):
        gn_own[rows, :] = value

    project_back((1 - place.s) * own_rows, put_send)
    gn_copy.start()
    for pair in range(TWO):
        columns = 2 * 4 * qkv_grad.shape[3]
        value = lax.dot_general(
            normed_ref[:, pair * columns : (pair + 1) * columns], grad_proj[...], (((0,), (0,)), ((), ())),
            preferred_element_type=jnp.float32,
        )
        qkv_grad[2 * pair : 2 * pair + 2] = value.astype(jnp.bfloat16).reshape((2,) + qkv_grad.shape[1:])
    core_copy(QKV, 0).start()
    project_back(place.s * own_rows, put_own)
    add_y(U0)
    y_copy(U1).start()
    add_core(QKV)
    add_z(D1)
    start_z(U0)
    load_spectrum(3).wait()
    product(width, spectrum.at[1], wave_ref, True, high_ref, None)
    small_rows[...] = jnp.zeros(small_rows.shape, jnp.float32)
    small_rows[:TAP_ROWS, pl.ds(pl.multiple_of(place.s * width, LANES), width)] = first_positions(
        width, TAP_ROWS, from_ref, high_ref, None
    )
    decay_gradients(0, length, ssm_ref, decay_ref, ssm_ref_all)
    add_y(U1)
    y_copy(QKV).start()
    add_z(U0)
    start_z(U1)
    decay_gradients(1, length, ssm_ref, decay_ref, ssm_ref_all)
    add_y(QKV)
    start_z(QKV)
    y_copy(OUT).start()
    add_z(U1)
    decay_gradients(2, length, ssm_ref, decay_ref, ssm_ref_all)
    over_peers(lambda step: to_peer(ssm_ref_all, ssm_all, ss_s, ss_r, step).start())
    gn_copy.wait_recv()
    for k in (D0, D1, U0, U1):
        last_copy(k).start()

    def norm_back(index, sums):
        rows = pl.ds(pl.multiple_of(index * 32, 32), 32)
        normal, inverse = layer_norm_parts(token_ref[rows, :].astype(jnp.float32))
        upstream = gn_own[rows, :] + gn_last[rows, :].astype(jnp.float32)
        into, gain, bias = layer_norm_back(upstream, normal, inverse, small_t[TAP_ROWS : TAP_ROWS + 1, :])
        input_out[rows, :] = residual_ref[rows, :] + into
        return sums[0] + gain, sums[1] + bias

    zero = jnp.sum(norm_two_ref[...], axis=0, keepdims=True) * 0.0
    gain, bias = lax.fori_loop(0, own_rows // 32, norm_back, (zero, zero))
    small_rows[TAP_ROWS : TAP_ROWS + 1, :] = gain
    small_rows[TAP_ROWS + 1 : TAP_ROWS + 2, :] = bias
    small_rows[TAP_ROWS + 2 : TAP_ROWS + 4, :] = norm_two_ref[...]
    small_ref[...] = small_rows[...].T.astype(jnp.bfloat16).reshape(small_ref.shape)
    over_peers(lambda step: to_peer(small_ref, small_all, sm_s, sm_r, step).start())
    add_y(OUT)
    start_z(OUT)
    add_z(QKV)
    last_copy(QKV).start()

    over_peers(lambda step: from_peer(ssm_all, ss_s, ss_r, step).wait_recv())
    ssm_all[place.d] = ssm_ref_all[place.d]
    total = ssm_all[0]
    for index in range(1, 16):
        total = total + ssm_all[index]
    ssm_sum[place.d] = total
    over_peers(lambda step: share(step).start())
    over_peers(lambda step: from_peer(small_all, sm_s, sm_r, step).wait_recv())

    def add_small(step, total):
        return total + small_all[(place.d + step) % 16].astype(jnp.float32)

    small_sum[...] = lax.fori_loop(1, 16, add_small, small_ref[place.d].astype(jnp.float32)).astype(jnp.bfloat16)
    small_copy.start()
    add_z(OUT)
    last_copy(OUT).start()
    for k in range(count):
        finish(k)
    over_peers(lambda step: from_peer(ssm_sum, sg_s, sg_r, step).wait_recv())
    ssm_out[...] = ssm_sum[...]
    small_copy.wait_recv()
    small_out[...] = small_sum[...].astype(jnp.float32) + small_last[...].astype(jnp.float32)

    for k in range(count):
        for h in range(piece_halves(k)):
            core_copy(k, h).wait_send()
        if piece_halves(k) == TWO:
            x_copy(k).wait_send()
        y_copy(k).wait_send()
        for step in range(1, 4):
            z_copy(k, step).wait_send()
        last_copy(k).wait_send()
    for copy in (gn_copy, small_copy):
        copy.wait_send()
    over_peers(lambda step: to_peer(small_ref, small_all, sm_s, sm_r, step).wait_send())
    over_peers(lambda step: to_peer(ssm_ref_all, ssm_all, ss_s, ss_r, step).wait_send())
    over_peers(lambda step: share(step).wait_send())


def backward_mixer(
    gated_grad, query, value, conv, shifted, kernel_w, taps_w, keys_w, mixed_w, ssm, to_table, from_table, normed, qkv, tokens,
    residual, small, norm_two, down, up, out,
):
    f32, low = jnp.float32, jnp.bfloat16
    count = len(PIECES)
    length, width = conv.shape
    own_rows, model = tokens.shape
    owned = down.shape[3]
    waves = (RADIX, 2 * HALF, width)
    vmem, anywhere = pl.BlockSpec(memory_space=pltpu.VMEM), pl.BlockSpec(memory_space=pl.ANY)
    results, near, from_x, from_y, from_z, final, last = [], [], [], [], [], [], []
    for k, (_, _, columns, way) in enumerate(PIECES):
        halves = piece_halves(k)
        part = columns // halves
        whole = way == "whole"
        results.append(jax.ShapeDtypeStruct((owned, part) if whole else (TWO, owned, part), f32 if whole else low))
        near.append(pltpu.VMEM((halves, FOUR, TWO, owned, part), low))
        if halves == TWO:
            from_x.append(pltpu.VMEM((FOUR, TWO, owned, part), low))
        from_y.append(pltpu.VMEM((FOUR, owned, part), low))
        from_z.append(pltpu.VMEM((3, owned, part), low))
        final.append(pltpu.VMEM((owned, part), low))
        last.append(pltpu.VMEM((owned, part), low))
    dma = pltpu.SemaphoreType.DMA
    slots = (16, 8, width)
    packed = (16, owned, LANES)
    results += [
        jax.ShapeDtypeStruct(packed[1:], f32),
        jax.ShapeDtypeStruct(slots, f32),
        jax.ShapeDtypeStruct((own_rows, model), f32),
    ]
    return pl.pallas_call(
        backward_body,
        out_shape=tuple(results),
        in_specs=[vmem, anywhere, anywhere, vmem, vmem] + [anywhere] * 4 + [vmem] * 9 + [anywhere] * 3,
        out_specs=(vmem,) * len(results),
        scratch_shapes=near
        + from_x
        + from_y
        + from_z
        + final
        + last
        + [
            pltpu.VMEM((2, FOUR, TWO, owned, 1536), low),
            pltpu.VMEM((length, width), f32),
            pltpu.VMEM((length, width), f32),
            pltpu.VMEM((2,) + waves, f32),
            pltpu.VMEM((length, width), f32),
            pltpu.VMEM((length, width), f32),
            pltpu.VMEM(waves, f32),
            pltpu.VMEM(waves, low),
            pltpu.VMEM(waves, f32),
            pltpu.VMEM((length, 3 * width), low),
            pltpu.VMEM((FOUR, TWO, TWO, owned, 3 * width), low),
            pltpu.VMEM((own_rows, model), low),
            pltpu.VMEM((own_rows, model), f32),
            pltpu.VMEM((own_rows, model), low),
            pltpu.VMEM((LANES, model), f32),
            pltpu.VMEM(packed, low),
            pltpu.VMEM(packed, low),
            pltpu.VMEM(packed[1:], low),
            pltpu.VMEM(packed[1:], low),
            pltpu.VMEM(slots, f32),
            pltpu.VMEM(slots, f32),
            pltpu.VMEM(slots, f32),
            dma((4,)),
            dma((2, TWO)),
            dma((count, TWO)),
            dma((count, TWO)),
        ]
        + [dma((count,))] * 4
        + [dma((count, 3))] * 2
        + [dma((count,))] * 2
        + [dma((16,))] * 6
        + [dma((3,))] * 2,
        compiler_params=pltpu.CompilerParams(collective_id=1, has_side_effects=True, vmem_limit_bytes=VMEM_LIMIT),
        name="backward_mixer",
    )(
        gated_grad, query, value, conv, shifted, kernel_w, taps_w, keys_w, mixed_w, ssm, to_table, from_table, normed, qkv, tokens,
        residual, small, norm_two, down, up, out,
    )


def adam_parts(param, first, second, gradient, learn_rate, decay_weight):
    first_new = BETA_ONE * first + (1.0 - BETA_ONE) * gradient
    second_new = BETA_TWO * second + (1.0 - BETA_TWO) * gradient * gradient
    first_hat = first_new / (1.0 - BETA_ONE**STEP_COUNT)
    second_hat = second_new / (1.0 - BETA_TWO**STEP_COUNT)
    step = learn_rate * (first_hat / (jnp.sqrt(second_hat) + ADAM_EPS) + decay_weight * param)
    return step, first_new, second_new


def adam_body(
    down_first, up_last, down_last, out_sum, up_first, qkv_sum, small_sum, ssm_sum,
    attn_p, mlp_p, norm_p, tap_p, ssm_p, attn_m, mlp_m, norm_m, tap_m, ssm_m,
    attn_step, attn_new, mlp_step, mlp_new, norm_step, norm_new, tap_step, tap_new, ssm_step, ssm_new,
    *, scale,
):
    f32 = jnp.float32
    width = out_sum.shape[2]

    def attn(start, gradient):
        cols = slice(start, start + width)
        attn_step[:, cols], attn_new[0, :, cols], attn_new[1, :, cols] = adam_parts(
            attn_p[:, cols].astype(f32), attn_m[0, :, cols], attn_m[1, :, cols], gradient.astype(f32) * scale,
            LEARN_RATE, DECAY_RATE,
        )

    def mlp(plane, start, source, slot):
        count = source.shape[-1]
        for begin in range(0, count, width):
            gradient = source[:, begin : begin + width] if slot is None else source[slot, :, begin : begin + width]
            cols = slice(start + begin, start + begin + width)
            mlp_step[plane, :, cols], mlp_new[0, plane, :, cols], mlp_new[1, plane, :, cols] = adam_parts(
                mlp_p[plane, :, cols].astype(f32), mlp_m[0, plane, :, cols], mlp_m[1, plane, :, cols],
                gradient.astype(f32) * scale, LEARN_RATE, DECAY_RATE,
            )

    for half in range(2):
        for place in range(3):
            attn((2 * place + half) * width, qkv_sum[half, :, place * width : (place + 1) * width])
        attn((6 + half) * width, out_sum[half])
        mlp(0, up_first.shape[1] + half * up_last.shape[2], up_last, half)
    mlp(0, 0, up_first, None)
    mlp(1, 0, down_first, None)
    mlp(1, down_first.shape[1], down_last, None)
    tap_step[...], tap_new[0], tap_new[1] = adam_parts(
        tap_p[...].astype(f32), tap_m[0], tap_m[1], small_sum[:, :TAP_ROWS] * scale, LEARN_RATE, DECAY_RATE
    )
    small = small_sum[...].T * scale
    norm_step[...], norm_new[0], norm_new[1] = adam_parts(
        norm_p[...].astype(f32), norm_m[0], norm_m[1], small[TAP_ROWS : TAP_ROWS + 4], LEARN_RATE, 0.0
    )
    for plane in range(2):
        gradient = ssm_sum[plane * 8 : plane * 8 + 8].reshape(ssm_p.shape[1:]) * scale
        ssm_step[plane], ssm_new[0, plane], ssm_new[1, plane] = adam_parts(
            ssm_p[plane], ssm_m[0, plane], ssm_m[1, plane], gradient, SSM_LEARN_RATE, 0.0
        )


def adam_all(sums, params, moments, scale):
    vmem = pl.BlockSpec(memory_space=pltpu.VMEM)
    outs = []
    for param, moment in zip(params, moments):
        outs += [jax.ShapeDtypeStruct(param.shape, jnp.float32), jax.ShapeDtypeStruct(moment.shape, jnp.float32)]
    return pl.pallas_call(
        partial(adam_body, scale=scale),
        out_shape=tuple(outs),
        in_specs=[vmem] * (len(sums) + 2 * len(params)),
        out_specs=(vmem,) * len(outs),
        compiler_params=pltpu.CompilerParams(vmem_limit_bytes=VMEM_LIMIT),
        name="adam",
    )(*sums, *params, *moments)


def turned_last(value):
    return jnp.swapaxes(value, -1, -2)


def per_device_split(
    tokens,
    cotangent,
    attn_weight,
    mlp_weight,
    norms,
    taps,
    ssm_params,
    attn_moments,
    mlp_moments,
    norm_moments,
    tap_moments,
    ssm_moments,
):
    f32, low = jnp.float32, jnp.bfloat16
    rows, width = tokens.shape[1:]
    shares = lax.axis_size("seq")
    owners = lax.axis_size("dp")
    length = rows * shares
    part = width // shares
    tap_count = taps.shape[0]
    to_table, from_table = map(jnp.asarray, transform_tables())

    owned = attn_weight.shape[0]
    small = jnp.concatenate([taps, norms, jnp.zeros((LANES - 4 - tap_count, owned), low)]).T
    ssm_turned = jnp.swapaxes(ssm_params, 1, 2)
    (
        qkv_full, _, _, small_full, normed_low, query, value, conv, shifted, kernel_w, taps_w, keys_w, mixed_w,
        layer_out, grad_residual, grad_norm_two, grad_gated, grad_up, grad_down, grad_out,
    ) = forward_layer(
        tokens[0], cotangent[0], attn_weight, mlp_weight, small, ssm_turned,
        to_table, from_table,
    )
    scale = 1.0 / math.sqrt(owners * length)
    sums = backward_mixer(
        grad_gated, query, value, conv, shifted, kernel_w, taps_w, keys_w, mixed_w, ssm_turned, to_table, from_table,
        normed_low, qkv_full.reshape(width, 3 * part), tokens[0], grad_residual, small_full, grad_norm_two,
        grad_down, grad_up, grad_out,
    )
    (
        attn_step, attn_new, mlp_step, mlp_new, norms_step, norm_new, taps_step, tap_new, ssm_step, ssm_new
    ) = adam_all(
        sums[:8],
        (attn_weight, mlp_weight, norms, taps.T, ssm_turned),
        (attn_moments, mlp_moments, norm_moments, turned_last(tap_moments), turned_last(ssm_moments)),
        scale,
    )
    taps_step, tap_new, ssm_step, ssm_new = map(turned_last, (taps_step, tap_new, ssm_step, ssm_new))
    input_grad = sums[8]
    return (
        layer_out[None],
        input_grad[None],
        attn_step,
        attn_new,
        mlp_step,
        mlp_new,
        norms_step,
        norm_new,
        taps_step,
        tap_new,
        ssm_step,
        ssm_new,
    )


def solution(mesh):
    fits = (mesh.shape["seq"], mesh.shape["dp"]) == (2, 16)

    def chosen(tokens, cotangent, attn_weight, mlp_weight, norms, taps, *others):
        fast = fits and tokens.shape[1:] == (RADIX * HALF // 2, 6 * LANES) and taps.shape[0] == TAP_ROWS
        plan = per_device_split if fast else per_device
        return plan(tokens, cotangent, attn_weight, mlp_weight, norms, taps, *others)

    return jax.shard_map(
        chosen,
        mesh=mesh,
        in_specs=(
            P("dp", "seq", None),
            P("dp", "seq", None),
            P("dp", None),
            P(None, "dp", None),
            P(None, "dp"),
            P(None, "dp"),
            P(None, "seq", None),
            P(None, "dp", None),
            P(None, None, "dp", None),
            P(None, None, "dp"),
            P(None, None, "dp"),
            P(None, None, "seq", None),
        ),
        out_specs=(
            P("dp", "seq", None),
            P("dp", "seq", None),
            P("dp", None),
            P(None, "dp", None),
            P(None, "dp", None),
            P(None, None, "dp", None),
            P(None, "dp"),
            P(None, None, "dp"),
            P(None, "dp"),
            P(None, None, "dp"),
            P(None, "seq", None),
            P(None, None, "seq", None),
        ),
        check_vma=False,
    )
```

```python
from functools import partial
import math

import jax
import jax.numpy as jnp
import ml_dtypes
import numpy as np
from jax import lax
from jax.experimental import pallas as pl
from jax.experimental.pallas import tpu as pltpu
from jax.sharding import PartitionSpec as P

DFT_ROWS = 256


EPS_NORM = 1e-05
BETA_ONE = 0.9
BETA_TWO = 0.999
ADAM_EPS = 1e-08
LEARN_RATE = 0.001
SSM_LEARN_RATE = 0.00025
DECAY_RATE = 0.1
STEP_COUNT = 10.0
HIGHEST = lax.Precision.HIGHEST


def from_behind(block, axis, distance):
    devices = range(lax.axis_size(axis))
    route = [(i - distance, i) for i in devices if i - distance in devices]
    return lax.ppermute(block, axis, route)


def as_sent(value):

    def short(part):
        return part.astype(jnp.bfloat16) if part.dtype == jnp.float32 else part

    return jax.tree.map(short, value)


def layer_norm(values, gain_row, bias_row):
    average = jnp.mean(values, axis=-1, keepdims=True)
    centred = values - average
    variance = jnp.mean(centred * centred, axis=-1, keepdims=True)
    return centred * lax.rsqrt(variance + EPS_NORM) * gain_row + bias_row


def shift_mix(rim_rows, keys_part, taps_full):
    tap_count = taps_full.shape[0]
    row_count = keys_part.shape[0]
    extended = jnp.concatenate([rim_rows, keys_part], axis=0)
    summed = jnp.zeros_like(keys_part)
    for tap_index in range(tap_count):
        begin_row = tap_count - 1 - tap_index
        summed = summed + taps_full[tap_index] * extended[begin_row : begin_row + row_count]
    return summed


def kernel_rows(length_total, ssm_full):
    inner_count = math.gcd(length_total, 128)
    outer_count = length_total // inner_count
    decay_rates = jnp.exp(ssm_full[0])
    outer_offsets = (jnp.arange(outer_count) * inner_count).astype(jnp.float32)
    inner_offsets = jnp.arange(inner_count).astype(jnp.float32)
    outer_part = ssm_full[1][:, :, None] * jnp.exp(
        -decay_rates[:, :, None] * outer_offsets[None, None, :]
    )
    inner_part = jnp.exp(-decay_rates[:, :, None] * inner_offsets[None, None, :])
    kernel = jnp.einsum("cna,cnb->cab", outer_part, inner_part, precision=HIGHEST)
    return kernel.reshape(kernel.shape[0], length_total)


def dft_tables(length_total, first_count):
    full_length = 2 * length_total
    col_count = full_length // first_count
    half_rows = first_count // 2
    row_index = jnp.arange(half_rows, dtype=jnp.int32)
    freq_index = jnp.arange(first_count, dtype=jnp.int32)
    col_index = jnp.arange(col_count, dtype=jnp.int32)
    angle_first = (
        2.0
        * math.pi
        / first_count
        * (row_index[:, None] * freq_index[None, :] % first_count).astype(jnp.float32)
    )
    angle_twist = (
        2.0 * math.pi / full_length * (freq_index[:, None] * col_index[None, :]).astype(jnp.float32)
    )
    angle_last = (
        2.0
        * math.pi
        / col_count
        * (col_index[:, None] * col_index[None, :] % col_count).astype(jnp.float32)
    )
    return (
        jnp.cos(angle_first),
        jnp.sin(angle_first),
        jnp.cos(angle_twist),
        jnp.sin(angle_twist),
        jnp.cos(angle_last),
        jnp.sin(angle_last),
    )


def forward_dft(signal, tables):
    cos_first, sin_first, cos_twist, sin_twist, cos_last, sin_last = tables
    half_rows = cos_first.shape[0]
    col_count = cos_last.shape[0]
    folded = signal.reshape(signal.shape[0], half_rows, col_count)
    real_first = jnp.einsum("cmp,mk->ckp", folded, cos_first, precision=HIGHEST)
    imaginary_first = -jnp.einsum("cmp,mk->ckp", folded, sin_first, precision=HIGHEST)
    real_twist = real_first * cos_twist + imaginary_first * sin_twist
    imaginary_twist = imaginary_first * cos_twist - real_first * sin_twist
    real_last = jnp.einsum("ckp,pq->ckq", real_twist, cos_last, precision=HIGHEST) + jnp.einsum(
        "ckp,pq->ckq", imaginary_twist, sin_last, precision=HIGHEST
    )
    imaginary_last = jnp.einsum(
        "ckp,pq->ckq", imaginary_twist, cos_last, precision=HIGHEST
    ) - jnp.einsum("ckp,pq->ckq", real_twist, sin_last, precision=HIGHEST)
    return (real_last, imaginary_last)


def inverse_dft(spectrum, tables):
    cos_first, sin_first, cos_twist, sin_twist, cos_last, sin_last = tables
    real_part, imaginary_part = spectrum
    full_length = cos_first.shape[1] * cos_last.shape[0]
    real_inner = jnp.einsum("ckq,qp->ckp", real_part, cos_last, precision=HIGHEST) - jnp.einsum(
        "ckq,qp->ckp", imaginary_part, sin_last, precision=HIGHEST
    )
    imaginary_inner = jnp.einsum(
        "ckq,qp->ckp", imaginary_part, cos_last, precision=HIGHEST
    ) + jnp.einsum("ckq,qp->ckp", real_part, sin_last, precision=HIGHEST)
    real_twist = real_inner * cos_twist - imaginary_inner * sin_twist
    imaginary_twist = imaginary_inner * cos_twist + real_inner * sin_twist
    signal = jnp.einsum("ckp,mk->cmp", real_twist, cos_first, precision=HIGHEST) - jnp.einsum(
        "ckp,mk->cmp", imaginary_twist, sin_first, precision=HIGHEST
    )
    return signal.reshape(signal.shape[0], signal.shape[1] * signal.shape[2]) / full_length


def complex_product(left, right, conjugate_left):
    left_real, left_imaginary = left
    right_real, right_imaginary = right
    if conjugate_left:
        return (
            left_real * right_real + left_imaginary * right_imaginary,
            left_real * right_imaginary - left_imaginary * right_real,
        )
    return (
        left_real * right_real - left_imaginary * right_imaginary,
        left_real * right_imaginary + left_imaginary * right_real,
    )


def adam_update(param_now, moments, gradient, learn_rate, decay_weight):
    first_new = BETA_ONE * moments[0] + (1.0 - BETA_ONE) * gradient
    second_new = BETA_TWO * moments[1] + (1.0 - BETA_TWO) * gradient * gradient
    first_hat = first_new / (1.0 - BETA_ONE**STEP_COUNT)
    second_hat = second_new / (1.0 - BETA_TWO**STEP_COUNT)
    step_size = learn_rate * (
        first_hat / (jnp.sqrt(second_hat) + ADAM_EPS) + decay_weight * param_now
    )
    return (step_size, jnp.stack([first_new, second_new]))


def per_device(
    tokens,
    cotangent,
    attn_weight,
    mlp_weight,
    norms,
    taps,
    ssm_params,
    attn_moments,
    mlp_moments,
    norm_moments,
    tap_moments,
    ssm_moments,
):
    row_count = tokens.shape[1]
    model_width = tokens.shape[2]
    group_count = lax.axis_size("seq")
    owner_count = lax.axis_size("dp")
    length_total = row_count * group_count
    attn_full, mlp_full, norm_full, taps_full = (
        lax.all_gather(attn_weight, "dp", axis=0, tiled=True),
        lax.all_gather(mlp_weight, "dp", axis=1, tiled=True),
        lax.all_gather(norms, "dp", axis=1, tiled=True),
        lax.all_gather(taps, "dp", axis=1, tiled=True),
    )
    inputs = tokens[0].astype(jnp.float32)
    cot_rows = cotangent[0].astype(jnp.float32)
    norm_values = norm_full.astype(jnp.float32)
    taps_values = taps_full.astype(jnp.float32)
    tap_count = taps_values.shape[0]
    normed, norm_pull = jax.vjp(layer_norm, inputs, norm_values[0], norm_values[1])
    normed_low = normed.astype(jnp.bfloat16)
    project = jnp.dot(
        normed_low, attn_full[:, : 3 * model_width], preferred_element_type=jnp.float32
    )
    queries = project[:, :model_width]
    keys_part = project[:, model_width : 2 * model_width]
    values = project[:, 2 * model_width :]
    rim_rows = from_behind(
        keys_part[row_count - tap_count + 1 :].astype(jnp.bfloat16), "seq", 1
    ).astype(jnp.float32)
    shifted, shift_pull = jax.vjp(shift_mix, rim_rows, keys_part, taps_values)
    mixed_rows = (shifted * values).astype(jnp.bfloat16)
    moved_in = lax.all_to_all(mixed_rows.T, "seq", split_axis=0, concat_axis=1, tiled=True).astype(
        jnp.float32
    )
    tables = dft_tables(length_total, DFT_ROWS)
    kernel, kernel_pull = jax.vjp(partial(kernel_rows, length_total), ssm_params)
    kernel_freq = forward_dft(kernel, tables)
    input_freq = forward_dft(moved_in, tables)
    conv_channels = inverse_dft(complex_product(input_freq, kernel_freq, False), tables)
    conv_back = lax.all_to_all(
        conv_channels.astype(jnp.bfloat16), "seq", split_axis=1, concat_axis=0, tiled=True
    )
    conv_rows = conv_back.T.astype(jnp.float32)
    gated_rows = (queries * conv_rows).astype(jnp.bfloat16)
    branch = jnp.dot(
        gated_rows, attn_full[:, 3 * model_width :], preferred_element_type=jnp.float32
    )
    residual_one = inputs + branch
    normed_two, norm_two_pull = jax.vjp(layer_norm, residual_one, norm_values[2], norm_values[3])
    normed_two_low = normed_two.astype(jnp.bfloat16)
    before = jnp.dot(normed_two_low, mlp_full[0], preferred_element_type=jnp.float32)
    active, gelu_pull = jax.vjp(jax.nn.gelu, before)
    active_low = active.astype(jnp.bfloat16)
    mlp_out = jnp.einsum("tf,df->td", active_low, mlp_full[1], preferred_element_type=jnp.float32)
    layer_out = (residual_one + mlp_out).astype(jnp.bfloat16)
    attn_back, mlp_back = (
        lax.all_gather(attn_weight, "dp", axis=0, tiled=True),
        lax.all_gather(mlp_weight, "dp", axis=1, tiled=True),
    )
    grad_after = cotangent[0]
    grad_active = jnp.dot(grad_after, mlp_back[1], preferred_element_type=jnp.float32)
    grad_down = jnp.einsum("td,tf->df", grad_after, active_low, preferred_element_type=jnp.float32)
    grad_before = gelu_pull(grad_active)[0].astype(jnp.bfloat16)
    grad_up = jnp.einsum(
        "td,tf->df", normed_two_low, grad_before, preferred_element_type=jnp.float32
    )
    grad_normed_two = jnp.einsum(
        "tf,df->td", grad_before, mlp_back[0], preferred_element_type=jnp.float32
    )
    grad_residual_part, grad_gain_two, grad_bias_two = norm_two_pull(grad_normed_two)
    grad_residual = cot_rows + grad_residual_part
    grad_branch = grad_residual.astype(jnp.bfloat16)
    grad_out = jnp.einsum("td,te->de", gated_rows, grad_branch, preferred_element_type=jnp.float32)
    grad_gated = jnp.einsum(
        "te,de->td",
        grad_branch,
        attn_back[:, 3 * model_width :],
        preferred_element_type=jnp.float32,
    )
    grad_queries = grad_gated * conv_rows
    grad_conv = (grad_gated * queries).astype(jnp.bfloat16)
    grad_moved = lax.all_to_all(grad_conv.T, "seq", split_axis=0, concat_axis=1, tiled=True).astype(
        jnp.float32
    )
    grad_freq = forward_dft(grad_moved, tables)
    grad_input = inverse_dft(complex_product(kernel_freq, grad_freq, True), tables)
    grad_kernel = inverse_dft(complex_product(input_freq, grad_freq, True), tables)
    grad_ssm_local = kernel_pull(grad_kernel)[0]
    grad_ssm = lax.psum(grad_ssm_local, "dp")
    grad_mixed_back = lax.all_to_all(
        grad_input.astype(jnp.bfloat16), "seq", split_axis=1, concat_axis=0, tiled=True
    )
    grad_mixed = grad_mixed_back.T.astype(jnp.float32)
    grad_shifted = grad_mixed * values
    grad_values = grad_mixed * shifted
    grad_rim, grad_keys, grad_taps = shift_pull(grad_shifted)
    returned = from_behind(as_sent(grad_rim), "seq", -1).astype(grad_rim.dtype)
    grad_keys = grad_keys + jnp.pad(returned, ((row_count - tap_count + 1, 0), (0, 0)))
    grad_project = jnp.concatenate([grad_queries, grad_keys, grad_values], axis=1).astype(
        jnp.bfloat16
    )
    grad_qkv = jnp.einsum("td,te->de", normed_low, grad_project, preferred_element_type=jnp.float32)
    grad_normed = jnp.einsum(
        "te,de->td",
        grad_project,
        attn_back[:, : 3 * model_width],
        preferred_element_type=jnp.float32,
    )
    grad_input_part, grad_gain_one, grad_bias_one = norm_pull(grad_normed)
    input_grad = grad_residual + grad_input_part
    grad_attn = jnp.concatenate([grad_qkv, grad_out], axis=1)
    grad_mlp = jnp.stack([grad_up, grad_down])
    grad_norms = jnp.stack([grad_gain_one, grad_bias_one, grad_gain_two, grad_bias_two])
    owned_part = (
        lax.psum_scatter(
            grad_attn.astype(jnp.bfloat16), "dp", scatter_dimension=0, tiled=True
        ).astype(jnp.float32),
        lax.psum_scatter(
            grad_mlp.astype(jnp.bfloat16), "dp", scatter_dimension=1, tiled=True
        ).astype(jnp.float32),
        lax.psum_scatter(
            grad_norms.astype(jnp.bfloat16), "dp", scatter_dimension=1, tiled=True
        ).astype(jnp.float32),
        lax.psum_scatter(
            grad_taps.astype(jnp.bfloat16), "dp", scatter_dimension=1, tiled=True
        ).astype(jnp.float32),
    )
    summed = (
        lax.psum(owned_part[0].astype(jnp.bfloat16), "seq").astype(jnp.float32),
        lax.psum(owned_part[1].astype(jnp.bfloat16), "seq").astype(jnp.float32),
        lax.psum(owned_part[2].astype(jnp.bfloat16), "seq").astype(jnp.float32),
        lax.psum(owned_part[3].astype(jnp.bfloat16), "seq").astype(jnp.float32),
    )
    grad_scale = 1.0 / math.sqrt(owner_count * length_total)
    attn_step, attn_moments_new = adam_update(
        attn_weight.astype(jnp.float32),
        attn_moments,
        summed[0] * grad_scale,
        LEARN_RATE,
        DECAY_RATE,
    )
    mlp_step, mlp_moments_new = adam_update(
        mlp_weight.astype(jnp.float32), mlp_moments, summed[1] * grad_scale, LEARN_RATE, DECAY_RATE
    )
    norms_step, norm_moments_new = adam_update(
        norms.astype(jnp.float32), norm_moments, summed[2] * grad_scale, LEARN_RATE, 0.0
    )
    taps_step, tap_moments_new = adam_update(
        taps.astype(jnp.float32), tap_moments, summed[3] * grad_scale, LEARN_RATE, DECAY_RATE
    )
    ssm_step, ssm_moments_new = adam_update(
        ssm_params, ssm_moments, grad_ssm * grad_scale, SSM_LEARN_RATE, 0.0
    )
    return (
        layer_out[None],
        input_grad[None],
        attn_step,
        attn_moments_new,
        mlp_step,
        mlp_moments_new,
        norms_step,
        norm_moments_new,
        taps_step,
        tap_moments_new,
        ssm_step,
        ssm_moments_new,
    )


LANES = 128
RADIX = 8
HALF = 128


def transform_tables():
    rows = np.arange(HALF)
    length = RADIX * HALF
    waves = RADIX * rows[None, :, None] + np.arange(RADIX)[:, None, None] + 0.25
    angles = 2.0 * np.pi * np.mod(rows[None, None, :] * waves, length) / length
    cosines, sines = np.cos(angles), np.sin(angles)
    full = np.concatenate(
        [np.concatenate([cosines, sines], axis=2), np.concatenate([-sines, cosines], axis=2)], axis=1
    )


    def parts(matrix):
        matrix = matrix.astype(np.float32)
        high = matrix.astype(ml_dtypes.bfloat16)
        rest = (matrix - high.astype(np.float32)).astype(ml_dtypes.bfloat16)
        return np.stack([high, rest])

    return parts(full), parts(np.swapaxes(full, 1, 2))


def turned(value, angle):
    real, imaginary = value
    cosine, sine = math.cos(angle), math.sin(angle)
    if abs(sine) < 1e-12:
        return (real, imaginary) if cosine > 0 else (-real, -imaginary)
    if abs(cosine) < 1e-12:
        return (-imaginary, real) if sine > 0 else (imaginary, -real)
    return (real * cosine - imaginary * sine, real * sine + imaginary * cosine)


def small_transform(values, sign):
    count = len(values)
    if count == 1:
        return values
    even = small_transform(values[::2], sign)
    odd = small_transform(values[1::2], sign)
    low, high = [], []
    for index in range(count // 2):
        (er, ei), (tr, ti) = even[index], turned(odd[index], sign * 2.0 * math.pi * index / count)
        low.append((er + tr, ei + ti))
        high.append((er - tr, ei - ti))
    return low + high


def dot(left, right):
    return jnp.dot(left, right, preferred_element_type=jnp.float32)


def keep_parts(high_ref, low_ref, wave, row, cols, value):
    high = value.astype(jnp.bfloat16)
    high_ref[wave, pl.ds(row, 16), cols] = high
    if low_ref is not None:
        low_ref[wave, pl.ds(row, 16), cols] = (value - high.astype(jnp.float32)).astype(jnp.bfloat16)


def table_dot(table_high, table_low, high_ref, low_ref, wave):
    high = high_ref[wave]
    total = dot(table_high, high) + dot(table_low, high)
    return total if low_ref is None else total + dot(table_high, low_ref[wave])


def each_tile(width, rows, step, body):
    for block in range(width // LANES):

        def one(index, carry, block=block):
            body(pl.multiple_of(index * step, step), pl.ds(block * LANES, LANES))
            return carry

        lax.fori_loop(0, rows // step, one, 0)


def to_waves(width, read, used, w_ref, high_ref, low_ref, store):
    def first(row, cols):
        inputs = []
        for part in range(used):
            x = read(part * HALF, row, cols)
            angle = -2.0 * math.pi * part / 32.0
            inputs.append((x * math.cos(angle), x * math.sin(angle)) if part else (x, jnp.zeros_like(x)))
        while len(inputs) < RADIX:
            inputs.append((jnp.zeros_like(x), jnp.zeros_like(x)))
        for wave, value in enumerate(small_transform(inputs, -1.0)):
            for place, part in enumerate(value):
                keep_parts(high_ref, low_ref, wave, row + place * HALF, cols, part)

    each_tile(width, HALF, 16, first)

    def second(wave, carry):
        store(wave, table_dot(w_ref[0, wave], w_ref[1, wave], high_ref, low_ref, wave))
        return carry

    lax.fori_loop(0, RADIX, second, 0)


def product(width, left_ref, right_ref, conjugate, high_ref, low_ref):
    sign = -1.0 if conjugate else 1.0

    def one(wave, carry):
        def tile(row, cols):
            lr, li = left_ref[wave, pl.ds(row, 16), cols], left_ref[wave, pl.ds(row + HALF, 16), cols] * sign
            rr, ri = right_ref[wave, pl.ds(row, 16), cols], right_ref[wave, pl.ds(row + HALF, 16), cols]
            for place, part in enumerate((lr * rr - li * ri, lr * ri + li * rr)):
                keep_parts(high_ref, low_ref, wave, row + place * HALF, cols, part)

        each_tile(width, HALF, 16, tile)
        return carry

    lax.fori_loop(0, RADIX, one, 0)


def from_waves(width, w_ref, high_ref, low_ref, back_ref, put):
    def second(wave, carry):
        back_ref[wave] = table_dot(w_ref[0, wave], w_ref[1, wave], high_ref, low_ref, wave)
        return carry

    lax.fori_loop(0, RADIX, second, 0)
    scale = 1.0 / (RADIX * HALF)

    def first(row, cols):
        values = [
            (back_ref[wave, pl.ds(row, 16), cols], back_ref[wave, pl.ds(row + HALF, 16), cols])
            for wave in range(RADIX)
        ]
        for part, (real, imaginary) in enumerate(small_transform(values, 1.0)):
            angle = 2.0 * math.pi * part / 32.0
            put(part * HALF, row, cols, real * (math.cos(angle) * scale) - imaginary * (math.sin(angle) * scale))

    each_tile(width, HALF, 16, first)


def first_positions(width, count, w_ref, high_ref, low_ref):
    total = jnp.zeros((count, width), jnp.float32)
    for wave in range(RADIX):
        total = total + table_dot(w_ref[0, wave, :count, :], w_ref[1, wave, :count, :], high_ref, low_ref, wave)
    return total * (1.0 / (RADIX * HALF))


FINE = 32


def decay_sums(block, length, ssm_ref, out_ref):
    modes = ssm_ref.shape[1]
    steps = length // FINE
    cols = pl.ds(block * LANES, LANES)
    out_ref[:, cols] = jnp.zeros((length, LANES), jnp.float32)
    offsets = lax.broadcasted_iota(jnp.int32, (FINE, LANES), 0).astype(jnp.float32)

    def group(index, carry):
        base = pl.multiple_of(index * 8, 8)
        rates = jnp.exp(ssm_ref[0, pl.ds(base, 8), cols])
        leaps = jnp.exp(-rates * FINE)
        weights = ssm_ref[1, pl.ds(base, 8), cols]
        terms = tuple(weights[i : i + 1] * jnp.exp(-rates[i : i + 1] * offsets) for i in range(8))
        leap_rows = [jnp.broadcast_to(leaps[i : i + 1], (FINE, LANES)) for i in range(8)]

        def step(number, terms):
            rows = pl.ds(pl.multiple_of(number * FINE, FINE), FINE)
            total = out_ref[rows, cols]
            for term in terms:
                total = total + term
            out_ref[rows, cols] = total
            return tuple(term * leap for term, leap in zip(terms, leap_rows))

        lax.fori_loop(0, steps, step, terms, unroll=4)
        return carry

    lax.fori_loop(0, modes // 8, group, 0)


def decay_gradients(block, length, ssm_ref, grad_ref, out_ref):
    modes = ssm_ref.shape[1]
    steps = length // FINE
    cols = pl.ds(block * LANES, LANES)
    offsets = lax.broadcasted_iota(jnp.int32, (FINE, LANES), 0).astype(jnp.float32)

    def group(index, carry):
        base = pl.multiple_of(index * 8, 8)
        rates = jnp.exp(ssm_ref[0, pl.ds(base, 8), cols])
        leaps = jnp.exp(-rates * FINE)
        plain_rows, slope_rows = [], []
        for modes_now in ((0, 1, 2, 3), (4, 5, 6, 7)):
            zero = offsets * 0.0
            leap_rows = [jnp.broadcast_to(leaps[i : i + 1], (FINE, LANES)) for i in modes_now]

            def step(number, sums, leap_rows=leap_rows):
                rows = grad_ref[pl.ds(pl.multiple_of((steps - 1 - number) * FINE, FINE), FINE), cols]
                return tuple((v * leap + rows, w * leap + v) for (v, w), leap in zip(sums, leap_rows))

            sums = lax.fori_loop(0, steps, step, tuple((zero, zero) for _ in modes_now), unroll=8)
            for i, (v, w) in zip(modes_now, sums):
                fine = jnp.exp(-rates[i : i + 1] * offsets)
                plain = fine * v
                slope = fine * w * (leaps[i : i + 1] * FINE) + plain * offsets
                plain_rows.append(jnp.sum(plain, axis=0, keepdims=True))
                slope_rows.append(jnp.sum(slope, axis=0, keepdims=True))
        out_ref[modes // 8 + index, :, cols] = jnp.concatenate(plain_rows, axis=0)
        out_ref[index, :, cols] = (
            -ssm_ref[1, pl.ds(base, 8), cols] * rates * jnp.concatenate(slope_rows, axis=0)
        )
        return carry

    lax.fori_loop(0, modes // 8, group, 0)


def layer_norm_parts(values):
    average = jnp.mean(values, axis=-1, keepdims=True)
    centred = values - average
    variance = jnp.mean(centred * centred, axis=-1, keepdims=True)
    inverse = lax.rsqrt(variance + EPS_NORM)
    return centred * inverse, inverse


def layer_norm_back(upstream, normal, inverse, gain_row):
    weighted = upstream * gain_row
    average = jnp.mean(weighted, axis=-1, keepdims=True)
    overlap = jnp.mean(weighted * normal, axis=-1, keepdims=True)
    into = (weighted - average - normal * overlap) * inverse
    return into, jnp.sum(upstream * normal, axis=0, keepdims=True), jnp.sum(upstream, axis=0, keepdims=True)


MESH = pl.DeviceIdType.MESH
TWO, FOUR = 2, 4
TAP_ROWS = 64
VMEM_LIMIT = 62 * 1024 * 1024


class Place:
    def __init__(self):
        self.s, self.d = lax.axis_index("seq"), lax.axis_index("dp")
        self.z, self.y, self.c = self.d // 4, (self.d // 2) % 2, self.d % 2

    def over_x(self):
        return (1 - self.s, self.d)

    def over_y(self):
        return (self.s, self.d + 2 - 4 * self.y)

    def over_core(self):
        return (self.s, self.d + 1 - 2 * self.c)

    def along_z(self, step):
        return (self.s, (self.d + 4 * step) % 16)

    def owner(self, index):
        return (self.s, index)


def send(source, target, send_sem, recv_sem, device):
    return pltpu.make_async_remote_copy(
        src_ref=source, dst_ref=target, send_sem=send_sem, recv_sem=recv_sem, device_id=device, device_id_type=MESH
    )


def greet_all(place):
    barrier = pltpu.get_barrier_semaphore()
    pl.semaphore_signal(barrier, inc=1, device_id=place.over_x(), device_id_type=MESH)

    def greet(step, carry):
        pl.semaphore_signal(
            barrier, inc=1, device_id=place.owner((place.d + step) % 16), device_id_type=MESH
        )
        return carry

    lax.fori_loop(1, 16, greet, 0)
    pl.semaphore_wait(barrier, 16)


def add_blocks(put, sources, count):
    def one(index, carry):
        total = sources[0](index).astype(jnp.float32)
        for source in sources[1:]:
            total = total + source(index).astype(jnp.float32)
        put(index, total)
        return carry

    lax.fori_loop(0, count, one, 0)


WEIGHTS = (
    ("out", 0, 768, "whole"),
    ("up", 0, 1536, "halved"),
    ("down", 0, 1536, "whole"),
    ("up", 1536, 1536, "halved"),
    ("down", 1536, 768, "whole"),
    ("down", 2304, 768, "whole"),
)
OUT_W, UP_FIRST, DOWN_FIRST, UP_LAST, DOWN_THIRD, DOWN_LAST, QKV_W = range(len(WEIGHTS) + 1)
HIDDEN_BLOCK = 768
EARLY = 1


def dot_right(left, right):
    return lax.dot_general(left, right, (((1,), (1,)), ((), ())), preferred_element_type=jnp.float32)


def dot_left(left, right):
    return lax.dot_general(left, right, (((0,), (0,)), ((), ())), preferred_element_type=jnp.float32)


def gelu_parts(x):
    slope = math.sqrt(2.0 / math.pi)
    square = x * x
    bent = jnp.tanh(slope * x * (1.0 + 0.044715 * square))
    upper = 0.5 + 0.5 * bent
    return x * upper, upper + 0.5 * x * (1.0 - bent * bent) * (slope * (1.0 + 3.0 * 0.044715 * square))


def forward_body(
    token_ref, cotangent_ref, attn_shard, mlp_shard, small_ref, ssm_ref, to_ref, from_ref,
    qkv_full, up_full, down_full, small_t, normed_ref, query_out, value_out, conv_ref, shifted_ref,
    kernel_out, taps_out, keys_out, mixed_out, layer_out, residual_grad, norm_two_out, gated_grad, up_grad, down_grad, out_grad, early_out,
    qkv_ref, token_all, small_all, gated_ref, rows_ref, out_full, grad_send, near, from_y, from_z, final, last,
    own_sem, z_s, z_r, y_s, y_r, x_s, x_r, core_s, core_r, small_s, small_r, side_s, side_r, store_sem, load_sem, nc_s, nc_r, ny_s, ny_r, nz_s, nz_r, nf_s, nf_r,
):
    length, width = conv_ref.shape
    own_rows, model = token_ref.shape
    place = Place()
    f32, low = jnp.float32, jnp.bfloat16
    shards = {"up": mlp_shard.at[0], "down": mlp_shard.at[1], "out": attn_shard.at[:, pl.ds(3 * model, model)]}
    fulls = {"up": up_full, "down": down_full, "out": out_full}

    def columns(k):
        source, start, count, way = WEIGHTS[k]
        if way == "whole":
            return source, pl.ds(start, count)
        return source, pl.ds(pl.multiple_of(start + place.s * (count // 2), LANES), count // 2)

    def z_copy(k, step):
        if k == QKV_W:
            source, target = qkv_ref, qkv_full.at[place.z, place.y, place.c]
        else:
            name, cols = columns(k)
            source, target = shards[name].at[:, cols], fulls[name].at[place.z, place.y, place.c, :, cols]
        return send(source, target, z_s.at[k, step - 1], z_r.at[k, step - 1], place.along_z(step))

    def y_copy(k):
        if k == QKV_W:
            blocks = qkv_full.at[:, place.y, place.c]
        else:
            name, cols = columns(k)
            blocks = fulls[name].at[:, place.y, place.c, :, cols]
        return send(blocks, blocks, y_s.at[k], y_r.at[k], place.over_y())

    def x_copy(k):
        name, cols = columns(k)
        blocks = fulls[name].at[:, :, place.c, :, cols]
        return send(blocks, blocks, x_s.at[k], x_r.at[k], place.over_x())

    def core_copy(k):
        if k == QKV_W:
            blocks = qkv_full.at[:, :, place.c]
        else:
            name, start, count, _ = WEIGHTS[k]
            blocks = fulls[name].at[:, :, place.c, :, pl.ds(start, count)]
        return send(blocks, blocks, core_s.at[k], core_r.at[k], place.over_core())

    def own_copies():
        copies = []
        for k in range(QKV_W):
            name, cols = columns(k)
            target = fulls[name].at[place.z, place.y, place.c, :, cols]
            copies.append(pltpu.make_async_copy(shards[name].at[:, cols], target, own_sem.at[k]))
        return copies

    def start_z(k):
        for step in range(1, 4):
            z_copy(k, step).start()

    def wait_z(k):
        for step in range(1, 4):
            z_copy(k, step).wait_recv()

    def over_peers(action):
        def one(step, carry):
            action(step)
            return carry

        lax.fori_loop(1, 16, one, 0)

    def small_copy(step):
        other = (place.d + step) % 16
        return send(small_ref, small_all.at[place.d], small_s.at[other], small_r.at[place.d], place.owner(other))

    def small_arrival(step):
        other = (place.d + step) % 16
        return send(small_ref, small_all.at[other], small_s.at[other], small_r.at[other], place.owner(other))

    token_copy = send(token_ref, token_all.at[place.s], side_s.at[0], side_r.at[0], place.over_x())
    gated_copy = send(gated_ref.at[1 - place.s], rows_ref.at[place.s], side_s.at[1], side_r.at[1], place.over_x())
    grad_copy = send(grad_send, gated_grad.at[place.s], side_s.at[2], side_r.at[2], place.over_x())

    def early_y(e):
        return send(near.at[e, :, 1 - place.y], from_y.at[e], ny_s.at[e], ny_r.at[e], place.over_y())

    def early_z(e, step):
        other = (place.z + step) % 4
        return send(
            near.at[e, other, place.y], from_z.at[e, step - 1], nz_s.at[e, step - 1], nz_r.at[e, step - 1],
            place.along_z(step),
        )

    def early_last(e):
        return send(final.at[e], last.at[e], nf_s.at[e], nf_r.at[e], place.over_x())

    def early_add_y(e):
        early_y(e).wait_recv()

        def put(i, total):
            near[e, i, place.y] = total.astype(low)

        add_blocks(put, [lambda i: near[e, i, place.y], lambda i: from_y[e, i]], 4)
        for step in range(1, 4):
            early_z(e, step).start()

    def early_add_z(e):
        for step in range(1, 4):
            early_z(e, step).wait_recv()
        total = near[e, place.z, place.y].astype(f32)
        for step in range(3):
            total = total + from_z[e, step].astype(f32)
        final[e] = total.astype(low)
        early_last(e).start()

    def step_one():
        wait_z(QKV_W)
        y_copy(QKV_W).start()
        start_z(UP_FIRST)

    def step_two():
        for copy in own_copies():
            copy.wait()
        wait_z(OUT_W)
        y_copy(OUT_W).start()
        start_z(DOWN_FIRST)

    def step_three():
        y_copy(QKV_W).wait_recv()
        core_copy(QKV_W).start()

    def step_four():
        wait_z(UP_FIRST)
        y_copy(UP_FIRST).start()
        start_z(UP_LAST)

    def step_five():
        y_copy(OUT_W).wait_recv()
        core_copy(OUT_W).start()

    def step_six():
        y_copy(UP_FIRST).wait_recv()
        x_copy(UP_FIRST).start()

    def step_seven():
        wait_z(DOWN_FIRST)
        y_copy(DOWN_FIRST).start()
        start_z(DOWN_THIRD)

    def step_eight():
        wait_z(UP_LAST)
        y_copy(UP_LAST).start()
        start_z(DOWN_LAST)

    def step_nine():
        x_copy(UP_FIRST).wait_recv()
        core_copy(UP_FIRST).start()

    def step_ten():
        y_copy(DOWN_FIRST).wait_recv()
        core_copy(DOWN_FIRST).start()

    def step_eleven():
        wait_z(DOWN_THIRD)
        y_copy(DOWN_THIRD).start()
        y_copy(UP_LAST).wait_recv()
        x_copy(UP_LAST).start()

    def step_twelve():
        wait_z(DOWN_LAST)
        y_copy(DOWN_LAST).start()
        y_copy(DOWN_THIRD).wait_recv()
        core_copy(DOWN_THIRD).start()

    def step_thirteen():
        x_copy(UP_LAST).wait_recv()
        core_copy(UP_LAST).start()

    def step_fourteen():
        y_copy(DOWN_LAST).wait_recv()
        core_copy(DOWN_LAST).start()

    for j in range(3):
        cols = pl.ds(pl.multiple_of((2 * j + place.s) * width, LANES), width)
        qkv_ref[:, j * width : (j + 1) * width] = attn_shard[:, cols]
    greet_all(place)
    start_z(QKV_W)
    over_peers(lambda step: small_copy(step).start())
    token_copy.start()
    for copy in own_copies():
        copy.start()
    qkv_full[place.z, place.y, place.c] = qkv_ref[...]
    small_all[place.d] = small_ref[...]

    def mixer(line_ref, high_ref, low_ref, back_ref, proj_ref, kernel_w, other_w, keys_w):
        def keep(target):
            def store(wave, value):
                target[wave] = value

            return store

        def lines(base, row, cols):
            return line_ref[pl.ds(base + row, 16), cols]

        def column(index, cols):
            return pl.ds(index * width + cols.start, cols.size)

        stores = [
            pltpu.make_async_copy(kernel_w, kernel_out, store_sem.at[0]),
            pltpu.make_async_copy(other_w, taps_out, store_sem.at[1]),
            pltpu.make_async_copy(keys_w, keys_out, store_sem.at[2]),
            pltpu.make_async_copy(other_w, mixed_out, store_sem.at[3]),
            pltpu.make_async_copy(proj_ref.at[:, pl.ds(0, width)], query_out, store_sem.at[4]),
            pltpu.make_async_copy(proj_ref.at[:, pl.ds(2 * width, width)], value_out, store_sem.at[5]),
        ]
        for block in range(width // LANES):
            decay_sums(block, length, ssm_ref, line_ref)
            if not block:
                start_z(OUT_W)
        step_one()
        to_waves(width, lines, RADIX, to_ref, high_ref, low_ref, keep(kernel_w))
        stores[0].start()
        over_peers(lambda step: small_arrival(step).wait_recv())
        small_t[...] = small_all[...].reshape(16 * small_all.shape[1], LANES).astype(f32).T
        taps_cols = pl.multiple_of(place.s * width, LANES)

        def read_taps(base, row, cols):
            taps = small_t[pl.ds(base + row, 16), pl.ds(pl.multiple_of(taps_cols + cols.start, LANES), LANES)]
            inside = lax.broadcasted_iota(jnp.int32, taps.shape, 0) + (base + row) < TAP_ROWS
            return jnp.where(inside, taps, 0.0)

        def normalize(source, begin):
            def one(index, carry):
                row = pl.multiple_of(index * 32, 32)
                normal, _ = layer_norm_parts(source[pl.ds(row, 32), :].astype(f32))
                scaled = normal * small_t[TAP_ROWS : TAP_ROWS + 1, :] + small_t[TAP_ROWS + 1 : TAP_ROWS + 2, :]
                normed_ref[pl.ds(pl.multiple_of(begin + row, 32), 32), :] = scaled.astype(low)
                return carry

            lax.fori_loop(0, own_rows // 32, one, 0, unroll=4)

        def project(begin):
            weight = qkv_full[...].reshape(model, 3 * width)

            def one(index, carry):
                row = pl.ds(pl.multiple_of(begin + index * 256, 256), 256)
                proj_ref[row, :] = dot(normed_ref[row, :], weight)
                return carry

            lax.fori_loop(0, own_rows // 256, one, 0)

        own_begin, other_begin = place.s * own_rows, (1 - place.s) * own_rows
        normalize(token_ref, own_begin)
        step_two()
        token_copy.wait_recv()
        normalize(token_all.at[1 - place.s], other_begin)
        step_three()
        to_waves(width, read_taps, 1, to_ref, high_ref, low_ref, keep(other_w))
        stores[1].start()
        core_copy(QKV_W).wait_recv()
        project(own_begin)
        project(other_begin)
        stores[4].start()
        stores[5].start()
        step_four()
        step_five()
        to_waves(
            width, lambda base, row, cols: proj_ref[pl.ds(base + row, 16), column(1, cols)],
            RADIX, to_ref, high_ref, low_ref, keep(keys_w),
        )
        stores[2].start()
        product(width, other_w, keys_w, False, high_ref, low_ref)
        step_six()

        def put_shifted(base, row, cols, value):
            rows = pl.ds(base + row, 16)
            shifted_ref[rows, cols] = value
            mixed = value * proj_ref[rows, column(2, cols)]
            line_ref[rows, cols] = mixed.astype(low).astype(f32)

        from_waves(width, from_ref, high_ref, low_ref, back_ref, put_shifted)
        step_seven()
        stores[1].wait()
        to_waves(width, lines, RADIX, to_ref, high_ref, low_ref, keep(other_w))
        stores[3].start()
        product(width, kernel_w, other_w, False, high_ref, low_ref)
        step_eight()

        def put_conv(base, row, cols, value):
            rows = pl.ds(base + row, 16)
            rounded = value.astype(low)
            conv_ref[rows, cols] = rounded
            gated = (proj_ref[rows, cols] * rounded.astype(f32)).astype(low)
            gated_ref[base // own_rows, pl.ds(base % own_rows + row, 16), cols] = gated

        from_waves(width, from_ref, high_ref, low_ref, back_ref, put_conv)
        gated_copy.start()
        for i in (0, 2, 3, 4, 5):
            stores[i].wait()

    waves = (RADIX, 2 * HALF, width)
    pl.run_scoped(
        mixer,
        pltpu.VMEM((length, width), f32),
        pltpu.VMEM(waves, low),
        pltpu.VMEM(waves, low),
        pltpu.VMEM(waves, f32),
        pltpu.VMEM((length, 3 * width), f32),
        pltpu.VMEM(waves, f32),
        pltpu.VMEM(waves, f32),
        pltpu.VMEM(waves, f32),
    )
    rows_ref[place.s] = gated_ref[place.s]

    def feed_forward(
        up_w, down_w, up_g, down_g, residual_ref, normed_two, normed_turned, cot_turned, active_ref, before_ref,
        out_sum, normed_grad,
    ):
        block_shape = up_g.shape
        blocks = up_full.shape[4] // HIDDEN_BLOCK

        def load(j):
            cols = pl.ds(j * HIDDEN_BLOCK, HIDDEN_BLOCK)
            return [
                pltpu.make_async_copy(full.at[:, :, :, :, cols], held.at[j % 2], load_sem.at[i, j % 2])
                for i, (full, held) in enumerate(((up_full, up_w), (down_full, down_w)))
            ]

        def store(j):
            cols = pl.ds(j * HIDDEN_BLOCK, HIDDEN_BLOCK)
            return [
                pltpu.make_async_copy(held, full.at[:, :, :, :, cols], store_sem.at[i])
                for i, (full, held) in enumerate(((up_grad, up_g), (down_grad, down_g)))
            ]

        def early_core(e):
            source = up_g if e % 2 else down_g
            return send(source.at[:, :, 1 - place.c], near.at[e], nc_s.at[e], nc_r.at[e], place.over_core())

        def early_add_core(e):
            source = up_g if e % 2 else down_g
            early_core(e).wait_recv()

            def put(i, total):
                near[e, i // 2, i % 2] = total.astype(low)

            add_blocks(put, [lambda i: source[i // 2, i % 2, place.c], lambda i: near[e, i // 2, i % 2]], 8)
            early_core(e).wait_send()

        step_nine()
        cot_turned[...] = cotangent_ref[...].T
        step_ten()
        core_copy(OUT_W).wait_recv()
        gated_copy.wait_recv()
        out_w = out_full[...].reshape(model, model)

        def branch(index, carry):
            rows = pl.ds(pl.multiple_of(index * 256, 256), 256)
            value = dot(rows_ref[0, rows, :], out_w[:width]) + dot(rows_ref[1, rows, :], out_w[width:])
            residual_ref[rows, :] = token_ref[rows, :].astype(f32) + value
            return carry

        lax.fori_loop(0, own_rows // 256, branch, 0)

        def normalize(index, carry):
            rows = pl.ds(pl.multiple_of(index * 32, 32), 32)
            normal, _ = layer_norm_parts(residual_ref[rows, :])
            scaled = normal * small_t[TAP_ROWS + 2 : TAP_ROWS + 3, :] + small_t[TAP_ROWS + 3 : TAP_ROWS + 4, :]
            normed_two[rows, :] = scaled.astype(low)
            return carry

        lax.fori_loop(0, own_rows // 32, normalize, 0, unroll=4)
        core_copy(UP_FIRST).wait_recv()
        core_copy(DOWN_FIRST).wait_recv()
        for copy in load(0) + load(1):
            copy.start()
        normed_turned[...] = normed_two[...].T
        step_eleven()
        for j in range(blocks):
            if j == 1:
                step_twelve()
            if j == 2:
                step_thirteen()
                core_copy(UP_LAST).wait_recv()
                core_copy(DOWN_THIRD).wait_recv()
                for copy in load(j):
                    copy.start()
            if j == 3:
                step_fourteen()
                early_y(0).start()
                early_y(1).start()
                core_copy(DOWN_LAST).wait_recv()
                for copy in load(j):
                    copy.start()
            for copy in load(j):
                copy.wait()
            up = up_w[j % 2].reshape(model, HIDDEN_BLOCK)
            down = down_w[j % 2].reshape(model, HIDDEN_BLOCK)

            def rows_of(index, carry, up=up, down=down, j=j):
                rows = pl.ds(pl.multiple_of(index * 256, 256), 256)
                active, slope = gelu_parts(dot(normed_two[rows, :], up))
                active = active.astype(low)
                active_ref[rows, :] = active
                grad_before = (dot(cotangent_ref[rows, :], down) * slope).astype(low)
                before_ref[rows, :] = grad_before
                out_part = dot_right(active, down)
                grad_part = dot_right(grad_before, up)
                if j:
                    out_part = out_part + out_sum[rows, :]
                    grad_part = grad_part + normed_grad[rows, :]
                out_sum[rows, :] = out_part
                normed_grad[rows, :] = grad_part
                return carry

            lax.fori_loop(0, own_rows // 256, rows_of, 0)
            if j == 1:
                early_add_core(0)
                early_add_core(1)
            if j > EARLY:
                for copy in store(j - 1):
                    copy.wait()
            down_g[...] = dot(cot_turned[...], active_ref[...]).astype(low).reshape(block_shape)
            up_g[...] = dot(normed_turned[...], before_ref[...]).astype(low).reshape(block_shape)
            if j < EARLY:
                for e in (2 * j, 2 * j + 1):
                    early_core(e).start()
            else:
                for copy in store(j):
                    copy.start()

        def norm_back(index, sums):
            rows = pl.ds(pl.multiple_of(index * 32, 32), 32)
            normal, inverse = layer_norm_parts(residual_ref[rows, :])
            into, gain, bias = layer_norm_back(
                normed_grad[rows, :], normal, inverse, small_t[TAP_ROWS + 2 : TAP_ROWS + 3, :]
            )
            total = cotangent_ref[rows, :].astype(f32) + into
            residual_grad[rows, :] = total
            active_ref[rows, :] = total.astype(low)
            layer_out[rows, :] = (residual_ref[rows, :] + out_sum[rows, :]).astype(low)
            return sums[0] + gain, sums[1] + bias

        zero = small_t[TAP_ROWS : TAP_ROWS + 1, :] * 0.0
        gain, bias = lax.fori_loop(0, own_rows // 32, norm_back, (zero, zero), unroll=4)
        norm_two_out[0:1, :] = gain
        norm_two_out[1:2, :] = bias
        part_shape = (2,) + out_full.shape[1:]
        other_w = out_full[pl.ds(2 * (1 - place.s), 2)].reshape(width, model)
        grad_send[...] = dot_right(active_ref[...], other_w).astype(low)
        grad_copy.start()
        own_w = out_full[pl.ds(2 * place.s, 2)].reshape(width, model)
        gated_grad[place.s] = dot_right(active_ref[...], own_w).astype(low)
        early_add_y(0)
        early_add_y(1)
        for h in range(2):
            out_grad[2 * h : 2 * h + 2] = dot_left(rows_ref[h], active_ref[...]).astype(low).reshape(part_shape)
        for copy in store(blocks - 1):
            copy.wait()
        early_add_z(0)
        early_add_z(1)
        grad_copy.wait_recv()
        for e in range(2 * EARLY):
            early_last(e).wait_recv()
            early_out[e] = final[e].astype(f32) + last[e].astype(f32)

    block = (FOUR, TWO, TWO, out_full.shape[3], HIDDEN_BLOCK)
    pl.run_scoped(
        feed_forward,
        pltpu.VMEM((2,) + block, low),
        pltpu.VMEM((2,) + block, low),
        pltpu.VMEM(block, low),
        pltpu.VMEM(block, low),
        pltpu.VMEM((own_rows, model), f32),
        pltpu.VMEM((own_rows, model), low),
        pltpu.VMEM((model, own_rows), low),
        pltpu.VMEM((model, own_rows), low),
        pltpu.VMEM((own_rows, HIDDEN_BLOCK), low),
        pltpu.VMEM((own_rows, HIDDEN_BLOCK), low),
        pltpu.VMEM((own_rows, model), f32),
        pltpu.VMEM((own_rows, model), f32),
    )

    for e in range(2 * EARLY):
        early_y(e).wait_send()
        for step in range(1, 4):
            early_z(e, step).wait_send()
        early_last(e).wait_send()
    over_peers(lambda step: small_copy(step).wait_send())
    for copy in (token_copy, gated_copy, grad_copy):
        copy.wait_send()
    for k in range(QKV_W + 1):
        for step in range(1, 4):
            z_copy(k, step).wait_send()
        y_copy(k).wait_send()
        core_copy(k).wait_send()
        if k != QKV_W and WEIGHTS[k][3] == "halved":
            x_copy(k).wait_send()


def forward_layer(tokens, cotangent, attn_shard, mlp_shard, small, ssm, to_table, from_table):
    own_rows, model = tokens.shape
    owned = attn_shard.shape[0]
    width = model // 2
    length = 2 * own_rows
    hidden = mlp_shard.shape[2]
    f32, low = jnp.float32, jnp.bfloat16
    waves = (RADIX, 2 * HALF, width)
    vmem, anywhere = pl.BlockSpec(memory_space=pltpu.VMEM), pl.BlockSpec(memory_space=pl.ANY)
    shape = jax.ShapeDtypeStruct
    owners = (FOUR, TWO, TWO, owned)
    count = len(WEIGHTS) + 1
    dma = pltpu.SemaphoreType.DMA
    outs = (
        (shape(owners + (3 * width,), low), vmem),
        (shape(owners + (hidden,), low), anywhere),
        (shape(owners + (hidden,), low), anywhere),
        (shape((LANES, model), f32), vmem),
        (shape((length, model), low), vmem),
        (shape((length, width), f32), anywhere),
        (shape((length, width), f32), anywhere),
        (shape((length, width), low), vmem),
        (shape((length, width), f32), vmem),
        (shape(waves, f32), anywhere),
        (shape(waves, f32), anywhere),
        (shape(waves, f32), anywhere),
        (shape(waves, f32), anywhere),
        (shape((own_rows, model), low), vmem),
        (shape((own_rows, model), f32), vmem),
        (shape((2, model), f32), vmem),
        (shape((2, own_rows, width), low), vmem),
        (shape(owners + (hidden,), low), anywhere),
        (shape(owners + (hidden,), low), anywhere),
        (shape(owners + (model,), low), vmem),
        (shape((2 * EARLY, owned, HIDDEN_BLOCK), f32), vmem),
    )
    return pl.pallas_call(
        forward_body,
        out_shape=tuple(out for out, _ in outs),
        in_specs=[vmem, vmem, vmem, anywhere, vmem, vmem, vmem, vmem],
        out_specs=tuple(spec for _, spec in outs),
        scratch_shapes=[
            pltpu.VMEM((owned, 3 * width), low),
            pltpu.VMEM((2, own_rows, model), low),
            pltpu.VMEM((16,) + small.shape, low),
            pltpu.VMEM((2, own_rows, width), low),
            pltpu.VMEM((2, own_rows, width), low),
            pltpu.VMEM(owners + (model,), low),
            pltpu.VMEM((own_rows, width), low),
            pltpu.VMEM((2 * EARLY, FOUR, TWO, owned, HIDDEN_BLOCK), low),
            pltpu.VMEM((2 * EARLY, FOUR, owned, HIDDEN_BLOCK), low),
            pltpu.VMEM((2 * EARLY, 3, owned, HIDDEN_BLOCK), low),
            pltpu.VMEM((2 * EARLY, owned, HIDDEN_BLOCK), low),
            pltpu.VMEM((2 * EARLY, owned, HIDDEN_BLOCK), low),
            dma((count,)),
            dma((count, 3)),
            dma((count, 3)),
            dma((count,)),
            dma((count,)),
            dma((count,)),
            dma((count,)),
            dma((count,)),
            dma((count,)),
            dma((16,)),
            dma((16,)),
            dma((3,)),
            dma((3,)),
            dma((6,)),
            dma((2, 2)),
        ]
        + [dma((2 * EARLY,))] * 4
        + [dma((2 * EARLY, 3))] * 2
        + [dma((2 * EARLY,))] * 2,
        compiler_params=pltpu.CompilerParams(collective_id=2, has_side_effects=True, vmem_limit_bytes=VMEM_LIMIT),
        name="forward_layer",
    )(tokens, cotangent, attn_shard, mlp_shard, small, ssm, to_table, from_table)


PIECES = (
    ("down", 1536, 1536, "whole"),
    ("up", 1536, 1536, "halved"),
    ("down", 768, 768, "whole"),
    ("up", 768, 768, "whole"),
    ("out", 0, 768, "halved"),
    ("qkv", 0, 1152, "apart"),
)
D1, U1, DM, UM, OUT, QKV = range(len(PIECES))


def piece_halves(k):
    return TWO if PIECES[k][3] == "halved" else 1


def backward_body(*refs):
    count = len(PIECES)
    (
        grad_all, query_hbm, value_hbm, conv_ref, shifted_ref, kernel_w, taps_w, keys_w, mixed_w, ssm_ref, to_ref, from_ref,
        normed_ref, qkv_ref, token_ref, residual_ref, small_t, norm_two_ref, down_ref, up_ref, out_ref,
    ), refs = refs[:21], refs[21:]
    outs, refs = refs[:count], refs[count:]
    (small_out, ssm_out, input_out), refs = refs[:3], refs[3:]
    near, refs = refs[:count], refs[count:]
    from_x = dict(zip([k for k in range(count) if piece_halves(k) == TWO], refs))
    refs = refs[len(from_x):]
    from_y, from_z, final, last = (refs[i * count : (i + 1) * count] for i in range(4))
    refs = refs[4 * count :]
    (
        own_ref, query_ref, value_ref, spectrum, line_ref, decay_ref, wave_ref, high_ref, back_ref,
        grad_proj, qkv_grad, gn_send, gn_own, gn_last, small_rows, small_ref, small_all, small_sum, small_last,
        ssm_ref_all, ssm_all, ssm_sum,
    ), refs = refs[:22], refs[22:]
    (
        load_sem, own_sem, core_s, core_r, x_s, x_r, y_s, y_r, z_s, z_r, f_s, f_r, sm_s, sm_r, ss_s, ss_r, sg_s, sg_r,
        side_s, side_r,
    ) = refs
    length, width = conv_ref.shape
    own_rows = token_ref.shape[0]
    place = Place()
    grads = {"down": down_ref, "up": up_ref, "out": out_ref, "qkv": qkv_grad}

    def core_copy(k, h):
        source, start, columns, _ = PIECES[k]
        part = columns // piece_halves(k)
        blocks = grads[source].at[:, :, 1 - place.c, :, pl.ds(start + h * part, part)]
        return send(blocks, near[k].at[h], core_s.at[k, h], core_r.at[k, h], place.over_core())

    def own_copy(k, h):
        source, start, columns, _ = PIECES[k]
        part = columns // piece_halves(k)
        blocks = grads[source].at[:, :, place.c, :, pl.ds(start + h * part, part)]
        return pltpu.make_async_copy(blocks, own_ref.at[k % 2, :, :, :, pl.ds(h * part, part)], own_sem.at[k % 2, h])

    def x_copy(k):
        return send(near[k].at[1 - place.s], from_x[k], x_s.at[k], x_r.at[k], place.over_x())

    def kept(k):
        return near[k].at[place.s] if piece_halves(k) == TWO else near[k].at[0]

    def y_copy(k):
        return send(kept(k).at[:, 1 - place.y], from_y[k], y_s.at[k], y_r.at[k], place.over_y())

    def z_copy(k, step):
        other = (place.z + step) % 4
        return send(
            kept(k).at[other, place.y], from_z[k].at[step - 1], z_s.at[k, step - 1], z_r.at[k, step - 1],
            place.along_z(step),
        )

    def last_copy(k):
        return send(final[k], last[k], f_s.at[k], f_r.at[k], place.over_x())

    def load_own(k):
        for h in range(piece_halves(k)):
            own_copy(k, h).start()

    def add_core(k):
        part = PIECES[k][2] // piece_halves(k)
        for h in range(piece_halves(k)):
            core_copy(k, h).wait_recv()
            if k != QKV:
                own_copy(k, h).wait()

            def own(i, h=h):
                if k == QKV:
                    return qkv_grad[i // 2, i % 2, place.c]
                return own_ref[k % 2, i // 2, i % 2, :, h * part : (h + 1) * part]

            def put(i, total, h=h):
                near[k][h, i // 2, i % 2] = total.astype(jnp.bfloat16)

            add_blocks(put, [own, lambda i, h=h: near[k][h, i // 2, i % 2]], 8)

    def add_x(k):
        x_copy(k).wait_recv()

        def put(i, total):
            kept(k)[i // 2, i % 2] = total.astype(jnp.bfloat16)

        add_blocks(put, [lambda i: kept(k)[i // 2, i % 2], lambda i: from_x[k][i // 2, i % 2]], 8)

    def add_y(k):
        y_copy(k).wait_recv()

        def put(i, total):
            kept(k)[i, place.y] = total.astype(jnp.bfloat16)

        add_blocks(put, [lambda i: kept(k)[i, place.y], lambda i: from_y[k][i]], 4)

    def start_z(k):
        for step in range(1, 4):
            z_copy(k, step).start()

    def add_z(k):
        for step in range(1, 4):
            z_copy(k, step).wait_recv()
        total = kept(k)[place.z, place.y].astype(jnp.float32)
        for step in range(3):
            total = total + from_z[k][step].astype(jnp.float32)
        final[k][...] = total.astype(jnp.bfloat16)

    def finish(k):
        last_copy(k).wait_recv()
        if PIECES[k][3] == "whole":
            outs[k][...] = final[k][...].astype(jnp.float32) + last[k][...].astype(jnp.float32)
        else:
            outs[k][place.s] = final[k][...]
            outs[k][1 - place.s] = last[k][...]

    def over_peers(action):
        def one(step, carry):
            action(step)
            return carry

        lax.fori_loop(1, 16, one, 0)

    def to_peer(source, target, send_sem, recv_sem, step):
        other = (place.d + step) % 16
        return send(source.at[other], target.at[place.d], send_sem.at[other], recv_sem.at[place.d], place.owner(other))

    def from_peer(target, send_sem, recv_sem, step):
        other = (place.d + step) % 16
        return send(target.at[other], target.at[other], send_sem.at[other], recv_sem.at[other], place.owner(other))

    def share(step):
        other = (place.d + step) % 16
        return send(ssm_sum.at[place.d], ssm_sum.at[place.d], sg_s.at[other], sg_r.at[place.d], place.owner(other))

    gn_copy = send(gn_send, gn_last, side_s.at[1], side_r.at[1], place.over_x())
    small_copy = send(small_sum, small_last, side_s.at[2], side_r.at[2], place.over_x())
    spectra = (kernel_w, mixed_w, taps_w, keys_w)

    def load_spectrum(i):
        return pltpu.make_async_copy(spectra[i], spectrum.at[i % 2], load_sem.at[i % 2])

    query_copy = pltpu.make_async_copy(query_hbm, query_ref, load_sem.at[2])
    value_copy = pltpu.make_async_copy(value_hbm, value_ref, load_sem.at[3])

    greet_all(place)
    for k in range(QKV):
        for h in range(piece_halves(k)):
            core_copy(k, h).start()
    load_own(D1)
    load_own(U1)
    query_copy.start()
    load_spectrum(0).start()
    value_copy.start()
    load_spectrum(1).start()
    add_core(D1)
    y_copy(D1).start()
    load_own(DM)
    add_core(U1)
    x_copy(U1).start()
    load_own(UM)
    add_core(DM)
    load_own(OUT)
    add_core(UM)
    add_core(OUT)

    def keep(wave, value):
        wave_ref[wave] = value

    def lines(base, row, cols):
        return line_ref[pl.ds(base + row, 16), cols]

    def column(index, cols):
        return pl.ds(index * width + cols.start, cols.size)

    def read_conv_grad(base, row, cols):
        rows = pl.ds(base + row, 16)
        gradient = grad_all[base // own_rows, pl.ds(base % own_rows + row, 16), cols].astype(jnp.float32)
        grad_proj[rows, cols] = (gradient * conv_ref[rows, cols].astype(jnp.float32)).astype(jnp.bfloat16)
        return (gradient * query_ref[rows, cols]).astype(jnp.bfloat16).astype(jnp.float32)

    query_copy.wait()
    value_copy.wait()
    to_waves(width, read_conv_grad, RADIX, to_ref, high_ref, None, keep)
    load_spectrum(0).wait()
    product(width, spectrum.at[0], wave_ref, True, high_ref, None)
    load_spectrum(2).start()

    def put_mixed(base, row, cols, value):
        rows = pl.ds(base + row, 16)
        gradient = value.astype(jnp.bfloat16).astype(jnp.float32)
        grad_proj[rows, column(2, cols)] = (gradient * shifted_ref[rows, cols]).astype(jnp.bfloat16)
        line_ref[rows, cols] = gradient * value_ref[rows, cols]

    from_waves(width, from_ref, high_ref, None, back_ref, put_mixed)
    add_y(D1)
    start_z(D1)
    y_copy(DM).start()
    load_spectrum(1).wait()
    product(width, spectrum.at[1], wave_ref, True, high_ref, None)
    load_spectrum(3).start()

    def put_kernel(base, row, cols, value):
        decay_ref[pl.ds(base + row, 16), cols] = value

    from_waves(width, from_ref, high_ref, None, back_ref, put_kernel)
    add_x(U1)
    x_copy(OUT).start()
    to_waves(width, lines, RADIX, to_ref, high_ref, None, keep)
    add_y(DM)
    start_z(DM)
    y_copy(UM).start()
    y_copy(U1).start()
    load_spectrum(2).wait()
    product(width, spectrum.at[0], wave_ref, True, high_ref, None)

    def put_keys(base, row, cols, value):
        grad_proj[pl.ds(base + row, 16), column(1, cols)] = value.astype(jnp.bfloat16)

    from_waves(width, from_ref, high_ref, None, back_ref, put_keys)
    add_x(OUT)

    def project_back(begin, put):
        def one(index, carry):
            row = pl.multiple_of(index * 256, 256)
            value = lax.dot_general(
                grad_proj[pl.ds(pl.multiple_of(begin + row, 256), 256), :], qkv_ref[...], (((1,), (1,)), ((), ())),
                preferred_element_type=jnp.float32,
            )
            put(pl.ds(row, 256), value)
            return carry

        lax.fori_loop(0, own_rows // 256, one, 0)

    def put_send(rows, value):
        gn_send[rows, :] = value.astype(jnp.bfloat16)

    def put_own(rows, value):
        gn_own[rows, :] = value

    project_back((1 - place.s) * own_rows, put_send)
    gn_copy.start()
    for pair in range(TWO):
        columns = 2 * 4 * qkv_grad.shape[3]
        value = lax.dot_general(
            normed_ref[:, pair * columns : (pair + 1) * columns], grad_proj[...], (((0,), (0,)), ((), ())),
            preferred_element_type=jnp.float32,
        )
        qkv_grad[2 * pair : 2 * pair + 2] = value.astype(jnp.bfloat16).reshape((2,) + qkv_grad.shape[1:])
    core_copy(QKV, 0).start()
    project_back(place.s * own_rows, put_own)
    add_y(UM)
    start_z(UM)
    add_core(QKV)
    y_copy(QKV).start()
    add_y(U1)
    start_z(U1)
    load_spectrum(3).wait()
    product(width, spectrum.at[1], wave_ref, True, high_ref, None)
    small_rows[...] = jnp.zeros(small_rows.shape, jnp.float32)
    small_rows[:TAP_ROWS, pl.ds(pl.multiple_of(place.s * width, LANES), width)] = first_positions(
        width, TAP_ROWS, from_ref, high_ref, None
    )
    decay_gradients(0, length, ssm_ref, decay_ref, ssm_ref_all)
    add_y(QKV)
    start_z(QKV)
    y_copy(OUT).start()
    add_z(D1)
    add_z(DM)
    decay_gradients(1, length, ssm_ref, decay_ref, ssm_ref_all)
    add_z(UM)
    add_z(U1)
    add_y(OUT)
    start_z(OUT)
    decay_gradients(2, length, ssm_ref, decay_ref, ssm_ref_all)
    over_peers(lambda step: to_peer(ssm_ref_all, ssm_all, ss_s, ss_r, step).start())
    gn_copy.wait_recv()
    for k in (D1, DM, UM, U1):
        last_copy(k).start()

    def norm_back(index, sums):
        rows = pl.ds(pl.multiple_of(index * 32, 32), 32)
        normal, inverse = layer_norm_parts(token_ref[rows, :].astype(jnp.float32))
        upstream = gn_own[rows, :] + gn_last[rows, :].astype(jnp.float32)
        into, gain, bias = layer_norm_back(upstream, normal, inverse, small_t[TAP_ROWS : TAP_ROWS + 1, :])
        input_out[rows, :] = residual_ref[rows, :] + into
        return sums[0] + gain, sums[1] + bias

    zero = jnp.sum(norm_two_ref[...], axis=0, keepdims=True) * 0.0
    gain, bias = lax.fori_loop(0, own_rows // 32, norm_back, (zero, zero), unroll=4)
    small_rows[TAP_ROWS : TAP_ROWS + 1, :] = gain
    small_rows[TAP_ROWS + 1 : TAP_ROWS + 2, :] = bias
    small_rows[TAP_ROWS + 2 : TAP_ROWS + 4, :] = norm_two_ref[...]
    small_ref[...] = small_rows[...].T.astype(jnp.bfloat16).reshape(small_ref.shape)
    over_peers(lambda step: to_peer(small_ref, small_all, sm_s, sm_r, step).start())
    add_z(QKV)
    last_copy(QKV).start()
    add_z(OUT)
    last_copy(OUT).start()

    over_peers(lambda step: from_peer(ssm_all, ss_s, ss_r, step).wait_recv())
    ssm_all[place.d] = ssm_ref_all[place.d]
    total = ssm_all[0]
    for index in range(1, 16):
        total = total + ssm_all[index]
    ssm_sum[place.d] = total
    over_peers(lambda step: share(step).start())
    over_peers(lambda step: from_peer(small_all, sm_s, sm_r, step).wait_recv())

    def add_small(step, total):
        return total + small_all[(place.d + step) % 16].astype(jnp.float32)

    small_sum[...] = lax.fori_loop(1, 16, add_small, small_ref[place.d].astype(jnp.float32)).astype(jnp.bfloat16)
    small_copy.start()
    for k in range(count):
        finish(k)
    over_peers(lambda step: from_peer(ssm_sum, sg_s, sg_r, step).wait_recv())
    ssm_out[...] = ssm_sum[...]
    small_copy.wait_recv()
    small_out[...] = small_sum[...].astype(jnp.float32) + small_last[...].astype(jnp.float32)

    for k in range(count):
        for h in range(piece_halves(k)):
            core_copy(k, h).wait_send()
        if piece_halves(k) == TWO:
            x_copy(k).wait_send()
        y_copy(k).wait_send()
        for step in range(1, 4):
            z_copy(k, step).wait_send()
        last_copy(k).wait_send()
    for copy in (gn_copy, small_copy):
        copy.wait_send()
    over_peers(lambda step: to_peer(small_ref, small_all, sm_s, sm_r, step).wait_send())
    over_peers(lambda step: to_peer(ssm_ref_all, ssm_all, ss_s, ss_r, step).wait_send())
    over_peers(lambda step: share(step).wait_send())


def backward_mixer(
    gated_grad, query, value, conv, shifted, kernel_w, taps_w, keys_w, mixed_w, ssm, to_table, from_table, normed, qkv, tokens,
    residual, small, norm_two, down, up, out,
):
    f32, low = jnp.float32, jnp.bfloat16
    count = len(PIECES)
    length, width = conv.shape
    own_rows, model = tokens.shape
    owned = down.shape[3]
    waves = (RADIX, 2 * HALF, width)
    vmem, anywhere = pl.BlockSpec(memory_space=pltpu.VMEM), pl.BlockSpec(memory_space=pl.ANY)
    results, near, from_x, from_y, from_z, final, last = [], [], [], [], [], [], []
    for k, (_, _, columns, way) in enumerate(PIECES):
        halves = piece_halves(k)
        part = columns // halves
        whole = way == "whole"
        results.append(jax.ShapeDtypeStruct((owned, part) if whole else (TWO, owned, part), f32 if whole else low))
        near.append(pltpu.VMEM((halves, FOUR, TWO, owned, part), low))
        if halves == TWO:
            from_x.append(pltpu.VMEM((FOUR, TWO, owned, part), low))
        from_y.append(pltpu.VMEM((FOUR, owned, part), low))
        from_z.append(pltpu.VMEM((3, owned, part), low))
        final.append(pltpu.VMEM((owned, part), low))
        last.append(pltpu.VMEM((owned, part), low))
    dma = pltpu.SemaphoreType.DMA
    slots = (16, 8, width)
    packed = (16, owned, LANES)
    results += [
        jax.ShapeDtypeStruct(packed[1:], f32),
        jax.ShapeDtypeStruct(slots, f32),
        jax.ShapeDtypeStruct((own_rows, model), f32),
    ]
    return pl.pallas_call(
        backward_body,
        out_shape=tuple(results),
        in_specs=[vmem, anywhere, anywhere, vmem, vmem] + [anywhere] * 4 + [vmem] * 9 + [anywhere] * 3,
        out_specs=(vmem,) * len(results),
        scratch_shapes=near
        + from_x
        + from_y
        + from_z
        + final
        + last
        + [
            pltpu.VMEM((2, FOUR, TWO, owned, 1536), low),
            pltpu.VMEM((length, width), f32),
            pltpu.VMEM((length, width), f32),
            pltpu.VMEM((2,) + waves, f32),
            pltpu.VMEM((length, width), f32),
            pltpu.VMEM((length, width), f32),
            pltpu.VMEM(waves, f32),
            pltpu.VMEM(waves, low),
            pltpu.VMEM(waves, f32),
            pltpu.VMEM((length, 3 * width), low),
            pltpu.VMEM((FOUR, TWO, TWO, owned, 3 * width), low),
            pltpu.VMEM((own_rows, model), low),
            pltpu.VMEM((own_rows, model), f32),
            pltpu.VMEM((own_rows, model), low),
            pltpu.VMEM((LANES, model), f32),
            pltpu.VMEM(packed, low),
            pltpu.VMEM(packed, low),
            pltpu.VMEM(packed[1:], low),
            pltpu.VMEM(packed[1:], low),
            pltpu.VMEM(slots, f32),
            pltpu.VMEM(slots, f32),
            pltpu.VMEM(slots, f32),
            dma((4,)),
            dma((2, TWO)),
            dma((count, TWO)),
            dma((count, TWO)),
        ]
        + [dma((count,))] * 4
        + [dma((count, 3))] * 2
        + [dma((count,))] * 2
        + [dma((16,))] * 6
        + [dma((3,))] * 2,
        compiler_params=pltpu.CompilerParams(collective_id=1, has_side_effects=True, vmem_limit_bytes=VMEM_LIMIT),
        name="backward_mixer",
    )(
        gated_grad, query, value, conv, shifted, kernel_w, taps_w, keys_w, mixed_w, ssm, to_table, from_table, normed, qkv, tokens,
        residual, small, norm_two, down, up, out,
    )


def adam_parts(param, first, second, gradient, learn_rate, decay_weight):
    first_new = BETA_ONE * first + (1.0 - BETA_ONE) * gradient
    second_new = BETA_TWO * second + (1.0 - BETA_TWO) * gradient * gradient
    first_hat = first_new / (1.0 - BETA_ONE**STEP_COUNT)
    second_hat = second_new / (1.0 - BETA_TWO**STEP_COUNT)
    step = learn_rate * (first_hat / (jnp.sqrt(second_hat) + ADAM_EPS) + decay_weight * param)
    return step, first_new, second_new


def adam_body(
    early_sum, down_last, up_last, down_next, up_next, out_sum, qkv_sum, small_sum, ssm_sum,
    attn_p, mlp_p, norm_p, tap_p, ssm_p, attn_m, mlp_m, norm_m, tap_m, ssm_m,
    attn_step, attn_new, mlp_step, mlp_new, norm_step, norm_new, tap_step, tap_new, ssm_step, ssm_new,
    *, scale,
):
    f32 = jnp.float32
    width = out_sum.shape[2]

    def attn(start, gradient):
        cols = slice(start, start + width)
        attn_step[:, cols], attn_new[0, :, cols], attn_new[1, :, cols] = adam_parts(
            attn_p[:, cols].astype(f32), attn_m[0, :, cols], attn_m[1, :, cols], gradient.astype(f32) * scale,
            LEARN_RATE, DECAY_RATE,
        )

    def mlp(plane, start, source, slot):
        count = source.shape[-1]
        for begin in range(0, count, width):
            gradient = source[:, begin : begin + width] if slot is None else source[slot, :, begin : begin + width]
            cols = slice(start + begin, start + begin + width)
            mlp_step[plane, :, cols], mlp_new[0, plane, :, cols], mlp_new[1, plane, :, cols] = adam_parts(
                mlp_p[plane, :, cols].astype(f32), mlp_m[0, plane, :, cols], mlp_m[1, plane, :, cols],
                gradient.astype(f32) * scale, LEARN_RATE, DECAY_RATE,
            )

    for half in range(2):
        for place in range(3):
            attn((2 * place + half) * width, qkv_sum[half, :, place * width : (place + 1) * width])
        attn((6 + half) * width, out_sum[half])
        mlp(0, up_last.shape[2] * 2 + half * up_last.shape[2], up_last, half)
    for piece in range(early_sum.shape[0]):
        mlp(1 - piece % 2, piece // 2 * HIDDEN_BLOCK, early_sum, piece)
    mlp(0, HIDDEN_BLOCK, up_next, None)
    mlp(1, HIDDEN_BLOCK, down_next, None)
    mlp(1, down_last.shape[1], down_last, None)
    tap_step[...], tap_new[0], tap_new[1] = adam_parts(
        tap_p[...].astype(f32), tap_m[0], tap_m[1], small_sum[:, :TAP_ROWS] * scale, LEARN_RATE, DECAY_RATE
    )
    small = small_sum[...].T * scale
    norm_step[...], norm_new[0], norm_new[1] = adam_parts(
        norm_p[...].astype(f32), norm_m[0], norm_m[1], small[TAP_ROWS : TAP_ROWS + 4], LEARN_RATE, 0.0
    )
    for plane in range(2):
        gradient = ssm_sum[plane * 8 : plane * 8 + 8].reshape(ssm_p.shape[1:]) * scale
        ssm_step[plane], ssm_new[0, plane], ssm_new[1, plane] = adam_parts(
            ssm_p[plane], ssm_m[0, plane], ssm_m[1, plane], gradient, SSM_LEARN_RATE, 0.0
        )


def adam_all(sums, params, moments, scale):
    vmem = pl.BlockSpec(memory_space=pltpu.VMEM)
    outs = []
    for param, moment in zip(params, moments):
        outs += [jax.ShapeDtypeStruct(param.shape, jnp.float32), jax.ShapeDtypeStruct(moment.shape, jnp.float32)]
    return pl.pallas_call(
        partial(adam_body, scale=scale),
        out_shape=tuple(outs),
        in_specs=[vmem] * (len(sums) + 2 * len(params)),
        out_specs=(vmem,) * len(outs),
        compiler_params=pltpu.CompilerParams(vmem_limit_bytes=VMEM_LIMIT),
        name="adam",
    )(*sums, *params, *moments)


def turned_last(value):
    return jnp.swapaxes(value, -1, -2)


def per_device_split(
    tokens,
    cotangent,
    attn_weight,
    mlp_weight,
    norms,
    taps,
    ssm_params,
    attn_moments,
    mlp_moments,
    norm_moments,
    tap_moments,
    ssm_moments,
):
    f32, low = jnp.float32, jnp.bfloat16
    rows, width = tokens.shape[1:]
    shares = lax.axis_size("seq")
    owners = lax.axis_size("dp")
    length = rows * shares
    part = width // shares
    tap_count = taps.shape[0]
    to_table, from_table = map(jnp.asarray, transform_tables())

    owned = attn_weight.shape[0]
    small = jnp.concatenate([taps, norms, jnp.zeros((LANES - 4 - tap_count, owned), low)]).T
    ssm_turned = jnp.swapaxes(ssm_params, 1, 2)
    (
        qkv_full, _, _, small_full, normed_low, query, value, conv, shifted, kernel_w, taps_w, keys_w, mixed_w,
        layer_out, grad_residual, grad_norm_two, grad_gated, grad_up, grad_down, grad_out, early_sums,
    ) = forward_layer(
        tokens[0], cotangent[0], attn_weight, mlp_weight, small, ssm_turned,
        to_table, from_table,
    )
    scale = 1.0 / math.sqrt(owners * length)
    sums = backward_mixer(
        grad_gated, query, value, conv, shifted, kernel_w, taps_w, keys_w, mixed_w, ssm_turned, to_table, from_table,
        normed_low, qkv_full.reshape(width, 3 * part), tokens[0], grad_residual, small_full, grad_norm_two,
        grad_down, grad_up, grad_out,
    )
    (
        attn_step, attn_new, mlp_step, mlp_new, norms_step, norm_new, taps_step, tap_new, ssm_step, ssm_new
    ) = adam_all(
        (early_sums,) + tuple(sums[:8]),
        (attn_weight, mlp_weight, norms, taps.T, ssm_turned),
        (attn_moments, mlp_moments, norm_moments, turned_last(tap_moments), turned_last(ssm_moments)),
        scale,
    )
    taps_step, tap_new, ssm_step, ssm_new = map(turned_last, (taps_step, tap_new, ssm_step, ssm_new))
    input_grad = sums[8]
    return (
        layer_out[None],
        input_grad[None],
        attn_step,
        attn_new,
        mlp_step,
        mlp_new,
        norms_step,
        norm_new,
        taps_step,
        tap_new,
        ssm_step,
        ssm_new,
    )


def solution(mesh):
    fits = (mesh.shape["seq"], mesh.shape["dp"]) == (2, 16)

    def chosen(tokens, cotangent, attn_weight, mlp_weight, norms, taps, *others):
        fast = fits and tokens.shape[1:] == (RADIX * HALF // 2, 6 * LANES) and taps.shape[0] == TAP_ROWS
        plan = per_device_split if fast else per_device
        return plan(tokens, cotangent, attn_weight, mlp_weight, norms, taps, *others)

    return jax.shard_map(
        chosen,
        mesh=mesh,
        in_specs=(
            P("dp", "seq", None),
            P("dp", "seq", None),
            P("dp", None),
            P(None, "dp", None),
            P(None, "dp"),
            P(None, "dp"),
            P(None, "seq", None),
            P(None, "dp", None),
            P(None, None, "dp", None),
            P(None, None, "dp"),
            P(None, None, "dp"),
            P(None, None, "seq", None),
        ),
        out_specs=(
            P("dp", "seq", None),
            P("dp", "seq", None),
            P("dp", None),
            P(None, "dp", None),
            P(None, "dp", None),
            P(None, None, "dp", None),
            P(None, "dp"),
            P(None, None, "dp"),
            P(None, "dp"),
            P(None, None, "dp"),
            P(None, "seq", None),
            P(None, None, "seq", None),
        ),
        check_vma=False,
    )
```

```python
from functools import partial
import math

import jax
import jax.numpy as jnp
import ml_dtypes
import numpy as np
from jax import lax
from jax.experimental import pallas as pl
from jax.experimental.pallas import tpu as pltpu
from jax.sharding import PartitionSpec as P

DFT_ROWS = 256


EPS_NORM = 1e-05
BETA_ONE = 0.9
BETA_TWO = 0.999
ADAM_EPS = 1e-08
LEARN_RATE = 0.001
SSM_LEARN_RATE = 0.00025
DECAY_RATE = 0.1
STEP_COUNT = 10.0
HIGHEST = lax.Precision.HIGHEST


def from_behind(block, axis, distance):
    devices = range(lax.axis_size(axis))
    route = [(i - distance, i) for i in devices if i - distance in devices]
    return lax.ppermute(block, axis, route)


def as_sent(value):

    def short(part):
        return part.astype(jnp.bfloat16) if part.dtype == jnp.float32 else part

    return jax.tree.map(short, value)


def layer_norm(values, gain_row, bias_row):
    average = jnp.mean(values, axis=-1, keepdims=True)
    centred = values - average
    variance = jnp.mean(centred * centred, axis=-1, keepdims=True)
    return centred * lax.rsqrt(variance + EPS_NORM) * gain_row + bias_row


def shift_mix(rim_rows, keys_part, taps_full):
    tap_count = taps_full.shape[0]
    row_count = keys_part.shape[0]
    extended = jnp.concatenate([rim_rows, keys_part], axis=0)
    summed = jnp.zeros_like(keys_part)
    for tap_index in range(tap_count):
        begin_row = tap_count - 1 - tap_index
        summed = summed + taps_full[tap_index] * extended[begin_row : begin_row + row_count]
    return summed


def kernel_rows(length_total, ssm_full):
    inner_count = math.gcd(length_total, 128)
    outer_count = length_total // inner_count
    decay_rates = jnp.exp(ssm_full[0])
    outer_offsets = (jnp.arange(outer_count) * inner_count).astype(jnp.float32)
    inner_offsets = jnp.arange(inner_count).astype(jnp.float32)
    outer_part = ssm_full[1][:, :, None] * jnp.exp(
        -decay_rates[:, :, None] * outer_offsets[None, None, :]
    )
    inner_part = jnp.exp(-decay_rates[:, :, None] * inner_offsets[None, None, :])
    kernel = jnp.einsum("cna,cnb->cab", outer_part, inner_part, precision=HIGHEST)
    return kernel.reshape(kernel.shape[0], length_total)


def dft_tables(length_total, first_count):
    full_length = 2 * length_total
    col_count = full_length // first_count
    half_rows = first_count // 2
    row_index = jnp.arange(half_rows, dtype=jnp.int32)
    freq_index = jnp.arange(first_count, dtype=jnp.int32)
    col_index = jnp.arange(col_count, dtype=jnp.int32)
    angle_first = (
        2.0
        * math.pi
        / first_count
        * (row_index[:, None] * freq_index[None, :] % first_count).astype(jnp.float32)
    )
    angle_twist = (
        2.0 * math.pi / full_length * (freq_index[:, None] * col_index[None, :]).astype(jnp.float32)
    )
    angle_last = (
        2.0
        * math.pi
        / col_count
        * (col_index[:, None] * col_index[None, :] % col_count).astype(jnp.float32)
    )
    return (
        jnp.cos(angle_first),
        jnp.sin(angle_first),
        jnp.cos(angle_twist),
        jnp.sin(angle_twist),
        jnp.cos(angle_last),
        jnp.sin(angle_last),
    )


def forward_dft(signal, tables):
    cos_first, sin_first, cos_twist, sin_twist, cos_last, sin_last = tables
    half_rows = cos_first.shape[0]
    col_count = cos_last.shape[0]
    folded = signal.reshape(signal.shape[0], half_rows, col_count)
    real_first = jnp.einsum("cmp,mk->ckp", folded, cos_first, precision=HIGHEST)
    imaginary_first = -jnp.einsum("cmp,mk->ckp", folded, sin_first, precision=HIGHEST)
    real_twist = real_first * cos_twist + imaginary_first * sin_twist
    imaginary_twist = imaginary_first * cos_twist - real_first * sin_twist
    real_last = jnp.einsum("ckp,pq->ckq", real_twist, cos_last, precision=HIGHEST) + jnp.einsum(
        "ckp,pq->ckq", imaginary_twist, sin_last, precision=HIGHEST
    )
    imaginary_last = jnp.einsum(
        "ckp,pq->ckq", imaginary_twist, cos_last, precision=HIGHEST
    ) - jnp.einsum("ckp,pq->ckq", real_twist, sin_last, precision=HIGHEST)
    return (real_last, imaginary_last)


def inverse_dft(spectrum, tables):
    cos_first, sin_first, cos_twist, sin_twist, cos_last, sin_last = tables
    real_part, imaginary_part = spectrum
    full_length = cos_first.shape[1] * cos_last.shape[0]
    real_inner = jnp.einsum("ckq,qp->ckp", real_part, cos_last, precision=HIGHEST) - jnp.einsum(
        "ckq,qp->ckp", imaginary_part, sin_last, precision=HIGHEST
    )
    imaginary_inner = jnp.einsum(
        "ckq,qp->ckp", imaginary_part, cos_last, precision=HIGHEST
    ) + jnp.einsum("ckq,qp->ckp", real_part, sin_last, precision=HIGHEST)
    real_twist = real_inner * cos_twist - imaginary_inner * sin_twist
    imaginary_twist = imaginary_inner * cos_twist + real_inner * sin_twist
    signal = jnp.einsum("ckp,mk->cmp", real_twist, cos_first, precision=HIGHEST) - jnp.einsum(
        "ckp,mk->cmp", imaginary_twist, sin_first, precision=HIGHEST
    )
    return signal.reshape(signal.shape[0], signal.shape[1] * signal.shape[2]) / full_length


def complex_product(left, right, conjugate_left):
    left_real, left_imaginary = left
    right_real, right_imaginary = right
    if conjugate_left:
        return (
            left_real * right_real + left_imaginary * right_imaginary,
            left_real * right_imaginary - left_imaginary * right_real,
        )
    return (
        left_real * right_real - left_imaginary * right_imaginary,
        left_real * right_imaginary + left_imaginary * right_real,
    )


def adam_update(param_now, moments, gradient, learn_rate, decay_weight):
    first_new = BETA_ONE * moments[0] + (1.0 - BETA_ONE) * gradient
    second_new = BETA_TWO * moments[1] + (1.0 - BETA_TWO) * gradient * gradient
    first_hat = first_new / (1.0 - BETA_ONE**STEP_COUNT)
    second_hat = second_new / (1.0 - BETA_TWO**STEP_COUNT)
    step_size = learn_rate * (
        first_hat / (jnp.sqrt(second_hat) + ADAM_EPS) + decay_weight * param_now
    )
    return (step_size, jnp.stack([first_new, second_new]))


def per_device(
    tokens,
    cotangent,
    attn_weight,
    mlp_weight,
    norms,
    taps,
    ssm_params,
    attn_moments,
    mlp_moments,
    norm_moments,
    tap_moments,
    ssm_moments,
):
    row_count = tokens.shape[1]
    model_width = tokens.shape[2]
    group_count = lax.axis_size("seq")
    owner_count = lax.axis_size("dp")
    length_total = row_count * group_count
    attn_full, mlp_full, norm_full, taps_full = (
        lax.all_gather(attn_weight, "dp", axis=0, tiled=True),
        lax.all_gather(mlp_weight, "dp", axis=1, tiled=True),
        lax.all_gather(norms, "dp", axis=1, tiled=True),
        lax.all_gather(taps, "dp", axis=1, tiled=True),
    )
    inputs = tokens[0].astype(jnp.float32)
    cot_rows = cotangent[0].astype(jnp.float32)
    norm_values = norm_full.astype(jnp.float32)
    taps_values = taps_full.astype(jnp.float32)
    tap_count = taps_values.shape[0]
    normed, norm_pull = jax.vjp(layer_norm, inputs, norm_values[0], norm_values[1])
    normed_low = normed.astype(jnp.bfloat16)
    project = jnp.dot(
        normed_low, attn_full[:, : 3 * model_width], preferred_element_type=jnp.float32
    )
    queries = project[:, :model_width]
    keys_part = project[:, model_width : 2 * model_width]
    values = project[:, 2 * model_width :]
    rim_rows = from_behind(
        keys_part[row_count - tap_count + 1 :].astype(jnp.bfloat16), "seq", 1
    ).astype(jnp.float32)
    shifted, shift_pull = jax.vjp(shift_mix, rim_rows, keys_part, taps_values)
    mixed_rows = (shifted * values).astype(jnp.bfloat16)
    moved_in = lax.all_to_all(mixed_rows.T, "seq", split_axis=0, concat_axis=1, tiled=True).astype(
        jnp.float32
    )
    tables = dft_tables(length_total, DFT_ROWS)
    kernel, kernel_pull = jax.vjp(partial(kernel_rows, length_total), ssm_params)
    kernel_freq = forward_dft(kernel, tables)
    input_freq = forward_dft(moved_in, tables)
    conv_channels = inverse_dft(complex_product(input_freq, kernel_freq, False), tables)
    conv_back = lax.all_to_all(
        conv_channels.astype(jnp.bfloat16), "seq", split_axis=1, concat_axis=0, tiled=True
    )
    conv_rows = conv_back.T.astype(jnp.float32)
    gated_rows = (queries * conv_rows).astype(jnp.bfloat16)
    branch = jnp.dot(
        gated_rows, attn_full[:, 3 * model_width :], preferred_element_type=jnp.float32
    )
    residual_one = inputs + branch
    normed_two, norm_two_pull = jax.vjp(layer_norm, residual_one, norm_values[2], norm_values[3])
    normed_two_low = normed_two.astype(jnp.bfloat16)
    before = jnp.dot(normed_two_low, mlp_full[0], preferred_element_type=jnp.float32)
    active, gelu_pull = jax.vjp(jax.nn.gelu, before)
    active_low = active.astype(jnp.bfloat16)
    mlp_out = jnp.einsum("tf,df->td", active_low, mlp_full[1], preferred_element_type=jnp.float32)
    layer_out = (residual_one + mlp_out).astype(jnp.bfloat16)
    attn_back, mlp_back = (
        lax.all_gather(attn_weight, "dp", axis=0, tiled=True),
        lax.all_gather(mlp_weight, "dp", axis=1, tiled=True),
    )
    grad_after = cotangent[0]
    grad_active = jnp.dot(grad_after, mlp_back[1], preferred_element_type=jnp.float32)
    grad_down = jnp.einsum("td,tf->df", grad_after, active_low, preferred_element_type=jnp.float32)
    grad_before = gelu_pull(grad_active)[0].astype(jnp.bfloat16)
    grad_up = jnp.einsum(
        "td,tf->df", normed_two_low, grad_before, preferred_element_type=jnp.float32
    )
    grad_normed_two = jnp.einsum(
        "tf,df->td", grad_before, mlp_back[0], preferred_element_type=jnp.float32
    )
    grad_residual_part, grad_gain_two, grad_bias_two = norm_two_pull(grad_normed_two)
    grad_residual = cot_rows + grad_residual_part
    grad_branch = grad_residual.astype(jnp.bfloat16)
    grad_out = jnp.einsum("td,te->de", gated_rows, grad_branch, preferred_element_type=jnp.float32)
    grad_gated = jnp.einsum(
        "te,de->td",
        grad_branch,
        attn_back[:, 3 * model_width :],
        preferred_element_type=jnp.float32,
    )
    grad_queries = grad_gated * conv_rows
    grad_conv = (grad_gated * queries).astype(jnp.bfloat16)
    grad_moved = lax.all_to_all(grad_conv.T, "seq", split_axis=0, concat_axis=1, tiled=True).astype(
        jnp.float32
    )
    grad_freq = forward_dft(grad_moved, tables)
    grad_input = inverse_dft(complex_product(kernel_freq, grad_freq, True), tables)
    grad_kernel = inverse_dft(complex_product(input_freq, grad_freq, True), tables)
    grad_ssm_local = kernel_pull(grad_kernel)[0]
    grad_ssm = lax.psum(grad_ssm_local, "dp")
    grad_mixed_back = lax.all_to_all(
        grad_input.astype(jnp.bfloat16), "seq", split_axis=1, concat_axis=0, tiled=True
    )
    grad_mixed = grad_mixed_back.T.astype(jnp.float32)
    grad_shifted = grad_mixed * values
    grad_values = grad_mixed * shifted
    grad_rim, grad_keys, grad_taps = shift_pull(grad_shifted)
    returned = from_behind(as_sent(grad_rim), "seq", -1).astype(grad_rim.dtype)
    grad_keys = grad_keys + jnp.pad(returned, ((row_count - tap_count + 1, 0), (0, 0)))
    grad_project = jnp.concatenate([grad_queries, grad_keys, grad_values], axis=1).astype(
        jnp.bfloat16
    )
    grad_qkv = jnp.einsum("td,te->de", normed_low, grad_project, preferred_element_type=jnp.float32)
    grad_normed = jnp.einsum(
        "te,de->td",
        grad_project,
        attn_back[:, : 3 * model_width],
        preferred_element_type=jnp.float32,
    )
    grad_input_part, grad_gain_one, grad_bias_one = norm_pull(grad_normed)
    input_grad = grad_residual + grad_input_part
    grad_attn = jnp.concatenate([grad_qkv, grad_out], axis=1)
    grad_mlp = jnp.stack([grad_up, grad_down])
    grad_norms = jnp.stack([grad_gain_one, grad_bias_one, grad_gain_two, grad_bias_two])
    owned_part = (
        lax.psum_scatter(
            grad_attn.astype(jnp.bfloat16), "dp", scatter_dimension=0, tiled=True
        ).astype(jnp.float32),
        lax.psum_scatter(
            grad_mlp.astype(jnp.bfloat16), "dp", scatter_dimension=1, tiled=True
        ).astype(jnp.float32),
        lax.psum_scatter(
            grad_norms.astype(jnp.bfloat16), "dp", scatter_dimension=1, tiled=True
        ).astype(jnp.float32),
        lax.psum_scatter(
            grad_taps.astype(jnp.bfloat16), "dp", scatter_dimension=1, tiled=True
        ).astype(jnp.float32),
    )
    summed = (
        lax.psum(owned_part[0].astype(jnp.bfloat16), "seq").astype(jnp.float32),
        lax.psum(owned_part[1].astype(jnp.bfloat16), "seq").astype(jnp.float32),
        lax.psum(owned_part[2].astype(jnp.bfloat16), "seq").astype(jnp.float32),
        lax.psum(owned_part[3].astype(jnp.bfloat16), "seq").astype(jnp.float32),
    )
    grad_scale = 1.0 / math.sqrt(owner_count * length_total)
    attn_step, attn_moments_new = adam_update(
        attn_weight.astype(jnp.float32),
        attn_moments,
        summed[0] * grad_scale,
        LEARN_RATE,
        DECAY_RATE,
    )
    mlp_step, mlp_moments_new = adam_update(
        mlp_weight.astype(jnp.float32), mlp_moments, summed[1] * grad_scale, LEARN_RATE, DECAY_RATE
    )
    norms_step, norm_moments_new = adam_update(
        norms.astype(jnp.float32), norm_moments, summed[2] * grad_scale, LEARN_RATE, 0.0
    )
    taps_step, tap_moments_new = adam_update(
        taps.astype(jnp.float32), tap_moments, summed[3] * grad_scale, LEARN_RATE, DECAY_RATE
    )
    ssm_step, ssm_moments_new = adam_update(
        ssm_params, ssm_moments, grad_ssm * grad_scale, SSM_LEARN_RATE, 0.0
    )
    return (
        layer_out[None],
        input_grad[None],
        attn_step,
        attn_moments_new,
        mlp_step,
        mlp_moments_new,
        norms_step,
        norm_moments_new,
        taps_step,
        tap_moments_new,
        ssm_step,
        ssm_moments_new,
    )


LANES = 128
RADIX = 8
HALF = 128


def transform_tables():
    rows = np.arange(HALF)
    length = RADIX * HALF
    waves = RADIX * rows[None, :, None] + np.arange(RADIX)[:, None, None] + 0.25
    angles = 2.0 * np.pi * np.mod(rows[None, None, :] * waves, length) / length
    cosines, sines = np.cos(angles), np.sin(angles)
    full = np.concatenate(
        [np.concatenate([cosines, sines], axis=2), np.concatenate([-sines, cosines], axis=2)], axis=1
    )


    def parts(matrix):
        matrix = matrix.astype(np.float32)
        high = matrix.astype(ml_dtypes.bfloat16)
        rest = (matrix - high.astype(np.float32)).astype(ml_dtypes.bfloat16)
        return np.stack([high, rest])

    return parts(full), parts(np.swapaxes(full, 1, 2))


def turned(value, angle):
    real, imaginary = value
    cosine, sine = math.cos(angle), math.sin(angle)
    if abs(sine) < 1e-12:
        return (real, imaginary) if cosine > 0 else (-real, -imaginary)
    if abs(cosine) < 1e-12:
        return (-imaginary, real) if sine > 0 else (imaginary, -real)
    return (real * cosine - imaginary * sine, real * sine + imaginary * cosine)


def small_transform(values, sign):
    count = len(values)
    if count == 1:
        return values
    even = small_transform(values[::2], sign)
    odd = small_transform(values[1::2], sign)
    low, high = [], []
    for index in range(count // 2):
        (er, ei), (tr, ti) = even[index], turned(odd[index], sign * 2.0 * math.pi * index / count)
        low.append((er + tr, ei + ti))
        high.append((er - tr, ei - ti))
    return low + high


def dot(left, right):
    return jnp.dot(left, right, preferred_element_type=jnp.float32)


def keep_parts(high_ref, low_ref, wave, row, cols, value):
    high = value.astype(jnp.bfloat16)
    high_ref[wave, pl.ds(row, 16), cols] = high
    if low_ref is not None:
        low_ref[wave, pl.ds(row, 16), cols] = (value - high.astype(jnp.float32)).astype(jnp.bfloat16)


def table_dot(table_high, table_low, high_ref, low_ref, wave):
    high = high_ref[wave]
    total = dot(table_high, high) + dot(table_low, high)
    return total if low_ref is None else total + dot(table_high, low_ref[wave])


def each_tile(width, rows, step, body):
    for block in range(width // LANES):

        def one(index, carry, block=block):
            body(pl.multiple_of(index * step, step), pl.ds(block * LANES, LANES))
            return carry

        lax.fori_loop(0, rows // step, one, 0)


def to_waves(width, read, used, w_ref, high_ref, low_ref, store):
    def first(row, cols):
        inputs = []
        for part in range(used):
            x = read(part * HALF, row, cols)
            angle = -2.0 * math.pi * part / 32.0
            inputs.append((x * math.cos(angle), x * math.sin(angle)) if part else (x, jnp.zeros_like(x)))
        while len(inputs) < RADIX:
            inputs.append((jnp.zeros_like(x), jnp.zeros_like(x)))
        for wave, value in enumerate(small_transform(inputs, -1.0)):
            for place, part in enumerate(value):
                keep_parts(high_ref, low_ref, wave, row + place * HALF, cols, part)

    each_tile(width, HALF, 16, first)

    def second(wave, carry):
        store(wave, table_dot(w_ref[0, wave], w_ref[1, wave], high_ref, low_ref, wave))
        return carry

    lax.fori_loop(0, RADIX, second, 0)


def product(width, left_ref, right_ref, conjugate, high_ref, low_ref):
    sign = -1.0 if conjugate else 1.0

    def one(wave, carry):
        def tile(row, cols):
            lr, li = left_ref[wave, pl.ds(row, 16), cols], left_ref[wave, pl.ds(row + HALF, 16), cols] * sign
            rr, ri = right_ref[wave, pl.ds(row, 16), cols], right_ref[wave, pl.ds(row + HALF, 16), cols]
            for place, part in enumerate((lr * rr - li * ri, lr * ri + li * rr)):
                keep_parts(high_ref, low_ref, wave, row + place * HALF, cols, part)

        each_tile(width, HALF, 16, tile)
        return carry

    lax.fori_loop(0, RADIX, one, 0)


def from_waves(width, w_ref, high_ref, low_ref, back_ref, put):
    def second(wave, carry):
        back_ref[wave] = table_dot(w_ref[0, wave], w_ref[1, wave], high_ref, low_ref, wave)
        return carry

    lax.fori_loop(0, RADIX, second, 0)
    scale = 1.0 / (RADIX * HALF)

    def first(row, cols):
        values = [
            (back_ref[wave, pl.ds(row, 16), cols], back_ref[wave, pl.ds(row + HALF, 16), cols])
            for wave in range(RADIX)
        ]
        for part, (real, imaginary) in enumerate(small_transform(values, 1.0)):
            angle = 2.0 * math.pi * part / 32.0
            put(part * HALF, row, cols, real * (math.cos(angle) * scale) - imaginary * (math.sin(angle) * scale))

    each_tile(width, HALF, 16, first)


def first_positions(width, count, w_ref, high_ref, low_ref):
    total = jnp.zeros((count, width), jnp.float32)
    for wave in range(RADIX):
        total = total + table_dot(w_ref[0, wave, :count, :], w_ref[1, wave, :count, :], high_ref, low_ref, wave)
    return total * (1.0 / (RADIX * HALF))


FINE = 32


def decay_sums(block, length, ssm_ref, out_ref):
    modes = ssm_ref.shape[1]
    steps = length // FINE
    cols = pl.ds(block * LANES, LANES)
    out_ref[:, cols] = jnp.zeros((length, LANES), jnp.float32)
    offsets = lax.broadcasted_iota(jnp.int32, (FINE, LANES), 0).astype(jnp.float32)

    def group(index, carry):
        base = pl.multiple_of(index * 8, 8)
        rates = jnp.exp(ssm_ref[0, pl.ds(base, 8), cols])
        leaps = jnp.exp(-rates * FINE)
        weights = ssm_ref[1, pl.ds(base, 8), cols]
        terms = tuple(weights[i : i + 1] * jnp.exp(-rates[i : i + 1] * offsets) for i in range(8))
        leap_rows = [jnp.broadcast_to(leaps[i : i + 1], (FINE, LANES)) for i in range(8)]

        def step(number, terms):
            rows = pl.ds(pl.multiple_of(number * FINE, FINE), FINE)
            total = out_ref[rows, cols]
            for term in terms:
                total = total + term
            out_ref[rows, cols] = total
            return tuple(term * leap for term, leap in zip(terms, leap_rows))

        lax.fori_loop(0, steps, step, terms, unroll=4)
        return carry

    lax.fori_loop(0, modes // 8, group, 0)


def decay_gradients(block, length, ssm_ref, grad_ref, out_ref):
    modes = ssm_ref.shape[1]
    steps = length // FINE
    cols = pl.ds(block * LANES, LANES)
    offsets = lax.broadcasted_iota(jnp.int32, (FINE, LANES), 0).astype(jnp.float32)

    def group(index, carry):
        base = pl.multiple_of(index * 8, 8)
        rates = jnp.exp(ssm_ref[0, pl.ds(base, 8), cols])
        leaps = jnp.exp(-rates * FINE)
        plain_rows, slope_rows = [], []
        for modes_now in ((0, 1, 2, 3), (4, 5, 6, 7)):
            zero = offsets * 0.0
            leap_rows = [jnp.broadcast_to(leaps[i : i + 1], (FINE, LANES)) for i in modes_now]

            def step(number, sums, leap_rows=leap_rows):
                rows = grad_ref[pl.ds(pl.multiple_of((steps - 1 - number) * FINE, FINE), FINE), cols]
                return tuple((v * leap + rows, w * leap + v) for (v, w), leap in zip(sums, leap_rows))

            sums = lax.fori_loop(0, steps, step, tuple((zero, zero) for _ in modes_now), unroll=8)
            for i, (v, w) in zip(modes_now, sums):
                fine = jnp.exp(-rates[i : i + 1] * offsets)
                plain = fine * v
                slope = fine * w * (leaps[i : i + 1] * FINE) + plain * offsets
                plain_rows.append(jnp.sum(plain, axis=0, keepdims=True))
                slope_rows.append(jnp.sum(slope, axis=0, keepdims=True))
        out_ref[modes // 8 + index, :, cols] = jnp.concatenate(plain_rows, axis=0)
        out_ref[index, :, cols] = (
            -ssm_ref[1, pl.ds(base, 8), cols] * rates * jnp.concatenate(slope_rows, axis=0)
        )
        return carry

    lax.fori_loop(0, modes // 8, group, 0)


def layer_norm_parts(values):
    average = jnp.mean(values, axis=-1, keepdims=True)
    centred = values - average
    variance = jnp.mean(centred * centred, axis=-1, keepdims=True)
    inverse = lax.rsqrt(variance + EPS_NORM)
    return centred * inverse, inverse


def layer_norm_back(upstream, normal, inverse, gain_row):
    weighted = upstream * gain_row
    average = jnp.mean(weighted, axis=-1, keepdims=True)
    overlap = jnp.mean(weighted * normal, axis=-1, keepdims=True)
    into = (weighted - average - normal * overlap) * inverse
    return into, jnp.sum(upstream * normal, axis=0, keepdims=True), jnp.sum(upstream, axis=0, keepdims=True)


MESH = pl.DeviceIdType.MESH
TWO, FOUR = 2, 4
TAP_ROWS = 64
VMEM_LIMIT = 62 * 1024 * 1024


class Place:
    def __init__(self):
        self.s, self.d = lax.axis_index("seq"), lax.axis_index("dp")
        self.z, self.y, self.c = self.d // 4, (self.d // 2) % 2, self.d % 2

    def over_x(self):
        return (1 - self.s, self.d)

    def over_y(self):
        return (self.s, self.d + 2 - 4 * self.y)

    def over_core(self):
        return (self.s, self.d + 1 - 2 * self.c)

    def along_z(self, step):
        return (self.s, (self.d + 4 * step) % 16)

    def owner(self, index):
        return (self.s, index)


def send(source, target, send_sem, recv_sem, device):
    return pltpu.make_async_remote_copy(
        src_ref=source, dst_ref=target, send_sem=send_sem, recv_sem=recv_sem, device_id=device, device_id_type=MESH
    )


def greet_all(place):
    barrier = pltpu.get_barrier_semaphore()
    pl.semaphore_signal(barrier, inc=1, device_id=place.over_x(), device_id_type=MESH)

    def greet(step, carry):
        pl.semaphore_signal(
            barrier, inc=1, device_id=place.owner((place.d + step) % 16), device_id_type=MESH
        )
        return carry

    lax.fori_loop(1, 16, greet, 0)
    pl.semaphore_wait(barrier, 16)


def add_blocks(put, sources, count):
    def one(index, carry):
        total = sources[0](index).astype(jnp.float32)
        for source in sources[1:]:
            total = total + source(index).astype(jnp.float32)
        put(index, total)
        return carry

    lax.fori_loop(0, count, one, 0)


WEIGHTS = (
    ("out", 0, 768, "whole"),
    ("up", 0, 1536, "halved"),
    ("down", 0, 1536, "whole"),
    ("up", 1536, 1536, "halved"),
    ("down", 1536, 768, "whole"),
    ("down", 2304, 768, "whole"),
)
OUT_W, UP_FIRST, DOWN_FIRST, UP_LAST, DOWN_THIRD, DOWN_LAST, QKV_W = range(len(WEIGHTS) + 1)
HIDDEN_BLOCK = 768
EARLY = 1


def dot_right(left, right):
    return lax.dot_general(left, right, (((1,), (1,)), ((), ())), preferred_element_type=jnp.float32)


def dot_left(left, right):
    return lax.dot_general(left, right, (((0,), (0,)), ((), ())), preferred_element_type=jnp.float32)


def gelu_parts(x):
    slope = math.sqrt(2.0 / math.pi)
    square = x * x
    bent = jnp.tanh(slope * x * (1.0 + 0.044715 * square))
    upper = 0.5 + 0.5 * bent
    return x * upper, upper + 0.5 * x * (1.0 - bent * bent) * (slope * (1.0 + 3.0 * 0.044715 * square))


def forward_body(
    token_ref, cotangent_ref, attn_shard, mlp_shard, small_ref, ssm_ref, to_ref, from_ref,
    qkv_full, up_full, down_full, small_t, normed_ref, query_out, value_out, conv_ref, shifted_ref,
    kernel_out, taps_out, keys_out, mixed_out, layer_out, residual_grad, norm_two_out, gated_grad, up_grad, down_grad, out_grad, early_out,
    qkv_ref, token_all, small_all, gated_ref, rows_ref, out_full, grad_send, near, from_y, from_z, final, last,
    own_sem, z_s, z_r, y_s, y_r, x_s, x_r, core_s, core_r, small_s, small_r, side_s, side_r, store_sem, load_sem, nc_s, nc_r, ny_s, ny_r, nz_s, nz_r, nf_s, nf_r,
):
    length, width = conv_ref.shape
    own_rows, model = token_ref.shape
    place = Place()
    f32, low = jnp.float32, jnp.bfloat16
    shards = {"up": mlp_shard.at[0], "down": mlp_shard.at[1], "out": attn_shard.at[:, pl.ds(3 * model, model)]}
    fulls = {"up": up_full, "down": down_full, "out": out_full}

    def columns(k):
        source, start, count, way = WEIGHTS[k]
        if way == "whole":
            return source, pl.ds(start, count)
        return source, pl.ds(pl.multiple_of(start + place.s * (count // 2), LANES), count // 2)

    def z_copy(k, step):
        if k == QKV_W:
            source, target = qkv_ref, qkv_full.at[place.z, place.y, place.c]
        else:
            name, cols = columns(k)
            source, target = shards[name].at[:, cols], fulls[name].at[place.z, place.y, place.c, :, cols]
        return send(source, target, z_s.at[k, step - 1], z_r.at[k, step - 1], place.along_z(step))

    def y_copy(k):
        if k == QKV_W:
            blocks = qkv_full.at[:, place.y, place.c]
        else:
            name, cols = columns(k)
            blocks = fulls[name].at[:, place.y, place.c, :, cols]
        return send(blocks, blocks, y_s.at[k], y_r.at[k], place.over_y())

    def x_copy(k):
        name, cols = columns(k)
        blocks = fulls[name].at[:, :, place.c, :, cols]
        return send(blocks, blocks, x_s.at[k], x_r.at[k], place.over_x())

    def core_copy(k):
        if k == QKV_W:
            blocks = qkv_full.at[:, :, place.c]
        else:
            name, start, count, _ = WEIGHTS[k]
            blocks = fulls[name].at[:, :, place.c, :, pl.ds(start, count)]
        return send(blocks, blocks, core_s.at[k], core_r.at[k], place.over_core())

    def own_copies():
        copies = []
        for k in range(QKV_W):
            name, cols = columns(k)
            target = fulls[name].at[place.z, place.y, place.c, :, cols]
            copies.append(pltpu.make_async_copy(shards[name].at[:, cols], target, own_sem.at[k]))
        return copies

    def start_z(k):
        for step in range(1, 4):
            z_copy(k, step).start()

    def wait_z(k):
        for step in range(1, 4):
            z_copy(k, step).wait_recv()

    def over_peers(action):
        def one(step, carry):
            action(step)
            return carry

        lax.fori_loop(1, 16, one, 0)

    def small_copy(step):
        other = (place.d + step) % 16
        return send(small_ref, small_all.at[place.d], small_s.at[other], small_r.at[place.d], place.owner(other))

    def small_arrival(step):
        other = (place.d + step) % 16
        return send(small_ref, small_all.at[other], small_s.at[other], small_r.at[other], place.owner(other))

    token_copy = send(token_ref, token_all.at[place.s], side_s.at[0], side_r.at[0], place.over_x())
    gated_copy = send(gated_ref.at[1 - place.s], rows_ref.at[place.s], side_s.at[1], side_r.at[1], place.over_x())
    grad_copy = send(grad_send, gated_grad.at[place.s], side_s.at[2], side_r.at[2], place.over_x())

    def early_y(e):
        return send(near.at[e, :, 1 - place.y], from_y.at[e], ny_s.at[e], ny_r.at[e], place.over_y())

    def early_z(e, step):
        other = (place.z + step) % 4
        return send(
            near.at[e, other, place.y], from_z.at[e, step - 1], nz_s.at[e, step - 1], nz_r.at[e, step - 1],
            place.along_z(step),
        )

    def early_last(e):
        return send(final.at[e], last.at[e], nf_s.at[e], nf_r.at[e], place.over_x())

    def early_add_y(e):
        early_y(e).wait_recv()

        def put(i, total):
            near[e, i, place.y] = total.astype(low)

        add_blocks(put, [lambda i: near[e, i, place.y], lambda i: from_y[e, i]], 4)
        for step in range(1, 4):
            early_z(e, step).start()

    def early_add_z(e):
        for step in range(1, 4):
            early_z(e, step).wait_recv()
        total = near[e, place.z, place.y].astype(f32)
        for step in range(3):
            total = total + from_z[e, step].astype(f32)
        final[e] = total.astype(low)
        early_last(e).start()

    def step_one():
        wait_z(QKV_W)
        y_copy(QKV_W).start()
        start_z(UP_FIRST)

    def step_two():
        for copy in own_copies():
            copy.wait()
        wait_z(OUT_W)
        y_copy(OUT_W).start()
        start_z(DOWN_FIRST)

    def step_three():
        y_copy(QKV_W).wait_recv()
        core_copy(QKV_W).start()

    def step_four():
        wait_z(UP_FIRST)
        y_copy(UP_FIRST).start()
        start_z(UP_LAST)

    def step_five():
        y_copy(OUT_W).wait_recv()
        core_copy(OUT_W).start()

    def step_six():
        y_copy(UP_FIRST).wait_recv()
        x_copy(UP_FIRST).start()

    def step_seven():
        wait_z(DOWN_FIRST)
        y_copy(DOWN_FIRST).start()
        start_z(DOWN_THIRD)

    def step_eight():
        wait_z(UP_LAST)
        y_copy(UP_LAST).start()
        start_z(DOWN_LAST)

    def step_nine():
        x_copy(UP_FIRST).wait_recv()
        core_copy(UP_FIRST).start()

    def step_ten():
        y_copy(DOWN_FIRST).wait_recv()
        core_copy(DOWN_FIRST).start()

    def step_eleven():
        wait_z(DOWN_THIRD)
        y_copy(DOWN_THIRD).start()
        y_copy(UP_LAST).wait_recv()
        x_copy(UP_LAST).start()

    def step_twelve():
        wait_z(DOWN_LAST)
        y_copy(DOWN_LAST).start()
        y_copy(DOWN_THIRD).wait_recv()
        core_copy(DOWN_THIRD).start()

    def step_thirteen():
        x_copy(UP_LAST).wait_recv()
        core_copy(UP_LAST).start()

    def step_fourteen():
        y_copy(DOWN_LAST).wait_recv()
        core_copy(DOWN_LAST).start()

    for j in range(3):
        cols = pl.ds(pl.multiple_of((2 * j + place.s) * width, LANES), width)
        qkv_ref[:, j * width : (j + 1) * width] = attn_shard[:, cols]
    greet_all(place)
    start_z(QKV_W)
    over_peers(lambda step: small_copy(step).start())
    token_copy.start()
    for copy in own_copies():
        copy.start()
    qkv_full[place.z, place.y, place.c] = qkv_ref[...]
    small_all[place.d] = small_ref[...]

    def mixer(line_ref, high_ref, low_ref, back_ref, proj_ref, kernel_w, other_w, keys_w):
        def keep(target):
            def store(wave, value):
                target[wave] = value

            return store

        def lines(base, row, cols):
            return line_ref[pl.ds(base + row, 16), cols]

        def column(index, cols):
            return pl.ds(index * width + cols.start, cols.size)

        stores = [
            pltpu.make_async_copy(kernel_w, kernel_out, store_sem.at[0]),
            pltpu.make_async_copy(other_w, taps_out, store_sem.at[1]),
            pltpu.make_async_copy(keys_w, keys_out, store_sem.at[2]),
            pltpu.make_async_copy(other_w, mixed_out, store_sem.at[3]),
            pltpu.make_async_copy(proj_ref.at[:, pl.ds(0, width)], query_out, store_sem.at[4]),
            pltpu.make_async_copy(proj_ref.at[:, pl.ds(2 * width, width)], value_out, store_sem.at[5]),
        ]
        for block in range(width // LANES):
            decay_sums(block, length, ssm_ref, line_ref)
            if not block:
                start_z(OUT_W)
        step_one()
        to_waves(width, lines, RADIX, to_ref, high_ref, low_ref, keep(kernel_w))
        stores[0].start()
        over_peers(lambda step: small_arrival(step).wait_recv())
        small_t[...] = small_all[...].reshape(16 * small_all.shape[1], LANES).astype(f32).T
        taps_cols = pl.multiple_of(place.s * width, LANES)

        def read_taps(base, row, cols):
            taps = small_t[pl.ds(base + row, 16), pl.ds(pl.multiple_of(taps_cols + cols.start, LANES), LANES)]
            inside = lax.broadcasted_iota(jnp.int32, taps.shape, 0) + (base + row) < TAP_ROWS
            return jnp.where(inside, taps, 0.0)

        def normalize(source, begin):
            def one(index, carry):
                row = pl.multiple_of(index * 32, 32)
                normal, _ = layer_norm_parts(source[pl.ds(row, 32), :].astype(f32))
                scaled = normal * small_t[TAP_ROWS : TAP_ROWS + 1, :] + small_t[TAP_ROWS + 1 : TAP_ROWS + 2, :]
                normed_ref[pl.ds(pl.multiple_of(begin + row, 32), 32), :] = scaled.astype(low)
                return carry

            lax.fori_loop(0, own_rows // 32, one, 0, unroll=4)

        def project(begin):
            weight = qkv_full[...].reshape(model, 3 * width)

            def one(index, carry):
                row = pl.ds(pl.multiple_of(begin + index * 256, 256), 256)
                proj_ref[row, :] = dot(normed_ref[row, :], weight)
                return carry

            lax.fori_loop(0, own_rows // 256, one, 0)

        own_begin, other_begin = place.s * own_rows, (1 - place.s) * own_rows
        normalize(token_ref, own_begin)
        step_two()
        token_copy.wait_recv()
        normalize(token_all.at[1 - place.s], other_begin)
        step_three()
        to_waves(width, read_taps, 1, to_ref, high_ref, low_ref, keep(other_w))
        stores[1].start()
        core_copy(QKV_W).wait_recv()
        project(own_begin)
        project(other_begin)
        stores[4].start()
        stores[5].start()
        step_four()
        step_five()
        to_waves(
            width, lambda base, row, cols: proj_ref[pl.ds(base + row, 16), column(1, cols)],
            RADIX, to_ref, high_ref, low_ref, keep(keys_w),
        )
        stores[2].start()
        product(width, other_w, keys_w, False, high_ref, low_ref)
        step_six()

        def put_shifted(base, row, cols, value):
            rows = pl.ds(base + row, 16)
            shifted_ref[rows, cols] = value
            mixed = value * proj_ref[rows, column(2, cols)]
            line_ref[rows, cols] = mixed.astype(low).astype(f32)

        from_waves(width, from_ref, high_ref, low_ref, back_ref, put_shifted)
        step_seven()
        stores[1].wait()
        to_waves(width, lines, RADIX, to_ref, high_ref, low_ref, keep(other_w))
        stores[3].start()
        product(width, kernel_w, other_w, False, high_ref, low_ref)
        step_eight()

        def put_conv(base, row, cols, value):
            rows = pl.ds(base + row, 16)
            rounded = value.astype(low)
            conv_ref[rows, cols] = rounded
            gated = (proj_ref[rows, cols] * rounded.astype(f32)).astype(low)
            gated_ref[base // own_rows, pl.ds(base % own_rows + row, 16), cols] = gated

        from_waves(width, from_ref, high_ref, low_ref, back_ref, put_conv)
        gated_copy.start()
        for i in (0, 2, 3, 4, 5):
            stores[i].wait()

    waves = (RADIX, 2 * HALF, width)
    pl.run_scoped(
        mixer,
        pltpu.VMEM((length, width), f32),
        pltpu.VMEM(waves, low),
        pltpu.VMEM(waves, low),
        pltpu.VMEM(waves, f32),
        pltpu.VMEM((length, 3 * width), f32),
        pltpu.VMEM(waves, f32),
        pltpu.VMEM(waves, f32),
        pltpu.VMEM(waves, f32),
    )
    rows_ref[place.s] = gated_ref[place.s]

    def feed_forward(
        up_w, down_w, up_g, down_g, residual_ref, normed_two, normed_turned, cot_turned, active_ref, before_ref,
        out_sum, normed_grad,
    ):
        block_shape = up_g.shape
        blocks = up_full.shape[4] // HIDDEN_BLOCK

        def load(j):
            cols = pl.ds(j * HIDDEN_BLOCK, HIDDEN_BLOCK)
            return [
                pltpu.make_async_copy(full.at[:, :, :, :, cols], held.at[j % 2], load_sem.at[i, j % 2])
                for i, (full, held) in enumerate(((up_full, up_w), (down_full, down_w)))
            ]

        def store(j):
            cols = pl.ds(j * HIDDEN_BLOCK, HIDDEN_BLOCK)
            return [
                pltpu.make_async_copy(held, full.at[:, :, :, :, cols], store_sem.at[i])
                for i, (full, held) in enumerate(((up_grad, up_g), (down_grad, down_g)))
            ]

        def early_core(e):
            source = up_g if e % 2 else down_g
            return send(source.at[:, :, 1 - place.c], near.at[e], nc_s.at[e], nc_r.at[e], place.over_core())

        def early_add_core(e):
            source = up_g if e % 2 else down_g
            early_core(e).wait_recv()

            def put(i, total):
                near[e, i // 2, i % 2] = total.astype(low)

            add_blocks(put, [lambda i: source[i // 2, i % 2, place.c], lambda i: near[e, i // 2, i % 2]], 8)
            early_core(e).wait_send()

        step_nine()
        cot_turned[...] = cotangent_ref[...].T
        step_ten()
        core_copy(OUT_W).wait_recv()
        gated_copy.wait_recv()
        out_w = out_full[...].reshape(model, model)

        def branch(index, carry):
            rows = pl.ds(pl.multiple_of(index * 256, 256), 256)
            value = dot(rows_ref[0, rows, :], out_w[:width]) + dot(rows_ref[1, rows, :], out_w[width:])
            residual_ref[rows, :] = token_ref[rows, :].astype(f32) + value
            return carry

        lax.fori_loop(0, own_rows // 256, branch, 0)

        def normalize(index, carry):
            rows = pl.ds(pl.multiple_of(index * 32, 32), 32)
            normal, _ = layer_norm_parts(residual_ref[rows, :])
            scaled = normal * small_t[TAP_ROWS + 2 : TAP_ROWS + 3, :] + small_t[TAP_ROWS + 3 : TAP_ROWS + 4, :]
            normed_two[rows, :] = scaled.astype(low)
            return carry

        lax.fori_loop(0, own_rows // 32, normalize, 0, unroll=4)
        core_copy(UP_FIRST).wait_recv()
        core_copy(DOWN_FIRST).wait_recv()
        for copy in load(0) + load(1):
            copy.start()
        normed_turned[...] = normed_two[...].T
        step_eleven()
        for j in range(blocks):
            if j == 1:
                step_twelve()
            if j == 2:
                step_thirteen()
                core_copy(UP_LAST).wait_recv()
                core_copy(DOWN_THIRD).wait_recv()
                for copy in load(j):
                    copy.start()
                early_y(1).start()
            if j == 3:
                step_fourteen()
                early_add_y(0)
                core_copy(DOWN_LAST).wait_recv()
                for copy in load(j):
                    copy.start()
            for copy in load(j):
                copy.wait()
            up = up_w[j % 2].reshape(model, HIDDEN_BLOCK)
            down = down_w[j % 2].reshape(model, HIDDEN_BLOCK)

            def rows_of(index, carry, up=up, down=down, j=j):
                rows = pl.ds(pl.multiple_of(index * 256, 256), 256)
                active, slope = gelu_parts(dot(normed_two[rows, :], up))
                active = active.astype(low)
                active_ref[rows, :] = active
                grad_before = (dot(cotangent_ref[rows, :], down) * slope).astype(low)
                before_ref[rows, :] = grad_before
                out_part = dot_right(active, down)
                grad_part = dot_right(grad_before, up)
                if j:
                    out_part = out_part + out_sum[rows, :]
                    grad_part = grad_part + normed_grad[rows, :]
                out_sum[rows, :] = out_part
                normed_grad[rows, :] = grad_part
                return carry

            lax.fori_loop(0, own_rows // 256, rows_of, 0)
            if j == 1:
                early_add_core(0)
                early_y(0).start()
                early_add_core(1)
            if j > EARLY:
                for copy in store(j - 1):
                    copy.wait()
            down_g[...] = dot(cot_turned[...], active_ref[...]).astype(low).reshape(block_shape)
            up_g[...] = dot(normed_turned[...], before_ref[...]).astype(low).reshape(block_shape)
            if j < EARLY:
                for e in (2 * j, 2 * j + 1):
                    early_core(e).start()
            else:
                for copy in store(j):
                    copy.start()
        early_add_y(1)

        def norm_back(index, sums):
            rows = pl.ds(pl.multiple_of(index * 32, 32), 32)
            normal, inverse = layer_norm_parts(residual_ref[rows, :])
            into, gain, bias = layer_norm_back(
                normed_grad[rows, :], normal, inverse, small_t[TAP_ROWS + 2 : TAP_ROWS + 3, :]
            )
            total = cotangent_ref[rows, :].astype(f32) + into
            residual_grad[rows, :] = total
            active_ref[rows, :] = total.astype(low)
            layer_out[rows, :] = (residual_ref[rows, :] + out_sum[rows, :]).astype(low)
            return sums[0] + gain, sums[1] + bias

        zero = small_t[TAP_ROWS : TAP_ROWS + 1, :] * 0.0
        gain, bias = lax.fori_loop(0, own_rows // 32, norm_back, (zero, zero), unroll=4)
        norm_two_out[0:1, :] = gain
        norm_two_out[1:2, :] = bias
        part_shape = (2,) + out_full.shape[1:]
        other_w = out_full[pl.ds(2 * (1 - place.s), 2)].reshape(width, model)
        grad_send[...] = dot_right(active_ref[...], other_w).astype(low)
        grad_copy.start()
        own_w = out_full[pl.ds(2 * place.s, 2)].reshape(width, model)
        gated_grad[place.s] = dot_right(active_ref[...], own_w).astype(low)
        early_add_z(0)
        for h in range(2):
            out_grad[2 * h : 2 * h + 2] = dot_left(rows_ref[h], active_ref[...]).astype(low).reshape(part_shape)
        for copy in store(blocks - 1):
            copy.wait()
        early_add_z(1)
        grad_copy.wait_recv()
        for e in range(2 * EARLY):
            early_last(e).wait_recv()
            early_out[e] = final[e].astype(f32) + last[e].astype(f32)

    block = (FOUR, TWO, TWO, out_full.shape[3], HIDDEN_BLOCK)
    pl.run_scoped(
        feed_forward,
        pltpu.VMEM((2,) + block, low),
        pltpu.VMEM((2,) + block, low),
        pltpu.VMEM(block, low),
        pltpu.VMEM(block, low),
        pltpu.VMEM((own_rows, model), f32),
        pltpu.VMEM((own_rows, model), low),
        pltpu.VMEM((model, own_rows), low),
        pltpu.VMEM((model, own_rows), low),
        pltpu.VMEM((own_rows, HIDDEN_BLOCK), low),
        pltpu.VMEM((own_rows, HIDDEN_BLOCK), low),
        pltpu.VMEM((own_rows, model), f32),
        pltpu.VMEM((own_rows, model), f32),
    )

    for e in range(2 * EARLY):
        early_y(e).wait_send()
        for step in range(1, 4):
            early_z(e, step).wait_send()
        early_last(e).wait_send()
    over_peers(lambda step: small_copy(step).wait_send())
    for copy in (token_copy, gated_copy, grad_copy):
        copy.wait_send()
    for k in range(QKV_W + 1):
        for step in range(1, 4):
            z_copy(k, step).wait_send()
        y_copy(k).wait_send()
        core_copy(k).wait_send()
        if k != QKV_W and WEIGHTS[k][3] == "halved":
            x_copy(k).wait_send()


def forward_layer(tokens, cotangent, attn_shard, mlp_shard, small, ssm, to_table, from_table):
    own_rows, model = tokens.shape
    owned = attn_shard.shape[0]
    width = model // 2
    length = 2 * own_rows
    hidden = mlp_shard.shape[2]
    f32, low = jnp.float32, jnp.bfloat16
    waves = (RADIX, 2 * HALF, width)
    vmem, anywhere = pl.BlockSpec(memory_space=pltpu.VMEM), pl.BlockSpec(memory_space=pl.ANY)
    shape = jax.ShapeDtypeStruct
    owners = (FOUR, TWO, TWO, owned)
    count = len(WEIGHTS) + 1
    dma = pltpu.SemaphoreType.DMA
    outs = (
        (shape(owners + (3 * width,), low), vmem),
        (shape(owners + (hidden,), low), anywhere),
        (shape(owners + (hidden,), low), anywhere),
        (shape((LANES, model), f32), vmem),
        (shape((length, model), low), vmem),
        (shape((length, width), f32), anywhere),
        (shape((length, width), f32), anywhere),
        (shape((length, width), low), vmem),
        (shape((length, width), f32), vmem),
        (shape(waves, f32), anywhere),
        (shape(waves, f32), anywhere),
        (shape(waves, f32), anywhere),
        (shape(waves, f32), anywhere),
        (shape((own_rows, model), low), vmem),
        (shape((own_rows, model), f32), vmem),
        (shape((2, model), f32), vmem),
        (shape((2, own_rows, width), low), vmem),
        (shape(owners + (hidden,), low), anywhere),
        (shape(owners + (hidden,), low), anywhere),
        (shape(owners + (model,), low), vmem),
        (shape((2 * EARLY, owned, HIDDEN_BLOCK), f32), vmem),
    )
    return pl.pallas_call(
        forward_body,
        out_shape=tuple(out for out, _ in outs),
        in_specs=[vmem, vmem, vmem, anywhere, vmem, vmem, vmem, vmem],
        out_specs=tuple(spec for _, spec in outs),
        scratch_shapes=[
            pltpu.VMEM((owned, 3 * width), low),
            pltpu.VMEM((2, own_rows, model), low),
            pltpu.VMEM((16,) + small.shape, low),
            pltpu.VMEM((2, own_rows, width), low),
            pltpu.VMEM((2, own_rows, width), low),
            pltpu.VMEM(owners + (model,), low),
            pltpu.VMEM((own_rows, width), low),
            pltpu.VMEM((2 * EARLY, FOUR, TWO, owned, HIDDEN_BLOCK), low),
            pltpu.VMEM((2 * EARLY, FOUR, owned, HIDDEN_BLOCK), low),
            pltpu.VMEM((2 * EARLY, 3, owned, HIDDEN_BLOCK), low),
            pltpu.VMEM((2 * EARLY, owned, HIDDEN_BLOCK), low),
            pltpu.VMEM((2 * EARLY, owned, HIDDEN_BLOCK), low),
            dma((count,)),
            dma((count, 3)),
            dma((count, 3)),
            dma((count,)),
            dma((count,)),
            dma((count,)),
            dma((count,)),
            dma((count,)),
            dma((count,)),
            dma((16,)),
            dma((16,)),
            dma((3,)),
            dma((3,)),
            dma((6,)),
            dma((2, 2)),
        ]
        + [dma((2 * EARLY,))] * 4
        + [dma((2 * EARLY, 3))] * 2
        + [dma((2 * EARLY,))] * 2,
        compiler_params=pltpu.CompilerParams(collective_id=2, has_side_effects=True, vmem_limit_bytes=VMEM_LIMIT),
        name="forward_layer",
    )(tokens, cotangent, attn_shard, mlp_shard, small, ssm, to_table, from_table)


PIECES = (
    ("down", 1536, 1536, "whole"),
    ("up", 1536, 1536, "halved"),
    ("down", 768, 768, "whole"),
    ("up", 768, 768, "whole"),
    ("out", 0, 768, "halved"),
    ("qkv", 0, 1152, "apart"),
)
D1, U1, DM, UM, OUT, QKV = range(len(PIECES))


def piece_halves(k):
    return TWO if PIECES[k][3] == "halved" else 1


def backward_body(*refs):
    count = len(PIECES)
    (
        grad_all, query_hbm, value_hbm, conv_ref, shifted_ref, kernel_w, taps_w, keys_w, mixed_w, ssm_ref, to_ref, from_ref,
        normed_hbm, qkv_hbm, token_hbm, residual_hbm, small_t, norm_two_ref, down_ref, up_ref, out_ref,
    ), refs = refs[:21], refs[21:]
    outs, refs = refs[:count], refs[count:]
    (small_out, ssm_out, input_out), refs = refs[:3], refs[3:]
    near, refs = refs[:count], refs[count:]
    from_x = dict(zip([k for k in range(count) if piece_halves(k) == TWO], refs))
    refs = refs[len(from_x):]
    from_y, from_z, final, last = (refs[i * count : (i + 1) * count] for i in range(4))
    refs = refs[4 * count :]
    (
        normed_ref, qkv_ref, token_ref, residual_ref, own_ref, query_ref, value_ref, spectrum, line_ref, decay_ref, wave_ref, high_ref, back_ref,
        grad_proj, qkv_grad, gn_send, gn_own, gn_last, small_rows, small_ref, small_all, small_sum, small_last,
        ssm_ref_all, ssm_all, ssm_sum,
    ), refs = refs[:26], refs[26:]
    (
        load_sem, late_sem, own_sem, core_s, core_r, x_s, x_r, y_s, y_r, z_s, z_r, f_s, f_r, sm_s, sm_r, ss_s, ss_r, sg_s, sg_r,
        side_s, side_r,
    ) = refs
    length, width = conv_ref.shape
    own_rows = token_ref.shape[0]
    place = Place()
    grads = {"down": down_ref, "up": up_ref, "out": out_ref, "qkv": qkv_grad}

    def core_copy(k, h):
        source, start, columns, _ = PIECES[k]
        part = columns // piece_halves(k)
        blocks = grads[source].at[:, :, 1 - place.c, :, pl.ds(start + h * part, part)]
        return send(blocks, near[k].at[h], core_s.at[k, h], core_r.at[k, h], place.over_core())

    def own_copy(k, h):
        source, start, columns, _ = PIECES[k]
        part = columns // piece_halves(k)
        blocks = grads[source].at[:, :, place.c, :, pl.ds(start + h * part, part)]
        return pltpu.make_async_copy(blocks, own_ref.at[k % 2, :, :, :, pl.ds(h * part, part)], own_sem.at[k % 2, h])

    def x_copy(k):
        return send(near[k].at[1 - place.s], from_x[k], x_s.at[k], x_r.at[k], place.over_x())

    def kept(k):
        return near[k].at[place.s] if piece_halves(k) == TWO else near[k].at[0]

    def y_copy(k):
        return send(kept(k).at[:, 1 - place.y], from_y[k], y_s.at[k], y_r.at[k], place.over_y())

    def z_copy(k, step):
        other = (place.z + step) % 4
        return send(
            kept(k).at[other, place.y], from_z[k].at[step - 1], z_s.at[k, step - 1], z_r.at[k, step - 1],
            place.along_z(step),
        )

    def last_copy(k):
        return send(final[k], last[k], f_s.at[k], f_r.at[k], place.over_x())

    def load_own(k):
        for h in range(piece_halves(k)):
            own_copy(k, h).start()

    def add_core(k):
        part = PIECES[k][2] // piece_halves(k)
        for h in range(piece_halves(k)):
            core_copy(k, h).wait_recv()
            if k != QKV:
                own_copy(k, h).wait()

            def own(i, h=h):
                if k == QKV:
                    return qkv_grad[i // 2, i % 2, place.c]
                return own_ref[k % 2, i // 2, i % 2, :, h * part : (h + 1) * part]

            def put(i, total, h=h):
                near[k][h, i // 2, i % 2] = total.astype(jnp.bfloat16)

            add_blocks(put, [own, lambda i, h=h: near[k][h, i // 2, i % 2]], 8)

    def add_x(k):
        x_copy(k).wait_recv()

        def put(i, total):
            kept(k)[i // 2, i % 2] = total.astype(jnp.bfloat16)

        add_blocks(put, [lambda i: kept(k)[i // 2, i % 2], lambda i: from_x[k][i // 2, i % 2]], 8)

    def add_y(k):
        y_copy(k).wait_recv()

        def put(i, total):
            kept(k)[i, place.y] = total.astype(jnp.bfloat16)

        add_blocks(put, [lambda i: kept(k)[i, place.y], lambda i: from_y[k][i]], 4)

    def start_z(k):
        for step in range(1, 4):
            z_copy(k, step).start()

    def add_z(k):
        for step in range(1, 4):
            z_copy(k, step).wait_recv()
        total = kept(k)[place.z, place.y].astype(jnp.float32)
        for step in range(3):
            total = total + from_z[k][step].astype(jnp.float32)
        final[k][...] = total.astype(jnp.bfloat16)

    def finish(k):
        last_copy(k).wait_recv()
        if PIECES[k][3] == "whole":
            outs[k][...] = final[k][...].astype(jnp.float32) + last[k][...].astype(jnp.float32)
        else:
            outs[k][place.s] = final[k][...]
            outs[k][1 - place.s] = last[k][...]

    def over_peers(action):
        def one(step, carry):
            action(step)
            return carry

        lax.fori_loop(1, 16, one, 0)

    def to_peer(source, target, send_sem, recv_sem, step):
        other = (place.d + step) % 16
        return send(source.at[other], target.at[place.d], send_sem.at[other], recv_sem.at[place.d], place.owner(other))

    def from_peer(target, send_sem, recv_sem, step):
        other = (place.d + step) % 16
        return send(target.at[other], target.at[other], send_sem.at[other], recv_sem.at[other], place.owner(other))

    def share(step):
        other = (place.d + step) % 16
        return send(ssm_sum.at[place.d], ssm_sum.at[place.d], sg_s.at[other], sg_r.at[place.d], place.owner(other))

    gn_copy = send(gn_send, gn_last, side_s.at[1], side_r.at[1], place.over_x())
    small_copy = send(small_sum, small_last, side_s.at[2], side_r.at[2], place.over_x())
    spectra = (kernel_w, mixed_w, taps_w, keys_w)

    def load_spectrum(i):
        return pltpu.make_async_copy(spectra[i], spectrum.at[i % 2], load_sem.at[i % 2])

    query_copy = pltpu.make_async_copy(query_hbm, query_ref, load_sem.at[2])
    value_copy = pltpu.make_async_copy(value_hbm, value_ref, load_sem.at[3])

    late_copies = [
        pltpu.make_async_copy(source, target, late_sem.at[i])
        for i, (source, target) in enumerate(
            ((qkv_hbm, qkv_ref), (normed_hbm, normed_ref), (token_hbm, token_ref), (residual_hbm, residual_ref))
        )
    ]
    greet_all(place)
    for k in range(QKV):
        for h in range(piece_halves(k)):
            core_copy(k, h).start()
    load_own(D1)
    load_own(U1)
    query_copy.start()
    load_spectrum(0).start()
    value_copy.start()
    load_spectrum(1).start()
    for copy in late_copies:
        copy.start()
    add_core(D1)
    y_copy(D1).start()
    load_own(DM)
    add_core(U1)
    x_copy(U1).start()
    load_own(UM)
    add_core(DM)
    load_own(OUT)
    add_core(UM)
    add_core(OUT)

    def keep(wave, value):
        wave_ref[wave] = value

    def lines(base, row, cols):
        return line_ref[pl.ds(base + row, 16), cols]

    def column(index, cols):
        return pl.ds(index * width + cols.start, cols.size)

    def read_conv_grad(base, row, cols):
        rows = pl.ds(base + row, 16)
        gradient = grad_all[base // own_rows, pl.ds(base % own_rows + row, 16), cols].astype(jnp.float32)
        grad_proj[rows, cols] = (gradient * conv_ref[rows, cols].astype(jnp.float32)).astype(jnp.bfloat16)
        return (gradient * query_ref[rows, cols]).astype(jnp.bfloat16).astype(jnp.float32)

    query_copy.wait()
    value_copy.wait()
    to_waves(width, read_conv_grad, RADIX, to_ref, high_ref, None, keep)
    load_spectrum(0).wait()
    product(width, spectrum.at[0], wave_ref, True, high_ref, None)
    load_spectrum(2).start()

    def put_mixed(base, row, cols, value):
        rows = pl.ds(base + row, 16)
        gradient = value.astype(jnp.bfloat16).astype(jnp.float32)
        grad_proj[rows, column(2, cols)] = (gradient * shifted_ref[rows, cols]).astype(jnp.bfloat16)
        line_ref[rows, cols] = gradient * value_ref[rows, cols]

    from_waves(width, from_ref, high_ref, None, back_ref, put_mixed)
    add_y(D1)
    start_z(D1)
    y_copy(DM).start()
    load_spectrum(1).wait()
    product(width, spectrum.at[1], wave_ref, True, high_ref, None)
    load_spectrum(3).start()

    def put_kernel(base, row, cols, value):
        decay_ref[pl.ds(base + row, 16), cols] = value

    from_waves(width, from_ref, high_ref, None, back_ref, put_kernel)
    add_x(U1)
    x_copy(OUT).start()
    to_waves(width, lines, RADIX, to_ref, high_ref, None, keep)
    add_y(DM)
    start_z(DM)
    y_copy(UM).start()
    y_copy(U1).start()
    load_spectrum(2).wait()
    product(width, spectrum.at[0], wave_ref, True, high_ref, None)

    def put_keys(base, row, cols, value):
        grad_proj[pl.ds(base + row, 16), column(1, cols)] = value.astype(jnp.bfloat16)

    from_waves(width, from_ref, high_ref, None, back_ref, put_keys)
    add_x(OUT)

    def project_back(begin, put):
        def one(index, carry):
            row = pl.multiple_of(index * 256, 256)
            value = lax.dot_general(
                grad_proj[pl.ds(pl.multiple_of(begin + row, 256), 256), :], qkv_ref[...], (((1,), (1,)), ((), ())),
                preferred_element_type=jnp.float32,
            )
            put(pl.ds(row, 256), value)
            return carry

        lax.fori_loop(0, own_rows // 256, one, 0)

    def put_send(rows, value):
        gn_send[rows, :] = value.astype(jnp.bfloat16)

    def put_own(rows, value):
        gn_own[rows, :] = value

    late_copies[0].wait()
    project_back((1 - place.s) * own_rows, put_send)
    gn_copy.start()
    for copy in late_copies[1:]:
        copy.wait()
    for pair in range(TWO):
        columns = 2 * 4 * qkv_grad.shape[3]
        value = lax.dot_general(
            normed_ref[:, pair * columns : (pair + 1) * columns], grad_proj[...], (((0,), (0,)), ((), ())),
            preferred_element_type=jnp.float32,
        )
        qkv_grad[2 * pair : 2 * pair + 2] = value.astype(jnp.bfloat16).reshape((2,) + qkv_grad.shape[1:])
    core_copy(QKV, 0).start()
    project_back(place.s * own_rows, put_own)
    add_y(UM)
    start_z(UM)
    add_core(QKV)
    y_copy(QKV).start()
    add_y(U1)
    start_z(U1)
    load_spectrum(3).wait()
    product(width, spectrum.at[1], wave_ref, True, high_ref, None)
    small_rows[...] = jnp.zeros(small_rows.shape, jnp.float32)
    small_rows[:TAP_ROWS, pl.ds(pl.multiple_of(place.s * width, LANES), width)] = first_positions(
        width, TAP_ROWS, from_ref, high_ref, None
    )
    decay_gradients(0, length, ssm_ref, decay_ref, ssm_ref_all)
    add_y(QKV)
    start_z(QKV)
    y_copy(OUT).start()
    add_z(D1)
    add_z(DM)
    decay_gradients(1, length, ssm_ref, decay_ref, ssm_ref_all)
    add_z(UM)
    add_z(U1)
    add_y(OUT)
    start_z(OUT)
    decay_gradients(2, length, ssm_ref, decay_ref, ssm_ref_all)
    over_peers(lambda step: to_peer(ssm_ref_all, ssm_all, ss_s, ss_r, step).start())
    gn_copy.wait_recv()
    for k in (D1, DM, UM, U1):
        last_copy(k).start()

    def norm_back(index, sums):
        rows = pl.ds(pl.multiple_of(index * 32, 32), 32)
        normal, inverse = layer_norm_parts(token_ref[rows, :].astype(jnp.float32))
        upstream = gn_own[rows, :] + gn_last[rows, :].astype(jnp.float32)
        into, gain, bias = layer_norm_back(upstream, normal, inverse, small_t[TAP_ROWS : TAP_ROWS + 1, :])
        input_out[rows, :] = residual_ref[rows, :] + into
        return sums[0] + gain, sums[1] + bias

    zero = jnp.sum(norm_two_ref[...], axis=0, keepdims=True) * 0.0
    gain, bias = lax.fori_loop(0, own_rows // 32, norm_back, (zero, zero), unroll=4)
    small_rows[TAP_ROWS : TAP_ROWS + 1, :] = gain
    small_rows[TAP_ROWS + 1 : TAP_ROWS + 2, :] = bias
    small_rows[TAP_ROWS + 2 : TAP_ROWS + 4, :] = norm_two_ref[...]
    small_ref[...] = small_rows[...].T.astype(jnp.bfloat16).reshape(small_ref.shape)
    over_peers(lambda step: to_peer(small_ref, small_all, sm_s, sm_r, step).start())
    add_z(QKV)
    last_copy(QKV).start()
    add_z(OUT)
    last_copy(OUT).start()

    over_peers(lambda step: from_peer(ssm_all, ss_s, ss_r, step).wait_recv())
    ssm_all[place.d] = ssm_ref_all[place.d]
    total = ssm_all[0]
    for index in range(1, 16):
        total = total + ssm_all[index]
    ssm_sum[place.d] = total
    over_peers(lambda step: share(step).start())
    over_peers(lambda step: from_peer(small_all, sm_s, sm_r, step).wait_recv())

    def add_small(step, total):
        return total + small_all[(place.d + step) % 16].astype(jnp.float32)

    small_sum[...] = lax.fori_loop(1, 16, add_small, small_ref[place.d].astype(jnp.float32)).astype(jnp.bfloat16)
    small_copy.start()
    for k in range(count):
        finish(k)
    over_peers(lambda step: from_peer(ssm_sum, sg_s, sg_r, step).wait_recv())
    ssm_out[...] = ssm_sum[...]
    small_copy.wait_recv()
    small_out[...] = small_sum[...].astype(jnp.float32) + small_last[...].astype(jnp.float32)

    for k in range(count):
        for h in range(piece_halves(k)):
            core_copy(k, h).wait_send()
        if piece_halves(k) == TWO:
            x_copy(k).wait_send()
        y_copy(k).wait_send()
        for step in range(1, 4):
            z_copy(k, step).wait_send()
        last_copy(k).wait_send()
    for copy in (gn_copy, small_copy):
        copy.wait_send()
    over_peers(lambda step: to_peer(small_ref, small_all, sm_s, sm_r, step).wait_send())
    over_peers(lambda step: to_peer(ssm_ref_all, ssm_all, ss_s, ss_r, step).wait_send())
    over_peers(lambda step: share(step).wait_send())


def backward_mixer(
    gated_grad, query, value, conv, shifted, kernel_w, taps_w, keys_w, mixed_w, ssm, to_table, from_table, normed, qkv, tokens,
    residual, small, norm_two, down, up, out,
):
    f32, low = jnp.float32, jnp.bfloat16
    count = len(PIECES)
    length, width = conv.shape
    own_rows, model = tokens.shape
    owned = down.shape[3]
    waves = (RADIX, 2 * HALF, width)
    vmem, anywhere = pl.BlockSpec(memory_space=pltpu.VMEM), pl.BlockSpec(memory_space=pl.ANY)
    results, near, from_x, from_y, from_z, final, last = [], [], [], [], [], [], []
    for k, (_, _, columns, way) in enumerate(PIECES):
        halves = piece_halves(k)
        part = columns // halves
        whole = way == "whole"
        results.append(jax.ShapeDtypeStruct((owned, part) if whole else (TWO, owned, part), f32 if whole else low))
        near.append(pltpu.VMEM((halves, FOUR, TWO, owned, part), low))
        if halves == TWO:
            from_x.append(pltpu.VMEM((FOUR, TWO, owned, part), low))
        from_y.append(pltpu.VMEM((FOUR, owned, part), low))
        from_z.append(pltpu.VMEM((3, owned, part), low))
        final.append(pltpu.VMEM((owned, part), low))
        last.append(pltpu.VMEM((owned, part), low))
    dma = pltpu.SemaphoreType.DMA
    slots = (16, 8, width)
    packed = (16, owned, LANES)
    results += [
        jax.ShapeDtypeStruct(packed[1:], f32),
        jax.ShapeDtypeStruct(slots, f32),
        jax.ShapeDtypeStruct((own_rows, model), f32),
    ]
    return pl.pallas_call(
        backward_body,
        out_shape=tuple(results),
        in_specs=[vmem, anywhere, anywhere, vmem, vmem]
        + [anywhere] * 4
        + [vmem] * 3
        + [anywhere] * 4
        + [vmem] * 2
        + [anywhere] * 3,
        out_specs=(vmem,) * len(results),
        scratch_shapes=near
        + from_x
        + from_y
        + from_z
        + final
        + last
        + [
            pltpu.VMEM((length, model), low),
            pltpu.VMEM((model, 3 * width), low),
            pltpu.VMEM((own_rows, model), low),
            pltpu.VMEM((own_rows, model), f32),
            pltpu.VMEM((2, FOUR, TWO, owned, 1536), low),
            pltpu.VMEM((length, width), f32),
            pltpu.VMEM((length, width), f32),
            pltpu.VMEM((2,) + waves, f32),
            pltpu.VMEM((length, width), f32),
            pltpu.VMEM((length, width), f32),
            pltpu.VMEM(waves, f32),
            pltpu.VMEM(waves, low),
            pltpu.VMEM(waves, f32),
            pltpu.VMEM((length, 3 * width), low),
            pltpu.VMEM((FOUR, TWO, TWO, owned, 3 * width), low),
            pltpu.VMEM((own_rows, model), low),
            pltpu.VMEM((own_rows, model), f32),
            pltpu.VMEM((own_rows, model), low),
            pltpu.VMEM((LANES, model), f32),
            pltpu.VMEM(packed, low),
            pltpu.VMEM(packed, low),
            pltpu.VMEM(packed[1:], low),
            pltpu.VMEM(packed[1:], low),
            pltpu.VMEM(slots, f32),
            pltpu.VMEM(slots, f32),
            pltpu.VMEM(slots, f32),
            dma((4,)),
            dma((4,)),
            dma((2, TWO)),
            dma((count, TWO)),
            dma((count, TWO)),
        ]
        + [dma((count,))] * 4
        + [dma((count, 3))] * 2
        + [dma((count,))] * 2
        + [dma((16,))] * 6
        + [dma((3,))] * 2,
        compiler_params=pltpu.CompilerParams(collective_id=1, has_side_effects=True, vmem_limit_bytes=VMEM_LIMIT),
        name="backward_mixer",
    )(
        gated_grad, query, value, conv, shifted, kernel_w, taps_w, keys_w, mixed_w, ssm, to_table, from_table, normed, qkv, tokens,
        residual, small, norm_two, down, up, out,
    )


def adam_parts(param, first, second, gradient, learn_rate, decay_weight):
    first_new = BETA_ONE * first + (1.0 - BETA_ONE) * gradient
    second_new = BETA_TWO * second + (1.0 - BETA_TWO) * gradient * gradient
    first_hat = first_new / (1.0 - BETA_ONE**STEP_COUNT)
    second_hat = second_new / (1.0 - BETA_TWO**STEP_COUNT)
    step = learn_rate * (first_hat / (jnp.sqrt(second_hat) + ADAM_EPS) + decay_weight * param)
    return step, first_new, second_new


def adam_body(
    early_sum, down_last, up_last, down_next, up_next, out_sum, qkv_sum, small_sum, ssm_sum,
    attn_p, mlp_p, norm_p, tap_p, ssm_p, attn_m, mlp_m, norm_m, tap_m, ssm_m,
    attn_step, attn_new, mlp_step, mlp_new, norm_step, norm_new, tap_step, tap_new, ssm_step, ssm_new,
    *, scale,
):
    f32 = jnp.float32
    width = out_sum.shape[2]

    def attn(start, gradient):
        cols = slice(start, start + width)
        attn_step[:, cols], attn_new[0, :, cols], attn_new[1, :, cols] = adam_parts(
            attn_p[:, cols].astype(f32), attn_m[0, :, cols], attn_m[1, :, cols], gradient.astype(f32) * scale,
            LEARN_RATE, DECAY_RATE,
        )

    def mlp(plane, start, source, slot):
        count = source.shape[-1]
        for begin in range(0, count, width):
            gradient = source[:, begin : begin + width] if slot is None else source[slot, :, begin : begin + width]
            cols = slice(start + begin, start + begin + width)
            mlp_step[plane, :, cols], mlp_new[0, plane, :, cols], mlp_new[1, plane, :, cols] = adam_parts(
                mlp_p[plane, :, cols].astype(f32), mlp_m[0, plane, :, cols], mlp_m[1, plane, :, cols],
                gradient.astype(f32) * scale, LEARN_RATE, DECAY_RATE,
            )

    for half in range(2):
        for place in range(3):
            attn((2 * place + half) * width, qkv_sum[half, :, place * width : (place + 1) * width])
        attn((6 + half) * width, out_sum[half])
        mlp(0, up_last.shape[2] * 2 + half * up_last.shape[2], up_last, half)
    for piece in range(early_sum.shape[0]):
        mlp(1 - piece % 2, piece // 2 * HIDDEN_BLOCK, early_sum, piece)
    mlp(0, HIDDEN_BLOCK, up_next, None)
    mlp(1, HIDDEN_BLOCK, down_next, None)
    mlp(1, down_last.shape[1], down_last, None)
    tap_step[...], tap_new[0], tap_new[1] = adam_parts(
        tap_p[...].astype(f32), tap_m[0], tap_m[1], small_sum[:, :TAP_ROWS] * scale, LEARN_RATE, DECAY_RATE
    )
    small = small_sum[...].T * scale
    norm_step[...], norm_new[0], norm_new[1] = adam_parts(
        norm_p[...].astype(f32), norm_m[0], norm_m[1], small[TAP_ROWS : TAP_ROWS + 4], LEARN_RATE, 0.0
    )
    for plane in range(2):
        gradient = ssm_sum[plane * 8 : plane * 8 + 8].reshape(ssm_p.shape[1:]) * scale
        ssm_step[plane], ssm_new[0, plane], ssm_new[1, plane] = adam_parts(
            ssm_p[plane], ssm_m[0, plane], ssm_m[1, plane], gradient, SSM_LEARN_RATE, 0.0
        )


def adam_all(sums, params, moments, scale):
    vmem = pl.BlockSpec(memory_space=pltpu.VMEM)
    outs = []
    for param, moment in zip(params, moments):
        outs += [jax.ShapeDtypeStruct(param.shape, jnp.float32), jax.ShapeDtypeStruct(moment.shape, jnp.float32)]
    return pl.pallas_call(
        partial(adam_body, scale=scale),
        out_shape=tuple(outs),
        in_specs=[vmem] * (len(sums) + 2 * len(params)),
        out_specs=(vmem,) * len(outs),
        compiler_params=pltpu.CompilerParams(vmem_limit_bytes=VMEM_LIMIT),
        name="adam",
    )(*sums, *params, *moments)


def turned_last(value):
    return jnp.swapaxes(value, -1, -2)


def per_device_split(
    tokens,
    cotangent,
    attn_weight,
    mlp_weight,
    norms,
    taps,
    ssm_params,
    attn_moments,
    mlp_moments,
    norm_moments,
    tap_moments,
    ssm_moments,
):
    f32, low = jnp.float32, jnp.bfloat16
    rows, width = tokens.shape[1:]
    shares = lax.axis_size("seq")
    owners = lax.axis_size("dp")
    length = rows * shares
    part = width // shares
    tap_count = taps.shape[0]
    to_table, from_table = map(jnp.asarray, transform_tables())

    owned = attn_weight.shape[0]
    small = jnp.concatenate([taps, norms, jnp.zeros((LANES - 4 - tap_count, owned), low)]).T
    ssm_turned = jnp.swapaxes(ssm_params, 1, 2)
    (
        qkv_full, _, _, small_full, normed_low, query, value, conv, shifted, kernel_w, taps_w, keys_w, mixed_w,
        layer_out, grad_residual, grad_norm_two, grad_gated, grad_up, grad_down, grad_out, early_sums,
    ) = forward_layer(
        tokens[0], cotangent[0], attn_weight, mlp_weight, small, ssm_turned,
        to_table, from_table,
    )
    scale = 1.0 / math.sqrt(owners * length)
    sums = backward_mixer(
        grad_gated, query, value, conv, shifted, kernel_w, taps_w, keys_w, mixed_w, ssm_turned, to_table, from_table,
        normed_low, qkv_full.reshape(width, 3 * part), tokens[0], grad_residual, small_full, grad_norm_two,
        grad_down, grad_up, grad_out,
    )
    (
        attn_step, attn_new, mlp_step, mlp_new, norms_step, norm_new, taps_step, tap_new, ssm_step, ssm_new
    ) = adam_all(
        (early_sums,) + tuple(sums[:8]),
        (attn_weight, mlp_weight, norms, taps.T, ssm_turned),
        (attn_moments, mlp_moments, norm_moments, turned_last(tap_moments), turned_last(ssm_moments)),
        scale,
    )
    taps_step, tap_new, ssm_step, ssm_new = map(turned_last, (taps_step, tap_new, ssm_step, ssm_new))
    input_grad = sums[8]
    return (
        layer_out[None],
        input_grad[None],
        attn_step,
        attn_new,
        mlp_step,
        mlp_new,
        norms_step,
        norm_new,
        taps_step,
        tap_new,
        ssm_step,
        ssm_new,
    )


def solution(mesh):
    fits = (mesh.shape["seq"], mesh.shape["dp"]) == (2, 16)

    def chosen(tokens, cotangent, attn_weight, mlp_weight, norms, taps, *others):
        fast = fits and tokens.shape[1:] == (RADIX * HALF // 2, 6 * LANES) and taps.shape[0] == TAP_ROWS
        plan = per_device_split if fast else per_device
        return plan(tokens, cotangent, attn_weight, mlp_weight, norms, taps, *others)

    return jax.shard_map(
        chosen,
        mesh=mesh,
        in_specs=(
            P("dp", "seq", None),
            P("dp", "seq", None),
            P("dp", None),
            P(None, "dp", None),
            P(None, "dp"),
            P(None, "dp"),
            P(None, "seq", None),
            P(None, "dp", None),
            P(None, None, "dp", None),
            P(None, None, "dp"),
            P(None, None, "dp"),
            P(None, None, "seq", None),
        ),
        out_specs=(
            P("dp", "seq", None),
            P("dp", "seq", None),
            P("dp", None),
            P(None, "dp", None),
            P(None, "dp", None),
            P(None, None, "dp", None),
            P(None, "dp"),
            P(None, None, "dp"),
            P(None, "dp"),
            P(None, None, "dp"),
            P(None, "seq", None),
            P(None, None, "seq", None),
        ),
        check_vma=False,
    )
```

```python
from functools import partial
import math

import jax
import jax.numpy as jnp
import ml_dtypes
import numpy as np
from jax import lax
from jax.experimental import pallas as pl
from jax.experimental.pallas import tpu as pltpu
from jax.sharding import PartitionSpec as P

DFT_ROWS = 256


EPS_NORM = 1e-05
BETA_ONE = 0.9
BETA_TWO = 0.999
ADAM_EPS = 1e-08
LEARN_RATE = 0.001
SSM_LEARN_RATE = 0.00025
DECAY_RATE = 0.1
STEP_COUNT = 10.0
HIGHEST = lax.Precision.HIGHEST


def from_behind(block, axis, distance):
    devices = range(lax.axis_size(axis))
    route = [(i - distance, i) for i in devices if i - distance in devices]
    return lax.ppermute(block, axis, route)


def as_sent(value):

    def short(part):
        return part.astype(jnp.bfloat16) if part.dtype == jnp.float32 else part

    return jax.tree.map(short, value)


def layer_norm(values, gain_row, bias_row):
    average = jnp.mean(values, axis=-1, keepdims=True)
    centred = values - average
    variance = jnp.mean(centred * centred, axis=-1, keepdims=True)
    return centred * lax.rsqrt(variance + EPS_NORM) * gain_row + bias_row


def shift_mix(rim_rows, keys_part, taps_full):
    tap_count = taps_full.shape[0]
    row_count = keys_part.shape[0]
    extended = jnp.concatenate([rim_rows, keys_part], axis=0)
    summed = jnp.zeros_like(keys_part)
    for tap_index in range(tap_count):
        begin_row = tap_count - 1 - tap_index
        summed = summed + taps_full[tap_index] * extended[begin_row : begin_row + row_count]
    return summed


def kernel_rows(length_total, ssm_full):
    inner_count = math.gcd(length_total, 128)
    outer_count = length_total // inner_count
    decay_rates = jnp.exp(ssm_full[0])
    outer_offsets = (jnp.arange(outer_count) * inner_count).astype(jnp.float32)
    inner_offsets = jnp.arange(inner_count).astype(jnp.float32)
    outer_part = ssm_full[1][:, :, None] * jnp.exp(
        -decay_rates[:, :, None] * outer_offsets[None, None, :]
    )
    inner_part = jnp.exp(-decay_rates[:, :, None] * inner_offsets[None, None, :])
    kernel = jnp.einsum("cna,cnb->cab", outer_part, inner_part, precision=HIGHEST)
    return kernel.reshape(kernel.shape[0], length_total)


def dft_tables(length_total, first_count):
    full_length = 2 * length_total
    col_count = full_length // first_count
    half_rows = first_count // 2
    row_index = jnp.arange(half_rows, dtype=jnp.int32)
    freq_index = jnp.arange(first_count, dtype=jnp.int32)
    col_index = jnp.arange(col_count, dtype=jnp.int32)
    angle_first = (
        2.0
        * math.pi
        / first_count
        * (row_index[:, None] * freq_index[None, :] % first_count).astype(jnp.float32)
    )
    angle_twist = (
        2.0 * math.pi / full_length * (freq_index[:, None] * col_index[None, :]).astype(jnp.float32)
    )
    angle_last = (
        2.0
        * math.pi
        / col_count
        * (col_index[:, None] * col_index[None, :] % col_count).astype(jnp.float32)
    )
    return (
        jnp.cos(angle_first),
        jnp.sin(angle_first),
        jnp.cos(angle_twist),
        jnp.sin(angle_twist),
        jnp.cos(angle_last),
        jnp.sin(angle_last),
    )


def forward_dft(signal, tables):
    cos_first, sin_first, cos_twist, sin_twist, cos_last, sin_last = tables
    half_rows = cos_first.shape[0]
    col_count = cos_last.shape[0]
    folded = signal.reshape(signal.shape[0], half_rows, col_count)
    real_first = jnp.einsum("cmp,mk->ckp", folded, cos_first, precision=HIGHEST)
    imaginary_first = -jnp.einsum("cmp,mk->ckp", folded, sin_first, precision=HIGHEST)
    real_twist = real_first * cos_twist + imaginary_first * sin_twist
    imaginary_twist = imaginary_first * cos_twist - real_first * sin_twist
    real_last = jnp.einsum("ckp,pq->ckq", real_twist, cos_last, precision=HIGHEST) + jnp.einsum(
        "ckp,pq->ckq", imaginary_twist, sin_last, precision=HIGHEST
    )
    imaginary_last = jnp.einsum(
        "ckp,pq->ckq", imaginary_twist, cos_last, precision=HIGHEST
    ) - jnp.einsum("ckp,pq->ckq", real_twist, sin_last, precision=HIGHEST)
    return (real_last, imaginary_last)


def inverse_dft(spectrum, tables):
    cos_first, sin_first, cos_twist, sin_twist, cos_last, sin_last = tables
    real_part, imaginary_part = spectrum
    full_length = cos_first.shape[1] * cos_last.shape[0]
    real_inner = jnp.einsum("ckq,qp->ckp", real_part, cos_last, precision=HIGHEST) - jnp.einsum(
        "ckq,qp->ckp", imaginary_part, sin_last, precision=HIGHEST
    )
    imaginary_inner = jnp.einsum(
        "ckq,qp->ckp", imaginary_part, cos_last, precision=HIGHEST
    ) + jnp.einsum("ckq,qp->ckp", real_part, sin_last, precision=HIGHEST)
    real_twist = real_inner * cos_twist - imaginary_inner * sin_twist
    imaginary_twist = imaginary_inner * cos_twist + real_inner * sin_twist
    signal = jnp.einsum("ckp,mk->cmp", real_twist, cos_first, precision=HIGHEST) - jnp.einsum(
        "ckp,mk->cmp", imaginary_twist, sin_first, precision=HIGHEST
    )
    return signal.reshape(signal.shape[0], signal.shape[1] * signal.shape[2]) / full_length


def complex_product(left, right, conjugate_left):
    left_real, left_imaginary = left
    right_real, right_imaginary = right
    if conjugate_left:
        return (
            left_real * right_real + left_imaginary * right_imaginary,
            left_real * right_imaginary - left_imaginary * right_real,
        )
    return (
        left_real * right_real - left_imaginary * right_imaginary,
        left_real * right_imaginary + left_imaginary * right_real,
    )


def adam_update(param_now, moments, gradient, learn_rate, decay_weight):
    first_new = BETA_ONE * moments[0] + (1.0 - BETA_ONE) * gradient
    second_new = BETA_TWO * moments[1] + (1.0 - BETA_TWO) * gradient * gradient
    first_hat = first_new / (1.0 - BETA_ONE**STEP_COUNT)
    second_hat = second_new / (1.0 - BETA_TWO**STEP_COUNT)
    step_size = learn_rate * (
        first_hat / (jnp.sqrt(second_hat) + ADAM_EPS) + decay_weight * param_now
    )
    return (step_size, jnp.stack([first_new, second_new]))


def per_device(
    tokens,
    cotangent,
    attn_weight,
    mlp_weight,
    norms,
    taps,
    ssm_params,
    attn_moments,
    mlp_moments,
    norm_moments,
    tap_moments,
    ssm_moments,
):
    row_count = tokens.shape[1]
    model_width = tokens.shape[2]
    group_count = lax.axis_size("seq")
    owner_count = lax.axis_size("dp")
    length_total = row_count * group_count
    attn_full, mlp_full, norm_full, taps_full = (
        lax.all_gather(attn_weight, "dp", axis=0, tiled=True),
        lax.all_gather(mlp_weight, "dp", axis=1, tiled=True),
        lax.all_gather(norms, "dp", axis=1, tiled=True),
        lax.all_gather(taps, "dp", axis=1, tiled=True),
    )
    inputs = tokens[0].astype(jnp.float32)
    cot_rows = cotangent[0].astype(jnp.float32)
    norm_values = norm_full.astype(jnp.float32)
    taps_values = taps_full.astype(jnp.float32)
    tap_count = taps_values.shape[0]
    normed, norm_pull = jax.vjp(layer_norm, inputs, norm_values[0], norm_values[1])
    normed_low = normed.astype(jnp.bfloat16)
    project = jnp.dot(
        normed_low, attn_full[:, : 3 * model_width], preferred_element_type=jnp.float32
    )
    queries = project[:, :model_width]
    keys_part = project[:, model_width : 2 * model_width]
    values = project[:, 2 * model_width :]
    rim_rows = from_behind(
        keys_part[row_count - tap_count + 1 :].astype(jnp.bfloat16), "seq", 1
    ).astype(jnp.float32)
    shifted, shift_pull = jax.vjp(shift_mix, rim_rows, keys_part, taps_values)
    mixed_rows = (shifted * values).astype(jnp.bfloat16)
    moved_in = lax.all_to_all(mixed_rows.T, "seq", split_axis=0, concat_axis=1, tiled=True).astype(
        jnp.float32
    )
    tables = dft_tables(length_total, DFT_ROWS)
    kernel, kernel_pull = jax.vjp(partial(kernel_rows, length_total), ssm_params)
    kernel_freq = forward_dft(kernel, tables)
    input_freq = forward_dft(moved_in, tables)
    conv_channels = inverse_dft(complex_product(input_freq, kernel_freq, False), tables)
    conv_back = lax.all_to_all(
        conv_channels.astype(jnp.bfloat16), "seq", split_axis=1, concat_axis=0, tiled=True
    )
    conv_rows = conv_back.T.astype(jnp.float32)
    gated_rows = (queries * conv_rows).astype(jnp.bfloat16)
    branch = jnp.dot(
        gated_rows, attn_full[:, 3 * model_width :], preferred_element_type=jnp.float32
    )
    residual_one = inputs + branch
    normed_two, norm_two_pull = jax.vjp(layer_norm, residual_one, norm_values[2], norm_values[3])
    normed_two_low = normed_two.astype(jnp.bfloat16)
    before = jnp.dot(normed_two_low, mlp_full[0], preferred_element_type=jnp.float32)
    active, gelu_pull = jax.vjp(jax.nn.gelu, before)
    active_low = active.astype(jnp.bfloat16)
    mlp_out = jnp.einsum("tf,df->td", active_low, mlp_full[1], preferred_element_type=jnp.float32)
    layer_out = (residual_one + mlp_out).astype(jnp.bfloat16)
    attn_back, mlp_back = (
        lax.all_gather(attn_weight, "dp", axis=0, tiled=True),
        lax.all_gather(mlp_weight, "dp", axis=1, tiled=True),
    )
    grad_after = cotangent[0]
    grad_active = jnp.dot(grad_after, mlp_back[1], preferred_element_type=jnp.float32)
    grad_down = jnp.einsum("td,tf->df", grad_after, active_low, preferred_element_type=jnp.float32)
    grad_before = gelu_pull(grad_active)[0].astype(jnp.bfloat16)
    grad_up = jnp.einsum(
        "td,tf->df", normed_two_low, grad_before, preferred_element_type=jnp.float32
    )
    grad_normed_two = jnp.einsum(
        "tf,df->td", grad_before, mlp_back[0], preferred_element_type=jnp.float32
    )
    grad_residual_part, grad_gain_two, grad_bias_two = norm_two_pull(grad_normed_two)
    grad_residual = cot_rows + grad_residual_part
    grad_branch = grad_residual.astype(jnp.bfloat16)
    grad_out = jnp.einsum("td,te->de", gated_rows, grad_branch, preferred_element_type=jnp.float32)
    grad_gated = jnp.einsum(
        "te,de->td",
        grad_branch,
        attn_back[:, 3 * model_width :],
        preferred_element_type=jnp.float32,
    )
    grad_queries = grad_gated * conv_rows
    grad_conv = (grad_gated * queries).astype(jnp.bfloat16)
    grad_moved = lax.all_to_all(grad_conv.T, "seq", split_axis=0, concat_axis=1, tiled=True).astype(
        jnp.float32
    )
    grad_freq = forward_dft(grad_moved, tables)
    grad_input = inverse_dft(complex_product(kernel_freq, grad_freq, True), tables)
    grad_kernel = inverse_dft(complex_product(input_freq, grad_freq, True), tables)
    grad_ssm_local = kernel_pull(grad_kernel)[0]
    grad_ssm = lax.psum(grad_ssm_local, "dp")
    grad_mixed_back = lax.all_to_all(
        grad_input.astype(jnp.bfloat16), "seq", split_axis=1, concat_axis=0, tiled=True
    )
    grad_mixed = grad_mixed_back.T.astype(jnp.float32)
    grad_shifted = grad_mixed * values
    grad_values = grad_mixed * shifted
    grad_rim, grad_keys, grad_taps = shift_pull(grad_shifted)
    returned = from_behind(as_sent(grad_rim), "seq", -1).astype(grad_rim.dtype)
    grad_keys = grad_keys + jnp.pad(returned, ((row_count - tap_count + 1, 0), (0, 0)))
    grad_project = jnp.concatenate([grad_queries, grad_keys, grad_values], axis=1).astype(
        jnp.bfloat16
    )
    grad_qkv = jnp.einsum("td,te->de", normed_low, grad_project, preferred_element_type=jnp.float32)
    grad_normed = jnp.einsum(
        "te,de->td",
        grad_project,
        attn_back[:, : 3 * model_width],
        preferred_element_type=jnp.float32,
    )
    grad_input_part, grad_gain_one, grad_bias_one = norm_pull(grad_normed)
    input_grad = grad_residual + grad_input_part
    grad_attn = jnp.concatenate([grad_qkv, grad_out], axis=1)
    grad_mlp = jnp.stack([grad_up, grad_down])
    grad_norms = jnp.stack([grad_gain_one, grad_bias_one, grad_gain_two, grad_bias_two])
    owned_part = (
        lax.psum_scatter(
            grad_attn.astype(jnp.bfloat16), "dp", scatter_dimension=0, tiled=True
        ).astype(jnp.float32),
        lax.psum_scatter(
            grad_mlp.astype(jnp.bfloat16), "dp", scatter_dimension=1, tiled=True
        ).astype(jnp.float32),
        lax.psum_scatter(
            grad_norms.astype(jnp.bfloat16), "dp", scatter_dimension=1, tiled=True
        ).astype(jnp.float32),
        lax.psum_scatter(
            grad_taps.astype(jnp.bfloat16), "dp", scatter_dimension=1, tiled=True
        ).astype(jnp.float32),
    )
    summed = (
        lax.psum(owned_part[0].astype(jnp.bfloat16), "seq").astype(jnp.float32),
        lax.psum(owned_part[1].astype(jnp.bfloat16), "seq").astype(jnp.float32),
        lax.psum(owned_part[2].astype(jnp.bfloat16), "seq").astype(jnp.float32),
        lax.psum(owned_part[3].astype(jnp.bfloat16), "seq").astype(jnp.float32),
    )
    grad_scale = 1.0 / math.sqrt(owner_count * length_total)
    attn_step, attn_moments_new = adam_update(
        attn_weight.astype(jnp.float32),
        attn_moments,
        summed[0] * grad_scale,
        LEARN_RATE,
        DECAY_RATE,
    )
    mlp_step, mlp_moments_new = adam_update(
        mlp_weight.astype(jnp.float32), mlp_moments, summed[1] * grad_scale, LEARN_RATE, DECAY_RATE
    )
    norms_step, norm_moments_new = adam_update(
        norms.astype(jnp.float32), norm_moments, summed[2] * grad_scale, LEARN_RATE, 0.0
    )
    taps_step, tap_moments_new = adam_update(
        taps.astype(jnp.float32), tap_moments, summed[3] * grad_scale, LEARN_RATE, DECAY_RATE
    )
    ssm_step, ssm_moments_new = adam_update(
        ssm_params, ssm_moments, grad_ssm * grad_scale, SSM_LEARN_RATE, 0.0
    )
    return (
        layer_out[None],
        input_grad[None],
        attn_step,
        attn_moments_new,
        mlp_step,
        mlp_moments_new,
        norms_step,
        norm_moments_new,
        taps_step,
        tap_moments_new,
        ssm_step,
        ssm_moments_new,
    )


LANES = 128
RADIX = 8
HALF = 128


def transform_tables():
    rows = np.arange(HALF)
    length = RADIX * HALF
    waves = RADIX * rows[None, :, None] + np.arange(RADIX)[:, None, None] + 0.25
    angles = 2.0 * np.pi * np.mod(rows[None, None, :] * waves, length) / length
    cosines, sines = np.cos(angles), np.sin(angles)
    full = np.concatenate(
        [np.concatenate([cosines, sines], axis=2), np.concatenate([-sines, cosines], axis=2)], axis=1
    )


    def parts(matrix):
        matrix = matrix.astype(np.float32)
        high = matrix.astype(ml_dtypes.bfloat16)
        rest = (matrix - high.astype(np.float32)).astype(ml_dtypes.bfloat16)
        return np.stack([high, rest])

    return parts(full), parts(np.swapaxes(full, 1, 2))


def turned(value, angle):
    real, imaginary = value
    cosine, sine = math.cos(angle), math.sin(angle)
    if abs(sine) < 1e-12:
        return (real, imaginary) if cosine > 0 else (-real, -imaginary)
    if abs(cosine) < 1e-12:
        return (-imaginary, real) if sine > 0 else (imaginary, -real)
    return (real * cosine - imaginary * sine, real * sine + imaginary * cosine)


def small_transform(values, sign):
    count = len(values)
    if count == 1:
        return values
    even = small_transform(values[::2], sign)
    odd = small_transform(values[1::2], sign)
    low, high = [], []
    for index in range(count // 2):
        (er, ei), (tr, ti) = even[index], turned(odd[index], sign * 2.0 * math.pi * index / count)
        low.append((er + tr, ei + ti))
        high.append((er - tr, ei - ti))
    return low + high


def dot(left, right):
    return jnp.dot(left, right, preferred_element_type=jnp.float32)


def keep_parts(high_ref, low_ref, wave, row, cols, value):
    high = value.astype(jnp.bfloat16)
    high_ref[wave, pl.ds(row, 16), cols] = high
    if low_ref is not None:
        low_ref[wave, pl.ds(row, 16), cols] = (value - high.astype(jnp.float32)).astype(jnp.bfloat16)


def table_dot(table_high, table_low, high_ref, low_ref, wave):
    high = high_ref[wave]
    total = dot(table_high, high) + dot(table_low, high)
    return total if low_ref is None else total + dot(table_high, low_ref[wave])


def each_tile(width, rows, step, body):
    for block in range(width // LANES):

        def one(index, carry, block=block):
            body(pl.multiple_of(index * step, step), pl.ds(block * LANES, LANES))
            return carry

        lax.fori_loop(0, rows // step, one, 0)


def to_waves(width, read, used, w_ref, high_ref, low_ref, store):
    def first(row, cols):
        inputs = []
        for part in range(used):
            x = read(part * HALF, row, cols)
            angle = -2.0 * math.pi * part / 32.0
            inputs.append((x * math.cos(angle), x * math.sin(angle)) if part else (x, jnp.zeros_like(x)))
        while len(inputs) < RADIX:
            inputs.append((jnp.zeros_like(x), jnp.zeros_like(x)))
        for wave, value in enumerate(small_transform(inputs, -1.0)):
            for place, part in enumerate(value):
                keep_parts(high_ref, low_ref, wave, row + place * HALF, cols, part)

    each_tile(width, HALF, 16, first)

    def second(wave, carry):
        store(wave, table_dot(w_ref[0, wave], w_ref[1, wave], high_ref, low_ref, wave))
        return carry

    lax.fori_loop(0, RADIX, second, 0)


def product(width, left_ref, right_ref, conjugate, high_ref, low_ref):
    sign = -1.0 if conjugate else 1.0

    def one(wave, carry):
        def tile(row, cols):
            lr, li = left_ref[wave, pl.ds(row, 16), cols], left_ref[wave, pl.ds(row + HALF, 16), cols] * sign
            rr, ri = right_ref[wave, pl.ds(row, 16), cols], right_ref[wave, pl.ds(row + HALF, 16), cols]
            for place, part in enumerate((lr * rr - li * ri, lr * ri + li * rr)):
                keep_parts(high_ref, low_ref, wave, row + place * HALF, cols, part)

        each_tile(width, HALF, 16, tile)
        return carry

    lax.fori_loop(0, RADIX, one, 0)


def from_waves(width, w_ref, high_ref, low_ref, back_ref, put):
    def second(wave, carry):
        back_ref[wave] = table_dot(w_ref[0, wave], w_ref[1, wave], high_ref, low_ref, wave)
        return carry

    lax.fori_loop(0, RADIX, second, 0)
    scale = 1.0 / (RADIX * HALF)

    def first(row, cols):
        values = [
            (back_ref[wave, pl.ds(row, 16), cols], back_ref[wave, pl.ds(row + HALF, 16), cols])
            for wave in range(RADIX)
        ]
        for part, (real, imaginary) in enumerate(small_transform(values, 1.0)):
            angle = 2.0 * math.pi * part / 32.0
            put(part * HALF, row, cols, real * (math.cos(angle) * scale) - imaginary * (math.sin(angle) * scale))

    each_tile(width, HALF, 16, first)


def first_positions(width, count, w_ref, high_ref, low_ref):
    total = jnp.zeros((count, width), jnp.float32)
    for wave in range(RADIX):
        total = total + table_dot(w_ref[0, wave, :count, :], w_ref[1, wave, :count, :], high_ref, low_ref, wave)
    return total * (1.0 / (RADIX * HALF))


FINE = 32


def decay_sums(block, length, ssm_ref, out_ref):
    modes = ssm_ref.shape[1]
    steps = length // FINE
    cols = pl.ds(block * LANES, LANES)
    out_ref[:, cols] = jnp.zeros((length, LANES), jnp.float32)
    offsets = lax.broadcasted_iota(jnp.int32, (FINE, LANES), 0).astype(jnp.float32)

    def group(index, carry):
        base = pl.multiple_of(index * 8, 8)
        rates = jnp.exp(ssm_ref[0, pl.ds(base, 8), cols])
        leaps = jnp.exp(-rates * FINE)
        weights = ssm_ref[1, pl.ds(base, 8), cols]
        terms = tuple(weights[i : i + 1] * jnp.exp(-rates[i : i + 1] * offsets) for i in range(8))
        leap_rows = [jnp.broadcast_to(leaps[i : i + 1], (FINE, LANES)) for i in range(8)]

        def step(number, terms):
            rows = pl.ds(pl.multiple_of(number * FINE, FINE), FINE)
            total = out_ref[rows, cols]
            for term in terms:
                total = total + term
            out_ref[rows, cols] = total
            return tuple(term * leap for term, leap in zip(terms, leap_rows))

        lax.fori_loop(0, steps, step, terms, unroll=4)
        return carry

    lax.fori_loop(0, modes // 8, group, 0)


def decay_gradients(block, length, ssm_ref, grad_ref, out_ref):
    modes = ssm_ref.shape[1]
    steps = length // FINE
    cols = pl.ds(block * LANES, LANES)
    offsets = lax.broadcasted_iota(jnp.int32, (FINE, LANES), 0).astype(jnp.float32)

    def group(index, carry):
        base = pl.multiple_of(index * 8, 8)
        rates = jnp.exp(ssm_ref[0, pl.ds(base, 8), cols])
        leaps = jnp.exp(-rates * FINE)
        plain_rows, slope_rows = [], []
        for modes_now in ((0, 1, 2, 3), (4, 5, 6, 7)):
            zero = offsets * 0.0
            leap_rows = [jnp.broadcast_to(leaps[i : i + 1], (FINE, LANES)) for i in modes_now]

            def step(number, sums, leap_rows=leap_rows):
                rows = grad_ref[pl.ds(pl.multiple_of((steps - 1 - number) * FINE, FINE), FINE), cols]
                return tuple((v * leap + rows, w * leap + v) for (v, w), leap in zip(sums, leap_rows))

            sums = lax.fori_loop(0, steps, step, tuple((zero, zero) for _ in modes_now), unroll=8)
            for i, (v, w) in zip(modes_now, sums):
                fine = jnp.exp(-rates[i : i + 1] * offsets)
                plain = fine * v
                slope = fine * w * (leaps[i : i + 1] * FINE) + plain * offsets
                plain_rows.append(jnp.sum(plain, axis=0, keepdims=True))
                slope_rows.append(jnp.sum(slope, axis=0, keepdims=True))
        out_ref[modes // 8 + index, :, cols] = jnp.concatenate(plain_rows, axis=0)
        out_ref[index, :, cols] = (
            -ssm_ref[1, pl.ds(base, 8), cols] * rates * jnp.concatenate(slope_rows, axis=0)
        )
        return carry

    lax.fori_loop(0, modes // 8, group, 0)


def layer_norm_parts(values):
    average = jnp.mean(values, axis=-1, keepdims=True)
    centred = values - average
    variance = jnp.mean(centred * centred, axis=-1, keepdims=True)
    inverse = lax.rsqrt(variance + EPS_NORM)
    return centred * inverse, inverse


def layer_norm_back(upstream, normal, inverse, gain_row):
    weighted = upstream * gain_row
    average = jnp.mean(weighted, axis=-1, keepdims=True)
    overlap = jnp.mean(weighted * normal, axis=-1, keepdims=True)
    into = (weighted - average - normal * overlap) * inverse
    return into, jnp.sum(upstream * normal, axis=0, keepdims=True), jnp.sum(upstream, axis=0, keepdims=True)


MESH = pl.DeviceIdType.MESH
TWO, FOUR = 2, 4
TAP_ROWS = 64
VMEM_LIMIT = 62 * 1024 * 1024


class Place:
    def __init__(self):
        self.s, self.d = lax.axis_index("seq"), lax.axis_index("dp")
        self.z, self.y, self.c = self.d // 4, (self.d // 2) % 2, self.d % 2

    def over_x(self):
        return (1 - self.s, self.d)

    def over_y(self):
        return (self.s, self.d + 2 - 4 * self.y)

    def over_core(self):
        return (self.s, self.d + 1 - 2 * self.c)

    def along_z(self, step):
        return (self.s, (self.d + 4 * step) % 16)

    def owner(self, index):
        return (self.s, index)


def send(source, target, send_sem, recv_sem, device):
    return pltpu.make_async_remote_copy(
        src_ref=source, dst_ref=target, send_sem=send_sem, recv_sem=recv_sem, device_id=device, device_id_type=MESH
    )


def greet_all(place):
    barrier = pltpu.get_barrier_semaphore()
    pl.semaphore_signal(barrier, inc=1, device_id=place.over_x(), device_id_type=MESH)

    def greet(step, carry):
        pl.semaphore_signal(
            barrier, inc=1, device_id=place.owner((place.d + step) % 16), device_id_type=MESH
        )
        return carry

    lax.fori_loop(1, 16, greet, 0)
    pl.semaphore_wait(barrier, 16)


def add_blocks(put, sources, count):
    def one(index, carry):
        total = sources[0](index).astype(jnp.float32)
        for source in sources[1:]:
            total = total + source(index).astype(jnp.float32)
        put(index, total)
        return carry

    lax.fori_loop(0, count, one, 0)


WEIGHTS = (
    ("out", 0, 768, "whole"),
    ("up", 0, 1536, "halved"),
    ("down", 0, 1536, "whole"),
    ("up", 1536, 1536, "halved"),
    ("down", 1536, 768, "whole"),
    ("down", 2304, 768, "whole"),
)
OUT_W, UP_FIRST, DOWN_FIRST, UP_LAST, DOWN_THIRD, DOWN_LAST, QKV_W = range(len(WEIGHTS) + 1)
HIDDEN_BLOCK = 768
EARLY = 1


def dot_right(left, right):
    return lax.dot_general(left, right, (((1,), (1,)), ((), ())), preferred_element_type=jnp.float32)


def dot_left(left, right):
    return lax.dot_general(left, right, (((0,), (0,)), ((), ())), preferred_element_type=jnp.float32)


def gelu_parts(x):
    slope = math.sqrt(2.0 / math.pi)
    square = x * x
    bent = jnp.tanh(slope * x * (1.0 + 0.044715 * square))
    upper = 0.5 + 0.5 * bent
    return x * upper, upper + 0.5 * x * (1.0 - bent * bent) * (slope * (1.0 + 3.0 * 0.044715 * square))


def forward_body(
    token_ref, cotangent_hbm, attn_shard, mlp_shard, small_ref, ssm_ref, to_hbm, from_hbm,
    qkv_full, up_full, down_full, small_t, normed_ref, query_out, value_out, conv_ref, shifted_ref,
    kernel_out, taps_out, keys_out, mixed_out, layer_out, residual_grad, norm_two_out, gated_grad, up_grad, down_grad, out_grad, early_out,
    cotangent_ref, to_ref, from_ref, qkv_ref, token_all, small_all, gated_ref, rows_ref, out_full, grad_send, near, from_y, from_z, final, last,
    own_sem, z_s, z_r, y_s, y_r, x_s, x_r, core_s, core_r, small_s, small_r, side_s, side_r, store_sem, load_sem, nc_s, nc_r, ny_s, ny_r, nz_s, nz_r, nf_s, nf_r, late_sem,
):
    length, width = conv_ref.shape
    own_rows, model = token_ref.shape
    place = Place()
    f32, low = jnp.float32, jnp.bfloat16
    shards = {"up": mlp_shard.at[0], "down": mlp_shard.at[1], "out": attn_shard.at[:, pl.ds(3 * model, model)]}
    fulls = {"up": up_full, "down": down_full, "out": out_full}

    def columns(k):
        source, start, count, way = WEIGHTS[k]
        if way == "whole":
            return source, pl.ds(start, count)
        return source, pl.ds(pl.multiple_of(start + place.s * (count // 2), LANES), count // 2)

    def z_copy(k, step):
        if k == QKV_W:
            source, target = qkv_ref, qkv_full.at[place.z, place.y, place.c]
        else:
            name, cols = columns(k)
            source, target = shards[name].at[:, cols], fulls[name].at[place.z, place.y, place.c, :, cols]
        return send(source, target, z_s.at[k, step - 1], z_r.at[k, step - 1], place.along_z(step))

    def y_copy(k):
        if k == QKV_W:
            blocks = qkv_full.at[:, place.y, place.c]
        else:
            name, cols = columns(k)
            blocks = fulls[name].at[:, place.y, place.c, :, cols]
        return send(blocks, blocks, y_s.at[k], y_r.at[k], place.over_y())

    def x_copy(k):
        name, cols = columns(k)
        blocks = fulls[name].at[:, :, place.c, :, cols]
        return send(blocks, blocks, x_s.at[k], x_r.at[k], place.over_x())

    def core_copy(k):
        if k == QKV_W:
            blocks = qkv_full.at[:, :, place.c]
        else:
            name, start, count, _ = WEIGHTS[k]
            blocks = fulls[name].at[:, :, place.c, :, pl.ds(start, count)]
        return send(blocks, blocks, core_s.at[k], core_r.at[k], place.over_core())

    def own_copies():
        copies = []
        for k in range(QKV_W):
            name, cols = columns(k)
            target = fulls[name].at[place.z, place.y, place.c, :, cols]
            copies.append(pltpu.make_async_copy(shards[name].at[:, cols], target, own_sem.at[k]))
        return copies

    def start_z(k):
        for step in range(1, 4):
            z_copy(k, step).start()

    def wait_z(k):
        for step in range(1, 4):
            z_copy(k, step).wait_recv()

    def over_peers(action):
        def one(step, carry):
            action(step)
            return carry

        lax.fori_loop(1, 16, one, 0)

    def small_copy(step):
        other = (place.d + step) % 16
        return send(small_ref, small_all.at[place.d], small_s.at[other], small_r.at[place.d], place.owner(other))

    def small_arrival(step):
        other = (place.d + step) % 16
        return send(small_ref, small_all.at[other], small_s.at[other], small_r.at[other], place.owner(other))

    token_copy = send(token_ref, token_all.at[place.s], side_s.at[0], side_r.at[0], place.over_x())
    gated_copy = send(gated_ref.at[1 - place.s], rows_ref.at[place.s], side_s.at[1], side_r.at[1], place.over_x())
    grad_copy = send(grad_send, gated_grad.at[place.s], side_s.at[2], side_r.at[2], place.over_x())

    def early_y(e):
        return send(near.at[e, :, 1 - place.y], from_y.at[e], ny_s.at[e], ny_r.at[e], place.over_y())

    def early_z(e, step):
        other = (place.z + step) % 4
        return send(
            near.at[e, other, place.y], from_z.at[e, step - 1], nz_s.at[e, step - 1], nz_r.at[e, step - 1],
            place.along_z(step),
        )

    def early_last(e):
        return send(final.at[e], last.at[e], nf_s.at[e], nf_r.at[e], place.over_x())

    def early_add_y(e):
        early_y(e).wait_recv()

        def put(i, total):
            near[e, i, place.y] = total.astype(low)

        add_blocks(put, [lambda i: near[e, i, place.y], lambda i: from_y[e, i]], 4)
        for step in range(1, 4):
            early_z(e, step).start()

    def early_add_z(e):
        for step in range(1, 4):
            early_z(e, step).wait_recv()
        total = near[e, place.z, place.y].astype(f32)
        for step in range(3):
            total = total + from_z[e, step].astype(f32)
        final[e] = total.astype(low)
        early_last(e).start()

    def step_one():
        wait_z(QKV_W)
        y_copy(QKV_W).start()
        start_z(UP_FIRST)

    def step_two():
        for copy in own_copies():
            copy.wait()
        wait_z(OUT_W)
        y_copy(OUT_W).start()
        start_z(DOWN_FIRST)

    def step_three():
        y_copy(QKV_W).wait_recv()
        core_copy(QKV_W).start()

    def step_four():
        wait_z(UP_FIRST)
        y_copy(UP_FIRST).start()
        start_z(UP_LAST)

    def step_five():
        y_copy(OUT_W).wait_recv()
        core_copy(OUT_W).start()

    def step_six():
        y_copy(UP_FIRST).wait_recv()
        x_copy(UP_FIRST).start()

    def step_seven():
        wait_z(DOWN_FIRST)
        y_copy(DOWN_FIRST).start()
        start_z(DOWN_THIRD)

    def step_eight():
        wait_z(UP_LAST)
        y_copy(UP_LAST).start()
        start_z(DOWN_LAST)

    def step_nine():
        x_copy(UP_FIRST).wait_recv()
        core_copy(UP_FIRST).start()

    def step_ten():
        y_copy(DOWN_FIRST).wait_recv()
        core_copy(DOWN_FIRST).start()

    def step_eleven():
        wait_z(DOWN_THIRD)
        y_copy(DOWN_THIRD).start()
        y_copy(UP_LAST).wait_recv()
        x_copy(UP_LAST).start()

    def step_twelve():
        wait_z(DOWN_LAST)
        y_copy(DOWN_LAST).start()
        y_copy(DOWN_THIRD).wait_recv()
        core_copy(DOWN_THIRD).start()

    def step_thirteen():
        x_copy(UP_LAST).wait_recv()
        core_copy(UP_LAST).start()

    def step_fourteen():
        y_copy(DOWN_LAST).wait_recv()
        core_copy(DOWN_LAST).start()

    for j in range(3):
        cols = pl.ds(pl.multiple_of((2 * j + place.s) * width, LANES), width)
        qkv_ref[:, j * width : (j + 1) * width] = attn_shard[:, cols]
    late_copies = [
        pltpu.make_async_copy(source, target, late_sem.at[i])
        for i, (source, target) in enumerate(((to_hbm, to_ref), (from_hbm, from_ref), (cotangent_hbm, cotangent_ref)))
    ]
    greet_all(place)
    start_z(QKV_W)
    for copy in late_copies:
        copy.start()
    over_peers(lambda step: small_copy(step).start())
    token_copy.start()
    for copy in own_copies():
        copy.start()
    qkv_full[place.z, place.y, place.c] = qkv_ref[...]
    small_all[place.d] = small_ref[...]

    def mixer(line_ref, high_ref, low_ref, back_ref, proj_ref, kernel_w, other_w, keys_w):
        def keep(target):
            def store(wave, value):
                target[wave] = value

            return store

        def lines(base, row, cols):
            return line_ref[pl.ds(base + row, 16), cols]

        def column(index, cols):
            return pl.ds(index * width + cols.start, cols.size)

        stores = [
            pltpu.make_async_copy(kernel_w, kernel_out, store_sem.at[0]),
            pltpu.make_async_copy(other_w, taps_out, store_sem.at[1]),
            pltpu.make_async_copy(keys_w, keys_out, store_sem.at[2]),
            pltpu.make_async_copy(other_w, mixed_out, store_sem.at[3]),
            pltpu.make_async_copy(proj_ref.at[:, pl.ds(0, width)], query_out, store_sem.at[4]),
            pltpu.make_async_copy(proj_ref.at[:, pl.ds(2 * width, width)], value_out, store_sem.at[5]),
        ]
        for block in range(width // LANES):
            decay_sums(block, length, ssm_ref, line_ref)
            if not block:
                start_z(OUT_W)
        step_one()
        for copy in late_copies:
            copy.wait()
        to_waves(width, lines, RADIX, to_ref, high_ref, low_ref, keep(kernel_w))
        stores[0].start()
        over_peers(lambda step: small_arrival(step).wait_recv())
        small_t[...] = small_all[...].reshape(16 * small_all.shape[1], LANES).astype(f32).T
        taps_cols = pl.multiple_of(place.s * width, LANES)

        def read_taps(base, row, cols):
            taps = small_t[pl.ds(base + row, 16), pl.ds(pl.multiple_of(taps_cols + cols.start, LANES), LANES)]
            inside = lax.broadcasted_iota(jnp.int32, taps.shape, 0) + (base + row) < TAP_ROWS
            return jnp.where(inside, taps, 0.0)

        def normalize(source, begin):
            def one(index, carry):
                row = pl.multiple_of(index * 32, 32)
                normal, _ = layer_norm_parts(source[pl.ds(row, 32), :].astype(f32))
                scaled = normal * small_t[TAP_ROWS : TAP_ROWS + 1, :] + small_t[TAP_ROWS + 1 : TAP_ROWS + 2, :]
                normed_ref[pl.ds(pl.multiple_of(begin + row, 32), 32), :] = scaled.astype(low)
                return carry

            lax.fori_loop(0, own_rows // 32, one, 0, unroll=4)

        def project(begin):
            weight = qkv_full[...].reshape(model, 3 * width)

            def one(index, carry):
                row = pl.ds(pl.multiple_of(begin + index * 256, 256), 256)
                proj_ref[row, :] = dot(normed_ref[row, :], weight)
                return carry

            lax.fori_loop(0, own_rows // 256, one, 0)

        own_begin, other_begin = place.s * own_rows, (1 - place.s) * own_rows
        normalize(token_ref, own_begin)
        step_two()
        token_copy.wait_recv()
        normalize(token_all.at[1 - place.s], other_begin)
        step_three()
        to_waves(width, read_taps, 1, to_ref, high_ref, low_ref, keep(other_w))
        stores[1].start()
        core_copy(QKV_W).wait_recv()
        project(own_begin)
        project(other_begin)
        stores[4].start()
        stores[5].start()
        step_four()
        step_five()
        to_waves(
            width, lambda base, row, cols: proj_ref[pl.ds(base + row, 16), column(1, cols)],
            RADIX, to_ref, high_ref, low_ref, keep(keys_w),
        )
        stores[2].start()
        product(width, other_w, keys_w, False, high_ref, low_ref)
        step_six()

        def put_shifted(base, row, cols, value):
            rows = pl.ds(base + row, 16)
            shifted_ref[rows, cols] = value
            mixed = value * proj_ref[rows, column(2, cols)]
            line_ref[rows, cols] = mixed.astype(low).astype(f32)

        from_waves(width, from_ref, high_ref, low_ref, back_ref, put_shifted)
        step_seven()
        stores[1].wait()
        to_waves(width, lines, RADIX, to_ref, high_ref, low_ref, keep(other_w))
        stores[3].start()
        product(width, kernel_w, other_w, False, high_ref, low_ref)
        step_eight()

        def put_conv(base, row, cols, value):
            rows = pl.ds(base + row, 16)
            rounded = value.astype(low)
            conv_ref[rows, cols] = rounded
            gated = (proj_ref[rows, cols] * rounded.astype(f32)).astype(low)
            gated_ref[base // own_rows, pl.ds(base % own_rows + row, 16), cols] = gated

        from_waves(width, from_ref, high_ref, low_ref, back_ref, put_conv)
        gated_copy.start()
        for i in (0, 2, 3, 4, 5):
            stores[i].wait()

    waves = (RADIX, 2 * HALF, width)
    pl.run_scoped(
        mixer,
        pltpu.VMEM((length, width), f32),
        pltpu.VMEM(waves, low),
        pltpu.VMEM(waves, low),
        pltpu.VMEM(waves, f32),
        pltpu.VMEM((length, 3 * width), f32),
        pltpu.VMEM(waves, f32),
        pltpu.VMEM(waves, f32),
        pltpu.VMEM(waves, f32),
    )
    rows_ref[place.s] = gated_ref[place.s]

    def feed_forward(
        up_w, down_w, up_g, down_g, residual_ref, normed_two, normed_turned, cot_turned, active_ref, before_ref,
        out_sum, normed_grad,
    ):
        block_shape = up_g.shape
        blocks = up_full.shape[4] // HIDDEN_BLOCK

        def load(j):
            cols = pl.ds(j * HIDDEN_BLOCK, HIDDEN_BLOCK)
            return [
                pltpu.make_async_copy(full.at[:, :, :, :, cols], held.at[j % 2], load_sem.at[i, j % 2])
                for i, (full, held) in enumerate(((up_full, up_w), (down_full, down_w)))
            ]

        def store(j):
            cols = pl.ds(j * HIDDEN_BLOCK, HIDDEN_BLOCK)
            return [
                pltpu.make_async_copy(held, full.at[:, :, :, :, cols], store_sem.at[i])
                for i, (full, held) in enumerate(((up_grad, up_g), (down_grad, down_g)))
            ]

        def early_core(e):
            source = up_g if e % 2 else down_g
            return send(source.at[:, :, 1 - place.c], near.at[e], nc_s.at[e], nc_r.at[e], place.over_core())

        def early_add_core(e):
            source = up_g if e % 2 else down_g
            early_core(e).wait_recv()

            def put(i, total):
                near[e, i // 2, i % 2] = total.astype(low)

            add_blocks(put, [lambda i: source[i // 2, i % 2, place.c], lambda i: near[e, i // 2, i % 2]], 8)
            early_core(e).wait_send()

        step_nine()
        cot_turned[...] = cotangent_ref[...].T
        step_ten()
        core_copy(OUT_W).wait_recv()
        gated_copy.wait_recv()
        out_w = out_full[...].reshape(model, model)

        def branch(index, carry):
            rows = pl.ds(pl.multiple_of(index * 256, 256), 256)
            value = dot(rows_ref[0, rows, :], out_w[:width]) + dot(rows_ref[1, rows, :], out_w[width:])
            residual_ref[rows, :] = token_ref[rows, :].astype(f32) + value
            return carry

        lax.fori_loop(0, own_rows // 256, branch, 0)

        def normalize(index, carry):
            rows = pl.ds(pl.multiple_of(index * 32, 32), 32)
            normal, _ = layer_norm_parts(residual_ref[rows, :])
            scaled = normal * small_t[TAP_ROWS + 2 : TAP_ROWS + 3, :] + small_t[TAP_ROWS + 3 : TAP_ROWS + 4, :]
            normed_two[rows, :] = scaled.astype(low)
            return carry

        lax.fori_loop(0, own_rows // 32, normalize, 0, unroll=4)
        core_copy(UP_FIRST).wait_recv()
        core_copy(DOWN_FIRST).wait_recv()
        for copy in load(0) + load(1):
            copy.start()
        normed_turned[...] = normed_two[...].T
        step_eleven()
        for j in range(blocks):
            if j == 1:
                step_twelve()
            if j == 2:
                step_thirteen()
                core_copy(UP_LAST).wait_recv()
                core_copy(DOWN_THIRD).wait_recv()
                for copy in load(j):
                    copy.start()
                early_y(1).start()
            if j == 3:
                step_fourteen()
                early_add_y(0)
                core_copy(DOWN_LAST).wait_recv()
                for copy in load(j):
                    copy.start()
            for copy in load(j):
                copy.wait()
            up = up_w[j % 2].reshape(model, HIDDEN_BLOCK)
            down = down_w[j % 2].reshape(model, HIDDEN_BLOCK)

            def rows_of(index, carry, up=up, down=down, j=j):
                rows = pl.ds(pl.multiple_of(index * 256, 256), 256)
                active, slope = gelu_parts(dot(normed_two[rows, :], up))
                active = active.astype(low)
                active_ref[rows, :] = active
                grad_before = (dot(cotangent_ref[rows, :], down) * slope).astype(low)
                before_ref[rows, :] = grad_before
                out_part = dot_right(active, down)
                grad_part = dot_right(grad_before, up)
                if j:
                    out_part = out_part + out_sum[rows, :]
                    grad_part = grad_part + normed_grad[rows, :]
                out_sum[rows, :] = out_part
                normed_grad[rows, :] = grad_part
                return carry

            lax.fori_loop(0, own_rows // 256, rows_of, 0)
            if j == 1:
                early_add_core(0)
                early_y(0).start()
                early_add_core(1)
            if j > EARLY:
                for copy in store(j - 1):
                    copy.wait()
            down_g[...] = dot(cot_turned[...], active_ref[...]).astype(low).reshape(block_shape)
            up_g[...] = dot(normed_turned[...], before_ref[...]).astype(low).reshape(block_shape)
            if j < EARLY:
                for e in (2 * j, 2 * j + 1):
                    early_core(e).start()
            else:
                for copy in store(j):
                    copy.start()
        early_add_y(1)

        def norm_back(index, sums):
            rows = pl.ds(pl.multiple_of(index * 32, 32), 32)
            normal, inverse = layer_norm_parts(residual_ref[rows, :])
            into, gain, bias = layer_norm_back(
                normed_grad[rows, :], normal, inverse, small_t[TAP_ROWS + 2 : TAP_ROWS + 3, :]
            )
            total = cotangent_ref[rows, :].astype(f32) + into
            residual_grad[rows, :] = total
            active_ref[rows, :] = total.astype(low)
            layer_out[rows, :] = (residual_ref[rows, :] + out_sum[rows, :]).astype(low)
            return sums[0] + gain, sums[1] + bias

        zero = small_t[TAP_ROWS : TAP_ROWS + 1, :] * 0.0
        gain, bias = lax.fori_loop(0, own_rows // 32, norm_back, (zero, zero), unroll=4)
        norm_two_out[0:1, :] = gain
        norm_two_out[1:2, :] = bias
        part_shape = (2,) + out_full.shape[1:]
        other_w = out_full[pl.ds(2 * (1 - place.s), 2)].reshape(width, model)
        grad_send[...] = dot_right(active_ref[...], other_w).astype(low)
        grad_copy.start()
        own_w = out_full[pl.ds(2 * place.s, 2)].reshape(width, model)
        gated_grad[place.s] = dot_right(active_ref[...], own_w).astype(low)
        early_add_z(0)
        for h in range(2):
            out_grad[2 * h : 2 * h + 2] = dot_left(rows_ref[h], active_ref[...]).astype(low).reshape(part_shape)
        for copy in store(blocks - 1):
            copy.wait()
        early_add_z(1)
        grad_copy.wait_recv()
        for e in range(2 * EARLY):
            early_last(e).wait_recv()
            early_out[e] = final[e].astype(f32) + last[e].astype(f32)

    block = (FOUR, TWO, TWO, out_full.shape[3], HIDDEN_BLOCK)
    pl.run_scoped(
        feed_forward,
        pltpu.VMEM((2,) + block, low),
        pltpu.VMEM((2,) + block, low),
        pltpu.VMEM(block, low),
        pltpu.VMEM(block, low),
        pltpu.VMEM((own_rows, model), f32),
        pltpu.VMEM((own_rows, model), low),
        pltpu.VMEM((model, own_rows), low),
        pltpu.VMEM((model, own_rows), low),
        pltpu.VMEM((own_rows, HIDDEN_BLOCK), low),
        pltpu.VMEM((own_rows, HIDDEN_BLOCK), low),
        pltpu.VMEM((own_rows, model), f32),
        pltpu.VMEM((own_rows, model), f32),
    )

    for e in range(2 * EARLY):
        early_y(e).wait_send()
        for step in range(1, 4):
            early_z(e, step).wait_send()
        early_last(e).wait_send()
    over_peers(lambda step: small_copy(step).wait_send())
    for copy in (token_copy, gated_copy, grad_copy):
        copy.wait_send()
    for k in range(QKV_W + 1):
        for step in range(1, 4):
            z_copy(k, step).wait_send()
        y_copy(k).wait_send()
        core_copy(k).wait_send()
        if k != QKV_W and WEIGHTS[k][3] == "halved":
            x_copy(k).wait_send()


def forward_layer(tokens, cotangent, attn_shard, mlp_shard, small, ssm, to_table, from_table):
    own_rows, model = tokens.shape
    owned = attn_shard.shape[0]
    width = model // 2
    length = 2 * own_rows
    hidden = mlp_shard.shape[2]
    f32, low = jnp.float32, jnp.bfloat16
    waves = (RADIX, 2 * HALF, width)
    vmem, anywhere = pl.BlockSpec(memory_space=pltpu.VMEM), pl.BlockSpec(memory_space=pl.ANY)
    shape = jax.ShapeDtypeStruct
    owners = (FOUR, TWO, TWO, owned)
    count = len(WEIGHTS) + 1
    dma = pltpu.SemaphoreType.DMA
    outs = (
        (shape(owners + (3 * width,), low), vmem),
        (shape(owners + (hidden,), low), anywhere),
        (shape(owners + (hidden,), low), anywhere),
        (shape((LANES, model), f32), vmem),
        (shape((length, model), low), vmem),
        (shape((length, width), f32), anywhere),
        (shape((length, width), f32), anywhere),
        (shape((length, width), low), vmem),
        (shape((length, width), f32), vmem),
        (shape(waves, f32), anywhere),
        (shape(waves, f32), anywhere),
        (shape(waves, f32), anywhere),
        (shape(waves, f32), anywhere),
        (shape((own_rows, model), low), vmem),
        (shape((own_rows, model), f32), vmem),
        (shape((2, model), f32), vmem),
        (shape((2, own_rows, width), low), vmem),
        (shape(owners + (hidden,), low), anywhere),
        (shape(owners + (hidden,), low), anywhere),
        (shape(owners + (model,), low), vmem),
        (shape((2 * EARLY, owned, HIDDEN_BLOCK), f32), vmem),
    )
    return pl.pallas_call(
        forward_body,
        out_shape=tuple(out for out, _ in outs),
        in_specs=[vmem, anywhere, vmem, anywhere, vmem, vmem, anywhere, anywhere],
        out_specs=tuple(spec for _, spec in outs),
        scratch_shapes=[
            pltpu.VMEM(cotangent.shape, low),
            pltpu.VMEM(to_table.shape, low),
            pltpu.VMEM(from_table.shape, low),
            pltpu.VMEM((owned, 3 * width), low),
            pltpu.VMEM((2, own_rows, model), low),
            pltpu.VMEM((16,) + small.shape, low),
            pltpu.VMEM((2, own_rows, width), low),
            pltpu.VMEM((2, own_rows, width), low),
            pltpu.VMEM(owners + (model,), low),
            pltpu.VMEM((own_rows, width), low),
            pltpu.VMEM((2 * EARLY, FOUR, TWO, owned, HIDDEN_BLOCK), low),
            pltpu.VMEM((2 * EARLY, FOUR, owned, HIDDEN_BLOCK), low),
            pltpu.VMEM((2 * EARLY, 3, owned, HIDDEN_BLOCK), low),
            pltpu.VMEM((2 * EARLY, owned, HIDDEN_BLOCK), low),
            pltpu.VMEM((2 * EARLY, owned, HIDDEN_BLOCK), low),
            dma((count,)),
            dma((count, 3)),
            dma((count, 3)),
            dma((count,)),
            dma((count,)),
            dma((count,)),
            dma((count,)),
            dma((count,)),
            dma((count,)),
            dma((16,)),
            dma((16,)),
            dma((3,)),
            dma((3,)),
            dma((6,)),
            dma((2, 2)),
        ]
        + [dma((2 * EARLY,))] * 4
        + [dma((2 * EARLY, 3))] * 2
        + [dma((2 * EARLY,))] * 2
        + [dma((3,))],
        compiler_params=pltpu.CompilerParams(collective_id=2, has_side_effects=True, vmem_limit_bytes=VMEM_LIMIT),
        name="forward_layer",
    )(tokens, cotangent, attn_shard, mlp_shard, small, ssm, to_table, from_table)


PIECES = (
    ("down", 1536, 1536, "whole"),
    ("up", 1536, 1536, "halved"),
    ("down", 768, 768, "whole"),
    ("up", 768, 768, "whole"),
    ("out", 0, 768, "halved"),
    ("qkv", 0, 1152, "apart"),
)
D1, U1, DM, UM, OUT, QKV = range(len(PIECES))


def piece_halves(k):
    return TWO if PIECES[k][3] == "halved" else 1


def backward_body(*refs):
    count = len(PIECES)
    (
        grad_all, query_hbm, value_hbm, conv_ref, shifted_ref, kernel_w, taps_w, keys_w, mixed_w, ssm_ref, to_hbm, from_hbm,
        normed_hbm, qkv_hbm, token_hbm, residual_hbm, small_t, norm_two_ref, down_ref, up_ref, out_ref,
    ), refs = refs[:21], refs[21:]
    outs, refs = refs[:count], refs[count:]
    (small_out, ssm_out, input_out), refs = refs[:3], refs[3:]
    near, refs = refs[:count], refs[count:]
    from_x = dict(zip([k for k in range(count) if piece_halves(k) == TWO], refs))
    refs = refs[len(from_x):]
    from_y, from_z, final, last = (refs[i * count : (i + 1) * count] for i in range(4))
    refs = refs[4 * count :]
    (
        to_ref, from_ref, normed_ref, qkv_ref, token_ref, residual_ref, own_ref, query_ref, value_ref, spectrum, line_ref, decay_ref, wave_ref, high_ref, back_ref,
        grad_proj, qkv_grad, gn_send, gn_own, gn_last, small_rows, small_ref, small_all, small_sum, small_last,
        ssm_ref_all, ssm_all, ssm_sum,
    ), refs = refs[:28], refs[28:]
    (
        load_sem, late_sem, own_sem, core_s, core_r, x_s, x_r, y_s, y_r, z_s, z_r, f_s, f_r, sm_s, sm_r, ss_s, ss_r, sg_s, sg_r,
        side_s, side_r,
    ) = refs
    length, width = conv_ref.shape
    own_rows = token_ref.shape[0]
    place = Place()
    grads = {"down": down_ref, "up": up_ref, "out": out_ref, "qkv": qkv_grad}

    def core_copy(k, h):
        source, start, columns, _ = PIECES[k]
        part = columns // piece_halves(k)
        blocks = grads[source].at[:, :, 1 - place.c, :, pl.ds(start + h * part, part)]
        return send(blocks, near[k].at[h], core_s.at[k, h], core_r.at[k, h], place.over_core())

    def own_copy(k, h):
        source, start, columns, _ = PIECES[k]
        part = columns // piece_halves(k)
        blocks = grads[source].at[:, :, place.c, :, pl.ds(start + h * part, part)]
        return pltpu.make_async_copy(blocks, own_ref.at[k % 2, :, :, :, pl.ds(h * part, part)], own_sem.at[k % 2, h])

    def x_copy(k):
        return send(near[k].at[1 - place.s], from_x[k], x_s.at[k], x_r.at[k], place.over_x())

    def kept(k):
        return near[k].at[place.s] if piece_halves(k) == TWO else near[k].at[0]

    def y_copy(k):
        return send(kept(k).at[:, 1 - place.y], from_y[k], y_s.at[k], y_r.at[k], place.over_y())

    def z_copy(k, step):
        other = (place.z + step) % 4
        return send(
            kept(k).at[other, place.y], from_z[k].at[step - 1], z_s.at[k, step - 1], z_r.at[k, step - 1],
            place.along_z(step),
        )

    def last_copy(k):
        return send(final[k], last[k], f_s.at[k], f_r.at[k], place.over_x())

    def load_own(k):
        for h in range(piece_halves(k)):
            own_copy(k, h).start()

    def add_core(k):
        part = PIECES[k][2] // piece_halves(k)
        for h in range(piece_halves(k)):
            core_copy(k, h).wait_recv()
            if k != QKV:
                own_copy(k, h).wait()

            def own(i, h=h):
                if k == QKV:
                    return qkv_grad[i // 2, i % 2, place.c]
                return own_ref[k % 2, i // 2, i % 2, :, h * part : (h + 1) * part]

            def put(i, total, h=h):
                near[k][h, i // 2, i % 2] = total.astype(jnp.bfloat16)

            add_blocks(put, [own, lambda i, h=h: near[k][h, i // 2, i % 2]], 8)

    def add_x(k):
        x_copy(k).wait_recv()

        def put(i, total):
            kept(k)[i // 2, i % 2] = total.astype(jnp.bfloat16)

        add_blocks(put, [lambda i: kept(k)[i // 2, i % 2], lambda i: from_x[k][i // 2, i % 2]], 8)

    def add_y(k):
        y_copy(k).wait_recv()

        def put(i, total):
            kept(k)[i, place.y] = total.astype(jnp.bfloat16)

        add_blocks(put, [lambda i: kept(k)[i, place.y], lambda i: from_y[k][i]], 4)

    def start_z(k):
        for step in range(1, 4):
            z_copy(k, step).start()

    def add_z(k):
        for step in range(1, 4):
            z_copy(k, step).wait_recv()
        total = kept(k)[place.z, place.y].astype(jnp.float32)
        for step in range(3):
            total = total + from_z[k][step].astype(jnp.float32)
        final[k][...] = total.astype(jnp.bfloat16)

    def finish(k):
        last_copy(k).wait_recv()
        if PIECES[k][3] == "whole":
            outs[k][...] = final[k][...].astype(jnp.float32) + last[k][...].astype(jnp.float32)
        else:
            outs[k][place.s] = final[k][...]
            outs[k][1 - place.s] = last[k][...]

    def over_peers(action):
        def one(step, carry):
            action(step)
            return carry

        lax.fori_loop(1, 16, one, 0)

    def to_peer(source, target, send_sem, recv_sem, step):
        other = (place.d + step) % 16
        return send(source.at[other], target.at[place.d], send_sem.at[other], recv_sem.at[place.d], place.owner(other))

    def from_peer(target, send_sem, recv_sem, step):
        other = (place.d + step) % 16
        return send(target.at[other], target.at[other], send_sem.at[other], recv_sem.at[other], place.owner(other))

    def share(step):
        other = (place.d + step) % 16
        return send(ssm_sum.at[place.d], ssm_sum.at[place.d], sg_s.at[other], sg_r.at[place.d], place.owner(other))

    gn_copy = send(gn_send, gn_last, side_s.at[1], side_r.at[1], place.over_x())
    small_copy = send(small_sum, small_last, side_s.at[2], side_r.at[2], place.over_x())
    spectra = (kernel_w, mixed_w, taps_w, keys_w)

    def load_spectrum(i):
        return pltpu.make_async_copy(spectra[i], spectrum.at[i % 2], load_sem.at[i % 2])

    query_copy = pltpu.make_async_copy(query_hbm, query_ref, load_sem.at[2])
    value_copy = pltpu.make_async_copy(value_hbm, value_ref, load_sem.at[3])

    late_copies = [
        pltpu.make_async_copy(source, target, late_sem.at[i])
        for i, (source, target) in enumerate(
            ((qkv_hbm, qkv_ref), (normed_hbm, normed_ref), (token_hbm, token_ref), (residual_hbm, residual_ref))
        )
    ]
    to_copy = pltpu.make_async_copy(to_hbm, to_ref, late_sem.at[4])
    from_copy = pltpu.make_async_copy(from_hbm, from_ref, late_sem.at[5])
    greet_all(place)
    for k in range(QKV):
        for h in range(piece_halves(k)):
            core_copy(k, h).start()
    load_own(D1)
    load_own(U1)
    query_copy.start()
    to_copy.start()
    from_copy.start()
    load_spectrum(0).start()
    value_copy.start()
    load_spectrum(1).start()
    for copy in late_copies:
        copy.start()
    add_core(D1)
    y_copy(D1).start()
    load_own(DM)
    add_core(U1)
    x_copy(U1).start()
    load_own(UM)
    add_core(DM)
    load_own(OUT)
    add_core(UM)
    add_core(OUT)

    def keep(wave, value):
        wave_ref[wave] = value

    def lines(base, row, cols):
        return line_ref[pl.ds(base + row, 16), cols]

    def column(index, cols):
        return pl.ds(index * width + cols.start, cols.size)

    def read_conv_grad(base, row, cols):
        rows = pl.ds(base + row, 16)
        gradient = grad_all[base // own_rows, pl.ds(base % own_rows + row, 16), cols].astype(jnp.float32)
        grad_proj[rows, cols] = (gradient * conv_ref[rows, cols].astype(jnp.float32)).astype(jnp.bfloat16)
        return (gradient * query_ref[rows, cols]).astype(jnp.bfloat16).astype(jnp.float32)

    query_copy.wait()
    to_copy.wait()
    from_copy.wait()
    value_copy.wait()
    to_waves(width, read_conv_grad, RADIX, to_ref, high_ref, None, keep)
    load_spectrum(0).wait()
    product(width, spectrum.at[0], wave_ref, True, high_ref, None)
    load_spectrum(2).start()

    def put_mixed(base, row, cols, value):
        rows = pl.ds(base + row, 16)
        gradient = value.astype(jnp.bfloat16).astype(jnp.float32)
        grad_proj[rows, column(2, cols)] = (gradient * shifted_ref[rows, cols]).astype(jnp.bfloat16)
        line_ref[rows, cols] = gradient * value_ref[rows, cols]

    from_waves(width, from_ref, high_ref, None, back_ref, put_mixed)
    add_y(D1)
    start_z(D1)
    y_copy(DM).start()
    load_spectrum(1).wait()
    product(width, spectrum.at[1], wave_ref, True, high_ref, None)
    load_spectrum(3).start()

    def put_kernel(base, row, cols, value):
        decay_ref[pl.ds(base + row, 16), cols] = value

    from_waves(width, from_ref, high_ref, None, back_ref, put_kernel)
    add_x(U1)
    x_copy(OUT).start()
    to_waves(width, lines, RADIX, to_ref, high_ref, None, keep)
    add_y(DM)
    start_z(DM)
    y_copy(UM).start()
    y_copy(U1).start()
    load_spectrum(2).wait()
    product(width, spectrum.at[0], wave_ref, True, high_ref, None)

    def put_keys(base, row, cols, value):
        grad_proj[pl.ds(base + row, 16), column(1, cols)] = value.astype(jnp.bfloat16)

    from_waves(width, from_ref, high_ref, None, back_ref, put_keys)
    add_x(OUT)

    def project_back(begin, put):
        def one(index, carry):
            row = pl.multiple_of(index * 256, 256)
            value = lax.dot_general(
                grad_proj[pl.ds(pl.multiple_of(begin + row, 256), 256), :], qkv_ref[...], (((1,), (1,)), ((), ())),
                preferred_element_type=jnp.float32,
            )
            put(pl.ds(row, 256), value)
            return carry

        lax.fori_loop(0, own_rows // 256, one, 0)

    def put_send(rows, value):
        gn_send[rows, :] = value.astype(jnp.bfloat16)

    def put_own(rows, value):
        gn_own[rows, :] = value

    late_copies[0].wait()
    project_back((1 - place.s) * own_rows, put_send)
    gn_copy.start()
    for copy in late_copies[1:]:
        copy.wait()
    for pair in range(TWO):
        columns = 2 * 4 * qkv_grad.shape[3]
        value = lax.dot_general(
            normed_ref[:, pair * columns : (pair + 1) * columns], grad_proj[...], (((0,), (0,)), ((), ())),
            preferred_element_type=jnp.float32,
        )
        qkv_grad[2 * pair : 2 * pair + 2] = value.astype(jnp.bfloat16).reshape((2,) + qkv_grad.shape[1:])
    core_copy(QKV, 0).start()
    project_back(place.s * own_rows, put_own)
    add_y(UM)
    start_z(UM)
    add_core(QKV)
    y_copy(QKV).start()
    add_y(U1)
    start_z(U1)
    load_spectrum(3).wait()
    product(width, spectrum.at[1], wave_ref, True, high_ref, None)
    small_rows[...] = jnp.zeros(small_rows.shape, jnp.float32)
    small_rows[:TAP_ROWS, pl.ds(pl.multiple_of(place.s * width, LANES), width)] = first_positions(
        width, TAP_ROWS, from_ref, high_ref, None
    )
    decay_gradients(0, length, ssm_ref, decay_ref, ssm_ref_all)
    add_y(QKV)
    start_z(QKV)
    y_copy(OUT).start()
    add_z(D1)
    add_z(DM)
    decay_gradients(1, length, ssm_ref, decay_ref, ssm_ref_all)
    add_z(UM)
    add_z(U1)
    add_y(OUT)
    start_z(OUT)
    decay_gradients(2, length, ssm_ref, decay_ref, ssm_ref_all)
    over_peers(lambda step: to_peer(ssm_ref_all, ssm_all, ss_s, ss_r, step).start())
    gn_copy.wait_recv()
    for k in (D1, DM, UM, U1):
        last_copy(k).start()

    def norm_back(index, sums):
        rows = pl.ds(pl.multiple_of(index * 32, 32), 32)
        normal, inverse = layer_norm_parts(token_ref[rows, :].astype(jnp.float32))
        upstream = gn_own[rows, :] + gn_last[rows, :].astype(jnp.float32)
        into, gain, bias = layer_norm_back(upstream, normal, inverse, small_t[TAP_ROWS : TAP_ROWS + 1, :])
        input_out[rows, :] = residual_ref[rows, :] + into
        return sums[0] + gain, sums[1] + bias

    zero = jnp.sum(norm_two_ref[...], axis=0, keepdims=True) * 0.0
    gain, bias = lax.fori_loop(0, own_rows // 32, norm_back, (zero, zero), unroll=4)
    small_rows[TAP_ROWS : TAP_ROWS + 1, :] = gain
    small_rows[TAP_ROWS + 1 : TAP_ROWS + 2, :] = bias
    small_rows[TAP_ROWS + 2 : TAP_ROWS + 4, :] = norm_two_ref[...]
    small_ref[...] = small_rows[...].T.astype(jnp.bfloat16).reshape(small_ref.shape)
    over_peers(lambda step: to_peer(small_ref, small_all, sm_s, sm_r, step).start())
    add_z(QKV)
    last_copy(QKV).start()
    add_z(OUT)
    last_copy(OUT).start()

    over_peers(lambda step: from_peer(ssm_all, ss_s, ss_r, step).wait_recv())
    ssm_all[place.d] = ssm_ref_all[place.d]
    total = ssm_all[0]
    for index in range(1, 16):
        total = total + ssm_all[index]
    ssm_sum[place.d] = total
    over_peers(lambda step: share(step).start())
    over_peers(lambda step: from_peer(small_all, sm_s, sm_r, step).wait_recv())

    def add_small(step, total):
        return total + small_all[(place.d + step) % 16].astype(jnp.float32)

    small_sum[...] = lax.fori_loop(1, 16, add_small, small_ref[place.d].astype(jnp.float32)).astype(jnp.bfloat16)
    small_copy.start()
    for k in range(count):
        finish(k)
    over_peers(lambda step: from_peer(ssm_sum, sg_s, sg_r, step).wait_recv())
    ssm_out[...] = ssm_sum[...]
    small_copy.wait_recv()
    small_out[...] = small_sum[...].astype(jnp.float32) + small_last[...].astype(jnp.float32)

    for k in range(count):
        for h in range(piece_halves(k)):
            core_copy(k, h).wait_send()
        if piece_halves(k) == TWO:
            x_copy(k).wait_send()
        y_copy(k).wait_send()
        for step in range(1, 4):
            z_copy(k, step).wait_send()
        last_copy(k).wait_send()
    for copy in (gn_copy, small_copy):
        copy.wait_send()
    over_peers(lambda step: to_peer(small_ref, small_all, sm_s, sm_r, step).wait_send())
    over_peers(lambda step: to_peer(ssm_ref_all, ssm_all, ss_s, ss_r, step).wait_send())
    over_peers(lambda step: share(step).wait_send())


def backward_mixer(
    gated_grad, query, value, conv, shifted, kernel_w, taps_w, keys_w, mixed_w, ssm, to_table, from_table, normed, qkv, tokens,
    residual, small, norm_two, down, up, out,
):
    f32, low = jnp.float32, jnp.bfloat16
    count = len(PIECES)
    length, width = conv.shape
    own_rows, model = tokens.shape
    owned = down.shape[3]
    waves = (RADIX, 2 * HALF, width)
    vmem, anywhere = pl.BlockSpec(memory_space=pltpu.VMEM), pl.BlockSpec(memory_space=pl.ANY)
    results, near, from_x, from_y, from_z, final, last = [], [], [], [], [], [], []
    for k, (_, _, columns, way) in enumerate(PIECES):
        halves = piece_halves(k)
        part = columns // halves
        whole = way == "whole"
        results.append(jax.ShapeDtypeStruct((owned, part) if whole else (TWO, owned, part), f32 if whole else low))
        near.append(pltpu.VMEM((halves, FOUR, TWO, owned, part), low))
        if halves == TWO:
            from_x.append(pltpu.VMEM((FOUR, TWO, owned, part), low))
        from_y.append(pltpu.VMEM((FOUR, owned, part), low))
        from_z.append(pltpu.VMEM((3, owned, part), low))
        final.append(pltpu.VMEM((owned, part), low))
        last.append(pltpu.VMEM((owned, part), low))
    dma = pltpu.SemaphoreType.DMA
    slots = (16, 8, width)
    packed = (16, owned, LANES)
    results += [
        jax.ShapeDtypeStruct(packed[1:], f32),
        jax.ShapeDtypeStruct(slots, f32),
        jax.ShapeDtypeStruct((own_rows, model), f32),
    ]
    return pl.pallas_call(
        backward_body,
        out_shape=tuple(results),
        in_specs=[vmem, anywhere, anywhere, vmem, vmem]
        + [anywhere] * 4
        + [vmem]
        + [anywhere] * 6
        + [vmem] * 2
        + [anywhere] * 3,
        out_specs=(vmem,) * len(results),
        scratch_shapes=near
        + from_x
        + from_y
        + from_z
        + final
        + last
        + [
            pltpu.VMEM(to_table.shape, low),
            pltpu.VMEM(from_table.shape, low),
            pltpu.VMEM((length, model), low),
            pltpu.VMEM((model, 3 * width), low),
            pltpu.VMEM((own_rows, model), low),
            pltpu.VMEM((own_rows, model), f32),
            pltpu.VMEM((2, FOUR, TWO, owned, 1536), low),
            pltpu.VMEM((length, width), f32),
            pltpu.VMEM((length, width), f32),
            pltpu.VMEM((2,) + waves, f32),
            pltpu.VMEM((length, width), f32),
            pltpu.VMEM((length, width), f32),
            pltpu.VMEM(waves, f32),
            pltpu.VMEM(waves, low),
            pltpu.VMEM(waves, f32),
            pltpu.VMEM((length, 3 * width), low),
            pltpu.VMEM((FOUR, TWO, TWO, owned, 3 * width), low),
            pltpu.VMEM((own_rows, model), low),
            pltpu.VMEM((own_rows, model), f32),
            pltpu.VMEM((own_rows, model), low),
            pltpu.VMEM((LANES, model), f32),
            pltpu.VMEM(packed, low),
            pltpu.VMEM(packed, low),
            pltpu.VMEM(packed[1:], low),
            pltpu.VMEM(packed[1:], low),
            pltpu.VMEM(slots, f32),
            pltpu.VMEM(slots, f32),
            pltpu.VMEM(slots, f32),
            dma((4,)),
            dma((6,)),
            dma((2, TWO)),
            dma((count, TWO)),
            dma((count, TWO)),
        ]
        + [dma((count,))] * 4
        + [dma((count, 3))] * 2
        + [dma((count,))] * 2
        + [dma((16,))] * 6
        + [dma((3,))] * 2,
        compiler_params=pltpu.CompilerParams(collective_id=1, has_side_effects=True, vmem_limit_bytes=VMEM_LIMIT),
        name="backward_mixer",
    )(
        gated_grad, query, value, conv, shifted, kernel_w, taps_w, keys_w, mixed_w, ssm, to_table, from_table, normed, qkv, tokens,
        residual, small, norm_two, down, up, out,
    )


def adam_parts(param, first, second, gradient, learn_rate, decay_weight):
    first_new = BETA_ONE * first + (1.0 - BETA_ONE) * gradient
    second_new = BETA_TWO * second + (1.0 - BETA_TWO) * gradient * gradient
    first_hat = first_new / (1.0 - BETA_ONE**STEP_COUNT)
    second_hat = second_new / (1.0 - BETA_TWO**STEP_COUNT)
    step = learn_rate * (first_hat / (jnp.sqrt(second_hat) + ADAM_EPS) + decay_weight * param)
    return step, first_new, second_new


def adam_body(
    early_sum, down_last, up_last, down_next, up_next, out_sum, qkv_sum, small_sum, ssm_sum,
    attn_p, mlp_p, norm_p, tap_p, ssm_p, attn_m, mlp_m, norm_m, tap_m, ssm_m,
    attn_step, attn_new, mlp_step, mlp_new, norm_step, norm_new, tap_step, tap_new, ssm_step, ssm_new,
    *, scale,
):
    f32 = jnp.float32
    width = out_sum.shape[2]

    def attn(start, gradient):
        cols = slice(start, start + width)
        attn_step[:, cols], attn_new[0, :, cols], attn_new[1, :, cols] = adam_parts(
            attn_p[:, cols].astype(f32), attn_m[0, :, cols], attn_m[1, :, cols], gradient.astype(f32) * scale,
            LEARN_RATE, DECAY_RATE,
        )

    def mlp(plane, start, source, slot):
        count = source.shape[-1]
        for begin in range(0, count, width):
            gradient = source[:, begin : begin + width] if slot is None else source[slot, :, begin : begin + width]
            cols = slice(start + begin, start + begin + width)
            mlp_step[plane, :, cols], mlp_new[0, plane, :, cols], mlp_new[1, plane, :, cols] = adam_parts(
                mlp_p[plane, :, cols].astype(f32), mlp_m[0, plane, :, cols], mlp_m[1, plane, :, cols],
                gradient.astype(f32) * scale, LEARN_RATE, DECAY_RATE,
            )

    for half in range(2):
        for place in range(3):
            attn((2 * place + half) * width, qkv_sum[half, :, place * width : (place + 1) * width])
        attn((6 + half) * width, out_sum[half])
        mlp(0, up_last.shape[2] * 2 + half * up_last.shape[2], up_last, half)
    for piece in range(early_sum.shape[0]):
        mlp(1 - piece % 2, piece // 2 * HIDDEN_BLOCK, early_sum, piece)
    mlp(0, HIDDEN_BLOCK, up_next, None)
    mlp(1, HIDDEN_BLOCK, down_next, None)
    mlp(1, down_last.shape[1], down_last, None)
    tap_step[...], tap_new[0], tap_new[1] = adam_parts(
        tap_p[...].astype(f32), tap_m[0], tap_m[1], small_sum[:, :TAP_ROWS] * scale, LEARN_RATE, DECAY_RATE
    )
    small = small_sum[...].T * scale
    norm_step[...], norm_new[0], norm_new[1] = adam_parts(
        norm_p[...].astype(f32), norm_m[0], norm_m[1], small[TAP_ROWS : TAP_ROWS + 4], LEARN_RATE, 0.0
    )
    for plane in range(2):
        gradient = ssm_sum[plane * 8 : plane * 8 + 8].reshape(ssm_p.shape[1:]) * scale
        ssm_step[plane], ssm_new[0, plane], ssm_new[1, plane] = adam_parts(
            ssm_p[plane], ssm_m[0, plane], ssm_m[1, plane], gradient, SSM_LEARN_RATE, 0.0
        )


def adam_all(sums, params, moments, scale):
    vmem = pl.BlockSpec(memory_space=pltpu.VMEM)
    outs = []
    for param, moment in zip(params, moments):
        outs += [jax.ShapeDtypeStruct(param.shape, jnp.float32), jax.ShapeDtypeStruct(moment.shape, jnp.float32)]
    return pl.pallas_call(
        partial(adam_body, scale=scale),
        out_shape=tuple(outs),
        in_specs=[vmem] * (len(sums) + 2 * len(params)),
        out_specs=(vmem,) * len(outs),
        compiler_params=pltpu.CompilerParams(vmem_limit_bytes=VMEM_LIMIT),
        name="adam",
    )(*sums, *params, *moments)


def turned_last(value):
    return jnp.swapaxes(value, -1, -2)


def per_device_split(
    tokens,
    cotangent,
    attn_weight,
    mlp_weight,
    norms,
    taps,
    ssm_params,
    attn_moments,
    mlp_moments,
    norm_moments,
    tap_moments,
    ssm_moments,
):
    f32, low = jnp.float32, jnp.bfloat16
    rows, width = tokens.shape[1:]
    shares = lax.axis_size("seq")
    owners = lax.axis_size("dp")
    length = rows * shares
    part = width // shares
    tap_count = taps.shape[0]
    to_table, from_table = map(jnp.asarray, transform_tables())

    owned = attn_weight.shape[0]
    small = jnp.concatenate([taps, norms, jnp.zeros((LANES - 4 - tap_count, owned), low)]).T
    ssm_turned = jnp.swapaxes(ssm_params, 1, 2)
    (
        qkv_full, _, _, small_full, normed_low, query, value, conv, shifted, kernel_w, taps_w, keys_w, mixed_w,
        layer_out, grad_residual, grad_norm_two, grad_gated, grad_up, grad_down, grad_out, early_sums,
    ) = forward_layer(
        tokens[0], cotangent[0], attn_weight, mlp_weight, small, ssm_turned,
        to_table, from_table,
    )
    scale = 1.0 / math.sqrt(owners * length)
    sums = backward_mixer(
        grad_gated, query, value, conv, shifted, kernel_w, taps_w, keys_w, mixed_w, ssm_turned, to_table, from_table,
        normed_low, qkv_full.reshape(width, 3 * part), tokens[0], grad_residual, small_full, grad_norm_two,
        grad_down, grad_up, grad_out,
    )
    (
        attn_step, attn_new, mlp_step, mlp_new, norms_step, norm_new, taps_step, tap_new, ssm_step, ssm_new
    ) = adam_all(
        (early_sums,) + tuple(sums[:8]),
        (attn_weight, mlp_weight, norms, taps.T, ssm_turned),
        (attn_moments, mlp_moments, norm_moments, turned_last(tap_moments), turned_last(ssm_moments)),
        scale,
    )
    taps_step, tap_new, ssm_step, ssm_new = map(turned_last, (taps_step, tap_new, ssm_step, ssm_new))
    input_grad = sums[8]
    return (
        layer_out[None],
        input_grad[None],
        attn_step,
        attn_new,
        mlp_step,
        mlp_new,
        norms_step,
        norm_new,
        taps_step,
        tap_new,
        ssm_step,
        ssm_new,
    )


def solution(mesh):
    fits = (mesh.shape["seq"], mesh.shape["dp"]) == (2, 16)

    def chosen(tokens, cotangent, attn_weight, mlp_weight, norms, taps, *others):
        fast = fits and tokens.shape[1:] == (RADIX * HALF // 2, 6 * LANES) and taps.shape[0] == TAP_ROWS
        plan = per_device_split if fast else per_device
        return plan(tokens, cotangent, attn_weight, mlp_weight, norms, taps, *others)

    return jax.shard_map(
        chosen,
        mesh=mesh,
        in_specs=(
            P("dp", "seq", None),
            P("dp", "seq", None),
            P("dp", None),
            P(None, "dp", None),
            P(None, "dp"),
            P(None, "dp"),
            P(None, "seq", None),
            P(None, "dp", None),
            P(None, None, "dp", None),
            P(None, None, "dp"),
            P(None, None, "dp"),
            P(None, None, "seq", None),
        ),
        out_specs=(
            P("dp", "seq", None),
            P("dp", "seq", None),
            P("dp", None),
            P(None, "dp", None),
            P(None, "dp", None),
            P(None, None, "dp", None),
            P(None, "dp"),
            P(None, None, "dp"),
            P(None, "dp"),
            P(None, None, "dp"),
            P(None, "seq", None),
            P(None, None, "seq", None),
        ),
        check_vma=False,
    )
```
